32 devices in a mesh: dp: 8 (over y, x, core), pipe: 4 (over z).
Axes of the slice: x: 2, y: 2, z: 4, core: 2. Of those that a mesh axis runs over, the one named last changes fastest.
Arguments:
- tokens: bfloat16 [16, 256, 1152], P('dp', 'pipe'), may hold values from -6 to 6
- cotangent: bfloat16 [16, 256, 1152], P('dp', 'pipe'), may hold values from -6 to 6
- timesteps: int32 [16], P('dp'), may hold values from 0 to 999
- labels: int32 [16], P('dp'), may hold values from 0 to 999
- class_table: bfloat16 [1000, 1152], replicated, may hold values from -6 to 6
- section_in_weights: bfloat16 [4, 1152, 4608], P('pipe', 'dp'), as said below
- section_out_weights: bfloat16 [4, 1152, 4608], P('pipe', 'dp'), as said below
- modulation_weights: bfloat16 [4, 1152, 3456], P('pipe', 'dp'), may hold values from -0.1875 to 0.1875
Outputs:
- output_tokens: bfloat16 [16, 256, 1152], P('dp', 'pipe')
- input_grad: float32 [16, 256, 1152], P('dp', 'pipe')
- grad_class_table: float32 [1000, 1152], replicated
- grad_section_in: float32 [4, 1152, 4608], P('pipe', 'dp')
- grad_section_out: float32 [4, 1152, 4608], P('pipe', 'dp')
- grad_modulation: float32 [4, 1152, 3456], P('pipe', 'dp')
The draws below stay inside these ranges and needn't reach their ends.
Inputs may be any that keep to these rules, and one draw needn't show every extreme that they name: `section_in_weights`: independent entries. `section_out_weights`: independent entries.
All inputs are finite; a program needn't handle non-finite values.
Results may differ from the reference program's by a relative error of at most 0.023.
Values may be sent and summed in bfloat16 or wider, within the bound.
A program may use at most 320 MiB of HBM per device.

```python
import math
import jax
import jax.numpy as jnp
from jax import lax

D = 1152
HEADS = 16
HEAD = 72
FF = 4608
CLASSES = 1000
TOK = 256
SECTIONS = 4
IMAGES = 16


def draw_section_in_weights(key, part):
    key = jax.random.fold_in(key, 11)
    noise = jnp.clip(jax.random.normal(key, (SECTIONS, D, FF), jnp.float32), -6.0, 6.0)
    section_ids = lax.broadcasted_iota(jnp.int32, (SECTIONS, D, FF), 0)
    column_ids = lax.broadcasted_iota(jnp.int32, (SECTIONS, D, FF), 2)
    factor = jnp.where((section_ids % 2 == 0) & (column_ids >= 3 * D), 3.0, 1.0)
    return (noise * factor * D ** (-0.5)).astype(jnp.bfloat16)


def draw_section_out_weights(key, part):
    key = jax.random.fold_in(key, 23)
    noise = jnp.clip(jax.random.normal(key, (SECTIONS, D, FF), jnp.float32), -6.0, 6.0)
    section_ids = lax.broadcasted_iota(jnp.int32, (SECTIONS, D, FF), 0)
    factor = jnp.where(section_ids % 2 == 0, D ** (-0.5), 1.5 * FF ** (-0.5))
    return (noise * factor).astype(jnp.bfloat16)


def set_ends(values, rng, least, top_value):
    extent = values.shape
    index_at = [jax.random.randint(jax.random.fold_in(rng, axis), (), 0, extent[axis]) for axis in range(len(extent))]
    values = values.at[tuple(index_at)].set(least)
    longest = extent.index(max(extent))
    index_at[longest] = (index_at[longest] + 1) % extent[longest]
    return values.at[tuple(index_at)].set(top_value)


def levels(key, dims, cuts, least, high):
    factor_of = 1.0
    for position, parts in cuts:
        heights = jax.random.uniform(jax.random.fold_in(jax.random.fold_in(key, 6), position), (parts,), jnp.float32, least / len(cuts), high / len(cuts))
        factor_of = factor_of * jnp.repeat(jnp.exp(heights), dims[position] // parts).reshape((-1,) + (1,) * (len(dims) - 1 - position))
    return factor_of


def normal_values(key, shape, width, reach, pieces=(), kind=jnp.bfloat16):
    entries = width * jax.random.normal(key, shape, jnp.float32)
    if pieces:
        entries = entries * levels(key, shape, pieces, -0.22, 0.18)
    return jnp.clip(entries, -reach, reach).astype(kind)


def setup_inputs(seed: int = 0) -> dict:
    seeds = jax.random.split(jax.random.key(seed), 9)
    return {
        "tokens": normal_values(seeds[0], (IMAGES, TOK, D), 1.0, 6.0, ((0, 8), (1, 4))),
        "cotangent": normal_values(seeds[1], (IMAGES, TOK, D), 1.0, 6.0, ((0, 8), (1, 4))),
        "timesteps": set_ends(jax.random.randint(seeds[2], (IMAGES,), 0, 1000), jax.random.fold_in(seeds[2], 1), 0, 999).astype(jnp.int32),
        "labels": set_ends(jax.random.randint(seeds[3], (IMAGES,), 0, CLASSES), jax.random.fold_in(seeds[3], 1), 0, CLASSES - 1).astype(jnp.int32),
        "class_table": normal_values(seeds[4], (CLASSES, D), 1.0, 6.0),
        "section_in_weights": draw_section_in_weights(jax.random.fold_in(seeds[8], 71), 0),
        "section_out_weights": draw_section_out_weights(jax.random.fold_in(seeds[8], 71), 0),
        "modulation_weights": normal_values(seeds[7], (SECTIONS, D, 3 * D), D ** -0.5, 0.1875, ((0, 4), (1, 8))),
    }


@jax.custom_vjp
def low(v):
    return lax.optimization_barrier(v.astype(jnp.bfloat16)).astype(jnp.float32)

@jax.custom_vjp
def low_back(v):
    return v

def low_keep(v):
    return (low(v), None)

def low_pass(kept, grad):
    return (grad,)

def back_keep(v):
    return (v, None)

def back_low(kept, grad):
    return (low(grad),)
low.defvjp(low_keep, low_pass)
low_back.defvjp(back_keep, back_low)
epsilon = 1e-06
highest = lax.Precision.HIGHEST

def both_ways(value):
    return low(low_back(value))

def product(former, latter):
    return jnp.matmul(former, latter, precision=highest)

def sinusoid(step_values, model_width):
    half_width = model_width // 2
    frequencies = jnp.exp(-math.log(10000.0) * jnp.arange(half_width, dtype=jnp.float32) / half_width)
    angles = step_values.astype(jnp.float32)[:, None] * frequencies[None, :]
    return jnp.concatenate([jnp.cos(angles), jnp.sin(angles)], axis=1)

def normalize(row_values):
    centered = row_values - lax.optimization_barrier(jnp.mean(row_values, axis=-1, keepdims=True))
    return centered * lax.rsqrt(lax.optimization_barrier(jnp.mean(centered * centered, axis=-1, keepdims=True)) + epsilon)

def modulate(conditioner, mod_weight, row_values):
    mod_values = low_back(product(conditioner, mod_weight))
    shift_vec = mod_values[:, None, :D]
    scale_vec = mod_values[:, None, D:2 * D]
    gate_vec = mod_values[:, None, 2 * D:]
    normed = low(normalize(row_values) * (1.0 + scale_vec) + shift_vec)
    return (normed, gate_vec)

def attend_image(operands):
    queries, keyed, valued = operands
    scores = low_back(jnp.einsum('qhd,khd->hqk', queries, keyed, precision=highest) * HEAD ** (-0.5))
    probs_low = low(jax.nn.softmax(scores, axis=-1))
    return jnp.einsum('hqk,khd->qhd', probs_low, valued, precision=highest)

def attention_section(row_values, conditioner, in_weight, out_weight, mod_weight):
    normed, gate_vec = modulate(conditioner, mod_weight, row_values)
    time_token = both_ways(product(conditioner, out_weight[:, 3 * D:]))
    time_bias = low_back(product(time_token, out_weight[:, :3 * D]))
    qkv = both_ways(product(normed, in_weight[:, :3 * D]) + time_bias[:, None, :])
    split_qkv = qkv.reshape(IMAGES, TOK, 3, HEADS, HEAD)
    mixed = lax.map(jax.checkpoint(attend_image), (split_qkv[:, :, 0], split_qkv[:, :, 1], split_qkv[:, :, 2]))
    head_rows = both_ways(mixed.reshape(IMAGES, TOK, D))
    branch = low_back(product(head_rows, in_weight[:, 3 * D:]))
    return row_values + gate_vec * branch

def feed_section(row_values, conditioner, in_weight, out_weight, mod_weight):
    normed, gate_vec = modulate(conditioner, mod_weight, row_values)
    pre_act = low_back(product(normed, in_weight))
    hidden = low(jax.nn.gelu(pre_act, approximate=True))
    branch = low_back(jnp.einsum('itf,df->itd', hidden, out_weight, precision=highest))
    return row_values + gate_vec * branch

def forward(row_values, table, in_weights, out_weights, mod_weights, timesteps, labels):
    condition = sinusoid(timesteps, D) + table[labels]
    conditioner = low(jax.nn.silu(condition))
    for section_index in range(SECTIONS):
        if section_index % 2 == 0:
            result = attention_section(row_values, conditioner, in_weights[section_index], out_weights[section_index], mod_weights[section_index])
        else:
            result = feed_section(row_values, conditioner, in_weights[section_index], out_weights[section_index], mod_weights[section_index])
        if section_index == SECTIONS - 1:
            row_values = low(result)
        else:
            row_values = both_ways(result)
    return row_values

def reference(tokens, cotangent, timesteps, labels, class_table, section_in_weights, section_out_weights, modulation_weights):

    def run(row_values, table, in_weights, out_weights, mod_weights):
        return forward(row_values, table, in_weights, out_weights, mod_weights, timesteps, labels)
    primal = (tokens.astype(jnp.float32), class_table.astype(jnp.float32), section_in_weights.astype(jnp.float32), section_out_weights.astype(jnp.float32), modulation_weights.astype(jnp.float32))
    result, pullback = jax.vjp(run, *primal)
    grads = pullback(cotangent.astype(jnp.float32))
    return (result.astype(jnp.bfloat16), grads[0], grads[1], grads[2], grads[3], grads[4])
```

```python
from functools import partial
import math

import jax
import jax.numpy as jnp
from jax import lax
from jax.sharding import PartitionSpec as P

HEADS = 16
HEAD = 72


epsilon = 1e-06
highest = lax.Precision.HIGHEST


def shifted(block, axis, distance):
    devices = range(lax.axis_size(axis))
    route = [(i - distance, i) for i in devices if i - distance in devices]
    return lax.ppermute(block, axis, route)


def sinusoid(step_values, model_width):
    half_width = model_width // 2
    frequencies = jnp.exp(
        -math.log(10000.0) * jnp.arange(half_width, dtype=jnp.float32) / half_width
    )
    angles = step_values.astype(jnp.float32)[:, None] * frequencies[None, :]
    return jnp.concatenate([jnp.cos(angles), jnp.sin(angles)], axis=1)


def product(former, latter):
    return jnp.dot(former, latter, preferred_element_type=jnp.float32)


def contract_rows(former, latter):
    return lax.dot_general(
        former, latter, (((0,), (0,)), ((), ())), preferred_element_type=jnp.float32
    )


def contract_cols(former, latter):
    return lax.dot_general(
        former, latter, (((1,), (1,)), ((), ())), preferred_element_type=jnp.float32
    )


def normalize_rows(row_values):
    centered = row_values - jnp.mean(row_values, axis=-1, keepdims=True)
    inverse = lax.rsqrt(jnp.mean(centered * centered, axis=-1, keepdims=True) + epsilon)
    return (centered * inverse, inverse)


def modulation_front(section_input, mod_row):
    model_width = section_input.shape[1]
    shift_vec = mod_row[:model_width]
    scale_vec = mod_row[model_width : 2 * model_width]
    gate_vec = mod_row[2 * model_width :]
    centred, inverse = normalize_rows(section_input.astype(jnp.float32))
    normed = (centred * (1.0 + scale_vec) + shift_vec).astype(jnp.bfloat16)
    return (normed, centred, inverse, scale_vec, gate_vec)


def modulation_back(grad_normed, centred, inverse, scale_vec, grad_rows, grad_gate):
    grad_shift = jnp.sum(grad_normed, axis=0)
    grad_scale = jnp.sum(grad_normed * centred, axis=0)
    grad_centred = grad_normed * (1.0 + scale_vec)
    grad_input = inverse * (
        grad_centred
        - jnp.mean(grad_centred, axis=-1, keepdims=True)
        - centred * jnp.mean(grad_centred * centred, axis=-1, keepdims=True)
    )
    grad_mod = jnp.concatenate([grad_shift, grad_scale, grad_gate]).astype(jnp.bfloat16)
    return (grad_rows + grad_input, grad_mod)


def attention_parts(section_input, mod_row, time_row, weights):
    in_weight = weights[0]
    model_width = section_input.shape[1]
    tok_len = section_input.shape[0]
    normed, centred, inverse, scale_vec, gate_vec = modulation_front(section_input, mod_row)
    qkv = (product(normed, in_weight[:, : 3 * model_width]) + time_row).astype(jnp.bfloat16)
    split_qkv = qkv.reshape(tok_len, 3, HEADS, HEAD)
    queries = split_qkv[:, 0]
    keyed = split_qkv[:, 1]
    valued = split_qkv[:, 2]
    scores = jnp.einsum(
        "qhd,khd->hqk", queries, keyed, preferred_element_type=jnp.float32
    ) * HEAD ** (-0.5)
    probs_full = jax.nn.softmax(scores, axis=-1)
    probs_low = probs_full.astype(jnp.bfloat16)
    mixed = jnp.einsum("hqk,khd->qhd", probs_low, valued, preferred_element_type=jnp.float32)
    head_rows = mixed.reshape(tok_len, model_width).astype(jnp.bfloat16)
    branch = product(head_rows, in_weight[:, 3 * model_width :])
    section_output = section_input.astype(jnp.float32) + gate_vec * branch
    saved_parts = (
        normed,
        centred,
        inverse,
        scale_vec,
        gate_vec,
        queries,
        keyed,
        valued,
        probs_full,
        probs_low,
        head_rows,
        branch,
    )
    return (section_output, saved_parts)


def attention_forward(section_input, mod_row, time_row, weights):
    return attention_parts(section_input, mod_row, time_row, weights)[0]


def attention_backward(section_input, grad_in, mod_row, time_row, weights):
    in_weight = weights[0]
    model_width = section_input.shape[1]
    tok_len = section_input.shape[0]
    unused, saved_parts = attention_parts(section_input, mod_row, time_row, weights)
    (
        normed,
        centred,
        inverse,
        scale_vec,
        gate_vec,
        queries,
        keyed,
        valued,
        probs_full,
        probs_low,
        head_rows,
        branch,
    ) = saved_parts
    grad_rows = grad_in.astype(jnp.float32)
    grad_branch = (gate_vec * grad_rows).astype(jnp.bfloat16)
    grad_gate = jnp.sum(grad_rows * branch, axis=0)
    grad_heads = contract_cols(grad_branch, in_weight[:, 3 * model_width :]).astype(jnp.bfloat16)
    heads_split = grad_heads.reshape(tok_len, HEADS, HEAD)
    grad_probs = jnp.einsum("qhd,khd->hqk", heads_split, valued, preferred_element_type=jnp.float32)
    grad_value = jnp.einsum(
        "hqk,qhd->khd", probs_low, heads_split, preferred_element_type=jnp.float32
    )
    grad_scores = (
        probs_full * (grad_probs - jnp.sum(probs_full * grad_probs, axis=-1, keepdims=True))
    ).astype(jnp.bfloat16)
    grad_query = jnp.einsum(
        "hqk,khd->qhd", grad_scores, keyed, preferred_element_type=jnp.float32
    ) * HEAD ** (-0.5)
    grad_key = jnp.einsum(
        "hqk,qhd->khd", grad_scores, queries, preferred_element_type=jnp.float32
    ) * HEAD ** (-0.5)
    grad_qkv = (
        jnp.stack([grad_query, grad_key, grad_value], axis=1)
        .reshape(tok_len, 3 * model_width)
        .astype(jnp.bfloat16)
    )
    grad_normed = contract_cols(grad_qkv, in_weight[:, : 3 * model_width])
    grad_time = jnp.sum(grad_qkv, axis=0, dtype=jnp.float32).astype(jnp.bfloat16)
    grad_input, grad_mod = modulation_back(
        grad_normed, centred, inverse, scale_vec, grad_rows, grad_gate
    )
    narrow_zero = jnp.zeros((tok_len, model_width), jnp.bfloat16)
    return (
        grad_input,
        normed,
        jnp.concatenate([grad_qkv, narrow_zero], axis=1),
        grad_branch,
        jnp.concatenate([head_rows, narrow_zero, narrow_zero, narrow_zero], axis=1),
        grad_mod,
        grad_time,
    )


def feed_parts(section_input, mod_row, weights):
    in_weight, out_weight = weights
    normed, centred, inverse, scale_vec, gate_vec = modulation_front(section_input, mod_row)
    pre_act = product(normed, in_weight)
    hidden = jax.nn.gelu(pre_act, approximate=True).astype(jnp.bfloat16)
    branch = contract_cols(hidden, out_weight)
    section_output = section_input.astype(jnp.float32) + gate_vec * branch
    return (
        section_output,
        (normed, centred, inverse, scale_vec, gate_vec, pre_act, hidden, branch),
    )


def feed_forward(section_input, mod_row, time_row, weights):
    return feed_parts(section_input, mod_row, weights)[0]


def feed_backward(section_input, grad_in, mod_row, time_row, weights):
    in_weight, out_weight = weights
    unused, saved_parts = feed_parts(section_input, mod_row, weights)
    normed, centred, inverse, scale_vec, gate_vec, pre_act, hidden, branch = saved_parts
    grad_rows = grad_in.astype(jnp.float32)
    grad_branch = (gate_vec * grad_rows).astype(jnp.bfloat16)
    grad_gate = jnp.sum(grad_rows * branch, axis=0)
    grad_hidden = product(grad_branch, out_weight)
    gelu_pull = jax.vjp(partial(jax.nn.gelu, approximate=True), pre_act)[1]
    grad_pre = gelu_pull(grad_hidden)[0].astype(jnp.bfloat16)
    grad_normed = contract_cols(grad_pre, in_weight)
    grad_input, grad_mod = modulation_back(
        grad_normed, centred, inverse, scale_vec, grad_rows, grad_gate
    )
    return (
        grad_input,
        normed,
        grad_pre,
        grad_branch,
        hidden,
        grad_mod,
        jnp.zeros(grad_mod.shape, jnp.bfloat16),
    )


def spare_forward(section_input, mod_row, time_row, weights):
    return jnp.zeros(section_input.shape, jnp.float32)


def spare_backward(section_input, grad_in, mod_row, time_row, weights):
    tok_len, model_width = section_input.shape
    hidden_width = weights[0].shape[1]
    narrow_zero = jnp.zeros((tok_len, model_width), jnp.bfloat16)
    wide_zero = jnp.zeros((tok_len, hidden_width), jnp.bfloat16)
    row_zero = jnp.zeros((3 * model_width,), jnp.bfloat16)
    return (
        jnp.zeros(section_input.shape, jnp.float32),
        narrow_zero,
        wide_zero,
        narrow_zero,
        wide_zero,
        row_zero,
        row_zero,
    )


def attention_weight_grads(left_one, right_one, left_two, right_two):
    width = left_two.shape[1]
    low = jnp.bfloat16
    qkv_term = contract_rows(left_one, right_one[:, : 3 * width]).astype(low)
    out_term = contract_rows(right_two[:, :width], left_two).astype(low)
    zero_term = jnp.zeros((width, right_two.shape[1]), low)
    return (jnp.concatenate([qkv_term, out_term], axis=1), zero_term)


def feed_weight_grads(left_one, right_one, left_two, right_two):
    low = jnp.bfloat16
    return (
        contract_rows(left_one, right_one).astype(low),
        contract_rows(left_two, right_two).astype(low),
    )


def replace_slot(buffer, slot_index, new_rows, active):
    old_rows = lax.dynamic_index_in_dim(buffer, slot_index, 0, keepdims=False)
    return lax.dynamic_update_index_in_dim(
        buffer, jnp.where(active, new_rows, old_rows), slot_index, 0
    )


def shards(
    tokens,
    cotangent,
    timesteps,
    labels,
    class_table,
    section_in_weights,
    section_out_weights,
    modulation_weights,
):
    micro_count = tokens.shape[0]
    model_width = tokens.shape[2]
    hidden_width = section_in_weights.shape[2]
    section_count = lax.axis_size("pipe")
    section_index = lax.axis_index("pipe")
    last_section = section_count - 1
    section_kind = 1 + section_index % 2
    own_rows = section_in_weights.shape[1]
    own_start = lax.axis_index("dp") * own_rows
    in_shard, out_shard, mod_shard = (
        section_in_weights[0],
        section_out_weights[0],
        modulation_weights[0],
    )
    whole_tokens, whole_cotangent = (
        lax.all_gather(tokens, "pipe", axis=1, tiled=True),
        lax.all_gather(cotangent, "pipe", axis=1, tiled=True),
    )
    tok_len = whole_tokens.shape[1]
    weights = (
        lax.all_gather(in_shard, "dp", axis=0, tiled=True),
        lax.all_gather(out_shard, "dp", axis=0, tiled=True),
    )
    all_steps = lax.all_gather(timesteps, "dp", axis=0, tiled=True)
    all_labels = lax.all_gather(labels, "dp", axis=0, tiled=True)
    image_count = all_steps.shape[0]
    classes = class_table.shape[0]
    matches = all_labels[:, None] == lax.broadcasted_iota(jnp.int32, (image_count, classes), 1)
    condition = sinusoid(all_steps, model_width) + product(
        matches.astype(jnp.bfloat16), class_table
    )
    conditioner = jax.nn.silu(condition).astype(jnp.bfloat16)
    own_conditioner = lax.dynamic_slice_in_dim(conditioner, own_start, own_rows, 1)
    mod_rows = lax.psum_scatter(
        product(own_conditioner, mod_shard), "dp", scatter_dimension=0, tiled=True
    )
    own_time = lax.psum_scatter(
        product(own_conditioner, out_shard[:, 3 * model_width :]),
        "dp",
        scatter_dimension=1,
        tiled=True,
    ).astype(jnp.bfloat16)
    time_rows = lax.psum_scatter(
        product(own_time, out_shard[:, : 3 * model_width]), "dp", scatter_dimension=0, tiled=True
    )

    def forward_tick(carry, tick_index):
        incoming, kept_inputs, finals = carry
        micro_index = tick_index - section_index
        active = (micro_index >= 0) & (micro_index < micro_count)
        slot_index = jnp.clip(micro_index, 0, micro_count - 1)
        first_rows = lax.dynamic_index_in_dim(whole_tokens, slot_index, 0, keepdims=False)
        section_input = jnp.where(section_index == 0, first_rows, incoming)
        section_output = lax.switch(
            jnp.where(active, section_kind, 0),
            (spare_forward, attention_forward, feed_forward),
            section_input,
            lax.dynamic_index_in_dim(mod_rows, slot_index, 0, keepdims=False),
            lax.dynamic_index_in_dim(time_rows, slot_index, 0, keepdims=False),
            weights,
        )
        output_low = section_output.astype(jnp.bfloat16)
        kept_inputs = replace_slot(kept_inputs, slot_index, section_input, active)
        finals = replace_slot(
            finals, slot_index, output_low, active & (section_index == last_section)
        )
        incoming = shifted(output_low, "pipe", 1)
        return ((incoming, kept_inputs, finals), None)

    empty_rows = jnp.zeros((tok_len, model_width), jnp.bfloat16)
    empty_store = jnp.zeros((micro_count, tok_len, model_width), jnp.bfloat16)
    forward_out, ignored = lax.scan(
        forward_tick,
        (empty_rows, empty_store, empty_store),
        jnp.arange(micro_count + section_count - 1),
    )
    kept_inputs = forward_out[1]
    finals = forward_out[2]
    wide_store = jnp.zeros((micro_count, tok_len, hidden_width), jnp.bfloat16)
    row_store = jnp.zeros((micro_count, 3 * model_width), jnp.bfloat16)
    start_factors = (empty_store, wide_store, empty_store, wide_store, row_store, row_store)

    def backward_tick(carry, tick_index):
        incoming, factors, input_grads = carry
        micro_index = tick_index - (last_section - section_index)
        active = (micro_index >= 0) & (micro_index < micro_count)
        slot_index = jnp.clip(micro_index, 0, micro_count - 1)
        top_grad = lax.dynamic_index_in_dim(whole_cotangent, slot_index, 0, keepdims=False)
        grad_in = jnp.where(section_index == last_section, top_grad, incoming)
        section_input = lax.dynamic_index_in_dim(kept_inputs, slot_index, 0, keepdims=False)
        results = lax.switch(
            jnp.where(active, section_kind, 0),
            (spare_backward, attention_backward, feed_backward),
            section_input,
            grad_in,
            lax.dynamic_index_in_dim(mod_rows, slot_index, 0, keepdims=False),
            lax.dynamic_index_in_dim(time_rows, slot_index, 0, keepdims=False),
            weights,
        )
        grad_low = results[0].astype(jnp.bfloat16)
        factors = tuple(
            (
                replace_slot(buffer, slot_index, fresh, active)
                for buffer, fresh in zip(factors, results[1:])
            )
        )
        input_grads = replace_slot(
            input_grads, slot_index, grad_low, active & (section_index == 0)
        )
        incoming = shifted(grad_low, "pipe", -1)
        return ((incoming, factors, input_grads), None)

    backward_out, ignored = lax.scan(
        backward_tick,
        (empty_rows, start_factors, empty_store),
        jnp.arange(micro_count + section_count - 1),
    )
    factors = backward_out[1]
    input_grads = backward_out[2]
    flat_rows = micro_count * tok_len
    left_one, right_one, left_two, right_two = (
        stored.reshape(flat_rows, stored.shape[2]) for stored in factors[:4]
    )
    in_term, out_term = lax.cond(
        section_index % 2 == 0,
        attention_weight_grads,
        feed_weight_grads,
        left_one,
        right_one,
        left_two,
        right_two,
    )
    in_grad = lax.psum_scatter(in_term, "dp", scatter_dimension=0, tiled=True)
    out_grad = lax.psum_scatter(out_term, "dp", scatter_dimension=0, tiled=True)
    own_out, own_in = (finals, input_grads)
    keep_out = jnp.where(section_index == last_section, own_out, 0)
    keep_in = jnp.where(section_index == 0, own_in, 0)
    output_share = lax.psum_scatter(keep_out, "pipe", scatter_dimension=1, tiled=True)
    input_share = lax.psum_scatter(keep_in, "pipe", scatter_dimension=1, tiled=True)
    small_outs = conditioning_grads(
        factors[4],
        factors[5],
        condition,
        own_conditioner,
        own_time,
        matches,
        out_shard,
        mod_shard,
        out_grad,
    )
    return (
        output_share,
        input_share.astype(jnp.float32),
        small_outs[0],
        in_grad.astype(jnp.float32)[None],
        small_outs[1][None],
        small_outs[2][None],
    )


def conditioning_grads(
    mod_grads,
    time_grads,
    condition,
    own_conditioner,
    own_time,
    matches,
    out_shard,
    mod_shard,
    out_grad,
):
    model_width = condition.shape[1]
    is_attention = lax.axis_index("pipe") % 2 == 0
    all_mod = lax.all_gather(mod_grads, "dp", axis=0, tiled=True)
    all_time = lax.all_gather(time_grads, "dp", axis=0, tiled=True)
    grad_mod_shard = contract_rows(own_conditioner, all_mod)
    cond_grads = contract_cols(all_mod, mod_shard)
    own_token = contract_cols(all_time, out_shard[:, : 3 * model_width]).astype(jnp.bfloat16)
    all_token = lax.all_gather(own_token, "dp", axis=1, tiled=True)
    token_grads = contract_cols(all_token, out_shard[:, 3 * model_width :])
    cond_grads = cond_grads + jnp.where(is_attention, token_grads, 0.0)
    time_out = jnp.concatenate(
        [contract_rows(own_time, all_time), contract_rows(own_conditioner, all_token)], axis=1
    )
    grad_out_shard = jnp.where(is_attention, time_out, out_grad.astype(jnp.float32))
    every_part = lax.all_gather(cond_grads, "pipe", axis=0)
    whole_grads = lax.all_gather(jnp.sum(every_part, axis=0), "dp", axis=1, tiled=True)
    grad_condition = jax.vjp(jax.nn.silu, condition)[1](whole_grads)[0]
    grad_table = lax.dot_general(
        matches.astype(jnp.float32),
        grad_condition,
        (((0,), (0,)), ((), ())),
        precision=highest,
        preferred_element_type=jnp.float32,
    )
    return (grad_table, grad_out_shard, grad_mod_shard)


def solution(mesh):
    return jax.shard_map(
        shards,
        mesh=mesh,
        in_specs=(
            P("dp", "pipe", None),
            P("dp", "pipe", None),
            P("dp"),
            P("dp"),
            P(),
            P("pipe", "dp", None),
            P("pipe", "dp", None),
            P("pipe", "dp", None),
        ),
        out_specs=(
            P("dp", "pipe", None),
            P("dp", "pipe", None),
            P(),
            P("pipe", "dp", None),
            P("pipe", "dp", None),
            P("pipe", "dp", None),
        ),
        check_vma=False,
    )
```

```python
from functools import partial
import math
from types import SimpleNamespace

import jax
import jax.numpy as jnp
from jax import lax
from jax.experimental import pallas as pl
from jax.experimental.pallas import tpu as pltpu
from jax.sharding import PartitionSpec as P

HEADS = 16
HEAD = 72


epsilon = 1e-06
highest = lax.Precision.HIGHEST


def shifted(block, axis, distance):
    devices = range(lax.axis_size(axis))
    route = [(i - distance, i) for i in devices if i - distance in devices]
    return lax.ppermute(block, axis, route)


def sinusoid(step_values, model_width):
    half_width = model_width // 2
    frequencies = jnp.exp(
        -math.log(10000.0) * jnp.arange(half_width, dtype=jnp.float32) / half_width
    )
    angles = step_values.astype(jnp.float32)[:, None] * frequencies[None, :]
    return jnp.concatenate([jnp.cos(angles), jnp.sin(angles)], axis=1)


def product(former, latter):
    return jnp.dot(former, latter, preferred_element_type=jnp.float32)


def contract_rows(former, latter):
    return lax.dot_general(
        former, latter, (((0,), (0,)), ((), ())), preferred_element_type=jnp.float32
    )


def contract_cols(former, latter):
    return lax.dot_general(
        former, latter, (((1,), (1,)), ((), ())), preferred_element_type=jnp.float32
    )


def normalize_rows(row_values):
    centered = row_values - jnp.mean(row_values, axis=-1, keepdims=True)
    inverse = lax.rsqrt(jnp.mean(centered * centered, axis=-1, keepdims=True) + epsilon)
    return (centered * inverse, inverse)


def modulation_front(section_input, mod_row):
    model_width = section_input.shape[1]
    shift_vec = mod_row[:model_width]
    scale_vec = mod_row[model_width : 2 * model_width]
    gate_vec = mod_row[2 * model_width :]
    centred, inverse = normalize_rows(section_input.astype(jnp.float32))
    normed = (centred * (1.0 + scale_vec) + shift_vec).astype(jnp.bfloat16)
    return (normed, centred, inverse, scale_vec, gate_vec)


def modulation_back(grad_normed, centred, inverse, scale_vec, grad_rows, grad_gate):
    grad_shift = jnp.sum(grad_normed, axis=0)
    grad_scale = jnp.sum(grad_normed * centred, axis=0)
    grad_centred = grad_normed * (1.0 + scale_vec)
    grad_input = inverse * (
        grad_centred
        - jnp.mean(grad_centred, axis=-1, keepdims=True)
        - centred * jnp.mean(grad_centred * centred, axis=-1, keepdims=True)
    )
    grad_mod = jnp.concatenate([grad_shift, grad_scale, grad_gate]).astype(jnp.bfloat16)
    return (grad_rows + grad_input, grad_mod)


def attention_parts(section_input, mod_row, time_row, weights):
    in_weight = weights[0]
    model_width = section_input.shape[1]
    tok_len = section_input.shape[0]
    normed, centred, inverse, scale_vec, gate_vec = modulation_front(section_input, mod_row)
    qkv = (product(normed, in_weight[:, : 3 * model_width]) + time_row).astype(jnp.bfloat16)
    split_qkv = qkv.reshape(tok_len, 3, HEADS, HEAD)
    queries = split_qkv[:, 0]
    keyed = split_qkv[:, 1]
    valued = split_qkv[:, 2]
    scores = jnp.einsum(
        "qhd,khd->hqk", queries, keyed, preferred_element_type=jnp.float32
    ) * HEAD ** (-0.5)
    probs_full = jax.nn.softmax(scores, axis=-1)
    probs_low = probs_full.astype(jnp.bfloat16)
    mixed = jnp.einsum("hqk,khd->qhd", probs_low, valued, preferred_element_type=jnp.float32)
    head_rows = mixed.reshape(tok_len, model_width).astype(jnp.bfloat16)
    branch = product(head_rows, in_weight[:, 3 * model_width :])
    section_output = section_input.astype(jnp.float32) + gate_vec * branch
    saved_parts = (
        normed,
        centred,
        inverse,
        scale_vec,
        gate_vec,
        queries,
        keyed,
        valued,
        probs_full,
        probs_low,
        head_rows,
        branch,
    )
    return (section_output, saved_parts)


def attention_forward(section_input, mod_row, time_row, weights):
    return attention_parts(section_input, mod_row, time_row, weights)[0]


def attention_backward(section_input, grad_in, mod_row, time_row, weights):
    in_weight = weights[0]
    model_width = section_input.shape[1]
    tok_len = section_input.shape[0]
    unused, saved_parts = attention_parts(section_input, mod_row, time_row, weights)
    (
        normed,
        centred,
        inverse,
        scale_vec,
        gate_vec,
        queries,
        keyed,
        valued,
        probs_full,
        probs_low,
        head_rows,
        branch,
    ) = saved_parts
    grad_rows = grad_in.astype(jnp.float32)
    grad_branch = (gate_vec * grad_rows).astype(jnp.bfloat16)
    grad_gate = jnp.sum(grad_rows * branch, axis=0)
    grad_heads = contract_cols(grad_branch, in_weight[:, 3 * model_width :]).astype(jnp.bfloat16)
    heads_split = grad_heads.reshape(tok_len, HEADS, HEAD)
    grad_probs = jnp.einsum("qhd,khd->hqk", heads_split, valued, preferred_element_type=jnp.float32)
    grad_value = jnp.einsum(
        "hqk,qhd->khd", probs_low, heads_split, preferred_element_type=jnp.float32
    )
    grad_scores = (
        probs_full * (grad_probs - jnp.sum(probs_full * grad_probs, axis=-1, keepdims=True))
    ).astype(jnp.bfloat16)
    grad_query = jnp.einsum(
        "hqk,khd->qhd", grad_scores, keyed, preferred_element_type=jnp.float32
    ) * HEAD ** (-0.5)
    grad_key = jnp.einsum(
        "hqk,qhd->khd", grad_scores, queries, preferred_element_type=jnp.float32
    ) * HEAD ** (-0.5)
    grad_qkv = (
        jnp.stack([grad_query, grad_key, grad_value], axis=1)
        .reshape(tok_len, 3 * model_width)
        .astype(jnp.bfloat16)
    )
    grad_normed = contract_cols(grad_qkv, in_weight[:, : 3 * model_width])
    grad_time = jnp.sum(grad_qkv, axis=0, dtype=jnp.float32).astype(jnp.bfloat16)
    grad_input, grad_mod = modulation_back(
        grad_normed, centred, inverse, scale_vec, grad_rows, grad_gate
    )
    narrow_zero = jnp.zeros((tok_len, model_width), jnp.bfloat16)
    return (
        grad_input,
        normed,
        jnp.concatenate([grad_qkv, narrow_zero], axis=1),
        grad_branch,
        jnp.concatenate([head_rows, narrow_zero, narrow_zero, narrow_zero], axis=1),
        grad_mod,
        grad_time,
    )


def feed_parts(section_input, mod_row, weights):
    in_weight, out_weight = weights
    normed, centred, inverse, scale_vec, gate_vec = modulation_front(section_input, mod_row)
    pre_act = product(normed, in_weight)
    hidden = jax.nn.gelu(pre_act, approximate=True).astype(jnp.bfloat16)
    branch = contract_cols(hidden, out_weight)
    section_output = section_input.astype(jnp.float32) + gate_vec * branch
    return (
        section_output,
        (normed, centred, inverse, scale_vec, gate_vec, pre_act, hidden, branch),
    )


def feed_forward(section_input, mod_row, time_row, weights):
    return feed_parts(section_input, mod_row, weights)[0]


def feed_backward(section_input, grad_in, mod_row, time_row, weights):
    in_weight, out_weight = weights
    unused, saved_parts = feed_parts(section_input, mod_row, weights)
    normed, centred, inverse, scale_vec, gate_vec, pre_act, hidden, branch = saved_parts
    grad_rows = grad_in.astype(jnp.float32)
    grad_branch = (gate_vec * grad_rows).astype(jnp.bfloat16)
    grad_gate = jnp.sum(grad_rows * branch, axis=0)
    grad_hidden = product(grad_branch, out_weight)
    gelu_pull = jax.vjp(partial(jax.nn.gelu, approximate=True), pre_act)[1]
    grad_pre = gelu_pull(grad_hidden)[0].astype(jnp.bfloat16)
    grad_normed = contract_cols(grad_pre, in_weight)
    grad_input, grad_mod = modulation_back(
        grad_normed, centred, inverse, scale_vec, grad_rows, grad_gate
    )
    return (
        grad_input,
        normed,
        grad_pre,
        grad_branch,
        hidden,
        grad_mod,
        jnp.zeros(grad_mod.shape, jnp.bfloat16),
    )


def spare_forward(section_input, mod_row, time_row, weights):
    return jnp.zeros(section_input.shape, jnp.float32)


def spare_backward(section_input, grad_in, mod_row, time_row, weights):
    tok_len, model_width = section_input.shape
    hidden_width = weights[0].shape[1]
    narrow_zero = jnp.zeros((tok_len, model_width), jnp.bfloat16)
    wide_zero = jnp.zeros((tok_len, hidden_width), jnp.bfloat16)
    row_zero = jnp.zeros((3 * model_width,), jnp.bfloat16)
    return (
        jnp.zeros(section_input.shape, jnp.float32),
        narrow_zero,
        wide_zero,
        narrow_zero,
        wide_zero,
        row_zero,
        row_zero,
    )


def attention_weight_grads(left_one, right_one, left_two, right_two):
    width = left_two.shape[1]
    low = jnp.bfloat16
    qkv_term = contract_rows(left_one, right_one[:, : 3 * width]).astype(low)
    out_term = contract_rows(right_two[:, :width], left_two).astype(low)
    zero_term = jnp.zeros((width, right_two.shape[1]), low)
    return (jnp.concatenate([qkv_term, out_term], axis=1), zero_term)


def feed_weight_grads(left_one, right_one, left_two, right_two):
    low = jnp.bfloat16
    return (
        contract_rows(left_one, right_one).astype(low),
        contract_rows(left_two, right_two).astype(low),
    )


def replace_slot(buffer, slot_index, new_rows, active):
    old_rows = lax.dynamic_index_in_dim(buffer, slot_index, 0, keepdims=False)
    return lax.dynamic_update_index_in_dim(
        buffer, jnp.where(active, new_rows, old_rows), slot_index, 0
    )


def shards(
    tokens,
    cotangent,
    timesteps,
    labels,
    class_table,
    section_in_weights,
    section_out_weights,
    modulation_weights,
):
    micro_count = tokens.shape[0]
    model_width = tokens.shape[2]
    hidden_width = section_in_weights.shape[2]
    section_count = lax.axis_size("pipe")
    section_index = lax.axis_index("pipe")
    last_section = section_count - 1
    section_kind = 1 + section_index % 2
    in_shard, out_shard, mod_shard = (
        section_in_weights[0],
        section_out_weights[0],
        modulation_weights[0],
    )
    whole_tokens, whole_cotangent = (
        lax.all_gather(tokens, "pipe", axis=1, tiled=True),
        lax.all_gather(cotangent, "pipe", axis=1, tiled=True),
    )
    tok_len = whole_tokens.shape[1]
    weights = (
        lax.all_gather(in_shard, "dp", axis=0, tiled=True),
        lax.all_gather(out_shard, "dp", axis=0, tiled=True),
    )
    condition, own_conditioner, own_time, matches, mod_rows, time_rows = conditioning(
        timesteps, labels, class_table, out_shard, mod_shard
    )

    def forward_tick(carry, tick_index):
        incoming, kept_inputs, finals = carry
        micro_index = tick_index - section_index
        active = (micro_index >= 0) & (micro_index < micro_count)
        slot_index = jnp.clip(micro_index, 0, micro_count - 1)
        first_rows = lax.dynamic_index_in_dim(whole_tokens, slot_index, 0, keepdims=False)
        section_input = jnp.where(section_index == 0, first_rows, incoming)
        section_output = lax.switch(
            jnp.where(active, section_kind, 0),
            (spare_forward, attention_forward, feed_forward),
            section_input,
            lax.dynamic_index_in_dim(mod_rows, slot_index, 0, keepdims=False),
            lax.dynamic_index_in_dim(time_rows, slot_index, 0, keepdims=False),
            weights,
        )
        output_low = section_output.astype(jnp.bfloat16)
        kept_inputs = replace_slot(kept_inputs, slot_index, section_input, active)
        finals = replace_slot(
            finals, slot_index, output_low, active & (section_index == last_section)
        )
        incoming = shifted(output_low, "pipe", 1)
        return ((incoming, kept_inputs, finals), None)

    empty_rows = jnp.zeros((tok_len, model_width), jnp.bfloat16)
    empty_store = jnp.zeros((micro_count, tok_len, model_width), jnp.bfloat16)
    forward_out, ignored = lax.scan(
        forward_tick,
        (empty_rows, empty_store, empty_store),
        jnp.arange(micro_count + section_count - 1),
    )
    kept_inputs = forward_out[1]
    finals = forward_out[2]
    wide_store = jnp.zeros((micro_count, tok_len, hidden_width), jnp.bfloat16)
    row_store = jnp.zeros((micro_count, 3 * model_width), jnp.bfloat16)
    start_factors = (empty_store, wide_store, empty_store, wide_store, row_store, row_store)

    def backward_tick(carry, tick_index):
        incoming, factors, input_grads = carry
        micro_index = tick_index - (last_section - section_index)
        active = (micro_index >= 0) & (micro_index < micro_count)
        slot_index = jnp.clip(micro_index, 0, micro_count - 1)
        top_grad = lax.dynamic_index_in_dim(whole_cotangent, slot_index, 0, keepdims=False)
        grad_in = jnp.where(section_index == last_section, top_grad, incoming)
        section_input = lax.dynamic_index_in_dim(kept_inputs, slot_index, 0, keepdims=False)
        results = lax.switch(
            jnp.where(active, section_kind, 0),
            (spare_backward, attention_backward, feed_backward),
            section_input,
            grad_in,
            lax.dynamic_index_in_dim(mod_rows, slot_index, 0, keepdims=False),
            lax.dynamic_index_in_dim(time_rows, slot_index, 0, keepdims=False),
            weights,
        )
        grad_low = results[0].astype(jnp.bfloat16)
        factors = tuple(
            (
                replace_slot(buffer, slot_index, fresh, active)
                for buffer, fresh in zip(factors, results[1:])
            )
        )
        input_grads = replace_slot(
            input_grads, slot_index, grad_low, active & (section_index == 0)
        )
        incoming = shifted(grad_low, "pipe", -1)
        return ((incoming, factors, input_grads), None)

    backward_out, ignored = lax.scan(
        backward_tick,
        (empty_rows, start_factors, empty_store),
        jnp.arange(micro_count + section_count - 1),
    )
    factors = backward_out[1]
    input_grads = backward_out[2]
    flat_rows = micro_count * tok_len
    left_one, right_one, left_two, right_two = (
        stored.reshape(flat_rows, stored.shape[2]) for stored in factors[:4]
    )
    in_term, out_term = lax.cond(
        section_index % 2 == 0,
        attention_weight_grads,
        feed_weight_grads,
        left_one,
        right_one,
        left_two,
        right_two,
    )
    in_grad = lax.psum_scatter(in_term, "dp", scatter_dimension=0, tiled=True)
    out_grad = lax.psum_scatter(out_term, "dp", scatter_dimension=0, tiled=True)
    own_out, own_in = (finals, input_grads)
    keep_out = jnp.where(section_index == last_section, own_out, 0)
    keep_in = jnp.where(section_index == 0, own_in, 0)
    output_share = lax.psum_scatter(keep_out, "pipe", scatter_dimension=1, tiled=True)
    input_share = lax.psum_scatter(keep_in, "pipe", scatter_dimension=1, tiled=True)
    small_outs = conditioning_grads(
        factors[4],
        factors[5],
        condition,
        own_conditioner,
        own_time,
        matches,
        out_shard,
        mod_shard,
        out_grad,
    )
    return (
        output_share,
        input_share.astype(jnp.float32),
        small_outs[0],
        in_grad.astype(jnp.float32)[None],
        small_outs[1][None],
        small_outs[2][None],
    )


def conditioning_grads(
    mod_grads,
    time_grads,
    condition,
    own_conditioner,
    own_time,
    matches,
    out_shard,
    mod_shard,
    out_grad,
):
    model_width = condition.shape[1]
    is_attention = lax.axis_index("pipe") % 2 == 0
    all_mod = lax.all_gather(mod_grads, "dp", axis=0, tiled=True)
    all_time = lax.all_gather(time_grads, "dp", axis=0, tiled=True)
    grad_mod_shard = contract_rows(own_conditioner, all_mod)
    cond_grads = contract_cols(all_mod, mod_shard)
    own_token = contract_cols(all_time, out_shard[:, : 3 * model_width]).astype(jnp.bfloat16)
    all_token = lax.all_gather(own_token, "dp", axis=1, tiled=True)
    token_grads = contract_cols(all_token, out_shard[:, 3 * model_width :])
    cond_grads = cond_grads + jnp.where(is_attention, token_grads, 0.0)
    time_out = jnp.concatenate(
        [contract_rows(own_time, all_time), contract_rows(own_conditioner, all_token)], axis=1
    )
    grad_out_shard = jnp.where(is_attention, time_out, out_grad.astype(jnp.float32))
    every_part = lax.all_gather(cond_grads, "pipe", axis=0)
    whole_grads = lax.all_gather(jnp.sum(every_part, axis=0), "dp", axis=1, tiled=True)
    grad_condition = jax.vjp(jax.nn.silu, condition)[1](whole_grads)[0]
    grad_table = lax.dot_general(
        matches.astype(jnp.float32),
        grad_condition,
        (((0,), (0,)), ((), ())),
        precision=highest,
        preferred_element_type=jnp.float32,
    )
    return (grad_table, grad_out_shard, grad_mod_shard)


def conditioning(timesteps, labels, class_table, out_shard, mod_shard):
    model_width = class_table.shape[1]
    own_rows = out_shard.shape[0]
    own_start = lax.axis_index("dp") * own_rows
    all_steps = lax.all_gather(timesteps, "dp", axis=0, tiled=True)
    all_labels = lax.all_gather(labels, "dp", axis=0, tiled=True)
    image_count = all_steps.shape[0]
    classes = class_table.shape[0]
    matches = all_labels[:, None] == lax.broadcasted_iota(jnp.int32, (image_count, classes), 1)
    condition = sinusoid(all_steps, model_width) + product(
        matches.astype(jnp.bfloat16), class_table
    )
    conditioner = jax.nn.silu(condition).astype(jnp.bfloat16)
    own_conditioner = lax.dynamic_slice_in_dim(conditioner, own_start, own_rows, 1)
    mod_rows = lax.psum_scatter(
        product(own_conditioner, mod_shard), "dp", scatter_dimension=0, tiled=True
    )
    own_time = lax.psum_scatter(
        product(own_conditioner, out_shard[:, 3 * model_width :]),
        "dp",
        scatter_dimension=1,
        tiled=True,
    ).astype(jnp.bfloat16)
    time_rows = lax.psum_scatter(
        product(own_time, out_shard[:, : 3 * model_width]), "dp", scatter_dimension=0, tiled=True
    )
    return (condition, own_conditioner, own_time, matches, mod_rows, time_rows)


ROWS = 256
SPAN = 768
THIRD = 384
PART = 1152
BLOCK = 144
MESH = pl.DeviceIdType.MESH
low = jnp.bfloat16
GELU_A = math.sqrt(2.0 / math.pi)
GELU_B = 0.044715


def product_nt(former, latter):
    return contract_cols(former, latter)


def spread(index, width):
    return pl.ds(pl.multiple_of(index * width, 128), width)


def image_rows(i):
    return pl.ds(pl.multiple_of(i * ROWS, ROWS), ROWS)


def block_rows(b):
    return pl.ds(pl.multiple_of(b * BLOCK, 16), BLOCK)


def front(i, s):
    rows = image_rows(i)
    xhat, inverse = normalize_rows(s.xin[rows, :].astype(jnp.float32))
    normed = (xhat * (1.0 + s.mod[i, pl.ds(1, 1), :]) + s.mod[i, pl.ds(0, 1), :]).astype(low)
    s.norm[rows, :] = normed
    s.left[0, :, rows] = normed.T


def finish(i, s):
    rows = image_rows(i)
    branch = s.acc[...]
    s.branch[rows, :] = branch.astype(low)
    gate = s.mod[i, pl.ds(2, 1), :]
    s.xout[rows, :] = (s.xin[rows, :].astype(jnp.float32) + gate * branch).astype(low)


def feed_up_down(i, s):
    rows = image_rows(i)
    s.acc[...] = jnp.zeros(s.acc.shape, jnp.float32)

    def tile(j, carry):
        cols = spread(j, SPAN)
        value = product(s.norm[rows, :], s.wa[:, cols])
        square = value * value
        wave = jnp.tanh(value * (GELU_A + (GELU_A * GELU_B) * square))
        half = 0.5 + 0.5 * wave
        hidden = (value * half).astype(low)
        slope = half + value * (0.5 - 0.5 * (wave * wave)) * (
            GELU_A + (3.0 * GELU_A * GELU_B) * square
        )
        s.wide[0, rows, cols] = hidden
        s.wide[1, rows, cols] = slope.astype(low)
        s.acc[...] += product_nt(hidden, s.wb[:, cols])
        return carry

    lax.fori_loop(0, s.wa.shape[1] // SPAN, tile, 0)


def feed_down_up(i, s):
    rows = image_rows(i)
    s.acc[...] = jnp.zeros(s.acc.shape, jnp.float32)

    def tile(j, carry):
        cols = spread(j, SPAN)
        grad_hidden = product(s.gb[...], s.wb[:, cols])
        grad_pre = (grad_hidden * s.wide[1, rows, cols].astype(jnp.float32)).astype(low)
        s.wide[1, rows, cols] = grad_pre
        s.acc[...] += product_nt(grad_pre, s.wa[:, cols])
        return carry

    lax.fori_loop(0, s.wa.shape[1] // SPAN, tile, 0)


def back_start(i, s):
    rows = image_rows(i)
    grad = s.gin[rows, :].astype(jnp.float32)
    gb = (s.mod[i, pl.ds(2, 1), :] * grad).astype(low)
    s.gb[...] = gb
    s.gmod[i, pl.ds(2, 1), :] = jnp.sum(
        grad * s.branch[rows, :].astype(jnp.float32), axis=0, keepdims=True
    )
    return gb


def back_finish(i, s):
    rows = image_rows(i)
    xhat, inverse = normalize_rows(s.xin[rows, :].astype(jnp.float32))
    gn = s.acc[...]
    s.gmod[i, pl.ds(0, 1), :] = jnp.sum(gn, axis=0, keepdims=True)
    s.gmod[i, pl.ds(1, 1), :] = jnp.sum(gn * xhat, axis=0, keepdims=True)
    gx = gn * (1.0 + s.mod[i, pl.ds(1, 1), :])
    first = jnp.mean(gx, axis=-1, keepdims=True)
    second = jnp.mean(gx * xhat, axis=-1, keepdims=True)
    grad = s.gin[rows, :].astype(jnp.float32)
    s.gout[rows, :] = (grad + inverse * (gx - first - xhat * second)).astype(low)


def kernel_feed_forward(i, s):
    front(i, s)
    feed_up_down(i, s)
    finish(i, s)


def kernel_feed_backward(i, s):
    gb = back_start(i, s)
    s.left[1, :, image_rows(i)] = gb.T
    feed_down_up(i, s)
    back_finish(i, s)


def project(i, s, part):
    rows = image_rows(i)

    def tile(j, carry):
        cols = pl.ds(pl.multiple_of(part * PART + j * THIRD, 128), THIRD)
        value = product(s.norm[rows, :], s.wa[:, cols]) + s.time[i, :, cols]
        s.wide[0, rows, cols] = value.astype(low)
        return carry

    lax.fori_loop(0, PART // THIRD, tile, 0)


def head_window(h):
    start = jnp.minimum((h * HEAD) // 128, PART // 128 - 2)
    offset = h * HEAD - start * 128
    lanes = lax.broadcasted_iota(jnp.int32, (ROWS, 256), 1)
    inside = (lanes >= offset) & (lanes < offset + HEAD)
    return start, inside


def window(start, part):
    return pl.ds(pl.multiple_of(part * PART + start * 128, 128), 256)


def prob_place(i, h):
    return (
        pl.ds(pl.multiple_of((h % 4) * ROWS, ROWS), ROWS),
        pl.ds(pl.multiple_of((4 * i + h // 4) * ROWS, ROWS), ROWS),
    )


def attend(i, s):
    rows = image_rows(i)
    s.acc[...] = jnp.zeros(s.acc.shape, jnp.float32)

    def head(h, carry):
        start, inside = head_window(h)
        zero = jnp.zeros((), low)
        query = jnp.where(inside, s.wide[0, rows, window(start, 0)], zero)
        key = s.wide[0, rows, window(start, 1)]
        value = jnp.where(inside, s.wide[0, rows, window(start, 2)], zero)
        scores = product_nt(query, key) * HEAD ** (-0.5)
        top = jnp.max(scores, axis=-1, keepdims=True)
        powers = jnp.exp(scores - top)
        probs = (powers * (1.0 / jnp.sum(powers, axis=-1, keepdims=True))).astype(low)
        place = prob_place(i, h)
        s.wb[place[0], place[1]] = probs
        s.acc[:, window(start, 0)] += product(probs, value)
        return carry

    lax.fori_loop(0, HEADS, head, 0)
    mixed = s.acc[...].astype(low)
    s.left[1, :, rows] = mixed.T
    s.acc[...] = product(mixed, s.wa[:, 3 * PART :])


def kernel_attention_backward(i, s):
    rows = image_rows(i)
    gb = back_start(i, s)
    s.wide[1, rows, 3 * PART :] = gb
    s.gb[...] = product_nt(gb, s.wa[:, 3 * PART :]).astype(low)
    s.wacc[...] = jnp.zeros(s.wacc.shape, jnp.float32)

    def head(h, carry):
        start, inside = head_window(h)
        zero = jnp.zeros((), low)
        query = jnp.where(inside, s.wide[0, rows, window(start, 0)], zero)
        key = jnp.where(inside, s.wide[0, rows, window(start, 1)], zero)
        value = s.wide[0, rows, window(start, 2)]
        grad_head = jnp.where(inside, s.gb[:, window(start, 0)], zero)
        place = prob_place(i, h)
        probs = s.wb[place[0], place[1]]
        probs_full = probs.astype(jnp.float32)
        grad_probs = product_nt(grad_head, value)
        s.wacc[:, window(start, 2)] += contract_rows(probs, grad_head)
        mixed = jnp.sum(probs_full * grad_probs, axis=-1, keepdims=True)
        grad_scores = (probs_full * (grad_probs - mixed)).astype(low)
        s.wacc[:, window(start, 0)] += product(grad_scores, key)
        s.wacc[:, window(start, 1)] += contract_rows(grad_scores, query)
        return carry

    lax.fori_loop(0, HEADS, head, 0)
    scale = HEAD ** (-0.5)
    for part, factor in ((0, scale), (1, scale), (2, 1.0)):
        cols = pl.ds(part * PART, PART)
        grads = (s.wacc[:, cols] * factor).astype(low)
        s.wide[1, rows, cols] = grads
        s.gtime[i, :, cols] = jnp.sum(grads.astype(jnp.float32), axis=0, keepdims=True)
    s.acc[...] = jnp.zeros(s.acc.shape, jnp.float32)

    def tile(j, carry):
        cols = spread(j, THIRD)
        s.acc[...] += product_nt(s.wide[1, rows, cols], s.wa[:, cols])
        return carry

    lax.fori_loop(0, 3 * PART // THIRD, tile, 0)
    back_finish(i, s)


def places():
    dp, pipe = lax.axis_index("dp"), lax.axis_index("pipe")
    core, x_bit, y_bit = dp % 2, (dp // 2) % 2, dp // 4
    sib = dp + 1 - 2 * core
    step_x, step_y = 2 - 4 * x_bit, 4 - 8 * y_bit
    return SimpleNamespace(
        dp=dp,
        pipe=pipe,
        core=core,
        sib=sib,
        x=dp + step_x,
        y=dp + step_y,
        d=dp + step_x + step_y,
        step_x=step_x,
        step_y=step_y,
        x_bit=x_bit,
        y_bit=y_bit,
    )


def gather_weights(s, at, chunks, ready):
    def held(k):
        return (s.wa if k < 4 else s.wb), pl.ds((k % 4) * PART, PART)

    def piece(k, block, first=0, count=BLOCK):
        ref, cols = held(k)
        return ref.at[pl.ds(pl.multiple_of(block * BLOCK + first, 16), count), cols]

    def copy(k, kind, ref, target, source=None):
        return pltpu.make_async_remote_copy(
            src_ref=ref if source is None else source,
            dst_ref=ref,
            send_sem=s.gather_send.at[k, kind],
            recv_sem=s.gather_recv.at[k, kind],
            device_id=(target, at.pipe),
            device_id_type=MESH,
        )

    def via_y(k):
        return (0, 80) if k % 2 == 0 else (0, 64)

    def via_x(k):
        return (80, 64) if k % 2 == 0 else (64, 80)

    sib_x, sib_y, sib_d = (
        at.sib + at.step_x,
        at.sib + at.step_y,
        at.sib + at.step_x + at.step_y,
    )

    def sends(k):
        shard = s.in_shard if k < 4 else s.out_shard
        source = shard.at[:, pl.ds((k % 4) * PART, PART)]
        return {
            0: lambda: copy(k, 0, piece(k, at.dp), at.x, source),
            1: lambda: copy(k, 1, piece(k, at.dp), at.y, source),
            2: lambda: copy(k, 2, piece(k, at.dp), at.sib, source),
            3: lambda: copy(k, 3, piece(k, at.x), at.sib),
            4: lambda: copy(k, 4, piece(k, at.x, *via_y(k)), at.y),
            5: lambda: copy(k, 5, piece(k, at.y), at.sib),
            6: lambda: copy(k, 6, piece(k, at.y, *via_x(k)), at.x),
            7: lambda: copy(k, 7, piece(k, at.d), at.sib),
        }

    def arrivals(k):
        return {
            0: lambda: copy(k, 0, piece(k, at.x), at.x),
            1: lambda: copy(k, 1, piece(k, at.y), at.y),
            2: lambda: copy(k, 2, piece(k, at.sib), at.sib),
            3: lambda: copy(k, 3, piece(k, sib_x), at.sib),
            4: lambda: copy(k, 4, piece(k, at.d, *via_y(k)), at.y),
            5: lambda: copy(k, 5, piece(k, sib_y), at.sib),
            6: lambda: copy(k, 6, piece(k, at.d, *via_x(k)), at.x),
            7: lambda: copy(k, 7, piece(k, sib_d), at.sib),
        }

    def start(k, *kinds):
        for kind in kinds:
            sends(k)[kind]().start()

    def arrive(k, *kinds):
        for kind in kinds:
            arrivals(k)[kind]().wait_recv()

    start(0, 0, 1, 2)
    start(1, 0, 1, 2)
    for k in range(chunks + 2):
        if k < chunks:
            arrive(k, 0)
            start(k, 3, 4)
            arrive(k, 1)
            start(k, 5, 6)
            if k + 2 < chunks:
                start(k + 2, 0, 1, 2)
        if 1 <= k <= chunks:
            arrive(k - 1, 4, 6)
            start(k - 1, 7)
        if k >= 2:
            arrive(k - 2, 2, 3, 5, 7)
            ready(k - 2)
    for k in range(chunks):
        for kind in range(8):
            sends(k)[kind]().wait_send()


def scatter_grads(s, at, is_feed):
    total = jnp.where(is_feed, 32, 16)
    chip = at.dp // 2
    chip_x, chip_y = chip + 1 - 2 * at.x_bit, chip + 2 - 4 * at.y_bit
    chip_d = chip_x + 2 - 4 * at.y_bit

    def unit(u):
        matrix, v = u // 16, u % 16
        group, turn, n = v // 4, v % 2, (v % 4) // 2
        near = chip_x + turn * (chip_y - chip_x)
        block = jnp.where(group == 0, chip_d, jnp.where(group == 3, chip, near))
        part = jnp.where(
            group == 3, v % 4, jnp.where(group == 2, 2 * (1 - turn) + n, 2 * turn + n)
        )
        return matrix, group, turn, n, block, part

    def sib_place(u):
        return s.wb.at[block_rows(u % 8), spread(u // 8, PART)]

    def near_place(matrix, turn, slot):
        index = turn * 12 + matrix * 6 + slot
        return s.wa.at[block_rows(index % 8), spread(index // 8, PART)]

    def sib_copy(u):
        return pltpu.make_async_remote_copy(
            src_ref=s.stage.at[u % 4, block_rows(1 - at.core), :],
            dst_ref=sib_place(u),
            send_sem=s.sib_send.at[u],
            recv_sem=s.sib_recv.at[u],
            device_id=(at.sib, at.pipe),
            device_id_type=MESH,
        )

    def near_copy(matrix, turn, slot):
        return pltpu.make_async_remote_copy(
            src_ref=s.near_stage.at[turn, (matrix * 6 + slot) % 3],
            dst_ref=near_place(matrix, turn, slot),
            send_sem=s.near_send.at[turn, matrix * 6 + slot],
            recv_sem=s.near_recv.at[turn, matrix * 6 + slot],
            device_id=(at.x + turn * (at.y - at.x), at.pipe),
            device_id_type=MESH,
        )

    def compute(u):
        matrix, group, turn, n, block, part = unit(u)
        first = is_feed & (matrix == 0)
        lhs = jnp.where(first | (jnp.logical_not(is_feed) & (part == 3)), 1, 0)
        rhs = jnp.where(first, 0, 1)

        @pl.when(u >= 4)
        def _():
            sib_copy(u - 4).wait_send()

        rows = pl.ds(pl.multiple_of(block * 288, 16), 288)
        s.stage[u % 4] = product(s.left[lhs, rows, :], s.wide[rhs, :, spread(part, PART)]).astype(
            low
        )
        sib_copy(u).start()

    def settle(u):
        matrix, group, turn, n, block, part = unit(u)
        sib_copy(u).wait_recv()
        own = s.stage[u % 4, block_rows(at.core), :].astype(jnp.float32)
        place = (block_rows(u % 8), spread(u // 8, PART))
        value = own + s.wb[place].astype(jnp.float32)
        slot = group * 2 + n

        def taken(from_turn, from_slot):
            near_copy(matrix, from_turn, from_slot).wait_recv()
            index = from_turn * 12 + matrix * 6 + from_slot
            return s.wa[block_rows(index % 8), spread(index // 8, PART)].astype(jnp.float32)

        @pl.when(group < 3)
        def _():
            @pl.when(matrix * 6 + slot >= 3)
            def _():
                near_copy(matrix + (slot - 3) // 6, turn, (slot + 3) % 6).wait_send()

            @pl.when(group < 2)
            def _():
                s.near_stage[turn, (matrix * 6 + slot) % 3] = value.astype(low)

            @pl.when(group == 2)
            def _():
                s.near_stage[turn, (matrix * 6 + slot) % 3] = (value + taken(1 - turn, n)).astype(
                    low
                )

            near_copy(matrix, turn, slot).start()

        @pl.when(group == 3)
        def _():
            @pl.when((matrix > 0) | (part >= 2))
            def _():
                grad_copy(u - jnp.where(part >= 2, 2, 14)).wait()

            whole = value + taken(0, 2 + part) + taken(1, (part + 2) % 4 + 2)
            s.out_stage[part % 2] = whole
            grad_copy(u).start()

    def grad_copy(u):
        matrix, v = u // 16, u % 16
        which = jnp.where(is_feed, 1 - matrix, 0)
        return pltpu.make_async_copy(
            s.out_stage.at[v % 2], s.grads.at[which, :, spread(v % 4, PART)], s.out_sem.at[v % 2]
        )

    def step(u, carry):
        @pl.when(u < total)
        def _():
            compute(u)

        @pl.when(u >= 2)
        def _():
            settle(u - 2)

        return carry

    lax.fori_loop(0, total + 2, step, 0)
    matrices = jnp.where(is_feed, 2, 1)

    def rest(k, carry):
        sib_copy(total - 4 + k).wait_send()
        return carry

    lax.fori_loop(0, 4, rest, 0)
    for turn in range(2):
        for slot in range(3, 6):
            near_copy(matrices - 1, turn, slot).wait_send()
    for k in (2, 1):
        grad_copy(total - k).wait()


def mega_body(*refs):
    s = SimpleNamespace(**dict(zip(REFS, refs)))
    at = places()
    is_feed = at.pipe % 2 == 1
    pipe = at.pipe
    barrier = pltpu.get_barrier_semaphore()
    for target in (
        (at.sib, pipe),
        (at.x, pipe),
        (at.y, pipe),
        (at.dp, (pipe + 1) % 4),
        (at.dp, (pipe + 2) % 4),
        (at.dp, (pipe + 3) % 4),
    ):
        pl.semaphore_signal(barrier, inc=1, device_id=target, device_id_type=MESH)
    pl.semaphore_wait(barrier, 6)

    def remote(source, target, send, recv, plane):
        return pltpu.make_async_remote_copy(
            src_ref=source,
            dst_ref=target,
            send_sem=send,
            recv_sem=recv,
            device_id=(at.dp, plane),
            device_id_type=MESH,
        )

    def share(i, plane):
        return pl.ds(pl.multiple_of(i * ROWS + plane * 64, 64), 64)

    def token_copy(i, plane):
        return remote(
            s.tokens.at[i],
            s.xin.at[share(i, plane), :],
            s.share_send.at[0, i],
            s.xin_recv.at[i, plane],
            0,
        )

    def cotangent_copy(i, plane):
        return remote(
            s.cotangent.at[i],
            s.gin.at[share(i, plane), :],
            s.share_send.at[1, i],
            s.gin_recv.at[i, plane],
            3,
        )

    def next_copy(i):
        whole = image_rows(i)
        return remote(
            s.xout.at[whole, :],
            s.xin.at[whole, :],
            s.hop_send.at[0, i],
            s.xin_recv.at[i, 0],
            jnp.minimum(pipe + 1, 3),
        )

    def back_copy(i):
        whole = image_rows(i)
        return remote(
            s.gout.at[whole, :],
            s.gin.at[whole, :],
            s.hop_send.at[1, i],
            s.gin_recv.at[i, 3],
            jnp.maximum(pipe - 1, 0),
        )

    def output_copy(i, plane):
        return remote(
            s.xout.at[share(i, plane), :],
            s.out_tokens.at[i],
            s.final_send.at[0, i, plane],
            s.final_recv.at[0, i],
            plane,
        )

    def input_copy(i, plane):
        return remote(
            s.gout.at[share(i, plane), :],
            s.input_grad.at[i],
            s.final_send.at[1, i, plane],
            s.final_recv.at[1, i],
            plane,
        )

    def local(source, target, index):
        return pltpu.make_async_copy(source, target, s.local_sem.at[index])

    own_in = local(s.in_shard, s.wa.at[block_rows(at.dp), :], 0)
    own_out = local(s.out_shard, s.wb.at[block_rows(at.dp), :], 1)
    own_in.start()

    @pl.when(is_feed)
    def _():
        own_out.start()

    for i in range(2):
        own_tokens = local(s.tokens.at[i], s.xin.at[pl.ds(i * ROWS, 64), :], 2 + i)
        own_cotangent = local(s.cotangent.at[i], s.gin.at[pl.ds(i * ROWS + 192, 64), :], 4 + i)

        @pl.when(pipe == 0)
        def _():
            own_tokens.start()

        @pl.when(pipe == 3)
        def _():
            own_cotangent.start()

        @pl.when(pipe != 0)
        def _():
            token_copy(i, pipe).start()

    def ready(k):
        if k == 0:
            for i in range(2):
                local(s.tokens.at[i], s.xin.at[pl.ds(i * ROWS, 64), :], 2 + i).wait()
                for plane in range(1, 4):
                    token_copy(i, plane).wait_recv()
                front(i, s)
        if k < 3:

            def one(i, carry):
                project(i, s, k)
                return carry

            lax.fori_loop(0, 2, one, 0)

    own_in.wait()

    @pl.when(pipe == 0)
    def _():
        gather_weights(s, at, 4, ready)

    @pl.when(pipe == 2)
    def _():
        gather_weights(s, at, 4, lambda k: None)

    @pl.when(is_feed)
    def _():
        own_out.wait()
        gather_weights(s, at, 8, lambda k: None)

    for i in range(2):

        @pl.when(pipe != 0)
        def _():
            token_copy(i, pipe).wait_send()

        @pl.when(pipe != 3)
        def _():
            cotangent_copy(i, pipe).start()

    def step(n, carry):
        at_end = pipe == 3
        goes_forward = jnp.where(at_end, n % 2 == 0, n < 2)
        i = jnp.where(at_end, n // 2, n % 2)

        @pl.when(goes_forward)
        def _():
            @pl.when(pipe != 0)
            def _():
                next_copy(i).wait_recv()

            @pl.when(is_feed)
            def _():
                kernel_feed_forward(i, s)

            @pl.when(jnp.logical_not(is_feed))
            def _():
                @pl.when(pipe != 0)
                def _():
                    front(i, s)

                    def one(part, carry):
                        project(i, s, part)
                        return carry

                    lax.fori_loop(0, 3, one, 0)

                attend(i, s)
                finish(i, s)

            @pl.when(pipe != 3)
            def _():
                next_copy(i).start()

            @pl.when(pipe == 3)
            def _():
                for plane in range(3):
                    output_copy(i, plane).start()
                local(s.xout.at[share(i, 3), :], s.out_tokens.at[i], 2 + i).start()

        @pl.when(jnp.logical_not(goes_forward))
        def _():
            @pl.when(pipe == 3)
            def _():
                local(s.cotangent.at[i], s.gin.at[share(i, 3), :], 4 + i).wait()
                for plane in range(3):
                    cotangent_copy(i, plane).wait_recv()

            @pl.when(pipe != 3)
            def _():
                back_copy(i).wait_recv()

            @pl.when(is_feed)
            def _():
                kernel_feed_backward(i, s)

            @pl.when(jnp.logical_not(is_feed))
            def _():
                kernel_attention_backward(i, s)

            @pl.when(pipe != 0)
            def _():
                back_copy(i).start()

            @pl.when(pipe == 0)
            def _():
                for plane in range(1, 4):
                    input_copy(i, plane).start()
                local(s.gout.at[share(i, 0), :], s.input_grad.at[i], 4 + i).start()

        return carry

    lax.fori_loop(0, 4, step, 0)

    for target, sem in ((at.sib, 0), (at.x, 1), (at.y, 2)):
        pl.semaphore_signal(
            s.free.at[sem], inc=1, device_id=(target, pipe), device_id_type=MESH
        )
    for sem in range(3):
        pl.semaphore_wait(s.free.at[sem], 1)
    scatter_grads(s, at, is_feed)

    for i in range(2):

        @pl.when(pipe != 3)
        def _():
            cotangent_copy(i, pipe).wait_send()
            next_copy(i).wait_send()
            output_copy(i, pipe).wait_recv()

        @pl.when(pipe == 3)
        def _():
            for plane in range(3):
                output_copy(i, plane).wait_send()
            local(s.xout.at[share(i, 3), :], s.out_tokens.at[i], 2 + i).wait()

        @pl.when(pipe != 0)
        def _():
            back_copy(i).wait_send()
            input_copy(i, pipe).wait_recv()

        @pl.when(pipe == 0)
        def _():
            for plane in range(1, 4):
                input_copy(i, plane).wait_send()
            local(s.gout.at[share(i, 0), :], s.input_grad.at[i], 4 + i).wait()


SCRATCH = dict(
    xin=pltpu.VMEM((512, 1152), low),
    gin=pltpu.VMEM((512, 1152), low),
    xout=pltpu.VMEM((512, 1152), low),
    gout=pltpu.VMEM((512, 1152), low),
    wa=pltpu.VMEM((1152, 4608), low),
    wb=pltpu.VMEM((1152, 4608), low),
    norm=pltpu.VMEM((512, 1152), low),
    left=pltpu.VMEM((2, 1152, 512), low),
    wide=pltpu.VMEM((2, 512, 4608), low),
    branch=pltpu.VMEM((512, 1152), low),
    acc=pltpu.VMEM((256, 1152), jnp.float32),
    gb=pltpu.VMEM((256, 1152), low),
    wacc=pltpu.VMEM((256, 3456), jnp.float32),
    stage=pltpu.VMEM((4, 288, 1152), low),
    near_stage=pltpu.VMEM((2, 3, 144, 1152), low),
    out_stage=pltpu.VMEM((2, 144, 1152), jnp.float32),
    gather_send=pltpu.SemaphoreType.DMA((8, 8)),
    gather_recv=pltpu.SemaphoreType.DMA((8, 8)),
    sib_send=pltpu.SemaphoreType.DMA((32,)),
    sib_recv=pltpu.SemaphoreType.DMA((32,)),
    near_send=pltpu.SemaphoreType.DMA((2, 12)),
    near_recv=pltpu.SemaphoreType.DMA((2, 12)),
    out_sem=pltpu.SemaphoreType.DMA((2,)),
    share_send=pltpu.SemaphoreType.DMA((2, 2)),
    xin_recv=pltpu.SemaphoreType.DMA((2, 4)),
    gin_recv=pltpu.SemaphoreType.DMA((2, 4)),
    hop_send=pltpu.SemaphoreType.DMA((2, 2)),
    final_send=pltpu.SemaphoreType.DMA((2, 2, 4)),
    final_recv=pltpu.SemaphoreType.DMA((2, 2)),
    local_sem=pltpu.SemaphoreType.DMA((6,)),
    free=pltpu.SemaphoreType.REGULAR((3,)),
)
REFS = (
    ["tokens", "cotangent", "in_shard", "out_shard", "mod", "time"]
    + ["out_tokens", "input_grad", "grads", "gmod", "gtime"]
    + list(SCRATCH)
)


def mega(tokens, cotangent, in_shard, out_shard, mod_rows, time_rows):
    anywhere = pl.BlockSpec(memory_space=pl.ANY)
    near = pl.BlockSpec(memory_space=pltpu.VMEM)
    width = tokens.shape[2]
    return pl.pallas_call(
        mega_body,
        out_shape=(
            jax.ShapeDtypeStruct(tokens.shape, low),
            jax.ShapeDtypeStruct(tokens.shape, low),
            jax.ShapeDtypeStruct((2,) + in_shard.shape, jnp.float32),
            jax.ShapeDtypeStruct((2, 3, width), jnp.float32),
            jax.ShapeDtypeStruct((2, 1, 3 * width), jnp.float32),
        ),
        in_specs=[anywhere] * 4 + [near] * 2,
        out_specs=[anywhere] * 3 + [near] * 2,
        scratch_shapes=list(SCRATCH.values()),
        compiler_params=pltpu.CompilerParams(
            collective_id=0, has_side_effects=True, vmem_limit_bytes=60 * 2**20
        ),
        cost_estimate=pl.CostEstimate(
            flops=25 * 10**9, bytes_accessed=10**7, transcendentals=10**7
        ),
        name="blocks",
    )(tokens, cotangent, in_shard, out_shard, mod_rows, time_rows)


def fast_shards(
    tokens,
    cotangent,
    timesteps,
    labels,
    class_table,
    section_in_weights,
    section_out_weights,
    modulation_weights,
):
    model_width = tokens.shape[2]
    in_shard, out_shard, mod_shard = (
        section_in_weights[0],
        section_out_weights[0],
        modulation_weights[0],
    )
    condition, own_conditioner, own_time, matches, mod_rows, time_rows = conditioning(
        timesteps, labels, class_table, out_shard, mod_shard
    )
    out_tokens, input_grad, grads, gmod, gtime = mega(
        tokens,
        cotangent,
        in_shard,
        out_shard,
        mod_rows.reshape(2, 3, model_width),
        time_rows.reshape(2, 1, 3 * model_width),
    )
    small_outs = conditioning_grads(
        gmod.reshape(2, 3 * model_width).astype(jnp.bfloat16),
        gtime.reshape(2, 3 * model_width).astype(jnp.bfloat16),
        condition,
        own_conditioner,
        own_time,
        matches,
        out_shard,
        mod_shard,
        grads[1],
    )
    return (
        out_tokens,
        input_grad.astype(jnp.float32),
        small_outs[0],
        grads[0][None],
        small_outs[1][None],
        small_outs[2][None],
    )


def solution(mesh):
    return jax.shard_map(
        fast_shards if mesh.shape["dp"] == 8 else shards,
        mesh=mesh,
        in_specs=(
            P("dp", "pipe", None),
            P("dp", "pipe", None),
            P("dp"),
            P("dp"),
            P(),
            P("pipe", "dp", None),
            P("pipe", "dp", None),
            P("pipe", "dp", None),
        ),
        out_specs=(
            P("dp", "pipe", None),
            P("dp", "pipe", None),
            P(),
            P("pipe", "dp", None),
            P("pipe", "dp", None),
            P("pipe", "dp", None),
        ),
        check_vma=False,
    )
```

```python
from functools import partial
import math
from types import SimpleNamespace

import jax
import jax.numpy as jnp
from jax import lax
from jax.experimental import pallas as pl
from jax.experimental.pallas import tpu as pltpu
from jax.sharding import PartitionSpec as P

HEADS = 16
HEAD = 72


epsilon = 1e-06
highest = lax.Precision.HIGHEST


def shifted(block, axis, distance):
    devices = range(lax.axis_size(axis))
    route = [(i - distance, i) for i in devices if i - distance in devices]
    return lax.ppermute(block, axis, route)


def sinusoid(step_values, model_width):
    half_width = model_width // 2
    frequencies = jnp.exp(
        -math.log(10000.0) * jnp.arange(half_width, dtype=jnp.float32) / half_width
    )
    angles = step_values.astype(jnp.float32)[:, None] * frequencies[None, :]
    return jnp.concatenate([jnp.cos(angles), jnp.sin(angles)], axis=1)


def product(former, latter):
    return jnp.dot(former, latter, preferred_element_type=jnp.float32)


def contract_rows(former, latter):
    return lax.dot_general(
        former, latter, (((0,), (0,)), ((), ())), preferred_element_type=jnp.float32
    )


def contract_cols(former, latter):
    return lax.dot_general(
        former, latter, (((1,), (1,)), ((), ())), preferred_element_type=jnp.float32
    )


def normalize_rows(row_values):
    centered = row_values - jnp.mean(row_values, axis=-1, keepdims=True)
    inverse = lax.rsqrt(jnp.mean(centered * centered, axis=-1, keepdims=True) + epsilon)
    return (centered * inverse, inverse)


def modulation_front(section_input, mod_row):
    model_width = section_input.shape[1]
    shift_vec = mod_row[:model_width]
    scale_vec = mod_row[model_width : 2 * model_width]
    gate_vec = mod_row[2 * model_width :]
    centred, inverse = normalize_rows(section_input.astype(jnp.float32))
    normed = (centred * (1.0 + scale_vec) + shift_vec).astype(jnp.bfloat16)
    return (normed, centred, inverse, scale_vec, gate_vec)


def modulation_back(grad_normed, centred, inverse, scale_vec, grad_rows, grad_gate):
    grad_shift = jnp.sum(grad_normed, axis=0)
    grad_scale = jnp.sum(grad_normed * centred, axis=0)
    grad_centred = grad_normed * (1.0 + scale_vec)
    grad_input = inverse * (
        grad_centred
        - jnp.mean(grad_centred, axis=-1, keepdims=True)
        - centred * jnp.mean(grad_centred * centred, axis=-1, keepdims=True)
    )
    grad_mod = jnp.concatenate([grad_shift, grad_scale, grad_gate]).astype(jnp.bfloat16)
    return (grad_rows + grad_input, grad_mod)


def attention_parts(section_input, mod_row, time_row, weights):
    in_weight = weights[0]
    model_width = section_input.shape[1]
    tok_len = section_input.shape[0]
    normed, centred, inverse, scale_vec, gate_vec = modulation_front(section_input, mod_row)
    qkv = (product(normed, in_weight[:, : 3 * model_width]) + time_row).astype(jnp.bfloat16)
    split_qkv = qkv.reshape(tok_len, 3, HEADS, HEAD)
    queries = split_qkv[:, 0]
    keyed = split_qkv[:, 1]
    valued = split_qkv[:, 2]
    scores = jnp.einsum(
        "qhd,khd->hqk", queries, keyed, preferred_element_type=jnp.float32
    ) * HEAD ** (-0.5)
    probs_full = jax.nn.softmax(scores, axis=-1)
    probs_low = probs_full.astype(jnp.bfloat16)
    mixed = jnp.einsum("hqk,khd->qhd", probs_low, valued, preferred_element_type=jnp.float32)
    head_rows = mixed.reshape(tok_len, model_width).astype(jnp.bfloat16)
    branch = product(head_rows, in_weight[:, 3 * model_width :])
    section_output = section_input.astype(jnp.float32) + gate_vec * branch
    saved_parts = (
        normed,
        centred,
        inverse,
        scale_vec,
        gate_vec,
        queries,
        keyed,
        valued,
        probs_full,
        probs_low,
        head_rows,
        branch,
    )
    return (section_output, saved_parts)


def attention_forward(section_input, mod_row, time_row, weights):
    return attention_parts(section_input, mod_row, time_row, weights)[0]


def attention_backward(section_input, grad_in, mod_row, time_row, weights):
    in_weight = weights[0]
    model_width = section_input.shape[1]
    tok_len = section_input.shape[0]
    unused, saved_parts = attention_parts(section_input, mod_row, time_row, weights)
    (
        normed,
        centred,
        inverse,
        scale_vec,
        gate_vec,
        queries,
        keyed,
        valued,
        probs_full,
        probs_low,
        head_rows,
        branch,
    ) = saved_parts
    grad_rows = grad_in.astype(jnp.float32)
    grad_branch = (gate_vec * grad_rows).astype(jnp.bfloat16)
    grad_gate = jnp.sum(grad_rows * branch, axis=0)
    grad_heads = contract_cols(grad_branch, in_weight[:, 3 * model_width :]).astype(jnp.bfloat16)
    heads_split = grad_heads.reshape(tok_len, HEADS, HEAD)
    grad_probs = jnp.einsum("qhd,khd->hqk", heads_split, valued, preferred_element_type=jnp.float32)
    grad_value = jnp.einsum(
        "hqk,qhd->khd", probs_low, heads_split, preferred_element_type=jnp.float32
    )
    grad_scores = (
        probs_full * (grad_probs - jnp.sum(probs_full * grad_probs, axis=-1, keepdims=True))
    ).astype(jnp.bfloat16)
    grad_query = jnp.einsum(
        "hqk,khd->qhd", grad_scores, keyed, preferred_element_type=jnp.float32
    ) * HEAD ** (-0.5)
    grad_key = jnp.einsum(
        "hqk,qhd->khd", grad_scores, queries, preferred_element_type=jnp.float32
    ) * HEAD ** (-0.5)
    grad_qkv = (
        jnp.stack([grad_query, grad_key, grad_value], axis=1)
        .reshape(tok_len, 3 * model_width)
        .astype(jnp.bfloat16)
    )
    grad_normed = contract_cols(grad_qkv, in_weight[:, : 3 * model_width])
    grad_time = jnp.sum(grad_qkv, axis=0, dtype=jnp.float32).astype(jnp.bfloat16)
    grad_input, grad_mod = modulation_back(
        grad_normed, centred, inverse, scale_vec, grad_rows, grad_gate
    )
    narrow_zero = jnp.zeros((tok_len, model_width), jnp.bfloat16)
    return (
        grad_input,
        normed,
        jnp.concatenate([grad_qkv, narrow_zero], axis=1),
        grad_branch,
        jnp.concatenate([head_rows, narrow_zero, narrow_zero, narrow_zero], axis=1),
        grad_mod,
        grad_time,
    )


def feed_parts(section_input, mod_row, weights):
    in_weight, out_weight = weights
    normed, centred, inverse, scale_vec, gate_vec = modulation_front(section_input, mod_row)
    pre_act = product(normed, in_weight)
    hidden = jax.nn.gelu(pre_act, approximate=True).astype(jnp.bfloat16)
    branch = contract_cols(hidden, out_weight)
    section_output = section_input.astype(jnp.float32) + gate_vec * branch
    return (
        section_output,
        (normed, centred, inverse, scale_vec, gate_vec, pre_act, hidden, branch),
    )


def feed_forward(section_input, mod_row, time_row, weights):
    return feed_parts(section_input, mod_row, weights)[0]


def feed_backward(section_input, grad_in, mod_row, time_row, weights):
    in_weight, out_weight = weights
    unused, saved_parts = feed_parts(section_input, mod_row, weights)
    normed, centred, inverse, scale_vec, gate_vec, pre_act, hidden, branch = saved_parts
    grad_rows = grad_in.astype(jnp.float32)
    grad_branch = (gate_vec * grad_rows).astype(jnp.bfloat16)
    grad_gate = jnp.sum(grad_rows * branch, axis=0)
    grad_hidden = product(grad_branch, out_weight)
    gelu_pull = jax.vjp(partial(jax.nn.gelu, approximate=True), pre_act)[1]
    grad_pre = gelu_pull(grad_hidden)[0].astype(jnp.bfloat16)
    grad_normed = contract_cols(grad_pre, in_weight)
    grad_input, grad_mod = modulation_back(
        grad_normed, centred, inverse, scale_vec, grad_rows, grad_gate
    )
    return (
        grad_input,
        normed,
        grad_pre,
        grad_branch,
        hidden,
        grad_mod,
        jnp.zeros(grad_mod.shape, jnp.bfloat16),
    )


def spare_forward(section_input, mod_row, time_row, weights):
    return jnp.zeros(section_input.shape, jnp.float32)


def spare_backward(section_input, grad_in, mod_row, time_row, weights):
    tok_len, model_width = section_input.shape
    hidden_width = weights[0].shape[1]
    narrow_zero = jnp.zeros((tok_len, model_width), jnp.bfloat16)
    wide_zero = jnp.zeros((tok_len, hidden_width), jnp.bfloat16)
    row_zero = jnp.zeros((3 * model_width,), jnp.bfloat16)
    return (
        jnp.zeros(section_input.shape, jnp.float32),
        narrow_zero,
        wide_zero,
        narrow_zero,
        wide_zero,
        row_zero,
        row_zero,
    )


def attention_weight_grads(left_one, right_one, left_two, right_two):
    width = left_two.shape[1]
    low = jnp.bfloat16
    qkv_term = contract_rows(left_one, right_one[:, : 3 * width]).astype(low)
    out_term = contract_rows(right_two[:, :width], left_two).astype(low)
    zero_term = jnp.zeros((width, right_two.shape[1]), low)
    return (jnp.concatenate([qkv_term, out_term], axis=1), zero_term)


def feed_weight_grads(left_one, right_one, left_two, right_two):
    low = jnp.bfloat16
    return (
        contract_rows(left_one, right_one).astype(low),
        contract_rows(left_two, right_two).astype(low),
    )


def replace_slot(buffer, slot_index, new_rows, active):
    old_rows = lax.dynamic_index_in_dim(buffer, slot_index, 0, keepdims=False)
    return lax.dynamic_update_index_in_dim(
        buffer, jnp.where(active, new_rows, old_rows), slot_index, 0
    )


def shards(
    tokens,
    cotangent,
    timesteps,
    labels,
    class_table,
    section_in_weights,
    section_out_weights,
    modulation_weights,
):
    micro_count = tokens.shape[0]
    model_width = tokens.shape[2]
    hidden_width = section_in_weights.shape[2]
    section_count = lax.axis_size("pipe")
    section_index = lax.axis_index("pipe")
    last_section = section_count - 1
    section_kind = 1 + section_index % 2
    in_shard, out_shard, mod_shard = (
        section_in_weights[0],
        section_out_weights[0],
        modulation_weights[0],
    )
    whole_tokens, whole_cotangent = (
        lax.all_gather(tokens, "pipe", axis=1, tiled=True),
        lax.all_gather(cotangent, "pipe", axis=1, tiled=True),
    )
    tok_len = whole_tokens.shape[1]
    weights = (
        lax.all_gather(in_shard, "dp", axis=0, tiled=True),
        lax.all_gather(out_shard, "dp", axis=0, tiled=True),
    )
    condition, own_conditioner, own_time, matches, mod_rows, time_rows = conditioning(
        timesteps, labels, class_table, out_shard, mod_shard
    )

    def forward_tick(carry, tick_index):
        incoming, kept_inputs, finals = carry
        micro_index = tick_index - section_index
        active = (micro_index >= 0) & (micro_index < micro_count)
        slot_index = jnp.clip(micro_index, 0, micro_count - 1)
        first_rows = lax.dynamic_index_in_dim(whole_tokens, slot_index, 0, keepdims=False)
        section_input = jnp.where(section_index == 0, first_rows, incoming)
        section_output = lax.switch(
            jnp.where(active, section_kind, 0),
            (spare_forward, attention_forward, feed_forward),
            section_input,
            lax.dynamic_index_in_dim(mod_rows, slot_index, 0, keepdims=False),
            lax.dynamic_index_in_dim(time_rows, slot_index, 0, keepdims=False),
            weights,
        )
        output_low = section_output.astype(jnp.bfloat16)
        kept_inputs = replace_slot(kept_inputs, slot_index, section_input, active)
        finals = replace_slot(
            finals, slot_index, output_low, active & (section_index == last_section)
        )
        incoming = shifted(output_low, "pipe", 1)
        return ((incoming, kept_inputs, finals), None)

    empty_rows = jnp.zeros((tok_len, model_width), jnp.bfloat16)
    empty_store = jnp.zeros((micro_count, tok_len, model_width), jnp.bfloat16)
    forward_out, ignored = lax.scan(
        forward_tick,
        (empty_rows, empty_store, empty_store),
        jnp.arange(micro_count + section_count - 1),
    )
    kept_inputs = forward_out[1]
    finals = forward_out[2]
    wide_store = jnp.zeros((micro_count, tok_len, hidden_width), jnp.bfloat16)
    row_store = jnp.zeros((micro_count, 3 * model_width), jnp.bfloat16)
    start_factors = (empty_store, wide_store, empty_store, wide_store, row_store, row_store)

    def backward_tick(carry, tick_index):
        incoming, factors, input_grads = carry
        micro_index = tick_index - (last_section - section_index)
        active = (micro_index >= 0) & (micro_index < micro_count)
        slot_index = jnp.clip(micro_index, 0, micro_count - 1)
        top_grad = lax.dynamic_index_in_dim(whole_cotangent, slot_index, 0, keepdims=False)
        grad_in = jnp.where(section_index == last_section, top_grad, incoming)
        section_input = lax.dynamic_index_in_dim(kept_inputs, slot_index, 0, keepdims=False)
        results = lax.switch(
            jnp.where(active, section_kind, 0),
            (spare_backward, attention_backward, feed_backward),
            section_input,
            grad_in,
            lax.dynamic_index_in_dim(mod_rows, slot_index, 0, keepdims=False),
            lax.dynamic_index_in_dim(time_rows, slot_index, 0, keepdims=False),
            weights,
        )
        grad_low = results[0].astype(jnp.bfloat16)
        factors = tuple(
            (
                replace_slot(buffer, slot_index, fresh, active)
                for buffer, fresh in zip(factors, results[1:])
            )
        )
        input_grads = replace_slot(
            input_grads, slot_index, grad_low, active & (section_index == 0)
        )
        incoming = shifted(grad_low, "pipe", -1)
        return ((incoming, factors, input_grads), None)

    backward_out, ignored = lax.scan(
        backward_tick,
        (empty_rows, start_factors, empty_store),
        jnp.arange(micro_count + section_count - 1),
    )
    factors = backward_out[1]
    input_grads = backward_out[2]
    flat_rows = micro_count * tok_len
    left_one, right_one, left_two, right_two = (
        stored.reshape(flat_rows, stored.shape[2]) for stored in factors[:4]
    )
    in_term, out_term = lax.cond(
        section_index % 2 == 0,
        attention_weight_grads,
        feed_weight_grads,
        left_one,
        right_one,
        left_two,
        right_two,
    )
    in_grad = lax.psum_scatter(in_term, "dp", scatter_dimension=0, tiled=True)
    out_grad = lax.psum_scatter(out_term, "dp", scatter_dimension=0, tiled=True)
    own_out, own_in = (finals, input_grads)
    keep_out = jnp.where(section_index == last_section, own_out, 0)
    keep_in = jnp.where(section_index == 0, own_in, 0)
    output_share = lax.psum_scatter(keep_out, "pipe", scatter_dimension=1, tiled=True)
    input_share = lax.psum_scatter(keep_in, "pipe", scatter_dimension=1, tiled=True)
    small_outs = conditioning_grads(
        factors[4],
        factors[5],
        condition,
        own_conditioner,
        own_time,
        matches,
        out_shard,
        mod_shard,
        out_grad,
    )
    return (
        output_share,
        input_share.astype(jnp.float32),
        small_outs[0],
        in_grad.astype(jnp.float32)[None],
        small_outs[1][None],
        small_outs[2][None],
    )


def conditioning_grads(
    mod_grads,
    time_grads,
    condition,
    own_conditioner,
    own_time,
    matches,
    out_shard,
    mod_shard,
    out_grad,
):
    model_width = condition.shape[1]
    is_attention = lax.axis_index("pipe") % 2 == 0
    all_mod = lax.all_gather(mod_grads, "dp", axis=0, tiled=True)
    all_time = lax.all_gather(time_grads, "dp", axis=0, tiled=True)
    grad_mod_shard = contract_rows(own_conditioner, all_mod)
    cond_grads = contract_cols(all_mod, mod_shard)
    own_token = contract_cols(all_time, out_shard[:, : 3 * model_width]).astype(jnp.bfloat16)
    all_token = lax.all_gather(own_token, "dp", axis=1, tiled=True)
    token_grads = contract_cols(all_token, out_shard[:, 3 * model_width :])
    cond_grads = cond_grads + jnp.where(is_attention, token_grads, 0.0)
    time_out = jnp.concatenate(
        [contract_rows(own_time, all_time), contract_rows(own_conditioner, all_token)], axis=1
    )
    grad_out_shard = jnp.where(is_attention, time_out, out_grad.astype(jnp.float32))
    every_part = lax.all_gather(cond_grads, "pipe", axis=0)
    whole_grads = lax.all_gather(jnp.sum(every_part, axis=0), "dp", axis=1, tiled=True)
    grad_condition = jax.vjp(jax.nn.silu, condition)[1](whole_grads)[0]
    grad_table = lax.dot_general(
        matches.astype(jnp.float32),
        grad_condition,
        (((0,), (0,)), ((), ())),
        precision=highest,
        preferred_element_type=jnp.float32,
    )
    return (grad_table, grad_out_shard, grad_mod_shard)


def conditioning(timesteps, labels, class_table, out_shard, mod_shard):
    model_width = class_table.shape[1]
    own_rows = out_shard.shape[0]
    own_start = lax.axis_index("dp") * own_rows
    all_steps = lax.all_gather(timesteps, "dp", axis=0, tiled=True)
    all_labels = lax.all_gather(labels, "dp", axis=0, tiled=True)
    image_count = all_steps.shape[0]
    classes = class_table.shape[0]
    matches = all_labels[:, None] == lax.broadcasted_iota(jnp.int32, (image_count, classes), 1)
    condition = sinusoid(all_steps, model_width) + product(
        matches.astype(jnp.bfloat16), class_table
    )
    conditioner = jax.nn.silu(condition).astype(jnp.bfloat16)
    own_conditioner = lax.dynamic_slice_in_dim(conditioner, own_start, own_rows, 1)
    mod_rows = lax.psum_scatter(
        product(own_conditioner, mod_shard), "dp", scatter_dimension=0, tiled=True
    )
    own_time = lax.psum_scatter(
        product(own_conditioner, out_shard[:, 3 * model_width :]),
        "dp",
        scatter_dimension=1,
        tiled=True,
    ).astype(jnp.bfloat16)
    time_rows = lax.psum_scatter(
        product(own_time, out_shard[:, : 3 * model_width]), "dp", scatter_dimension=0, tiled=True
    )
    return (condition, own_conditioner, own_time, matches, mod_rows, time_rows)


ROWS = 256
SPAN = 768
THIRD = 384
PART = 1152
BLOCK = 144
MESH = pl.DeviceIdType.MESH
low = jnp.bfloat16
GELU_A = math.sqrt(2.0 / math.pi)
GELU_B = 0.044715


def product_nt(former, latter):
    return contract_cols(former, latter)


def spread(index, width):
    return pl.ds(pl.multiple_of(index * width, 128), width)


def image_rows(i):
    return pl.ds(pl.multiple_of(i * ROWS, ROWS), ROWS)


def block_rows(b):
    return pl.ds(pl.multiple_of(b * BLOCK, 16), BLOCK)


def front(i, s):
    rows = image_rows(i)
    xhat, inverse = normalize_rows(s.xin[rows, :].astype(jnp.float32))
    normed = (xhat * (1.0 + s.mod[i, :, PART : 2 * PART]) + s.mod[i, :, 0:PART]).astype(low)
    s.norm[rows, :] = normed
    s.left[0, :, rows] = normed.T


def finish(i, s):
    rows = image_rows(i)
    branch = s.acc[...]
    s.branch[rows, :] = branch.astype(low)
    gate = s.mod[i, :, 2 * PART : 3 * PART]
    s.xout[rows, :] = (s.xin[rows, :].astype(jnp.float32) + gate * branch).astype(low)


def feed_up_down(i, s):
    rows = image_rows(i)
    s.acc[...] = jnp.zeros(s.acc.shape, jnp.float32)

    def tile(j, carry):
        cols = spread(j, SPAN)
        value = product(s.norm[rows, :], s.wa[:, cols])
        square = value * value
        wave = jnp.tanh(value * (GELU_A + (GELU_A * GELU_B) * square))
        half = 0.5 + 0.5 * wave
        hidden = (value * half).astype(low)
        slope = half + value * (0.5 - 0.5 * (wave * wave)) * (
            GELU_A + (3.0 * GELU_A * GELU_B) * square
        )
        s.wide[0, rows, cols] = hidden
        s.wide[1, rows, cols] = slope.astype(low)
        s.acc[...] += product_nt(hidden, s.wb[:, cols])
        return carry

    lax.fori_loop(0, s.wa.shape[1] // SPAN, tile, 0)


def feed_down_up(i, s):
    rows = image_rows(i)
    s.acc[...] = jnp.zeros(s.acc.shape, jnp.float32)

    def tile(j, carry):
        cols = spread(j, SPAN)
        grad_hidden = product(s.gb[...], s.wb[:, cols])
        grad_pre = (grad_hidden * s.wide[1, rows, cols].astype(jnp.float32)).astype(low)
        s.wide[1, rows, cols] = grad_pre
        s.acc[...] += product_nt(grad_pre, s.wa[:, cols])
        return carry

    lax.fori_loop(0, s.wa.shape[1] // SPAN, tile, 0)


def back_start(i, s):
    rows = image_rows(i)
    grad = s.gin[rows, :].astype(jnp.float32)
    gb = (s.mod[i, :, 2 * PART : 3 * PART] * grad).astype(low)
    s.gb[...] = gb
    s.grad_rows[i, :, 2 * PART : 3 * PART] = jnp.sum(
        grad * s.branch[rows, :].astype(jnp.float32), axis=0, keepdims=True
    )
    return gb


def back_finish(i, s):
    rows = image_rows(i)
    xhat, inverse = normalize_rows(s.xin[rows, :].astype(jnp.float32))
    gn = s.acc[...]
    s.grad_rows[i, :, 0:PART] = jnp.sum(gn, axis=0, keepdims=True)
    s.grad_rows[i, :, PART : 2 * PART] = jnp.sum(gn * xhat, axis=0, keepdims=True)
    gx = gn * (1.0 + s.mod[i, :, PART : 2 * PART])
    first = jnp.mean(gx, axis=-1, keepdims=True)
    second = jnp.mean(gx * xhat, axis=-1, keepdims=True)
    grad = s.gin[rows, :].astype(jnp.float32)
    s.gout[rows, :] = (grad + inverse * (gx - first - xhat * second)).astype(low)


def kernel_feed_forward(i, s):
    front(i, s)
    feed_up_down(i, s)
    finish(i, s)


def kernel_feed_backward(i, s):
    gb = back_start(i, s)
    s.left[1, :, image_rows(i)] = gb.T
    feed_down_up(i, s)
    back_finish(i, s)


def project(i, s, part):
    rows = image_rows(i)

    def tile(j, carry):
        cols = pl.ds(pl.multiple_of(part * PART + j * THIRD, 128), THIRD)
        value = product(s.norm[rows, :], s.wa[:, cols]) + s.time[i, :, cols]
        s.wide[0, rows, cols] = value.astype(low)
        return carry

    lax.fori_loop(0, PART // THIRD, tile, 0)


def head_window(h):
    start = jnp.minimum((h * HEAD) // 128, PART // 128 - 2)
    offset = h * HEAD - start * 128
    lanes = lax.broadcasted_iota(jnp.int32, (ROWS, 256), 1)
    inside = (lanes >= offset) & (lanes < offset + HEAD)
    return start, inside


def window(start, part):
    return pl.ds(pl.multiple_of(part * PART + start * 128, 128), 256)


def prob_place(i, h):
    return (
        pl.ds(pl.multiple_of((h % 4) * ROWS, ROWS), ROWS),
        pl.ds(pl.multiple_of((4 * i + h // 4) * ROWS, ROWS), ROWS),
    )


def attend(i, s):
    rows = image_rows(i)
    s.acc[...] = jnp.zeros(s.acc.shape, jnp.float32)

    def head(h, carry):
        start, inside = head_window(h)
        zero = jnp.zeros((), low)
        query = jnp.where(inside, s.wide[0, rows, window(start, 0)], zero)
        key = s.wide[0, rows, window(start, 1)]
        value = jnp.where(inside, s.wide[0, rows, window(start, 2)], zero)
        scores = product_nt(query, key) * HEAD ** (-0.5)
        top = jnp.max(scores, axis=-1, keepdims=True)
        powers = jnp.exp(scores - top)
        probs = (powers * (1.0 / jnp.sum(powers, axis=-1, keepdims=True))).astype(low)
        place = prob_place(i, h)
        s.wb[place[0], place[1]] = probs
        s.acc[:, window(start, 0)] += product(probs, value)
        return carry

    lax.fori_loop(0, HEADS, head, 0)
    mixed = s.acc[...].astype(low)
    s.left[1, :, rows] = mixed.T
    s.acc[...] = product(mixed, s.wa[:, 3 * PART :])


def kernel_attention_backward(i, s):
    rows = image_rows(i)
    gb = back_start(i, s)
    s.wide[1, rows, 3 * PART :] = gb
    s.gb[...] = product_nt(gb, s.wa[:, 3 * PART :]).astype(low)
    s.wacc[...] = jnp.zeros(s.wacc.shape, jnp.float32)

    def head(h, carry):
        start, inside = head_window(h)
        zero = jnp.zeros((), low)
        query = jnp.where(inside, s.wide[0, rows, window(start, 0)], zero)
        key = jnp.where(inside, s.wide[0, rows, window(start, 1)], zero)
        value = s.wide[0, rows, window(start, 2)]
        grad_head = jnp.where(inside, s.gb[:, window(start, 0)], zero)
        place = prob_place(i, h)
        probs = s.wb[place[0], place[1]]
        probs_full = probs.astype(jnp.float32)
        grad_probs = product_nt(grad_head, value)
        s.wacc[:, window(start, 2)] += contract_rows(probs, grad_head)
        mixed = jnp.sum(probs_full * grad_probs, axis=-1, keepdims=True)
        grad_scores = (probs_full * (grad_probs - mixed)).astype(low)
        s.wacc[:, window(start, 0)] += product(grad_scores, key)
        s.wacc[:, window(start, 1)] += contract_rows(grad_scores, query)
        return carry

    lax.fori_loop(0, HEADS, head, 0)
    scale = HEAD ** (-0.5)
    for part, factor in ((0, scale), (1, scale), (2, 1.0)):
        cols = pl.ds(part * PART, PART)
        grads = (s.wacc[:, cols] * factor).astype(low)
        s.wide[1, rows, cols] = grads
        s.grad_rows[i, :, pl.ds((3 + part) * PART, PART)] = jnp.sum(
            grads.astype(jnp.float32), axis=0, keepdims=True
        )
    s.acc[...] = jnp.zeros(s.acc.shape, jnp.float32)

    def tile(j, carry):
        cols = spread(j, THIRD)
        s.acc[...] += product_nt(s.wide[1, rows, cols], s.wa[:, cols])
        return carry

    lax.fori_loop(0, 3 * PART // THIRD, tile, 0)
    back_finish(i, s)


def places():
    dp, pipe = lax.axis_index("dp"), lax.axis_index("pipe")
    core, x_bit, y_bit = dp % 2, (dp // 2) % 2, dp // 4
    sib = dp + 1 - 2 * core
    step_x, step_y = 2 - 4 * x_bit, 4 - 8 * y_bit
    return SimpleNamespace(
        dp=dp,
        pipe=pipe,
        core=core,
        sib=sib,
        x=dp + step_x,
        y=dp + step_y,
        d=dp + step_x + step_y,
        step_x=step_x,
        step_y=step_y,
        x_bit=x_bit,
        y_bit=y_bit,
    )


def gather_weights(s, at, chunks, between, ready):
    def held(k):
        return (s.wa if k < 4 else s.wb), pl.ds((k % 4) * PART, PART)

    def piece(k, block, first=0, count=BLOCK):
        ref, cols = held(k)
        return ref.at[pl.ds(pl.multiple_of(block * BLOCK + first, 16), count), cols]

    def copy(k, kind, ref, target, source=None):
        return pltpu.make_async_remote_copy(
            src_ref=ref if source is None else source,
            dst_ref=ref,
            send_sem=s.gather_send.at[k, kind],
            recv_sem=s.gather_recv.at[k, kind],
            device_id=(target, at.pipe),
            device_id_type=MESH,
        )

    def via_y(k):
        return (0, 80) if k % 2 == 0 else (0, 64)

    def via_x(k):
        return (80, 64) if k % 2 == 0 else (64, 80)

    sib_x, sib_y, sib_d = (
        at.sib + at.step_x,
        at.sib + at.step_y,
        at.sib + at.step_x + at.step_y,
    )

    def sends(k):
        shard = s.in_shard if k < 4 else s.out_shard
        source = shard.at[:, pl.ds((k % 4) * PART, PART)]
        return {
            0: lambda: copy(k, 0, piece(k, at.dp), at.x, source),
            1: lambda: copy(k, 1, piece(k, at.dp), at.y, source),
            2: lambda: copy(k, 2, piece(k, at.dp), at.sib, source),
            3: lambda: copy(k, 3, piece(k, at.x), at.sib),
            4: lambda: copy(k, 4, piece(k, at.x, *via_y(k)), at.y),
            5: lambda: copy(k, 5, piece(k, at.y), at.sib),
            6: lambda: copy(k, 6, piece(k, at.y, *via_x(k)), at.x),
            7: lambda: copy(k, 7, piece(k, at.d), at.sib),
        }

    def arrivals(k):
        return {
            0: lambda: copy(k, 0, piece(k, at.x), at.x),
            1: lambda: copy(k, 1, piece(k, at.y), at.y),
            2: lambda: copy(k, 2, piece(k, at.sib), at.sib),
            3: lambda: copy(k, 3, piece(k, sib_x), at.sib),
            4: lambda: copy(k, 4, piece(k, at.d, *via_y(k)), at.y),
            5: lambda: copy(k, 5, piece(k, sib_y), at.sib),
            6: lambda: copy(k, 6, piece(k, at.d, *via_x(k)), at.x),
            7: lambda: copy(k, 7, piece(k, sib_d), at.sib),
        }

    def start(k, *kinds):
        for kind in kinds:
            sends(k)[kind]().start()

    def arrive(k, *kinds):
        for kind in kinds:
            arrivals(k)[kind]().wait_recv()

    for k in range(3):
        start(k, 0, 1, 2)
    between()
    for k in range(chunks + 2):
        if k < chunks:
            arrive(k, 0)
            start(k, 3, 4)
            arrive(k, 1)
            start(k, 5, 6)
            if k + 3 < chunks:
                start(k + 3, 0, 1, 2)
        if 1 <= k <= chunks:
            arrive(k - 1, 4, 6)
            start(k - 1, 7)
        if k >= 2:
            arrive(k - 2, 2, 3, 5, 7)
            ready(k - 2)
    for k in range(chunks):
        for kind in range(8):
            sends(k)[kind]().wait_send()


def scatter_grads(s, at, is_feed, between):
    total = jnp.where(is_feed, 32, 16)
    chip = at.dp // 2
    chip_x, chip_y = chip + 1 - 2 * at.x_bit, chip + 2 - 4 * at.y_bit
    chip_d = chip_x + 2 - 4 * at.y_bit

    def unit(u):
        matrix, v = u // 16, u % 16
        group, turn, n = v // 4, v % 2, (v % 4) // 2
        near = chip_x + turn * (chip_y - chip_x)
        block = jnp.where(group == 0, chip_d, jnp.where(group == 3, chip, near))
        part = jnp.where(
            group == 3, v % 4, jnp.where(group == 2, 2 * (1 - turn) + n, 2 * turn + n)
        )
        return matrix, group, turn, n, block, part

    def sib_place(u):
        return s.wb.at[block_rows(u % 8), spread(u // 8, PART)]

    def near_place(matrix, turn, slot):
        index = turn * 12 + matrix * 6 + slot
        return s.wa.at[block_rows(index % 8), spread(index // 8, PART)]

    def sib_copy(u):
        return pltpu.make_async_remote_copy(
            src_ref=s.stage.at[u % 4, block_rows(1 - at.core), :],
            dst_ref=sib_place(u),
            send_sem=s.sib_send.at[u],
            recv_sem=s.sib_recv.at[u],
            device_id=(at.sib, at.pipe),
            device_id_type=MESH,
        )

    def near_copy(matrix, turn, slot):
        return pltpu.make_async_remote_copy(
            src_ref=s.near_stage.at[turn, slot],
            dst_ref=near_place(matrix, turn, slot),
            send_sem=s.near_send.at[turn, matrix * 6 + slot],
            recv_sem=s.near_recv.at[turn, matrix * 6 + slot],
            device_id=(at.x + turn * (at.y - at.x), at.pipe),
            device_id_type=MESH,
        )

    def compute(u):
        matrix, group, turn, n, block, part = unit(u)
        first = is_feed & (matrix == 0)
        lhs = jnp.where(first | (jnp.logical_not(is_feed) & (part == 3)), 1, 0)
        rhs = jnp.where(first, 0, 1)

        @pl.when(u >= 4)
        def _():
            sib_copy(u - 4).wait_send()

        rows = pl.ds(pl.multiple_of(block * 288, 16), 288)
        s.stage[u % 4] = product(s.left[lhs, rows, :], s.wide[rhs, :, spread(part, PART)]).astype(
            low
        )
        sib_copy(u).start()

    def settle(u):
        matrix, group, turn, n, block, part = unit(u)
        sib_copy(u).wait_recv()
        own = s.stage[u % 4, block_rows(at.core), :].astype(jnp.float32)
        place = (block_rows(u % 8), spread(u // 8, PART))
        value = own + s.wb[place].astype(jnp.float32)
        slot = group * 2 + n

        def taken(from_turn, from_slot):
            near_copy(matrix, from_turn, from_slot).wait_recv()
            index = from_turn * 12 + matrix * 6 + from_slot
            return s.wa[block_rows(index % 8), spread(index // 8, PART)].astype(jnp.float32)

        @pl.when(group < 3)
        def _():
            @pl.when(matrix > 0)
            def _():
                near_copy(0, turn, slot).wait_send()

            @pl.when(group < 2)
            def _():
                s.near_stage[turn, slot] = value.astype(low)

            @pl.when(group == 2)
            def _():
                s.near_stage[turn, slot] = (value + taken(1 - turn, n)).astype(
                    low
                )

            near_copy(matrix, turn, slot).start()

        @pl.when(group == 3)
        def _():
            @pl.when((matrix > 0) | (part >= 2))
            def _():
                grad_copy(u - jnp.where(part >= 2, 2, 14)).wait()

            whole = value + taken(0, 2 + part) + taken(1, (part + 2) % 4 + 2)
            s.out_stage[part % 2] = whole
            grad_copy(u).start()

    def grad_copy(u):
        matrix, v = u // 16, u % 16
        which = jnp.where(is_feed, 1 - matrix, 0)
        return pltpu.make_async_copy(
            s.out_stage.at[v % 2], s.grads.at[which, :, spread(v % 4, PART)], s.out_sem.at[v % 2]
        )

    def step(u, carry):
        @pl.when(u < total)
        def _():
            compute(u)

        @pl.when(u >= 2)
        def _():
            settle(u - 2)

        @pl.when(u == 9)
        def _():
            between()

        return carry

    lax.fori_loop(0, total + 2, step, 0)
    matrices = jnp.where(is_feed, 2, 1)

    def rest(k, carry):
        sib_copy(total - 4 + k).wait_send()
        return carry

    lax.fori_loop(0, 4, rest, 0)
    for turn in range(2):
        for slot in range(6):
            near_copy(matrices - 1, turn, slot).wait_send()
    for k in (2, 1):
        grad_copy(total - k).wait()


def exchange(s, at, number, piece, landing):
    def copy(target, source):
        return pltpu.make_async_remote_copy(
            src_ref=piece(target),
            dst_ref=landing(source),
            send_sem=s.swap_send.at[number, target],
            recv_sem=s.swap_recv.at[number, source],
            device_id=(target, at.pipe),
            device_id_type=MESH,
        )

    others = [(at.dp + k) % 8 for k in range(1, 8)]

    def start():
        for other in others:
            copy(other, at.dp).start()

    def arrive():
        for other in others:
            copy(other, other).wait_recv()

    def done():
        for other in others:
            copy(other, at.dp).wait_send()

    return SimpleNamespace(start=start, arrive=arrive, done=done)


def exchanges(s, at):
    def pair(j):
        return pl.ds(2 * j, 2)

    return SimpleNamespace(
        rows=exchange(s, at, 0, lambda j: s.cond_in, lambda j: s.rows.at[pair(j)]),
        mods=exchange(s, at, 1, lambda j: s.mod_parts.at[pair(j)], lambda j: s.mod_all.at[j]),
        tokens=exchange(s, at, 2, lambda j: s.token, lambda j: s.token_all.at[pair(j)]),
        times=exchange(s, at, 3, lambda j: s.time_parts.at[pair(j)], lambda j: s.time_all.at[j]),
        grads=exchange(s, at, 4, lambda j: s.grad_rows, lambda j: s.grad_all.at[pair(j)]),
        backs=exchange(s, at, 5, lambda j: s.back, lambda j: s.back_all.at[j]),
        ends=exchange(s, at, 6, lambda j: s.end, lambda j: s.end_all.at[j]),
    )


def shard_copies(s, is_feed):
    copies = []
    for part in range(3):
        cols = pl.ds(part * PART, PART)
        rows = pl.ds(part * BLOCK, BLOCK)
        copies.append((s.mod_shard.at[:, cols], s.norm.at[rows, :]))
        copies.append((s.out_shard.at[:, cols], s.branch.at[rows, :]))
    copies.append((s.out_shard.at[:, pl.ds(3 * PART, PART)], s.gb.at[pl.ds(0, BLOCK), :]))
    return [
        pltpu.make_async_copy(source, target, s.shard_sem.at[k])
        for k, (source, target) in enumerate(copies)
    ]


def shard_part(ref, part):
    return ref[pl.ds(part * BLOCK, BLOCK), :]


def stack_rows(source, target, width):
    for k in range(16):
        target[k : k + 1, 0:width] = source[k, :, 0:width]


def chosen(at):
    places = lax.broadcasted_iota(jnp.int32, (PART, BLOCK), 0)
    lanes = lax.broadcasted_iota(jnp.int32, (PART, BLOCK), 1)
    return jnp.where(places == lanes + at.dp * BLOCK, 1.0, 0.0).astype(low)


def condition_front(s, at, swap, is_feed):
    for copy in shard_copies(s, is_feed):
        copy.start()
    s.rows[pl.ds(2 * at.dp, 2)] = s.cond_in[...]
    s.grad_rows[...] = jnp.zeros(s.grad_rows.shape, jnp.float32)
    swap.rows.arrive()
    stack_rows(s.rows, s.flat, PART)
    condition = s.flat[:, 0:PART]
    conditioner = (condition * (1.0 / (1.0 + jnp.exp(-condition)))).astype(low)
    pick = chosen(at)
    own = product(conditioner, pick).astype(low)
    s.own_cond[...] = own
    for copy in shard_copies(s, is_feed):
        copy.wait()
    for part in range(3):
        s.flat[:, part * PART : (part + 1) * PART] = product(own, shard_part(s.norm, part))
    s.flat[:, 3 * PART : 4 * PART] = product(own, s.gb[0:BLOCK, :])
    for k in range(16):
        s.mod_parts[k] = s.flat[k : k + 1, 0 : 4 * PART]
    swap.mods.start()
    s.mod_all[at.dp] = s.mod_parts[pl.ds(2 * at.dp, 2)]
    swap.mods.arrive()
    for i in range(2):
        total = jnp.sum(s.mod_all[:, i], axis=0)
        s.mod[i] = total[:, 0 : 3 * PART]
        s.token[i] = total[:, 3 * PART :]

    @pl.when(jnp.logical_not(is_feed))
    def _():
        swap.tokens.start()
        s.token_all[pl.ds(2 * at.dp, 2)] = s.token[...]
        swap.tokens.arrive()
        stack_rows(s.token_all, s.flat, PART)
        own_token = product(s.flat[:, 0:PART].astype(low), pick).astype(low)
        s.own_token[...] = own_token
        for part in range(3):
            s.flat[:, part * PART : (part + 1) * PART] = product(
                own_token, shard_part(s.branch, part)
            )
        for k in range(16):
            s.time_parts[k] = s.flat[k : k + 1, 0 : 3 * PART]
        swap.times.start()
        s.time_all[at.dp] = s.time_parts[pl.ds(2 * at.dp, 2)]
        swap.times.arrive()
        for i in range(2):
            s.time[i] = jnp.sum(s.time_all[:, i], axis=0)


def end_copy(s, at, plane):
    return pltpu.make_async_remote_copy(
        src_ref=s.end_parts.at[at.pipe],
        dst_ref=s.end_parts.at[at.pipe],
        send_sem=s.end_send.at[plane],
        recv_sem=s.end_recv.at[at.pipe],
        device_id=(at.dp, plane),
        device_id_type=MESH,
    )


def end_arrival(s, at, plane):
    return pltpu.make_async_remote_copy(
        src_ref=s.end_parts.at[plane],
        dst_ref=s.end_parts.at[plane],
        send_sem=s.end_send.at[plane],
        recv_sem=s.end_recv.at[plane],
        device_id=(at.dp, plane),
        device_id_type=MESH,
    )


def condition_back(s, at, swap, is_feed):
    for copy in shard_copies(s, is_feed):
        copy.start()
    s.grad_all[pl.ds(2 * at.dp, 2)] = s.grad_rows[...]
    swap.grads.arrive()
    stack_rows(s.grad_all, s.flat, 6 * PART)
    own = s.own_cond[...]
    for copy in shard_copies(s, is_feed):
        copy.wait()
    s.end[...] = jnp.zeros(s.end.shape, jnp.float32)
    for part in range(3):
        cols = slice(part * PART, (part + 1) * PART)
        grads = s.flat[:, cols].astype(low)
        s.wacc[0:BLOCK, cols] = contract_rows(own, grads)
        s.end[...] += product_nt(grads, shard_part(s.norm, part))
    mod_out = pltpu.make_async_copy(s.wacc.at[pl.ds(0, BLOCK), :], s.mod_grad, s.shard_sem.at[0])
    mod_out.start()

    @pl.when(jnp.logical_not(is_feed))
    def _():
        token = jnp.zeros((16, BLOCK), jnp.float32)
        for part in range(3):
            grads = s.flat[:, (3 + part) * PART : (4 + part) * PART].astype(low)
            token += product_nt(grads, shard_part(s.branch, part))
        s.back[...] = product_nt(token.astype(low), chosen(at)).astype(low)
        swap.backs.start()
        s.back_all[at.dp] = s.back[...]
        mod_out.wait()
        for part in range(3):
            grads = s.flat[:, (3 + part) * PART : (4 + part) * PART].astype(low)
            s.wacc[0:BLOCK, part * PART : (part + 1) * PART] = contract_rows(
                s.own_token[...], grads
            )
        swap.backs.arrive()
        whole = jnp.zeros((16, PART), jnp.float32)
        for k in range(8):
            whole += s.back_all[k].astype(jnp.float32)
        whole = whole.astype(low)
        s.acc[0:BLOCK, :] = contract_rows(own, whole)
        s.end[...] += product_nt(whole, s.gb[0:BLOCK, :])
        wide_out = pltpu.make_async_copy(
            s.wacc.at[pl.ds(0, BLOCK), :],
            s.grads.at[1, :, pl.ds(0, 3 * PART)],
            s.shard_sem.at[0],
        )
        thin_out = pltpu.make_async_copy(
            s.acc.at[pl.ds(0, BLOCK), :],
            s.grads.at[1, :, pl.ds(3 * PART, PART)],
            s.shard_sem.at[1],
        )
        wide_out.start()
        thin_out.start()
        wide_out.wait()
        thin_out.wait()

    @pl.when(is_feed)
    def _():
        mod_out.wait()

    s.end_parts[at.pipe] = s.end[...]
    for k in range(1, 4):
        end_copy(s, at, (at.pipe + k) % 4).start()


def condition_end(s, at, swap, is_feed):
    for k in range(1, 4):
        end_arrival(s, at, (at.pipe + k) % 4).wait_recv()
    s.end[...] = s.end_parts[0] + s.end_parts[1] + s.end_parts[2] + s.end_parts[3]
    swap.ends.start()
    s.end_all[at.dp] = s.end[...]
    swap.ends.arrive()
    s.cond_grads[...] = s.end_all[...]
    s.rows_out[...] = s.rows[...]
    for each in (swap.rows, swap.mods, swap.grads, swap.ends):
        each.done()
    for k in range(1, 4):
        end_copy(s, at, (at.pipe + k) % 4).wait_send()

    @pl.when(jnp.logical_not(is_feed))
    def _():
        for each in (swap.tokens, swap.times, swap.backs):
            each.done()


def mega_body(*refs):
    s = SimpleNamespace(**dict(zip(REFS, refs)))
    at = places()
    is_feed = at.pipe % 2 == 1
    pipe = at.pipe
    barrier = pltpu.get_barrier_semaphore()
    swap = exchanges(s, at)
    targets = [((at.dp + k) % 8, pipe) for k in range(1, 8)]
    targets += [(at.dp, (pipe + k) % 4) for k in range(1, 4)]
    for target in targets:
        pl.semaphore_signal(barrier, inc=1, device_id=target, device_id_type=MESH)
    pl.semaphore_wait(barrier, len(targets))
    swap.rows.start()

    def remote(source, target, send, recv, plane):
        return pltpu.make_async_remote_copy(
            src_ref=source,
            dst_ref=target,
            send_sem=send,
            recv_sem=recv,
            device_id=(at.dp, plane),
            device_id_type=MESH,
        )

    def share(i, plane):
        return pl.ds(pl.multiple_of(i * ROWS + plane * 64, 64), 64)

    def token_copy(i, plane):
        return remote(
            s.tokens.at[i],
            s.xin.at[share(i, plane), :],
            s.share_send.at[0, i],
            s.xin_recv.at[i, plane],
            0,
        )

    def cotangent_copy(i, plane):
        return remote(
            s.cotangent.at[i],
            s.gin.at[share(i, plane), :],
            s.share_send.at[1, i],
            s.gin_recv.at[i, plane],
            3,
        )

    def next_copy(i):
        whole = image_rows(i)
        return remote(
            s.xout.at[whole, :],
            s.xin.at[whole, :],
            s.hop_send.at[0, i],
            s.xin_recv.at[i, 0],
            jnp.minimum(pipe + 1, 3),
        )

    def back_copy(i):
        whole = image_rows(i)
        return remote(
            s.gout.at[whole, :],
            s.gin.at[whole, :],
            s.hop_send.at[1, i],
            s.gin_recv.at[i, 3],
            jnp.maximum(pipe - 1, 0),
        )

    def output_copy(i, plane):
        return remote(
            s.xout.at[share(i, plane), :],
            s.out_tokens.at[i],
            s.final_send.at[0, i, plane],
            s.final_recv.at[0, i],
            plane,
        )

    def input_copy(i, plane):
        return remote(
            s.gout.at[share(i, plane), :],
            s.input_grad.at[i],
            s.final_send.at[1, i, plane],
            s.final_recv.at[1, i],
            plane,
        )

    def local(source, target, index):
        return pltpu.make_async_copy(source, target, s.local_sem.at[index])

    own_in = local(s.in_shard, s.wa.at[block_rows(at.dp), :], 0)
    own_out = local(s.out_shard, s.wb.at[block_rows(at.dp), :], 1)
    own_in.start()

    @pl.when(is_feed)
    def _():
        own_out.start()

    for i in range(2):
        own_tokens = local(s.tokens.at[i], s.xin.at[pl.ds(i * ROWS, 64), :], 2 + i)
        own_cotangent = local(s.cotangent.at[i], s.gin.at[pl.ds(i * ROWS + 192, 64), :], 4 + i)

        @pl.when(pipe == 0)
        def _():
            own_tokens.start()

        @pl.when(pipe == 3)
        def _():
            own_cotangent.start()

        @pl.when(pipe != 0)
        def _():
            token_copy(i, pipe).start()

    def between():
        condition_front(s, at, swap, is_feed)

    def ready(k):
        if k == 0:
            for i in range(2):
                local(s.tokens.at[i], s.xin.at[pl.ds(i * ROWS, 64), :], 2 + i).wait()
                for plane in range(1, 4):
                    token_copy(i, plane).wait_recv()
                front(i, s)
        if k < 3:

            def one(i, carry):
                project(i, s, k)
                return carry

            lax.fori_loop(0, 2, one, 0)

    own_in.wait()

    @pl.when(pipe == 0)
    def _():
        gather_weights(s, at, 4, between, ready)

    @pl.when(pipe == 2)
    def _():
        gather_weights(s, at, 4, between, lambda k: None)

    @pl.when(is_feed)
    def _():
        own_out.wait()
        gather_weights(s, at, 8, between, lambda k: None)

    for i in range(2):

        @pl.when(pipe != 0)
        def _():
            token_copy(i, pipe).wait_send()

        @pl.when(pipe != 3)
        def _():
            cotangent_copy(i, pipe).start()

    def step(n, carry):
        at_end = pipe == 3
        goes_forward = jnp.where(at_end, n % 2 == 0, n < 2)
        i = jnp.where(at_end, n // 2, n % 2)

        @pl.when(goes_forward)
        def _():
            @pl.when(pipe != 0)
            def _():
                next_copy(i).wait_recv()

            @pl.when(is_feed)
            def _():
                kernel_feed_forward(i, s)

            @pl.when(jnp.logical_not(is_feed))
            def _():
                @pl.when(pipe != 0)
                def _():
                    front(i, s)

                    def one(part, carry):
                        project(i, s, part)
                        return carry

                    lax.fori_loop(0, 3, one, 0)

                attend(i, s)
                finish(i, s)

            @pl.when(pipe != 3)
            def _():
                next_copy(i).start()

            @pl.when(pipe == 3)
            def _():
                for plane in range(3):
                    output_copy(i, plane).start()
                local(s.xout.at[share(i, 3), :], s.out_tokens.at[i], 2 + i).start()

        @pl.when(jnp.logical_not(goes_forward))
        def _():
            @pl.when(pipe == 3)
            def _():
                local(s.cotangent.at[i], s.gin.at[share(i, 3), :], 4 + i).wait()
                for plane in range(3):
                    cotangent_copy(i, plane).wait_recv()

            @pl.when(pipe != 3)
            def _():
                back_copy(i).wait_recv()

            @pl.when(is_feed)
            def _():
                kernel_feed_backward(i, s)

            @pl.when(jnp.logical_not(is_feed))
            def _():
                kernel_attention_backward(i, s)

            @pl.when(pipe != 0)
            def _():
                back_copy(i).start()

            @pl.when(pipe == 0)
            def _():
                for plane in range(1, 4):
                    input_copy(i, plane).start()
                local(s.gout.at[share(i, 0), :], s.input_grad.at[i], 4 + i).start()

        return carry

    lax.fori_loop(0, 4, step, 0)
    swap.grads.start()

    for target, sem in ((at.sib, 0), (at.x, 1), (at.y, 2)):
        pl.semaphore_signal(
            s.free.at[sem], inc=1, device_id=(target, pipe), device_id_type=MESH
        )
    for sem in range(3):
        pl.semaphore_wait(s.free.at[sem], 1)
    scatter_grads(s, at, is_feed, lambda: condition_back(s, at, swap, is_feed))
    condition_end(s, at, swap, is_feed)

    for i in range(2):

        @pl.when(pipe != 3)
        def _():
            cotangent_copy(i, pipe).wait_send()
            next_copy(i).wait_send()
            output_copy(i, pipe).wait_recv()

        @pl.when(pipe == 3)
        def _():
            for plane in range(3):
                output_copy(i, plane).wait_send()
            local(s.xout.at[share(i, 3), :], s.out_tokens.at[i], 2 + i).wait()

        @pl.when(pipe != 0)
        def _():
            back_copy(i).wait_send()
            input_copy(i, pipe).wait_recv()

        @pl.when(pipe == 0)
        def _():
            for plane in range(1, 4):
                input_copy(i, plane).wait_send()
            local(s.gout.at[share(i, 0), :], s.input_grad.at[i], 4 + i).wait()


SCRATCH = dict(
    xin=pltpu.VMEM((512, 1152), low),
    gin=pltpu.VMEM((512, 1152), low),
    xout=pltpu.VMEM((512, 1152), low),
    gout=pltpu.VMEM((512, 1152), low),
    wa=pltpu.VMEM((1152, 4608), low),
    wb=pltpu.VMEM((1152, 4608), low),
    norm=pltpu.VMEM((512, 1152), low),
    left=pltpu.VMEM((2, 1152, 512), low),
    wide=pltpu.VMEM((2, 512, 4608), low),
    branch=pltpu.VMEM((512, 1152), low),
    acc=pltpu.VMEM((256, 1152), jnp.float32),
    gb=pltpu.VMEM((256, 1152), low),
    wacc=pltpu.VMEM((256, 3456), jnp.float32),
    stage=pltpu.VMEM((4, 288, 1152), low),
    near_stage=pltpu.VMEM((2, 6, 144, 1152), low),
    out_stage=pltpu.VMEM((2, 144, 1152), jnp.float32),
    gather_send=pltpu.SemaphoreType.DMA((8, 8)),
    gather_recv=pltpu.SemaphoreType.DMA((8, 8)),
    sib_send=pltpu.SemaphoreType.DMA((32,)),
    sib_recv=pltpu.SemaphoreType.DMA((32,)),
    near_send=pltpu.SemaphoreType.DMA((2, 12)),
    near_recv=pltpu.SemaphoreType.DMA((2, 12)),
    out_sem=pltpu.SemaphoreType.DMA((2,)),
    share_send=pltpu.SemaphoreType.DMA((2, 2)),
    xin_recv=pltpu.SemaphoreType.DMA((2, 4)),
    gin_recv=pltpu.SemaphoreType.DMA((2, 4)),
    hop_send=pltpu.SemaphoreType.DMA((2, 2)),
    final_send=pltpu.SemaphoreType.DMA((2, 2, 4)),
    final_recv=pltpu.SemaphoreType.DMA((2, 2)),
    local_sem=pltpu.SemaphoreType.DMA((6,)),
    free=pltpu.SemaphoreType.REGULAR((3,)),
    shard_sem=pltpu.SemaphoreType.DMA((7,)),
    swap_send=pltpu.SemaphoreType.DMA((7, 8)),
    swap_recv=pltpu.SemaphoreType.DMA((7, 8)),
    end_send=pltpu.SemaphoreType.DMA((4,)),
    end_recv=pltpu.SemaphoreType.DMA((4,)),
    mod=pltpu.VMEM((2, 1, 3456), jnp.float32),
    time=pltpu.VMEM((2, 1, 3456), jnp.float32),
    token=pltpu.VMEM((2, 1, 1152), jnp.float32),
    grad_rows=pltpu.VMEM((2, 1, 6912), jnp.float32),
    rows=pltpu.VMEM((16, 1, 1280), jnp.float32),
    flat=pltpu.VMEM((16, 6912), jnp.float32),
    own_cond=pltpu.VMEM((16, 144), low),
    own_token=pltpu.VMEM((16, 144), low),
    mod_parts=pltpu.VMEM((16, 1, 4608), jnp.float32),
    mod_all=pltpu.VMEM((8, 2, 1, 4608), jnp.float32),
    token_all=pltpu.VMEM((16, 1, 1152), jnp.float32),
    time_parts=pltpu.VMEM((16, 1, 3456), jnp.float32),
    time_all=pltpu.VMEM((8, 2, 1, 3456), jnp.float32),
    grad_all=pltpu.VMEM((16, 1, 6912), jnp.float32),
    back=pltpu.VMEM((16, 1152), low),
    back_all=pltpu.VMEM((8, 16, 1152), low),
    end=pltpu.VMEM((16, 144), jnp.float32),
    end_parts=pltpu.VMEM((4, 16, 144), jnp.float32),
    end_all=pltpu.VMEM((8, 16, 144), jnp.float32),
)
REFS = (
    ["tokens", "cotangent", "in_shard", "out_shard", "mod_shard", "cond_in"]
    + ["out_tokens", "input_grad", "grads", "mod_grad", "cond_grads", "rows_out"]
    + list(SCRATCH)
)


def mega(tokens, cotangent, in_shard, out_shard, mod_shard, cond_rows):
    anywhere = pl.BlockSpec(memory_space=pl.ANY)
    near = pl.BlockSpec(memory_space=pltpu.VMEM)
    return pl.pallas_call(
        mega_body,
        out_shape=(
            jax.ShapeDtypeStruct(tokens.shape, low),
            jax.ShapeDtypeStruct(tokens.shape, low),
            jax.ShapeDtypeStruct((2,) + in_shard.shape, jnp.float32),
            jax.ShapeDtypeStruct(mod_shard.shape, jnp.float32),
            jax.ShapeDtypeStruct((8, 16, in_shard.shape[0]), jnp.float32),
            jax.ShapeDtypeStruct((16,) + cond_rows.shape[1:], jnp.float32),
        ),
        in_specs=[anywhere] * 5 + [near],
        out_specs=[anywhere] * 4 + [near] * 2,
        scratch_shapes=list(SCRATCH.values()),
        compiler_params=pltpu.CompilerParams(
            collective_id=0, has_side_effects=True, vmem_limit_bytes=62 * 2**20
        ),
        cost_estimate=pl.CostEstimate(
            flops=25 * 10**9, bytes_accessed=10**7, transcendentals=10**7
        ),
        name="blocks",
    )(tokens, cotangent, in_shard, out_shard, mod_shard, cond_rows)


def fast_shards(
    tokens,
    cotangent,
    timesteps,
    labels,
    class_table,
    section_in_weights,
    section_out_weights,
    modulation_weights,
):
    model_width = tokens.shape[2]
    in_shard, out_shard, mod_shard = (
        section_in_weights[0],
        section_out_weights[0],
        modulation_weights[0],
    )
    images = tokens.shape[0]
    classes = class_table.shape[0]
    matches = labels[:, None] == lax.broadcasted_iota(jnp.int32, (images, classes), 1)
    condition = sinusoid(timesteps, model_width) + product(
        matches.astype(jnp.bfloat16), class_table
    )
    named = jnp.broadcast_to(labels.astype(jnp.float32)[:, None], (images, 128))
    cond_rows = jnp.concatenate([condition, named], axis=1)[:, None, :]
    out_tokens, input_grad, grads, mod_grad, cond_grads, all_rows = mega(
        tokens, cotangent, in_shard, out_shard, mod_shard, cond_rows
    )
    every_label = all_rows[:, 0, model_width].astype(jnp.int32)
    every_match = every_label[:, None] == lax.broadcasted_iota(
        jnp.int32, (every_label.shape[0], classes), 1
    )
    whole_grads = cond_grads.transpose(1, 0, 2).reshape(every_label.shape[0], model_width)
    grad_condition = jax.vjp(jax.nn.silu, all_rows[:, 0, :model_width])[1](whole_grads)[0]
    grad_table = lax.dot_general(
        every_match.astype(jnp.float32),
        grad_condition,
        (((0,), (0,)), ((), ())),
        precision=highest,
        preferred_element_type=jnp.float32,
    )
    return (
        out_tokens,
        input_grad.astype(jnp.float32),
        grad_table,
        grads[0][None],
        grads[1][None],
        mod_grad[None],
    )


def solution(mesh):
    return jax.shard_map(
        fast_shards if mesh.shape["dp"] == 8 else shards,
        mesh=mesh,
        in_specs=(
            P("dp", "pipe", None),
            P("dp", "pipe", None),
            P("dp"),
            P("dp"),
            P(),
            P("pipe", "dp", None),
            P("pipe", "dp", None),
            P("pipe", "dp", None),
        ),
        out_specs=(
            P("dp", "pipe", None),
            P("dp", "pipe", None),
            P(),
            P("pipe", "dp", None),
            P("pipe", "dp", None),
            P("pipe", "dp", None),
        ),
        check_vma=False,
    )
```

```python
from functools import partial
import math
from types import SimpleNamespace

import jax
import jax.numpy as jnp
from jax import lax
from jax.experimental import pallas as pl
from jax.experimental.pallas import tpu as pltpu
from jax.sharding import PartitionSpec as P

HEADS = 16
HEAD = 72


epsilon = 1e-06
highest = lax.Precision.HIGHEST


def shifted(block, axis, distance):
    devices = range(lax.axis_size(axis))
    route = [(i - distance, i) for i in devices if i - distance in devices]
    return lax.ppermute(block, axis, route)


def sinusoid(step_values, model_width):
    half_width = model_width // 2
    frequencies = jnp.exp(
        -math.log(10000.0) * jnp.arange(half_width, dtype=jnp.float32) / half_width
    )
    angles = step_values.astype(jnp.float32)[:, None] * frequencies[None, :]
    return jnp.concatenate([jnp.cos(angles), jnp.sin(angles)], axis=1)


def product(former, latter):
    return jnp.dot(former, latter, preferred_element_type=jnp.float32)


def contract_rows(former, latter):
    return lax.dot_general(
        former, latter, (((0,), (0,)), ((), ())), preferred_element_type=jnp.float32
    )


def contract_cols(former, latter):
    return lax.dot_general(
        former, latter, (((1,), (1,)), ((), ())), preferred_element_type=jnp.float32
    )


def normalize_rows(row_values):
    centered = row_values - jnp.mean(row_values, axis=-1, keepdims=True)
    inverse = lax.rsqrt(jnp.mean(centered * centered, axis=-1, keepdims=True) + epsilon)
    return (centered * inverse, inverse)


def modulation_front(section_input, mod_row):
    model_width = section_input.shape[1]
    shift_vec = mod_row[:model_width]
    scale_vec = mod_row[model_width : 2 * model_width]
    gate_vec = mod_row[2 * model_width :]
    centred, inverse = normalize_rows(section_input.astype(jnp.float32))
    normed = (centred * (1.0 + scale_vec) + shift_vec).astype(jnp.bfloat16)
    return (normed, centred, inverse, scale_vec, gate_vec)


def modulation_back(grad_normed, centred, inverse, scale_vec, grad_rows, grad_gate):
    grad_shift = jnp.sum(grad_normed, axis=0)
    grad_scale = jnp.sum(grad_normed * centred, axis=0)
    grad_centred = grad_normed * (1.0 + scale_vec)
    grad_input = inverse * (
        grad_centred
        - jnp.mean(grad_centred, axis=-1, keepdims=True)
        - centred * jnp.mean(grad_centred * centred, axis=-1, keepdims=True)
    )
    grad_mod = jnp.concatenate([grad_shift, grad_scale, grad_gate]).astype(jnp.bfloat16)
    return (grad_rows + grad_input, grad_mod)


def attention_parts(section_input, mod_row, time_row, weights):
    in_weight = weights[0]
    model_width = section_input.shape[1]
    tok_len = section_input.shape[0]
    normed, centred, inverse, scale_vec, gate_vec = modulation_front(section_input, mod_row)
    qkv = (product(normed, in_weight[:, : 3 * model_width]) + time_row).astype(jnp.bfloat16)
    split_qkv = qkv.reshape(tok_len, 3, HEADS, HEAD)
    queries = split_qkv[:, 0]
    keyed = split_qkv[:, 1]
    valued = split_qkv[:, 2]
    scores = jnp.einsum(
        "qhd,khd->hqk", queries, keyed, preferred_element_type=jnp.float32
    ) * HEAD ** (-0.5)
    probs_full = jax.nn.softmax(scores, axis=-1)
    probs_low = probs_full.astype(jnp.bfloat16)
    mixed = jnp.einsum("hqk,khd->qhd", probs_low, valued, preferred_element_type=jnp.float32)
    head_rows = mixed.reshape(tok_len, model_width).astype(jnp.bfloat16)
    branch = product(head_rows, in_weight[:, 3 * model_width :])
    section_output = section_input.astype(jnp.float32) + gate_vec * branch
    saved_parts = (
        normed,
        centred,
        inverse,
        scale_vec,
        gate_vec,
        queries,
        keyed,
        valued,
        probs_full,
        probs_low,
        head_rows,
        branch,
    )
    return (section_output, saved_parts)


def attention_forward(section_input, mod_row, time_row, weights):
    return attention_parts(section_input, mod_row, time_row, weights)[0]


def attention_backward(section_input, grad_in, mod_row, time_row, weights):
    in_weight = weights[0]
    model_width = section_input.shape[1]
    tok_len = section_input.shape[0]
    unused, saved_parts = attention_parts(section_input, mod_row, time_row, weights)
    (
        normed,
        centred,
        inverse,
        scale_vec,
        gate_vec,
        queries,
        keyed,
        valued,
        probs_full,
        probs_low,
        head_rows,
        branch,
    ) = saved_parts
    grad_rows = grad_in.astype(jnp.float32)
    grad_branch = (gate_vec * grad_rows).astype(jnp.bfloat16)
    grad_gate = jnp.sum(grad_rows * branch, axis=0)
    grad_heads = contract_cols(grad_branch, in_weight[:, 3 * model_width :]).astype(jnp.bfloat16)
    heads_split = grad_heads.reshape(tok_len, HEADS, HEAD)
    grad_probs = jnp.einsum("qhd,khd->hqk", heads_split, valued, preferred_element_type=jnp.float32)
    grad_value = jnp.einsum(
        "hqk,qhd->khd", probs_low, heads_split, preferred_element_type=jnp.float32
    )
    grad_scores = (
        probs_full * (grad_probs - jnp.sum(probs_full * grad_probs, axis=-1, keepdims=True))
    ).astype(jnp.bfloat16)
    grad_query = jnp.einsum(
        "hqk,khd->qhd", grad_scores, keyed, preferred_element_type=jnp.float32
    ) * HEAD ** (-0.5)
    grad_key = jnp.einsum(
        "hqk,qhd->khd", grad_scores, queries, preferred_element_type=jnp.float32
    ) * HEAD ** (-0.5)
    grad_qkv = (
        jnp.stack([grad_query, grad_key, grad_value], axis=1)
        .reshape(tok_len, 3 * model_width)
        .astype(jnp.bfloat16)
    )
    grad_normed = contract_cols(grad_qkv, in_weight[:, : 3 * model_width])
    grad_time = jnp.sum(grad_qkv, axis=0, dtype=jnp.float32).astype(jnp.bfloat16)
    grad_input, grad_mod = modulation_back(
        grad_normed, centred, inverse, scale_vec, grad_rows, grad_gate
    )
    narrow_zero = jnp.zeros((tok_len, model_width), jnp.bfloat16)
    return (
        grad_input,
        normed,
        jnp.concatenate([grad_qkv, narrow_zero], axis=1),
        grad_branch,
        jnp.concatenate([head_rows, narrow_zero, narrow_zero, narrow_zero], axis=1),
        grad_mod,
        grad_time,
    )


def feed_parts(section_input, mod_row, weights):
    in_weight, out_weight = weights
    normed, centred, inverse, scale_vec, gate_vec = modulation_front(section_input, mod_row)
    pre_act = product(normed, in_weight)
    hidden = jax.nn.gelu(pre_act, approximate=True).astype(jnp.bfloat16)
    branch = contract_cols(hidden, out_weight)
    section_output = section_input.astype(jnp.float32) + gate_vec * branch
    return (
        section_output,
        (normed, centred, inverse, scale_vec, gate_vec, pre_act, hidden, branch),
    )


def feed_forward(section_input, mod_row, time_row, weights):
    return feed_parts(section_input, mod_row, weights)[0]


def feed_backward(section_input, grad_in, mod_row, time_row, weights):
    in_weight, out_weight = weights
    unused, saved_parts = feed_parts(section_input, mod_row, weights)
    normed, centred, inverse, scale_vec, gate_vec, pre_act, hidden, branch = saved_parts
    grad_rows = grad_in.astype(jnp.float32)
    grad_branch = (gate_vec * grad_rows).astype(jnp.bfloat16)
    grad_gate = jnp.sum(grad_rows * branch, axis=0)
    grad_hidden = product(grad_branch, out_weight)
    gelu_pull = jax.vjp(partial(jax.nn.gelu, approximate=True), pre_act)[1]
    grad_pre = gelu_pull(grad_hidden)[0].astype(jnp.bfloat16)
    grad_normed = contract_cols(grad_pre, in_weight)
    grad_input, grad_mod = modulation_back(
        grad_normed, centred, inverse, scale_vec, grad_rows, grad_gate
    )
    return (
        grad_input,
        normed,
        grad_pre,
        grad_branch,
        hidden,
        grad_mod,
        jnp.zeros(grad_mod.shape, jnp.bfloat16),
    )


def spare_forward(section_input, mod_row, time_row, weights):
    return jnp.zeros(section_input.shape, jnp.float32)


def spare_backward(section_input, grad_in, mod_row, time_row, weights):
    tok_len, model_width = section_input.shape
    hidden_width = weights[0].shape[1]
    narrow_zero = jnp.zeros((tok_len, model_width), jnp.bfloat16)
    wide_zero = jnp.zeros((tok_len, hidden_width), jnp.bfloat16)
    row_zero = jnp.zeros((3 * model_width,), jnp.bfloat16)
    return (
        jnp.zeros(section_input.shape, jnp.float32),
        narrow_zero,
        wide_zero,
        narrow_zero,
        wide_zero,
        row_zero,
        row_zero,
    )


def attention_weight_grads(left_one, right_one, left_two, right_two):
    width = left_two.shape[1]
    low = jnp.bfloat16
    qkv_term = contract_rows(left_one, right_one[:, : 3 * width]).astype(low)
    out_term = contract_rows(right_two[:, :width], left_two).astype(low)
    zero_term = jnp.zeros((width, right_two.shape[1]), low)
    return (jnp.concatenate([qkv_term, out_term], axis=1), zero_term)


def feed_weight_grads(left_one, right_one, left_two, right_two):
    low = jnp.bfloat16
    return (
        contract_rows(left_one, right_one).astype(low),
        contract_rows(left_two, right_two).astype(low),
    )


def replace_slot(buffer, slot_index, new_rows, active):
    old_rows = lax.dynamic_index_in_dim(buffer, slot_index, 0, keepdims=False)
    return lax.dynamic_update_index_in_dim(
        buffer, jnp.where(active, new_rows, old_rows), slot_index, 0
    )


def shards(
    tokens,
    cotangent,
    timesteps,
    labels,
    class_table,
    section_in_weights,
    section_out_weights,
    modulation_weights,
):
    micro_count = tokens.shape[0]
    model_width = tokens.shape[2]
    hidden_width = section_in_weights.shape[2]
    section_count = lax.axis_size("pipe")
    section_index = lax.axis_index("pipe")
    last_section = section_count - 1
    section_kind = 1 + section_index % 2
    in_shard, out_shard, mod_shard = (
        section_in_weights[0],
        section_out_weights[0],
        modulation_weights[0],
    )
    whole_tokens, whole_cotangent = (
        lax.all_gather(tokens, "pipe", axis=1, tiled=True),
        lax.all_gather(cotangent, "pipe", axis=1, tiled=True),
    )
    tok_len = whole_tokens.shape[1]
    weights = (
        lax.all_gather(in_shard, "dp", axis=0, tiled=True),
        lax.all_gather(out_shard, "dp", axis=0, tiled=True),
    )
    condition, own_conditioner, own_time, matches, mod_rows, time_rows = conditioning(
        timesteps, labels, class_table, out_shard, mod_shard
    )

    def forward_tick(carry, tick_index):
        incoming, kept_inputs, finals = carry
        micro_index = tick_index - section_index
        active = (micro_index >= 0) & (micro_index < micro_count)
        slot_index = jnp.clip(micro_index, 0, micro_count - 1)
        first_rows = lax.dynamic_index_in_dim(whole_tokens, slot_index, 0, keepdims=False)
        section_input = jnp.where(section_index == 0, first_rows, incoming)
        section_output = lax.switch(
            jnp.where(active, section_kind, 0),
            (spare_forward, attention_forward, feed_forward),
            section_input,
            lax.dynamic_index_in_dim(mod_rows, slot_index, 0, keepdims=False),
            lax.dynamic_index_in_dim(time_rows, slot_index, 0, keepdims=False),
            weights,
        )
        output_low = section_output.astype(jnp.bfloat16)
        kept_inputs = replace_slot(kept_inputs, slot_index, section_input, active)
        finals = replace_slot(
            finals, slot_index, output_low, active & (section_index == last_section)
        )
        incoming = shifted(output_low, "pipe", 1)
        return ((incoming, kept_inputs, finals), None)

    empty_rows = jnp.zeros((tok_len, model_width), jnp.bfloat16)
    empty_store = jnp.zeros((micro_count, tok_len, model_width), jnp.bfloat16)
    forward_out, ignored = lax.scan(
        forward_tick,
        (empty_rows, empty_store, empty_store),
        jnp.arange(micro_count + section_count - 1),
    )
    kept_inputs = forward_out[1]
    finals = forward_out[2]
    wide_store = jnp.zeros((micro_count, tok_len, hidden_width), jnp.bfloat16)
    row_store = jnp.zeros((micro_count, 3 * model_width), jnp.bfloat16)
    start_factors = (empty_store, wide_store, empty_store, wide_store, row_store, row_store)

    def backward_tick(carry, tick_index):
        incoming, factors, input_grads = carry
        micro_index = tick_index - (last_section - section_index)
        active = (micro_index >= 0) & (micro_index < micro_count)
        slot_index = jnp.clip(micro_index, 0, micro_count - 1)
        top_grad = lax.dynamic_index_in_dim(whole_cotangent, slot_index, 0, keepdims=False)
        grad_in = jnp.where(section_index == last_section, top_grad, incoming)
        section_input = lax.dynamic_index_in_dim(kept_inputs, slot_index, 0, keepdims=False)
        results = lax.switch(
            jnp.where(active, section_kind, 0),
            (spare_backward, attention_backward, feed_backward),
            section_input,
            grad_in,
            lax.dynamic_index_in_dim(mod_rows, slot_index, 0, keepdims=False),
            lax.dynamic_index_in_dim(time_rows, slot_index, 0, keepdims=False),
            weights,
        )
        grad_low = results[0].astype(jnp.bfloat16)
        factors = tuple(
            (
                replace_slot(buffer, slot_index, fresh, active)
                for buffer, fresh in zip(factors, results[1:])
            )
        )
        input_grads = replace_slot(
            input_grads, slot_index, grad_low, active & (section_index == 0)
        )
        incoming = shifted(grad_low, "pipe", -1)
        return ((incoming, factors, input_grads), None)

    backward_out, ignored = lax.scan(
        backward_tick,
        (empty_rows, start_factors, empty_store),
        jnp.arange(micro_count + section_count - 1),
    )
    factors = backward_out[1]
    input_grads = backward_out[2]
    flat_rows = micro_count * tok_len
    left_one, right_one, left_two, right_two = (
        stored.reshape(flat_rows, stored.shape[2]) for stored in factors[:4]
    )
    in_term, out_term = lax.cond(
        section_index % 2 == 0,
        attention_weight_grads,
        feed_weight_grads,
        left_one,
        right_one,
        left_two,
        right_two,
    )
    in_grad = lax.psum_scatter(in_term, "dp", scatter_dimension=0, tiled=True)
    out_grad = lax.psum_scatter(out_term, "dp", scatter_dimension=0, tiled=True)
    own_out, own_in = (finals, input_grads)
    keep_out = jnp.where(section_index == last_section, own_out, 0)
    keep_in = jnp.where(section_index == 0, own_in, 0)
    output_share = lax.psum_scatter(keep_out, "pipe", scatter_dimension=1, tiled=True)
    input_share = lax.psum_scatter(keep_in, "pipe", scatter_dimension=1, tiled=True)
    small_outs = conditioning_grads(
        factors[4],
        factors[5],
        condition,
        own_conditioner,
        own_time,
        matches,
        out_shard,
        mod_shard,
        out_grad,
    )
    return (
        output_share,
        input_share.astype(jnp.float32),
        small_outs[0],
        in_grad.astype(jnp.float32)[None],
        small_outs[1][None],
        small_outs[2][None],
    )


def conditioning_grads(
    mod_grads,
    time_grads,
    condition,
    own_conditioner,
    own_time,
    matches,
    out_shard,
    mod_shard,
    out_grad,
):
    model_width = condition.shape[1]
    is_attention = lax.axis_index("pipe") % 2 == 0
    all_mod = lax.all_gather(mod_grads, "dp", axis=0, tiled=True)
    all_time = lax.all_gather(time_grads, "dp", axis=0, tiled=True)
    grad_mod_shard = contract_rows(own_conditioner, all_mod)
    cond_grads = contract_cols(all_mod, mod_shard)
    own_token = contract_cols(all_time, out_shard[:, : 3 * model_width]).astype(jnp.bfloat16)
    all_token = lax.all_gather(own_token, "dp", axis=1, tiled=True)
    token_grads = contract_cols(all_token, out_shard[:, 3 * model_width :])
    cond_grads = cond_grads + jnp.where(is_attention, token_grads, 0.0)
    time_out = jnp.concatenate(
        [contract_rows(own_time, all_time), contract_rows(own_conditioner, all_token)], axis=1
    )
    grad_out_shard = jnp.where(is_attention, time_out, out_grad.astype(jnp.float32))
    every_part = lax.all_gather(cond_grads, "pipe", axis=0)
    whole_grads = lax.all_gather(jnp.sum(every_part, axis=0), "dp", axis=1, tiled=True)
    grad_condition = jax.vjp(jax.nn.silu, condition)[1](whole_grads)[0]
    grad_table = lax.dot_general(
        matches.astype(jnp.float32),
        grad_condition,
        (((0,), (0,)), ((), ())),
        precision=highest,
        preferred_element_type=jnp.float32,
    )
    return (grad_table, grad_out_shard, grad_mod_shard)


def conditioning(timesteps, labels, class_table, out_shard, mod_shard):
    model_width = class_table.shape[1]
    own_rows = out_shard.shape[0]
    own_start = lax.axis_index("dp") * own_rows
    all_steps = lax.all_gather(timesteps, "dp", axis=0, tiled=True)
    all_labels = lax.all_gather(labels, "dp", axis=0, tiled=True)
    image_count = all_steps.shape[0]
    classes = class_table.shape[0]
    matches = all_labels[:, None] == lax.broadcasted_iota(jnp.int32, (image_count, classes), 1)
    condition = sinusoid(all_steps, model_width) + product(
        matches.astype(jnp.bfloat16), class_table
    )
    conditioner = jax.nn.silu(condition).astype(jnp.bfloat16)
    own_conditioner = lax.dynamic_slice_in_dim(conditioner, own_start, own_rows, 1)
    mod_rows = lax.psum_scatter(
        product(own_conditioner, mod_shard), "dp", scatter_dimension=0, tiled=True
    )
    own_time = lax.psum_scatter(
        product(own_conditioner, out_shard[:, 3 * model_width :]),
        "dp",
        scatter_dimension=1,
        tiled=True,
    ).astype(jnp.bfloat16)
    time_rows = lax.psum_scatter(
        product(own_time, out_shard[:, : 3 * model_width]), "dp", scatter_dimension=0, tiled=True
    )
    return (condition, own_conditioner, own_time, matches, mod_rows, time_rows)


ROWS = 256
SPAN = 2304
THIRD = 1152
PART = 1152
BLOCK = 144
GROUP = 4
MESH = pl.DeviceIdType.MESH
low = jnp.bfloat16
GELU_A = math.sqrt(2.0 / math.pi)
GELU_B = 0.044715


def product_nt(former, latter):
    return contract_cols(former, latter)


def spread(index, width):
    return pl.ds(pl.multiple_of(index * width, 128), width)


def image_rows(i):
    return pl.ds(pl.multiple_of(i * ROWS, ROWS), ROWS)


def block_rows(b):
    return pl.ds(pl.multiple_of(b * BLOCK, 16), BLOCK)


def front(i, s):
    rows = image_rows(i)
    xhat, inverse = normalize_rows(s.xin[rows, :].astype(jnp.float32))
    normed = (xhat * (1.0 + s.mod[i, :, PART : 2 * PART]) + s.mod[i, :, 0:PART]).astype(low)
    s.norm[rows, :] = normed
    s.left[0, :, rows] = normed.T


def finish(i, s):
    rows = image_rows(i)
    branch = s.acc[...]
    s.branch[rows, :] = branch.astype(low)
    gate = s.mod[i, :, 2 * PART : 3 * PART]
    s.xout[rows, :] = (s.xin[rows, :].astype(jnp.float32) + gate * branch).astype(low)


def feed_up_down(i, s):
    rows = image_rows(i)
    s.acc[...] = jnp.zeros(s.acc.shape, jnp.float32)

    def tile(j, carry):
        cols = spread(j, SPAN)
        value = product(s.norm[rows, :], s.wa[:, cols])
        square = value * value
        wave = jnp.tanh(value * (GELU_A + (GELU_A * GELU_B) * square))
        half = 0.5 + 0.5 * wave
        hidden = (value * half).astype(low)
        slope = half + value * (0.5 - 0.5 * (wave * wave)) * (
            GELU_A + (3.0 * GELU_A * GELU_B) * square
        )
        s.wide[0, rows, cols] = hidden
        s.wide[1, rows, cols] = slope.astype(low)
        s.acc[...] += product_nt(hidden, s.wb[:, cols])
        return carry

    lax.fori_loop(0, s.wa.shape[1] // SPAN, tile, 0)


def feed_down_up(i, s):
    rows = image_rows(i)
    s.acc[...] = jnp.zeros(s.acc.shape, jnp.float32)

    def tile(j, carry):
        cols = spread(j, SPAN)
        grad_hidden = product(s.gb[...], s.wb[:, cols])
        grad_pre = (grad_hidden * s.wide[1, rows, cols].astype(jnp.float32)).astype(low)
        s.wide[1, rows, cols] = grad_pre
        s.acc[...] += product_nt(grad_pre, s.wa[:, cols])
        return carry

    lax.fori_loop(0, s.wa.shape[1] // SPAN, tile, 0)


def back_start(i, s):
    rows = image_rows(i)
    grad = s.gin[rows, :].astype(jnp.float32)
    gb = (s.mod[i, :, 2 * PART : 3 * PART] * grad).astype(low)
    s.gb[...] = gb
    s.grad_rows[i, :, 2 * PART : 3 * PART] = jnp.sum(
        grad * s.branch[rows, :].astype(jnp.float32), axis=0, keepdims=True
    )
    return gb


def back_finish(i, s):
    rows = image_rows(i)
    xhat, inverse = normalize_rows(s.xin[rows, :].astype(jnp.float32))
    gn = s.acc[...]
    s.grad_rows[i, :, 0:PART] = jnp.sum(gn, axis=0, keepdims=True)
    s.grad_rows[i, :, PART : 2 * PART] = jnp.sum(gn * xhat, axis=0, keepdims=True)
    gx = gn * (1.0 + s.mod[i, :, PART : 2 * PART])
    first = jnp.mean(gx, axis=-1, keepdims=True)
    second = jnp.mean(gx * xhat, axis=-1, keepdims=True)
    grad = s.gin[rows, :].astype(jnp.float32)
    s.gout[rows, :] = (grad + inverse * (gx - first - xhat * second)).astype(low)


def kernel_feed_forward(i, s):
    front(i, s)
    feed_up_down(i, s)
    finish(i, s)


def kernel_feed_backward(i, s):
    gb = back_start(i, s)
    s.left[1, :, image_rows(i)] = gb.T
    feed_down_up(i, s)
    back_finish(i, s)


def project(i, s, part):
    rows = image_rows(i)

    def tile(j, carry):
        cols = pl.ds(pl.multiple_of(part * PART + j * THIRD, 128), THIRD)
        value = product(s.norm[rows, :], s.wa[:, cols]) + s.time[i, :, cols]
        s.wide[0, rows, cols] = value.astype(low)
        return carry

    lax.fori_loop(0, PART // THIRD, tile, 0)


def head_window(h):
    start = jnp.minimum((h * HEAD) // 128, PART // 128 - 2)
    offset = h * HEAD - start * 128
    lanes = lax.broadcasted_iota(jnp.int32, (ROWS, 256), 1)
    inside = (lanes >= offset) & (lanes < offset + HEAD)
    return start, inside


def window(start, part):
    return pl.ds(pl.multiple_of(part * PART + start * 128, 128), 256)


def prob_place(i, h):
    return (
        pl.ds(pl.multiple_of((h % 4) * ROWS, ROWS), ROWS),
        pl.ds(pl.multiple_of((4 * i + h // 4) * ROWS, ROWS), ROWS),
    )


def attend_heads(i, s):
    rows = image_rows(i)
    s.acc[...] = jnp.zeros(s.acc.shape, jnp.float32)
    zero = jnp.zeros((), low)

    def score(h, slot):
        start, inside = head_window(h)
        query = jnp.where(inside, s.wide[0, rows, window(start, 0)], zero)
        s.wacc[:, spread(slot, ROWS)] = product_nt(query, s.wide[0, rows, window(start, 1)])

    def soften(h, slot):
        scores = s.wacc[:, spread(slot, ROWS)]
        top = jnp.max(scores, axis=-1, keepdims=True)
        powers = jnp.exp2((scores - top) * (HEAD ** (-0.5) * math.log2(math.e)))
        place = prob_place(i, h)
        s.wb[place[0], place[1]] = (
            powers * (1.0 / jnp.sum(powers, axis=-1, keepdims=True))
        ).astype(low)

    def mix(h):
        start, inside = head_window(h)
        place = prob_place(i, h)
        value = jnp.where(inside, s.wide[0, rows, window(start, 2)], zero)
        s.acc[:, window(start, 0)] += product(s.wb[place[0], place[1]], value)

    for k in range(GROUP):
        score(k, k)

    def group(g, carry):
        for k in range(GROUP):
            soften(GROUP * g + k, k)
        for k in range(GROUP):
            score(jnp.minimum(GROUP * (g + 1) + k, HEADS - 1), k)
        for k in range(GROUP):
            mix(GROUP * g + k)
        return carry

    lax.fori_loop(0, HEADS // GROUP, group, 0)
    mixed = s.acc[...].astype(low)
    s.left[1, :, rows] = mixed.T
    s.wide[0, rows, 3 * PART :] = mixed


def attend_out(i, s):
    rows = image_rows(i)
    s.acc[...] = product(s.wide[0, rows, 3 * PART :], s.wa[:, 3 * PART :])


def kernel_attention_backward(i, s):
    rows = image_rows(i)
    gb = back_start(i, s)
    s.wide[1, rows, 3 * PART :] = gb
    s.gb[...] = product_nt(gb, s.wa[:, 3 * PART :]).astype(low)
    s.wacc[...] = jnp.zeros(s.wacc.shape, jnp.float32)

    zero = jnp.zeros((), low)

    def grad_of_probs(h):
        start, inside = head_window(h)
        grad_head = jnp.where(inside, s.gb[:, window(start, 0)], zero)
        return product_nt(grad_head, s.wide[0, rows, window(start, 2)])

    def grad_of_scores(h, grad_probs):
        place = prob_place(i, h)
        probs = s.wb[place[0], place[1]].astype(jnp.float32)
        mixed = jnp.sum(probs * grad_probs, axis=-1, keepdims=True)
        return (probs * (grad_probs - mixed)).astype(low)

    def grads_of_qkv(h, grad_scores):
        start, inside = head_window(h)
        place = prob_place(i, h)
        query = jnp.where(inside, s.wide[0, rows, window(start, 0)], zero)
        key = jnp.where(inside, s.wide[0, rows, window(start, 1)], zero)
        grad_head = jnp.where(inside, s.gb[:, window(start, 0)], zero)
        s.wacc[:, window(start, 2)] += contract_rows(s.wb[place[0], place[1]], grad_head)
        s.wacc[:, window(start, 0)] += product(grad_scores, key)
        s.wacc[:, window(start, 1)] += contract_rows(grad_scores, query)

    def group(g, carry):
        heads = [GROUP * g + k for k in range(GROUP)]
        first = [grad_of_probs(h) for h in heads]
        second = [grad_of_scores(h, value) for h, value in zip(heads, first)]
        for h, value in zip(heads, second):
            grads_of_qkv(h, value)
        return carry

    lax.fori_loop(0, HEADS // GROUP, group, 0)
    scale = HEAD ** (-0.5)
    for part, factor in ((0, scale), (1, scale), (2, 1.0)):
        cols = pl.ds(part * PART, PART)
        grads = (s.wacc[:, cols] * factor).astype(low)
        s.wide[1, rows, cols] = grads
        s.grad_rows[i, :, pl.ds((3 + part) * PART, PART)] = jnp.sum(
            grads.astype(jnp.float32), axis=0, keepdims=True
        )
    s.acc[...] = jnp.zeros(s.acc.shape, jnp.float32)

    def tile(j, carry):
        cols = spread(j, THIRD)
        s.acc[...] += product_nt(s.wide[1, rows, cols], s.wa[:, cols])
        return carry

    lax.fori_loop(0, 3 * PART // THIRD, tile, 0)
    back_finish(i, s)


def places():
    dp, pipe = lax.axis_index("dp"), lax.axis_index("pipe")
    core, x_bit, y_bit = dp % 2, (dp // 2) % 2, dp // 4
    sib = dp + 1 - 2 * core
    step_x, step_y = 2 - 4 * x_bit, 4 - 8 * y_bit
    return SimpleNamespace(
        dp=dp,
        pipe=pipe,
        core=core,
        sib=sib,
        x=dp + step_x,
        y=dp + step_y,
        d=dp + step_x + step_y,
        step_x=step_x,
        step_y=step_y,
        x_bit=x_bit,
        y_bit=y_bit,
    )


def gather_weights(s, at, chunks, between, ready):
    def held(k):
        return (s.wa if k < 4 else s.wb), pl.ds((k % 4) * PART, PART)

    def piece(k, block, first=0, count=BLOCK):
        ref, cols = held(k)
        return ref.at[pl.ds(pl.multiple_of(block * BLOCK + first, 16), count), cols]

    def copy(k, kind, ref, target, source=None):
        return pltpu.make_async_remote_copy(
            src_ref=ref if source is None else source,
            dst_ref=ref,
            send_sem=s.gather_send.at[k, kind],
            recv_sem=s.gather_recv.at[k, kind],
            device_id=(target, at.pipe),
            device_id_type=MESH,
        )

    def via_y(k):
        return (0, 80) if k % 2 == 0 else (0, 64)

    def via_x(k):
        return (80, 64) if k % 2 == 0 else (64, 80)

    sib_x, sib_y, sib_d = (
        at.sib + at.step_x,
        at.sib + at.step_y,
        at.sib + at.step_x + at.step_y,
    )

    def sends(k):
        shard = s.in_shard if k < 4 else s.out_shard
        source = shard.at[:, pl.ds((k % 4) * PART, PART)]
        return {
            0: lambda: copy(k, 0, piece(k, at.dp), at.x, source),
            1: lambda: copy(k, 1, piece(k, at.dp), at.y, source),
            2: lambda: copy(k, 2, piece(k, at.dp), at.sib, source),
            3: lambda: copy(k, 3, piece(k, at.x), at.sib),
            4: lambda: copy(k, 4, piece(k, at.x, *via_y(k)), at.y),
            5: lambda: copy(k, 5, piece(k, at.y), at.sib),
            6: lambda: copy(k, 6, piece(k, at.y, *via_x(k)), at.x),
            7: lambda: copy(k, 7, piece(k, at.d), at.sib),
        }

    def arrivals(k):
        return {
            0: lambda: copy(k, 0, piece(k, at.x), at.x),
            1: lambda: copy(k, 1, piece(k, at.y), at.y),
            2: lambda: copy(k, 2, piece(k, at.sib), at.sib),
            3: lambda: copy(k, 3, piece(k, sib_x), at.sib),
            4: lambda: copy(k, 4, piece(k, at.d, *via_y(k)), at.y),
            5: lambda: copy(k, 5, piece(k, sib_y), at.sib),
            6: lambda: copy(k, 6, piece(k, at.d, *via_x(k)), at.x),
            7: lambda: copy(k, 7, piece(k, sib_d), at.sib),
        }

    def start(k, *kinds):
        for kind in kinds:
            sends(k)[kind]().start()

    def arrive(k, *kinds):
        for kind in kinds:
            arrivals(k)[kind]().wait_recv()

    for k in range(2):
        start(k, 0, 1, 2)
    for k in range(chunks + 2):
        if k < chunks:
            arrive(k, 0)
            start(k, 3, 4)
            arrive(k, 1)
            start(k, 5, 6)
            if k + 2 < chunks:
                start(k + 2, 0, 1, 2)
            between(k)
        if 1 <= k <= chunks:
            arrive(k - 1, 4, 6)
            start(k - 1, 7)
        if k >= 2:
            arrive(k - 2, 2, 3, 5, 7)
            ready(k - 2)
    for k in range(chunks):
        for kind in range(8):
            sends(k)[kind]().wait_send()


def scatter_grads(s, at, is_feed, swap):
    total = jnp.where(is_feed, 32, 16)
    chip = at.dp // 2
    chip_x, chip_y = chip + 1 - 2 * at.x_bit, chip + 2 - 4 * at.y_bit
    chip_d = chip_x + 2 - 4 * at.y_bit

    def unit(u):
        stage = u // 4
        late = (stage >= 3) & is_feed
        matrix = jnp.where(late & (stage != 5), 1, 0)
        group = jnp.where(late, jnp.where(stage == 5, 3, stage - jnp.where(stage < 5, 3, 4)), stage)
        v, turn, n = u % 4, u % 2, (u % 4) // 2
        near = chip_x + turn * (chip_y - chip_x)
        block = jnp.where(group == 0, chip_d, jnp.where(group == 3, chip, near))
        part = jnp.where(
            group == 3, v, jnp.where(group == 2, 2 * (1 - turn) + n, 2 * turn + n)
        )
        return matrix, group, turn, n, block, part

    def sib_place(u):
        return s.wb.at[block_rows(u % 8), spread(u // 8, PART)]

    def near_place(matrix, turn, slot):
        index = turn * 12 + matrix * 6 + slot
        return s.wa.at[block_rows(index % 8), spread(index // 8, PART)]

    def sib_copy(u):
        return pltpu.make_async_remote_copy(
            src_ref=s.stage.at[u % 4, block_rows(1 - at.core), :],
            dst_ref=sib_place(u),
            send_sem=s.sib_send.at[u],
            recv_sem=s.sib_recv.at[u],
            device_id=(at.sib, at.pipe),
            device_id_type=MESH,
        )

    def near_copy(matrix, turn, slot):
        return pltpu.make_async_remote_copy(
            src_ref=s.near_stage.at[turn, slot],
            dst_ref=near_place(matrix, turn, slot),
            send_sem=s.near_send.at[turn, matrix * 6 + slot],
            recv_sem=s.near_recv.at[turn, matrix * 6 + slot],
            device_id=(at.x + turn * (at.y - at.x), at.pipe),
            device_id_type=MESH,
        )

    def compute(u):
        matrix, group, turn, n, block, part = unit(u)
        first = is_feed & (matrix == 0)
        lhs = jnp.where(first | (jnp.logical_not(is_feed) & (part == 3)), 1, 0)
        rhs = jnp.where(first, 0, 1)

        @pl.when(u >= 4)
        def _():
            sib_copy(u - 4).wait_send()

        rows = pl.ds(pl.multiple_of(block * 288, 16), 288)
        s.stage[u % 4] = product(s.left[lhs, rows, :], s.wide[rhs, :, spread(part, PART)]).astype(
            low
        )
        sib_copy(u).start()

    def settle(u):
        matrix, group, turn, n, block, part = unit(u)
        sib_copy(u).wait_recv()
        own = s.stage[u % 4, block_rows(at.core), :].astype(jnp.float32)
        place = (block_rows(u % 8), spread(u // 8, PART))
        value = own + s.wb[place].astype(jnp.float32)
        slot = group * 2 + n
        first = is_feed & (matrix == 0)

        def taken(from_turn, from_slot):
            near_copy(matrix, from_turn, from_slot).wait_recv()
            index = from_turn * 12 + matrix * 6 + from_slot
            return s.wa[block_rows(index % 8), spread(index // 8, PART)].astype(jnp.float32)

        @pl.when(group < 3)
        def _():
            @pl.when(matrix > 0)
            def _():
                near_copy(0, turn, slot).wait_send()

            @pl.when(group < 2)
            def _():
                s.near_stage[turn, slot] = value.astype(low)

            @pl.when(group == 2)
            def _():
                s.near_stage[turn, slot] = (value + taken(1 - turn, n)).astype(
                    low
                )

            near_copy(matrix, turn, slot).start()

        @pl.when(group == 3)
        def _():
            @pl.when((matrix > 0) | (part >= 2))
            def _():
                grad_copy(s.in_grad, part).wait()

            whole = value + taken(0, 2 + part) + taken(1, (part + 2) % 4 + 2)
            s.wacc[0:BLOCK, spread(1 + part % 2, PART)] = whole

            @pl.when(first)
            def _():
                grad_copy(s.out_grad, part).start()

            @pl.when(jnp.logical_not(first))
            def _():
                grad_copy(s.in_grad, part).start()

    def grad_copy(held, part):
        return pltpu.make_async_copy(
            s.wacc.at[pl.ds(0, BLOCK), spread(1 + part % 2, PART)],
            held.at[0, :, spread(part, PART)],
            s.out_sem.at[part % 2],
        )

    def step(u, carry):
        @pl.when(u < total)
        def _():
            compute(u)

        for when, rest in (
            (3, condition_back),
            (9, condition_token),
            (total - 5, condition_sum),
            (total - 1, condition_table),
        ):

            @pl.when(u == when)
            def _():
                rest(s, at, swap, is_feed)

        @pl.when(u >= 2)
        def _():
            settle(u - 2)

        return carry

    for copy in shard_copies(s, is_feed):
        copy.start()
    lax.fori_loop(0, total + 2, step, 0)
    matrices = jnp.where(is_feed, 2, 1)

    def rest(k, carry):
        sib_copy(total - 4 + k).wait_send()
        return carry

    lax.fori_loop(0, 4, rest, 0)
    for turn in range(2):
        for slot in range(6):
            near_copy(matrices - 1, turn, slot).wait_send()
    for part in (2, 3):
        grad_copy(s.in_grad, part).wait()


def exchange(s, at, number, piece, landing):
    def copy(target, source):
        return pltpu.make_async_remote_copy(
            src_ref=piece(target),
            dst_ref=landing(source),
            send_sem=s.swap_send.at[number, target],
            recv_sem=s.swap_recv.at[number, source],
            device_id=(target, at.pipe),
            device_id_type=MESH,
        )

    others = [(at.dp + k) % 8 for k in range(1, 8)]

    def start():
        for other in others:
            copy(other, at.dp).start()

    def arrive():
        for other in others:
            copy(other, other).wait_recv()

    def done():
        for other in others:
            copy(other, at.dp).wait_send()

    return SimpleNamespace(start=start, arrive=arrive, done=done)


def exchanges(s, at):
    def pair(j):
        return pl.ds(2 * j, 2)

    return SimpleNamespace(
        rows=exchange(s, at, 0, lambda j: s.cond_in, lambda j: s.rows.at[pair(j)]),
        mods=exchange(s, at, 1, lambda j: s.mod_parts.at[pair(j)], lambda j: s.mod_all.at[j]),
        tokens=exchange(s, at, 2, lambda j: s.token, lambda j: s.token_all.at[pair(j)]),
        times=exchange(s, at, 3, lambda j: s.time_parts.at[pair(j)], lambda j: s.time_all.at[j]),
        grads=exchange(s, at, 4, lambda j: s.grad_rows, lambda j: s.grad_all.at[pair(j)]),
        backs=exchange(s, at, 5, lambda j: s.back, lambda j: s.back_all.at[j]),
        ends=exchange(s, at, 6, lambda j: s.end, lambda j: s.end_all.at[j]),
    )


def shard_copies(s, is_feed):
    copies = []
    for part in range(3):
        cols = pl.ds(part * PART, PART)
        rows = pl.ds(part * BLOCK, BLOCK)
        copies.append((s.mod_shard.at[:, cols], s.norm.at[rows, :]))
        copies.append((s.out_shard.at[:, cols], s.branch.at[rows, :]))
    copies.append((s.out_shard.at[:, pl.ds(3 * PART, PART)], s.gb.at[pl.ds(0, BLOCK), :]))
    return [
        pltpu.make_async_copy(source, target, s.shard_sem.at[k])
        for k, (source, target) in enumerate(copies)
    ]


def shard_part(ref, part):
    return ref[pl.ds(part * BLOCK, BLOCK), :]


def stack_rows(source, target, width):
    for k in range(16):
        target[k : k + 1, 0:width] = source[k, :, 0:width]


def chosen(at):
    places = lax.broadcasted_iota(jnp.int32, (PART, BLOCK), 0)
    lanes = lax.broadcasted_iota(jnp.int32, (PART, BLOCK), 1)
    return jnp.where(places == lanes + at.dp * BLOCK, 1.0, 0.0).astype(low)


def condition_front(s, at, swap, is_feed):
    for copy in shard_copies(s, is_feed):
        copy.start()
    s.rows[pl.ds(2 * at.dp, 2)] = s.cond_in[...]
    s.grad_rows[...] = jnp.zeros(s.grad_rows.shape, jnp.float32)
    swap.rows.arrive()
    stack_rows(s.rows, s.flat, PART)
    condition = s.flat[:, 0:PART]
    conditioner = (condition * (1.0 / (1.0 + jnp.exp(-condition)))).astype(low)
    pick = chosen(at)
    own = product(conditioner, pick).astype(low)
    s.own_cond[...] = own
    for copy in shard_copies(s, is_feed):
        copy.wait()
    for part in range(3):
        s.flat[:, part * PART : (part + 1) * PART] = product(own, shard_part(s.norm, part))
    s.flat[:, 3 * PART : 4 * PART] = product(own, s.gb[0:BLOCK, :])
    for k in range(16):
        s.mod_parts[k] = s.flat[k : k + 1, 0 : 4 * PART]
    swap.mods.start()
    s.mod_all[at.dp] = s.mod_parts[pl.ds(2 * at.dp, 2)]


def condition_mods(s, at, swap, is_feed):
    swap.mods.arrive()
    for i in range(2):
        total = jnp.sum(s.mod_all[:, i], axis=0)
        s.mod[i] = total[:, 0 : 3 * PART]
        s.token[i] = total[:, 3 * PART :]

    @pl.when(jnp.logical_not(is_feed))
    def _():
        swap.tokens.start()
        s.token_all[pl.ds(2 * at.dp, 2)] = s.token[...]


def condition_tokens(s, at, swap, is_feed):
    @pl.when(jnp.logical_not(is_feed))
    def _():
        swap.tokens.arrive()
        stack_rows(s.token_all, s.flat, PART)
        own_token = product(s.flat[:, 0:PART].astype(low), chosen(at)).astype(low)
        s.own_token[...] = own_token
        for part in range(3):
            s.flat[:, part * PART : (part + 1) * PART] = product(
                own_token, shard_part(s.branch, part)
            )
        for k in range(16):
            s.time_parts[k] = s.flat[k : k + 1, 0 : 3 * PART]
        swap.times.start()
        s.time_all[at.dp] = s.time_parts[pl.ds(2 * at.dp, 2)]


def condition_times(s, at, swap, is_feed):
    @pl.when(jnp.logical_not(is_feed))
    def _():
        swap.times.arrive()
        for i in range(2):
            s.time[i] = jnp.sum(s.time_all[:, i], axis=0)


def end_copy(s, at, plane):
    return pltpu.make_async_remote_copy(
        src_ref=s.end_parts.at[at.pipe],
        dst_ref=s.end_parts.at[at.pipe],
        send_sem=s.end_send.at[plane],
        recv_sem=s.end_recv.at[at.pipe],
        device_id=(at.dp, plane),
        device_id_type=MESH,
    )


def end_arrival(s, at, plane):
    return pltpu.make_async_remote_copy(
        src_ref=s.end_parts.at[plane],
        dst_ref=s.end_parts.at[plane],
        send_sem=s.end_send.at[plane],
        recv_sem=s.end_recv.at[plane],
        device_id=(at.dp, plane),
        device_id_type=MESH,
    )


def mod_out(s):
    return pltpu.make_async_copy(
        s.wacc.at[pl.ds(0, BLOCK), :], s.mod_grad.at[0], s.shard_sem.at[0]
    )


def time_outs(s):
    held = s.out_grad.at[0]
    return (
        pltpu.make_async_copy(
            s.wacc.at[pl.ds(0, BLOCK), :], held.at[:, pl.ds(0, 3 * PART)], s.shard_sem.at[0]
        ),
        pltpu.make_async_copy(
            s.acc.at[pl.ds(0, BLOCK), :], held.at[:, pl.ds(3 * PART, PART)], s.shard_sem.at[1]
        ),
    )


def condition_back(s, at, swap, is_feed):
    s.grad_all[pl.ds(2 * at.dp, 2)] = s.grad_rows[...]
    swap.grads.arrive()
    stack_rows(s.grad_all, s.flat, 6 * PART)
    for copy in shard_copies(s, is_feed):
        copy.wait()

    @pl.when(jnp.logical_not(is_feed))
    def _():
        token = jnp.zeros((16, BLOCK), jnp.float32)
        for part in range(3):
            grads = s.flat[:, (3 + part) * PART : (4 + part) * PART].astype(low)
            token += product_nt(grads, shard_part(s.branch, part))
        s.back[...] = product_nt(token.astype(low), chosen(at)).astype(low)
        swap.backs.start()
        s.back_all[at.dp] = s.back[...]

    own = s.own_cond[...]
    s.end[...] = jnp.zeros(s.end.shape, jnp.float32)
    for part in range(3):
        cols = slice(part * PART, (part + 1) * PART)
        grads = s.flat[:, cols].astype(low)
        s.wacc[0:BLOCK, cols] = contract_rows(own, grads)
        s.end[...] += product_nt(grads, shard_part(s.norm, part))
    mod_out(s).start()


def condition_token(s, at, swap, is_feed):
    mod_out(s).wait()

    @pl.when(jnp.logical_not(is_feed))
    def _():
        for part in range(3):
            grads = s.flat[:, (3 + part) * PART : (4 + part) * PART].astype(low)
            s.wacc[0:BLOCK, part * PART : (part + 1) * PART] = contract_rows(
                s.own_token[...], grads
            )
        swap.backs.arrive()
        whole = jnp.zeros((16, PART), jnp.float32)
        for k in range(8):
            whole += s.back_all[k].astype(jnp.float32)
        whole = whole.astype(low)
        s.acc[0:BLOCK, :] = contract_rows(s.own_cond[...], whole)
        s.end[...] += product_nt(whole, s.gb[0:BLOCK, :])
        for copy in time_outs(s):
            copy.start()

    s.end_parts[at.pipe] = s.end[...]
    for k in range(1, 4):
        end_copy(s, at, (at.pipe + k) % 4).start()


def condition_sum(s, at, swap, is_feed):
    @pl.when(jnp.logical_not(is_feed))
    def _():
        for copy in time_outs(s):
            copy.wait()

    for k in range(1, 4):
        end_arrival(s, at, (at.pipe + k) % 4).wait_recv()
    s.end[...] = s.end_parts[0] + s.end_parts[1] + s.end_parts[2] + s.end_parts[3]
    swap.ends.start()
    s.end_all[at.dp] = s.end[...]


def condition_table(s, at, swap, is_feed):
    swap.ends.arrive()
    for k in range(8):
        s.flat[:, BLOCK * k : BLOCK * (k + 1)] = s.end_all[k]
    whole = s.flat[:, 0:PART]
    stack_rows(s.rows, s.flat, PART)
    condition = s.flat[:, 0:PART]
    gate = 1.0 / (1.0 + jnp.exp(-condition))
    grads = whole * (gate * (1.0 + condition * (1.0 - gate)))
    for k in range(3):
        term = grads.astype(low)
        s.terms[16 * k : 16 * (k + 1), :] = term
        grads = grads - term.astype(jnp.float32)
    lanes = lax.broadcasted_iota(jnp.int32, (1, 1024), 1).astype(jnp.float32)
    for k in range(16):
        label = s.rows[k, :, PART : PART + 1]
        s.flat[k : k + 1, 0:1024] = jnp.where(lanes == label, 1.0, 0.0)
    hot = s.flat[:, 0:1024].astype(low)
    for k in range(3):
        s.hot[16 * k : 16 * (k + 1), :] = hot


def condition_done(s, at, swap, is_feed):
    for each in (swap.rows, swap.mods, swap.grads, swap.ends):
        each.done()
    for k in range(1, 4):
        end_copy(s, at, (at.pipe + k) % 4).wait_send()

    @pl.when(jnp.logical_not(is_feed))
    def _():
        for each in (swap.tokens, swap.times, swap.backs):
            each.done()


def mega_body(*refs):
    s = SimpleNamespace(**dict(zip(REFS, refs)))
    at = places()
    is_feed = at.pipe % 2 == 1
    pipe = at.pipe
    barrier = pltpu.get_barrier_semaphore()
    swap = exchanges(s, at)
    targets = [((at.dp + k) % 8, pipe) for k in range(1, 8)]
    targets += [(at.dp, (pipe + k) % 4) for k in range(1, 4)]
    for target in targets:
        pl.semaphore_signal(barrier, inc=1, device_id=target, device_id_type=MESH)
    pl.semaphore_wait(barrier, len(targets))
    swap.rows.start()

    def remote(source, target, send, recv, plane):
        return pltpu.make_async_remote_copy(
            src_ref=source,
            dst_ref=target,
            send_sem=send,
            recv_sem=recv,
            device_id=(at.dp, plane),
            device_id_type=MESH,
        )

    def share(i, plane):
        return pl.ds(pl.multiple_of(i * ROWS + plane * 64, 64), 64)

    def token_copy(i, plane):
        return remote(
            s.tokens.at[i],
            s.xin.at[share(i, plane), :],
            s.share_send.at[0, i],
            s.xin_recv.at[i, plane],
            0,
        )

    def cotangent_copy(i, plane):
        return remote(
            s.cotangent.at[i],
            s.gin.at[share(i, plane), :],
            s.share_send.at[1, i],
            s.gin_recv.at[i, plane],
            3,
        )

    def next_copy(i):
        whole = image_rows(i)
        return remote(
            s.xout.at[whole, :],
            s.xin.at[whole, :],
            s.hop_send.at[0, i],
            s.xin_recv.at[i, 0],
            jnp.minimum(pipe + 1, 3),
        )

    def back_copy(i):
        whole = image_rows(i)
        return remote(
            s.gout.at[whole, :],
            s.gin.at[whole, :],
            s.hop_send.at[1, i],
            s.gin_recv.at[i, 3],
            jnp.maximum(pipe - 1, 0),
        )

    def output_copy(i, plane):
        return remote(
            s.xout.at[share(i, plane), :],
            s.out_tokens.at[i],
            s.final_send.at[0, i, plane],
            s.final_recv.at[0, i],
            plane,
        )

    def input_copy(i, plane):
        return remote(
            s.gout.at[share(i, plane), :],
            s.input_share.at[i],
            s.final_send.at[1, i, plane],
            s.final_recv.at[1, i],
            plane,
        )

    def local(source, target, index):
        return pltpu.make_async_copy(source, target, s.local_sem.at[index])

    own_in = local(s.in_shard, s.wa.at[block_rows(at.dp), :], 0)
    own_out = local(s.out_shard, s.wb.at[block_rows(at.dp), :], 1)
    own_in.start()

    @pl.when(is_feed)
    def _():
        own_out.start()

    for i in range(2):
        own_tokens = local(s.tokens.at[i], s.xin.at[pl.ds(i * ROWS, 64), :], 2 + i)
        own_cotangent = local(s.cotangent.at[i], s.gin.at[pl.ds(i * ROWS + 192, 64), :], 4 + i)

        @pl.when(pipe == 0)
        def _():
            own_tokens.start()

        @pl.when(pipe == 3)
        def _():
            own_cotangent.start()

        @pl.when(pipe != 0)
        def _():
            token_copy(i, pipe).start()

        @pl.when(pipe != 3)
        def _():
            cotangent_copy(i, pipe).start()

    rounds = (condition_front, condition_mods, condition_tokens, condition_times)

    def between(k):
        if k < 4:
            rounds[k](s, at, swap, is_feed)

    def ready(k):
        if k == 0:
            for i in range(2):
                local(s.tokens.at[i], s.xin.at[pl.ds(i * ROWS, 64), :], 2 + i).wait()
                for plane in range(1, 4):
                    token_copy(i, plane).wait_recv()
                front(i, s)

        def one(n, carry):
            project(n % 2, s, n // 2)
            return carry

        def two(i, carry):
            project(i, s, 2)
            attend_heads(i, s)
            return carry

        if k == 1:
            lax.fori_loop(0, 4, one, 0)
        if k == 2:
            lax.fori_loop(0, 2, two, 0)

    own_in.wait()

    @pl.when(pipe == 0)
    def _():
        gather_weights(s, at, 4, between, ready)

    @pl.when(pipe == 2)
    def _():
        gather_weights(s, at, 4, between, lambda k: None)

    @pl.when(is_feed)
    def _():
        own_out.wait()
        gather_weights(s, at, 8, between, lambda k: None)

    for i in range(2):

        @pl.when(pipe != 0)
        def _():
            token_copy(i, pipe).wait_send()

    def step(n, carry):
        at_end = pipe == 3
        goes_forward = jnp.where(at_end, n % 2 == 0, n < 2)
        i = jnp.where(at_end, n // 2, n % 2)

        @pl.when(goes_forward)
        def _():
            @pl.when(pipe != 0)
            def _():
                next_copy(i).wait_recv()

            @pl.when(is_feed)
            def _():
                kernel_feed_forward(i, s)

            @pl.when(jnp.logical_not(is_feed))
            def _():
                @pl.when(pipe != 0)
                def _():
                    front(i, s)

                    def one(part, carry):
                        project(i, s, part)
                        return carry

                    lax.fori_loop(0, 3, one, 0)

                @pl.when(pipe != 0)
                def _():
                    attend_heads(i, s)

                attend_out(i, s)
                finish(i, s)

            @pl.when(pipe == 0)
            def _():
                @pl.when((i > 0) | (at.core == 1))
                def _():
                    pl.semaphore_wait(s.turn, 1)

                next_copy(i).start()
                next_copy(i).wait_send()

                @pl.when((i == 0) | (at.core == 0))
                def _():
                    pl.semaphore_signal(
                        s.turn, inc=1, device_id=(at.sib, pipe), device_id_type=MESH
                    )

            @pl.when((pipe == 1) & (i == 0) & (at.core == 0))
            def _():
                next_copy(0).start()

            @pl.when((pipe == 1) & (i == 1))
            def _():
                @pl.when(at.core == 1)
                def _():
                    pl.semaphore_wait(s.turn, 1)
                    next_copy(0).start()

                next_copy(0).wait_send()
                pl.semaphore_signal(
                    s.turn, inc=1, device_id=(at.sib, pipe), device_id_type=MESH
                )
                pl.semaphore_wait(s.turn, 1)
                next_copy(1).start()
                next_copy(1).wait_send()

                @pl.when(at.core == 0)
                def _():
                    pl.semaphore_signal(
                        s.turn, inc=1, device_id=(at.sib, pipe), device_id_type=MESH
                    )

            @pl.when(pipe == 2)
            def _():
                next_copy(i).start()

            @pl.when(pipe == 3)
            def _():
                for plane in range(3):
                    output_copy(i, plane).start()
                local(s.xout.at[share(i, 3), :], s.out_tokens.at[i], 2 + i).start()

        @pl.when(jnp.logical_not(goes_forward))
        def _():
            @pl.when(pipe == 3)
            def _():
                local(s.cotangent.at[i], s.gin.at[share(i, 3), :], 4 + i).wait()
                for plane in range(3):
                    cotangent_copy(i, plane).wait_recv()

            @pl.when(pipe != 3)
            def _():
                back_copy(i).wait_recv()

            @pl.when(is_feed)
            def _():
                kernel_feed_backward(i, s)

            @pl.when(jnp.logical_not(is_feed))
            def _():
                kernel_attention_backward(i, s)

            @pl.when(pipe != 0)
            def _():
                back_copy(i).start()

            @pl.when(pipe == 0)
            def _():
                for plane in range(1, 4):
                    input_copy(i, plane).start()
                local(s.gout.at[share(i, 0), :], s.input_share.at[i], 4 + i).start()

        return carry

    lax.fori_loop(0, 4, step, 0)
    swap.grads.start()

    for target, sem in ((at.sib, 0), (at.x, 1), (at.y, 2)):
        pl.semaphore_signal(
            s.free.at[sem], inc=1, device_id=(target, pipe), device_id_type=MESH
        )
    for sem in range(3):
        pl.semaphore_wait(s.free.at[sem], 1)
    scatter_grads(s, at, is_feed, swap)
    condition_done(s, at, swap, is_feed)

    for i in range(2):

        @pl.when(pipe != 3)
        def _():
            cotangent_copy(i, pipe).wait_send()
            output_copy(i, pipe).wait_recv()

        @pl.when(pipe == 2)
        def _():
            next_copy(i).wait_send()

        @pl.when(pipe == 3)
        def _():
            for plane in range(3):
                output_copy(i, plane).wait_send()
            local(s.xout.at[share(i, 3), :], s.out_tokens.at[i], 2 + i).wait()

        @pl.when(pipe != 0)
        def _():
            back_copy(i).wait_send()
            input_copy(i, pipe).wait_recv()

        @pl.when(pipe == 0)
        def _():
            for plane in range(1, 4):
                input_copy(i, plane).wait_send()
            local(s.gout.at[share(i, 0), :], s.input_share.at[i], 4 + i).wait()

    s.input_grad[...] = s.input_share[...].astype(jnp.float32)


SCRATCH = dict(
    xin=pltpu.VMEM((512, 1152), low),
    gin=pltpu.VMEM((512, 1152), low),
    xout=pltpu.VMEM((512, 1152), low),
    gout=pltpu.VMEM((512, 1152), low),
    wa=pltpu.VMEM((1152, 4608), low),
    wb=pltpu.VMEM((1152, 4608), low),
    norm=pltpu.VMEM((512, 1152), low),
    left=pltpu.VMEM((2, 1152, 512), low),
    wide=pltpu.VMEM((2, 512, 4608), low),
    branch=pltpu.VMEM((512, 1152), low),
    acc=pltpu.VMEM((256, 1152), jnp.float32),
    gb=pltpu.VMEM((256, 1152), low),
    wacc=pltpu.VMEM((256, 3456), jnp.float32),
    stage=pltpu.VMEM((4, 288, 1152), low),
    near_stage=pltpu.VMEM((2, 6, 144, 1152), low),
    gather_send=pltpu.SemaphoreType.DMA((8, 8)),
    gather_recv=pltpu.SemaphoreType.DMA((8, 8)),
    sib_send=pltpu.SemaphoreType.DMA((32,)),
    sib_recv=pltpu.SemaphoreType.DMA((32,)),
    near_send=pltpu.SemaphoreType.DMA((2, 12)),
    near_recv=pltpu.SemaphoreType.DMA((2, 12)),
    out_sem=pltpu.SemaphoreType.DMA((2,)),
    share_send=pltpu.SemaphoreType.DMA((2, 2)),
    xin_recv=pltpu.SemaphoreType.DMA((2, 4)),
    gin_recv=pltpu.SemaphoreType.DMA((2, 4)),
    hop_send=pltpu.SemaphoreType.DMA((2, 2)),
    final_send=pltpu.SemaphoreType.DMA((2, 2, 4)),
    final_recv=pltpu.SemaphoreType.DMA((2, 2)),
    local_sem=pltpu.SemaphoreType.DMA((6,)),
    free=pltpu.SemaphoreType.REGULAR((3,)),
    turn=pltpu.SemaphoreType.REGULAR,
    shard_sem=pltpu.SemaphoreType.DMA((7,)),
    swap_send=pltpu.SemaphoreType.DMA((7, 8)),
    swap_recv=pltpu.SemaphoreType.DMA((7, 8)),
    end_send=pltpu.SemaphoreType.DMA((4,)),
    end_recv=pltpu.SemaphoreType.DMA((4,)),
    mod=pltpu.VMEM((2, 1, 3456), jnp.float32),
    time=pltpu.VMEM((2, 1, 3456), jnp.float32),
    token=pltpu.VMEM((2, 1, 1152), jnp.float32),
    grad_rows=pltpu.VMEM((2, 1, 6912), jnp.float32),
    rows=pltpu.VMEM((16, 1, 1280), jnp.float32),
    flat=pltpu.VMEM((16, 6912), jnp.float32),
    own_cond=pltpu.VMEM((16, 144), low),
    own_token=pltpu.VMEM((16, 144), low),
    mod_parts=pltpu.VMEM((16, 1, 4608), jnp.float32),
    mod_all=pltpu.VMEM((8, 2, 1, 4608), jnp.float32),
    token_all=pltpu.VMEM((16, 1, 1152), jnp.float32),
    time_parts=pltpu.VMEM((16, 1, 3456), jnp.float32),
    time_all=pltpu.VMEM((8, 2, 1, 3456), jnp.float32),
    grad_all=pltpu.VMEM((16, 1, 6912), jnp.float32),
    back=pltpu.VMEM((16, 1152), low),
    back_all=pltpu.VMEM((8, 16, 1152), low),
    end=pltpu.VMEM((16, 144), jnp.float32),
    input_share=pltpu.VMEM((2, 64, 1152), low),
    end_parts=pltpu.VMEM((4, 16, 144), jnp.float32),
    end_all=pltpu.VMEM((8, 16, 144), jnp.float32),
)
REFS = (
    ["tokens", "cotangent", "in_shard", "out_shard", "mod_shard", "cond_in"]
    + ["out_tokens", "input_grad", "terms", "hot", "in_grad", "out_grad", "mod_grad"]
    + list(SCRATCH)
)


def mega(tokens, cotangent, in_shard, out_shard, mod_shard, cond_rows):
    anywhere = pl.BlockSpec(memory_space=pl.ANY)
    near = pl.BlockSpec(memory_space=pltpu.VMEM)

    def wide(array):
        return jax.ShapeDtypeStruct((1,) + array.shape, jnp.float32)

    return pl.pallas_call(
        mega_body,
        out_shape=(
            jax.ShapeDtypeStruct(tokens.shape, low),
            jax.ShapeDtypeStruct(tokens.shape, jnp.float32),
            jax.ShapeDtypeStruct((48, tokens.shape[2]), low),
            jax.ShapeDtypeStruct((48, 1024), low),
            wide(in_shard),
            wide(out_shard),
            wide(mod_shard),
        ),
        in_specs=[anywhere] * 5 + [near],
        out_specs=[anywhere] + [near] * 3 + [anywhere] * 3,
        scratch_shapes=list(SCRATCH.values()),
        compiler_params=pltpu.CompilerParams(
            collective_id=0, has_side_effects=True, vmem_limit_bytes=62 * 2**20
        ),
        cost_estimate=pl.CostEstimate(
            flops=25 * 10**9, bytes_accessed=10**7, transcendentals=10**7
        ),
        name="blocks",
    )(tokens, cotangent, in_shard, out_shard, mod_shard, cond_rows)


def last_body(terms, hot, *refs):
    sources, (table, *targets) = refs[:3], refs[3:7]
    value, *held, sems = refs[7:]
    classes = table.shape[0]
    pieces = [
        (source.at[0, pl.ds(48 * part, 48), :], stage.at[pl.ds(48 * part, 48), :],
         target.at[0, pl.ds(48 * part, 48), :], 3 * k + part)
        for k, (source, stage, target) in enumerate(zip(sources, held, targets))
        for part in range(3)
    ]
    takes = [pltpu.make_async_copy(s, v, sems.at[0, n]) for s, v, t, n in pieces]
    gives = [pltpu.make_async_copy(v, t, sems.at[1, n]) for s, v, t, n in pieces]
    for take in takes:
        take.start()
    for k in range(4):
        count = min(256, classes - 256 * k)
        value[k] = contract_rows(hot[:, 256 * k : 256 * (k + 1)], terms[...])
        part = pltpu.make_async_copy(
            value.at[k, pl.ds(0, count), :],
            table.at[pl.ds(256 * k, count), :],
            sems.at[1, 9 + k],
        )
        part.start()
        gives.append(part)
    for take, give in zip(takes, gives):
        take.wait()
        give.start()
    for give in gives:
        give.wait()


def last_copies(terms, hot, grads, classes):
    anywhere = pl.BlockSpec(memory_space=pl.ANY)
    near = pl.BlockSpec(memory_space=pltpu.VMEM)
    width = terms.shape[1]
    return pl.pallas_call(
        last_body,
        out_shape=[jax.ShapeDtypeStruct((classes, width), jnp.float32)]
        + [jax.ShapeDtypeStruct(grad.shape, jnp.float32) for grad in grads],
        in_specs=[near, near] + [anywhere] * 3,
        out_specs=[anywhere] * 4,
        scratch_shapes=[
            pltpu.VMEM((4, 256, width), jnp.float32),
            *[pltpu.VMEM(grad.shape[1:], jnp.float32) for grad in grads],
            pltpu.SemaphoreType.DMA((2, 13)),
        ],
        compiler_params=pltpu.CompilerParams(vmem_limit_bytes=62 * 2**20),
        name="table",
    )(terms, hot, *grads)


def fast_shards(
    tokens,
    cotangent,
    timesteps,
    labels,
    class_table,
    section_in_weights,
    section_out_weights,
    modulation_weights,
):
    model_width = tokens.shape[2]
    in_shard, out_shard, mod_shard = (
        section_in_weights[0],
        section_out_weights[0],
        modulation_weights[0],
    )
    images = tokens.shape[0]
    classes = class_table.shape[0]
    matches = labels[:, None] == lax.broadcasted_iota(jnp.int32, (images, classes), 1)
    condition = sinusoid(timesteps, model_width) + product(
        matches.astype(jnp.bfloat16), class_table
    )
    named = jnp.broadcast_to(labels.astype(jnp.float32)[:, None], (images, 128))
    cond_rows = jnp.concatenate([condition, named], axis=1)[:, None, :]
    out_tokens, input_grad, terms, hot, *grads = mega(
        tokens, cotangent, in_shard, out_shard, mod_shard, cond_rows
    )
    return (out_tokens, input_grad, *last_copies(terms, hot, grads, classes))


def solution(mesh):
    return jax.shard_map(
        fast_shards if mesh.shape["dp"] == 8 else shards,
        mesh=mesh,
        in_specs=(
            P("dp", "pipe", None),
            P("dp", "pipe", None),
            P("dp"),
            P("dp"),
            P(),
            P("pipe", "dp", None),
            P("pipe", "dp", None),
            P("pipe", "dp", None),
        ),
        out_specs=(
            P("dp", "pipe", None),
            P("dp", "pipe", None),
            P(),
            P("pipe", "dp", None),
            P("pipe", "dp", None),
            P("pipe", "dp", None),
        ),
        check_vma=False,
    )
```

```python
from functools import partial
import math
from types import SimpleNamespace

import jax
import jax.numpy as jnp
from jax import lax
from jax.experimental import pallas as pl
from jax.experimental.pallas import tpu as pltpu
from jax.sharding import PartitionSpec as P

HEADS = 16
HEAD = 72


epsilon = 1e-06
highest = lax.Precision.HIGHEST


def shifted(block, axis, distance):
    devices = range(lax.axis_size(axis))
    route = [(i - distance, i) for i in devices if i - distance in devices]
    return lax.ppermute(block, axis, route)


def sinusoid(step_values, model_width):
    half_width = model_width // 2
    frequencies = jnp.exp(
        -math.log(10000.0) * jnp.arange(half_width, dtype=jnp.float32) / half_width
    )
    angles = step_values.astype(jnp.float32)[:, None] * frequencies[None, :]
    return jnp.concatenate([jnp.cos(angles), jnp.sin(angles)], axis=1)


def product(former, latter):
    return jnp.dot(former, latter, preferred_element_type=jnp.float32)


def contract_rows(former, latter):
    return lax.dot_general(
        former, latter, (((0,), (0,)), ((), ())), preferred_element_type=jnp.float32
    )


def contract_cols(former, latter):
    return lax.dot_general(
        former, latter, (((1,), (1,)), ((), ())), preferred_element_type=jnp.float32
    )


def normalize_rows(row_values):
    centered = row_values - jnp.mean(row_values, axis=-1, keepdims=True)
    inverse = lax.rsqrt(jnp.mean(centered * centered, axis=-1, keepdims=True) + epsilon)
    return (centered * inverse, inverse)


def modulation_front(section_input, mod_row):
    model_width = section_input.shape[1]
    shift_vec = mod_row[:model_width]
    scale_vec = mod_row[model_width : 2 * model_width]
    gate_vec = mod_row[2 * model_width :]
    centred, inverse = normalize_rows(section_input.astype(jnp.float32))
    normed = (centred * (1.0 + scale_vec) + shift_vec).astype(jnp.bfloat16)
    return (normed, centred, inverse, scale_vec, gate_vec)


def modulation_back(grad_normed, centred, inverse, scale_vec, grad_rows, grad_gate):
    grad_shift = jnp.sum(grad_normed, axis=0)
    grad_scale = jnp.sum(grad_normed * centred, axis=0)
    grad_centred = grad_normed * (1.0 + scale_vec)
    grad_input = inverse * (
        grad_centred
        - jnp.mean(grad_centred, axis=-1, keepdims=True)
        - centred * jnp.mean(grad_centred * centred, axis=-1, keepdims=True)
    )
    grad_mod = jnp.concatenate([grad_shift, grad_scale, grad_gate]).astype(jnp.bfloat16)
    return (grad_rows + grad_input, grad_mod)


def attention_parts(section_input, mod_row, time_row, weights):
    in_weight = weights[0]
    model_width = section_input.shape[1]
    tok_len = section_input.shape[0]
    normed, centred, inverse, scale_vec, gate_vec = modulation_front(section_input, mod_row)
    qkv = (product(normed, in_weight[:, : 3 * model_width]) + time_row).astype(jnp.bfloat16)
    split_qkv = qkv.reshape(tok_len, 3, HEADS, HEAD)
    queries = split_qkv[:, 0]
    keyed = split_qkv[:, 1]
    valued = split_qkv[:, 2]
    scores = jnp.einsum(
        "qhd,khd->hqk", queries, keyed, preferred_element_type=jnp.float32
    ) * HEAD ** (-0.5)
    probs_full = jax.nn.softmax(scores, axis=-1)
    probs_low = probs_full.astype(jnp.bfloat16)
    mixed = jnp.einsum("hqk,khd->qhd", probs_low, valued, preferred_element_type=jnp.float32)
    head_rows = mixed.reshape(tok_len, model_width).astype(jnp.bfloat16)
    branch = product(head_rows, in_weight[:, 3 * model_width :])
    section_output = section_input.astype(jnp.float32) + gate_vec * branch
    saved_parts = (
        normed,
        centred,
        inverse,
        scale_vec,
        gate_vec,
        queries,
        keyed,
        valued,
        probs_full,
        probs_low,
        head_rows,
        branch,
    )
    return (section_output, saved_parts)


def attention_forward(section_input, mod_row, time_row, weights):
    return attention_parts(section_input, mod_row, time_row, weights)[0]


def attention_backward(section_input, grad_in, mod_row, time_row, weights):
    in_weight = weights[0]
    model_width = section_input.shape[1]
    tok_len = section_input.shape[0]
    unused, saved_parts = attention_parts(section_input, mod_row, time_row, weights)
    (
        normed,
        centred,
        inverse,
        scale_vec,
        gate_vec,
        queries,
        keyed,
        valued,
        probs_full,
        probs_low,
        head_rows,
        branch,
    ) = saved_parts
    grad_rows = grad_in.astype(jnp.float32)
    grad_branch = (gate_vec * grad_rows).astype(jnp.bfloat16)
    grad_gate = jnp.sum(grad_rows * branch, axis=0)
    grad_heads = contract_cols(grad_branch, in_weight[:, 3 * model_width :]).astype(jnp.bfloat16)
    heads_split = grad_heads.reshape(tok_len, HEADS, HEAD)
    grad_probs = jnp.einsum("qhd,khd->hqk", heads_split, valued, preferred_element_type=jnp.float32)
    grad_value = jnp.einsum(
        "hqk,qhd->khd", probs_low, heads_split, preferred_element_type=jnp.float32
    )
    grad_scores = (
        probs_full * (grad_probs - jnp.sum(probs_full * grad_probs, axis=-1, keepdims=True))
    ).astype(jnp.bfloat16)
    grad_query = jnp.einsum(
        "hqk,khd->qhd", grad_scores, keyed, preferred_element_type=jnp.float32
    ) * HEAD ** (-0.5)
    grad_key = jnp.einsum(
        "hqk,qhd->khd", grad_scores, queries, preferred_element_type=jnp.float32
    ) * HEAD ** (-0.5)
    grad_qkv = (
        jnp.stack([grad_query, grad_key, grad_value], axis=1)
        .reshape(tok_len, 3 * model_width)
        .astype(jnp.bfloat16)
    )
    grad_normed = contract_cols(grad_qkv, in_weight[:, : 3 * model_width])
    grad_time = jnp.sum(grad_qkv, axis=0, dtype=jnp.float32).astype(jnp.bfloat16)
    grad_input, grad_mod = modulation_back(
        grad_normed, centred, inverse, scale_vec, grad_rows, grad_gate
    )
    narrow_zero = jnp.zeros((tok_len, model_width), jnp.bfloat16)
    return (
        grad_input,
        normed,
        jnp.concatenate([grad_qkv, narrow_zero], axis=1),
        grad_branch,
        jnp.concatenate([head_rows, narrow_zero, narrow_zero, narrow_zero], axis=1),
        grad_mod,
        grad_time,
    )


def feed_parts(section_input, mod_row, weights):
    in_weight, out_weight = weights
    normed, centred, inverse, scale_vec, gate_vec = modulation_front(section_input, mod_row)
    pre_act = product(normed, in_weight)
    hidden = jax.nn.gelu(pre_act, approximate=True).astype(jnp.bfloat16)
    branch = contract_cols(hidden, out_weight)
    section_output = section_input.astype(jnp.float32) + gate_vec * branch
    return (
        section_output,
        (normed, centred, inverse, scale_vec, gate_vec, pre_act, hidden, branch),
    )


def feed_forward(section_input, mod_row, time_row, weights):
    return feed_parts(section_input, mod_row, weights)[0]


def feed_backward(section_input, grad_in, mod_row, time_row, weights):
    in_weight, out_weight = weights
    unused, saved_parts = feed_parts(section_input, mod_row, weights)
    normed, centred, inverse, scale_vec, gate_vec, pre_act, hidden, branch = saved_parts
    grad_rows = grad_in.astype(jnp.float32)
    grad_branch = (gate_vec * grad_rows).astype(jnp.bfloat16)
    grad_gate = jnp.sum(grad_rows * branch, axis=0)
    grad_hidden = product(grad_branch, out_weight)
    gelu_pull = jax.vjp(partial(jax.nn.gelu, approximate=True), pre_act)[1]
    grad_pre = gelu_pull(grad_hidden)[0].astype(jnp.bfloat16)
    grad_normed = contract_cols(grad_pre, in_weight)
    grad_input, grad_mod = modulation_back(
        grad_normed, centred, inverse, scale_vec, grad_rows, grad_gate
    )
    return (
        grad_input,
        normed,
        grad_pre,
        grad_branch,
        hidden,
        grad_mod,
        jnp.zeros(grad_mod.shape, jnp.bfloat16),
    )


def spare_forward(section_input, mod_row, time_row, weights):
    return jnp.zeros(section_input.shape, jnp.float32)


def spare_backward(section_input, grad_in, mod_row, time_row, weights):
    tok_len, model_width = section_input.shape
    hidden_width = weights[0].shape[1]
    narrow_zero = jnp.zeros((tok_len, model_width), jnp.bfloat16)
    wide_zero = jnp.zeros((tok_len, hidden_width), jnp.bfloat16)
    row_zero = jnp.zeros((3 * model_width,), jnp.bfloat16)
    return (
        jnp.zeros(section_input.shape, jnp.float32),
        narrow_zero,
        wide_zero,
        narrow_zero,
        wide_zero,
        row_zero,
        row_zero,
    )


def attention_weight_grads(left_one, right_one, left_two, right_two):
    width = left_two.shape[1]
    low = jnp.bfloat16
    qkv_term = contract_rows(left_one, right_one[:, : 3 * width]).astype(low)
    out_term = contract_rows(right_two[:, :width], left_two).astype(low)
    zero_term = jnp.zeros((width, right_two.shape[1]), low)
    return (jnp.concatenate([qkv_term, out_term], axis=1), zero_term)


def feed_weight_grads(left_one, right_one, left_two, right_two):
    low = jnp.bfloat16
    return (
        contract_rows(left_one, right_one).astype(low),
        contract_rows(left_two, right_two).astype(low),
    )


def replace_slot(buffer, slot_index, new_rows, active):
    old_rows = lax.dynamic_index_in_dim(buffer, slot_index, 0, keepdims=False)
    return lax.dynamic_update_index_in_dim(
        buffer, jnp.where(active, new_rows, old_rows), slot_index, 0
    )


def shards(
    tokens,
    cotangent,
    timesteps,
    labels,
    class_table,
    section_in_weights,
    section_out_weights,
    modulation_weights,
):
    micro_count = tokens.shape[0]
    model_width = tokens.shape[2]
    hidden_width = section_in_weights.shape[2]
    section_count = lax.axis_size("pipe")
    section_index = lax.axis_index("pipe")
    last_section = section_count - 1
    section_kind = 1 + section_index % 2
    in_shard, out_shard, mod_shard = (
        section_in_weights[0],
        section_out_weights[0],
        modulation_weights[0],
    )
    whole_tokens, whole_cotangent = (
        lax.all_gather(tokens, "pipe", axis=1, tiled=True),
        lax.all_gather(cotangent, "pipe", axis=1, tiled=True),
    )
    tok_len = whole_tokens.shape[1]
    weights = (
        lax.all_gather(in_shard, "dp", axis=0, tiled=True),
        lax.all_gather(out_shard, "dp", axis=0, tiled=True),
    )
    condition, own_conditioner, own_time, matches, mod_rows, time_rows = conditioning(
        timesteps, labels, class_table, out_shard, mod_shard
    )

    def forward_tick(carry, tick_index):
        incoming, kept_inputs, finals = carry
        micro_index = tick_index - section_index
        active = (micro_index >= 0) & (micro_index < micro_count)
        slot_index = jnp.clip(micro_index, 0, micro_count - 1)
        first_rows = lax.dynamic_index_in_dim(whole_tokens, slot_index, 0, keepdims=False)
        section_input = jnp.where(section_index == 0, first_rows, incoming)
        section_output = lax.switch(
            jnp.where(active, section_kind, 0),
            (spare_forward, attention_forward, feed_forward),
            section_input,
            lax.dynamic_index_in_dim(mod_rows, slot_index, 0, keepdims=False),
            lax.dynamic_index_in_dim(time_rows, slot_index, 0, keepdims=False),
            weights,
        )
        output_low = section_output.astype(jnp.bfloat16)
        kept_inputs = replace_slot(kept_inputs, slot_index, section_input, active)
        finals = replace_slot(
            finals, slot_index, output_low, active & (section_index == last_section)
        )
        incoming = shifted(output_low, "pipe", 1)
        return ((incoming, kept_inputs, finals), None)

    empty_rows = jnp.zeros((tok_len, model_width), jnp.bfloat16)
    empty_store = jnp.zeros((micro_count, tok_len, model_width), jnp.bfloat16)
    forward_out, ignored = lax.scan(
        forward_tick,
        (empty_rows, empty_store, empty_store),
        jnp.arange(micro_count + section_count - 1),
    )
    kept_inputs = forward_out[1]
    finals = forward_out[2]
    wide_store = jnp.zeros((micro_count, tok_len, hidden_width), jnp.bfloat16)
    row_store = jnp.zeros((micro_count, 3 * model_width), jnp.bfloat16)
    start_factors = (empty_store, wide_store, empty_store, wide_store, row_store, row_store)

    def backward_tick(carry, tick_index):
        incoming, factors, input_grads = carry
        micro_index = tick_index - (last_section - section_index)
        active = (micro_index >= 0) & (micro_index < micro_count)
        slot_index = jnp.clip(micro_index, 0, micro_count - 1)
        top_grad = lax.dynamic_index_in_dim(whole_cotangent, slot_index, 0, keepdims=False)
        grad_in = jnp.where(section_index == last_section, top_grad, incoming)
        section_input = lax.dynamic_index_in_dim(kept_inputs, slot_index, 0, keepdims=False)
        results = lax.switch(
            jnp.where(active, section_kind, 0),
            (spare_backward, attention_backward, feed_backward),
            section_input,
            grad_in,
            lax.dynamic_index_in_dim(mod_rows, slot_index, 0, keepdims=False),
            lax.dynamic_index_in_dim(time_rows, slot_index, 0, keepdims=False),
            weights,
        )
        grad_low = results[0].astype(jnp.bfloat16)
        factors = tuple(
            (
                replace_slot(buffer, slot_index, fresh, active)
                for buffer, fresh in zip(factors, results[1:])
            )
        )
        input_grads = replace_slot(
            input_grads, slot_index, grad_low, active & (section_index == 0)
        )
        incoming = shifted(grad_low, "pipe", -1)
        return ((incoming, factors, input_grads), None)

    backward_out, ignored = lax.scan(
        backward_tick,
        (empty_rows, start_factors, empty_store),
        jnp.arange(micro_count + section_count - 1),
    )
    factors = backward_out[1]
    input_grads = backward_out[2]
    flat_rows = micro_count * tok_len
    left_one, right_one, left_two, right_two = (
        stored.reshape(flat_rows, stored.shape[2]) for stored in factors[:4]
    )
    in_term, out_term = lax.cond(
        section_index % 2 == 0,
        attention_weight_grads,
        feed_weight_grads,
        left_one,
        right_one,
        left_two,
        right_two,
    )
    in_grad = lax.psum_scatter(in_term, "dp", scatter_dimension=0, tiled=True)
    out_grad = lax.psum_scatter(out_term, "dp", scatter_dimension=0, tiled=True)
    own_out, own_in = (finals, input_grads)
    keep_out = jnp.where(section_index == last_section, own_out, 0)
    keep_in = jnp.where(section_index == 0, own_in, 0)
    output_share = lax.psum_scatter(keep_out, "pipe", scatter_dimension=1, tiled=True)
    input_share = lax.psum_scatter(keep_in, "pipe", scatter_dimension=1, tiled=True)
    small_outs = conditioning_grads(
        factors[4],
        factors[5],
        condition,
        own_conditioner,
        own_time,
        matches,
        out_shard,
        mod_shard,
        out_grad,
    )
    return (
        output_share,
        input_share.astype(jnp.float32),
        small_outs[0],
        in_grad.astype(jnp.float32)[None],
        small_outs[1][None],
        small_outs[2][None],
    )


def conditioning_grads(
    mod_grads,
    time_grads,
    condition,
    own_conditioner,
    own_time,
    matches,
    out_shard,
    mod_shard,
    out_grad,
):
    model_width = condition.shape[1]
    is_attention = lax.axis_index("pipe") % 2 == 0
    all_mod = lax.all_gather(mod_grads, "dp", axis=0, tiled=True)
    all_time = lax.all_gather(time_grads, "dp", axis=0, tiled=True)
    grad_mod_shard = contract_rows(own_conditioner, all_mod)
    cond_grads = contract_cols(all_mod, mod_shard)
    own_token = contract_cols(all_time, out_shard[:, : 3 * model_width]).astype(jnp.bfloat16)
    all_token = lax.all_gather(own_token, "dp", axis=1, tiled=True)
    token_grads = contract_cols(all_token, out_shard[:, 3 * model_width :])
    cond_grads = cond_grads + jnp.where(is_attention, token_grads, 0.0)
    time_out = jnp.concatenate(
        [contract_rows(own_time, all_time), contract_rows(own_conditioner, all_token)], axis=1
    )
    grad_out_shard = jnp.where(is_attention, time_out, out_grad.astype(jnp.float32))
    every_part = lax.all_gather(cond_grads, "pipe", axis=0)
    whole_grads = lax.all_gather(jnp.sum(every_part, axis=0), "dp", axis=1, tiled=True)
    grad_condition = jax.vjp(jax.nn.silu, condition)[1](whole_grads)[0]
    grad_table = lax.dot_general(
        matches.astype(jnp.float32),
        grad_condition,
        (((0,), (0,)), ((), ())),
        precision=highest,
        preferred_element_type=jnp.float32,
    )
    return (grad_table, grad_out_shard, grad_mod_shard)


def conditioning(timesteps, labels, class_table, out_shard, mod_shard):
    model_width = class_table.shape[1]
    own_rows = out_shard.shape[0]
    own_start = lax.axis_index("dp") * own_rows
    all_steps = lax.all_gather(timesteps, "dp", axis=0, tiled=True)
    all_labels = lax.all_gather(labels, "dp", axis=0, tiled=True)
    image_count = all_steps.shape[0]
    classes = class_table.shape[0]
    matches = all_labels[:, None] == lax.broadcasted_iota(jnp.int32, (image_count, classes), 1)
    condition = sinusoid(all_steps, model_width) + product(
        matches.astype(jnp.bfloat16), class_table
    )
    conditioner = jax.nn.silu(condition).astype(jnp.bfloat16)
    own_conditioner = lax.dynamic_slice_in_dim(conditioner, own_start, own_rows, 1)
    mod_rows = lax.psum_scatter(
        product(own_conditioner, mod_shard), "dp", scatter_dimension=0, tiled=True
    )
    own_time = lax.psum_scatter(
        product(own_conditioner, out_shard[:, 3 * model_width :]),
        "dp",
        scatter_dimension=1,
        tiled=True,
    ).astype(jnp.bfloat16)
    time_rows = lax.psum_scatter(
        product(own_time, out_shard[:, : 3 * model_width]), "dp", scatter_dimension=0, tiled=True
    )
    return (condition, own_conditioner, own_time, matches, mod_rows, time_rows)


ROWS = 256
SPAN = 2304
THIRD = 1152
PART = 1152
BLOCK = 144
GROUP = 4
MESH = pl.DeviceIdType.MESH
low = jnp.bfloat16
GELU_A = math.sqrt(2.0 / math.pi)
GELU_B = 0.044715


def product_nt(former, latter):
    return contract_cols(former, latter)


def spread(index, width):
    return pl.ds(pl.multiple_of(index * width, 128), width)


def image_rows(i):
    return pl.ds(pl.multiple_of(i * ROWS, ROWS), ROWS)


def block_rows(b):
    return pl.ds(pl.multiple_of(b * BLOCK, 16), BLOCK)


def front(i, s):
    rows = image_rows(i)
    xhat, inverse = normalize_rows(s.xin[rows, :].astype(jnp.float32))
    normed = (xhat * (1.0 + s.mod[i, :, PART : 2 * PART]) + s.mod[i, :, 0:PART]).astype(low)
    s.norm[rows, :] = normed
    s.left[0, :, rows] = normed.T


def finish(i, s):
    rows = image_rows(i)
    branch = s.acc[...]
    s.branch[rows, :] = branch.astype(low)
    gate = s.mod[i, :, 2 * PART : 3 * PART]
    s.xout[rows, :] = (s.xin[rows, :].astype(jnp.float32) + gate * branch).astype(low)


def bent(value):
    square = value * value
    wave = jnp.tanh(value * (GELU_A + (GELU_A * GELU_B) * square))
    half = 0.5 + 0.5 * wave
    slope = half + value * (0.5 - 0.5 * (wave * wave)) * (
        GELU_A + (3.0 * GELU_A * GELU_B) * square
    )
    return (value * half).astype(low), slope.astype(low)


def feed_up(i, s):
    rows = image_rows(i)

    def tile(j, carry):
        cols = spread(j, SPAN)
        hidden, slope = bent(product(s.norm[rows, :], s.wa[:, cols]))
        s.wide[0, rows, cols] = hidden
        s.wide[1, rows, cols] = slope
        return carry

    lax.fori_loop(0, s.wa.shape[1] // SPAN, tile, 0)


def feed_down(i, s):
    rows = image_rows(i)

    def tile(j, carry):
        some = pl.ds(pl.multiple_of(j * 384, 384), 384)
        s.acc[:, spread(j, 384)] = product_nt(s.wide[0, rows, :], s.wb[some, :])
        return carry

    lax.fori_loop(0, PART // 384, tile, 0)


def feed_down_up(i, s):
    rows = image_rows(i)
    s.acc[...] = jnp.zeros(s.acc.shape, jnp.float32)

    def tile(j, carry):
        cols = spread(j, SPAN)
        grad_hidden = product(s.gb[...], s.wb[:, cols])
        grad_pre = (grad_hidden * s.wide[1, rows, cols].astype(jnp.float32)).astype(low)
        s.wide[1, rows, cols] = grad_pre
        s.acc[...] += product_nt(grad_pre, s.wa[:, cols])
        return carry

    lax.fori_loop(0, s.wa.shape[1] // SPAN, tile, 0)


def back_start(i, s):
    rows = image_rows(i)
    grad = s.gin[rows, :].astype(jnp.float32)
    gb = (s.mod[i, :, 2 * PART : 3 * PART] * grad).astype(low)
    s.gb[...] = gb
    s.grad_rows[i, :, 2 * PART : 3 * PART] = jnp.sum(
        grad * s.branch[rows, :].astype(jnp.float32), axis=0, keepdims=True
    )
    return gb


def back_finish(i, s):
    rows = image_rows(i)
    xhat, inverse = normalize_rows(s.xin[rows, :].astype(jnp.float32))
    gn = s.acc[...]
    s.grad_rows[i, :, 0:PART] = jnp.sum(gn, axis=0, keepdims=True)
    s.grad_rows[i, :, PART : 2 * PART] = jnp.sum(gn * xhat, axis=0, keepdims=True)
    gx = gn * (1.0 + s.mod[i, :, PART : 2 * PART])
    first = jnp.mean(gx, axis=-1, keepdims=True)
    second = jnp.mean(gx * xhat, axis=-1, keepdims=True)
    grad = s.gin[rows, :].astype(jnp.float32)
    s.gout[rows, :] = (grad + inverse * (gx - first - xhat * second)).astype(low)


def kernel_feed_backward(i, s):
    gb = back_start(i, s)
    s.left[1, :, image_rows(i)] = gb.T
    feed_down_up(i, s)
    back_finish(i, s)


def project(i, s, part):
    rows = image_rows(i)

    def tile(j, carry):
        cols = pl.ds(pl.multiple_of(part * PART + j * THIRD, 128), THIRD)
        value = product(s.norm[rows, :], s.wa[:, cols]) + s.time[i, :, cols]
        s.wide[0, rows, cols] = value.astype(low)
        return carry

    lax.fori_loop(0, PART // THIRD, tile, 0)


def head_window(h):
    start = jnp.minimum((h * HEAD) // 128, PART // 128 - 2)
    offset = h * HEAD - start * 128
    lanes = lax.broadcasted_iota(jnp.int32, (ROWS, 256), 1)
    inside = (lanes >= offset) & (lanes < offset + HEAD)
    return start, inside


def window(start, part):
    return pl.ds(pl.multiple_of(part * PART + start * 128, 128), 256)


def prob_place(i, h):
    return (
        pl.ds(pl.multiple_of((h % 4) * ROWS, ROWS), ROWS),
        pl.ds(pl.multiple_of((4 * i + h // 4) * ROWS, ROWS), ROWS),
    )


def attend_heads(i, s):
    rows = image_rows(i)
    s.acc[...] = jnp.zeros(s.acc.shape, jnp.float32)
    zero = jnp.zeros((), low)

    def score(h, slot):
        start, inside = head_window(h)
        query = jnp.where(inside, s.wide[0, rows, window(start, 0)], zero)
        s.wacc[:, spread(slot, ROWS)] = product_nt(query, s.wide[0, rows, window(start, 1)])

    def soften(h, slot):
        scores = s.wacc[:, spread(slot, ROWS)]
        top = jnp.max(scores, axis=-1, keepdims=True)
        powers = jnp.exp2((scores - top) * (HEAD ** (-0.5) * math.log2(math.e)))
        place = prob_place(i, h)
        s.wb[place[0], place[1]] = (
            powers * (1.0 / jnp.sum(powers, axis=-1, keepdims=True))
        ).astype(low)

    def mix(h):
        start, inside = head_window(h)
        place = prob_place(i, h)
        value = jnp.where(inside, s.wide[0, rows, window(start, 2)], zero)
        s.acc[:, window(start, 0)] += product(s.wb[place[0], place[1]], value)

    for k in range(GROUP):
        score(k, k)

    def group(g, carry):
        for k in range(GROUP):
            soften(GROUP * g + k, k)
        for k in range(GROUP):
            score(jnp.minimum(GROUP * (g + 1) + k, HEADS - 1), k)
        for k in range(GROUP):
            mix(GROUP * g + k)
        return carry

    lax.fori_loop(0, HEADS // GROUP, group, 0)
    mixed = s.acc[...].astype(low)
    s.left[1, :, rows] = mixed.T
    s.wide[0, rows, 3 * PART :] = mixed


def attend_out(i, s):
    rows = image_rows(i)
    s.acc[...] = product(s.wide[0, rows, 3 * PART :], s.wa[:, 3 * PART :])


def kernel_attention_backward(i, s):
    rows = image_rows(i)
    gb = back_start(i, s)
    s.wide[1, rows, 3 * PART :] = gb
    s.gb[...] = product_nt(gb, s.wa[:, 3 * PART :]).astype(low)
    s.wacc[...] = jnp.zeros(s.wacc.shape, jnp.float32)

    zero = jnp.zeros((), low)

    def grad_of_probs(h):
        start, inside = head_window(h)
        grad_head = jnp.where(inside, s.gb[:, window(start, 0)], zero)
        return product_nt(grad_head, s.wide[0, rows, window(start, 2)])

    def grad_of_scores(h, grad_probs):
        place = prob_place(i, h)
        probs = s.wb[place[0], place[1]].astype(jnp.float32)
        mixed = jnp.sum(probs * grad_probs, axis=-1, keepdims=True)
        return (probs * (grad_probs - mixed)).astype(low)

    def grads_of_qkv(h, grad_scores):
        start, inside = head_window(h)
        place = prob_place(i, h)
        query = jnp.where(inside, s.wide[0, rows, window(start, 0)], zero)
        key = jnp.where(inside, s.wide[0, rows, window(start, 1)], zero)
        grad_head = jnp.where(inside, s.gb[:, window(start, 0)], zero)
        s.wacc[:, window(start, 2)] += contract_rows(s.wb[place[0], place[1]], grad_head)
        s.wacc[:, window(start, 0)] += product(grad_scores, key)
        s.wacc[:, window(start, 1)] += contract_rows(grad_scores, query)

    def group(g, carry):
        heads = [GROUP * g + k for k in range(GROUP)]
        first = [grad_of_probs(h) for h in heads]
        second = [grad_of_scores(h, value) for h, value in zip(heads, first)]
        for h, value in zip(heads, second):
            grads_of_qkv(h, value)
        return carry

    lax.fori_loop(0, HEADS // GROUP, group, 0)
    scale = HEAD ** (-0.5)
    for part, factor in ((0, scale), (1, scale), (2, 1.0)):
        cols = pl.ds(part * PART, PART)
        grads = (s.wacc[:, cols] * factor).astype(low)
        s.wide[1, rows, cols] = grads
        s.grad_rows[i, :, pl.ds((3 + part) * PART, PART)] = jnp.sum(
            grads.astype(jnp.float32), axis=0, keepdims=True
        )
    s.acc[...] = jnp.zeros(s.acc.shape, jnp.float32)

    def tile(j, carry):
        cols = spread(j, THIRD)
        s.acc[...] += product_nt(s.wide[1, rows, cols], s.wa[:, cols])
        return carry

    lax.fori_loop(0, 3 * PART // THIRD, tile, 0)
    back_finish(i, s)


def places():
    dp, pipe = lax.axis_index("dp"), lax.axis_index("pipe")
    core, x_bit, y_bit = dp % 2, (dp // 2) % 2, dp // 4
    sib = dp + 1 - 2 * core
    step_x, step_y = 2 - 4 * x_bit, 4 - 8 * y_bit
    return SimpleNamespace(
        dp=dp,
        pipe=pipe,
        core=core,
        sib=sib,
        x=dp + step_x,
        y=dp + step_y,
        d=dp + step_x + step_y,
        step_x=step_x,
        step_y=step_y,
        x_bit=x_bit,
        y_bit=y_bit,
    )


def relay(s, at, phase):
    def piece(j, role, first=0, count=BLOCK):
        index = 4 * j + role
        row = pl.multiple_of(BLOCK * (index % 8) + first, 16)
        return s.wb.at[pl.ds(row, count), spread(2 + index // 8, PART)]

    def copy(j, kind, source, target, device):
        return pltpu.make_async_remote_copy(
            src_ref=source,
            dst_ref=target,
            send_sem=s.relay_send.at[phase, j, kind],
            recv_sem=s.relay_recv.at[phase, j, kind],
            device_id=device,
            device_id_type=MESH,
        )

    def down_place(j):
        if phase == 0:
            return s.wb.at[block_rows(at.d), spread(j, PART)]
        return s.wa.at[block_rows(j), pl.ds(3 * PART, PART)]

    def hop(j, role, first, kind, device):
        part = (0, 80) if first else (80, 64)
        return copy(j, kind, piece(j, role[0], *part), piece(j, role[1], *part), device)

    x, y = (at.x, at.pipe), (at.y, at.pipe)

    def send(j, kind):
        if kind == 1:
            return hop(j, (0, 1), True, 1, x)
        if kind == 2:
            return hop(j, (0, 2), False, 2, y)
        if kind == 3:
            return hop(j, (1, 3), True, 3, y)
        if kind == 4:
            return hop(j, (2, 3), False, 4, x)
        return copy(j, 5, piece(j, 3), down_place(j), (at.dp, 1))

    def arrival(j, kind):
        if kind == 0:
            return copy(j, 0, piece(j, 0), piece(j, 0), (at.dp, 1))
        if kind == 1:
            return hop(j, (1, 1), True, 1, x)
        if kind == 2:
            return hop(j, (2, 2), False, 2, y)
        if kind == 3:
            return hop(j, (3, 3), True, 3, y)
        return hop(j, (3, 3), False, 4, x)

    def step(k, carry):
        @pl.when(k < 4)
        def _():
            arrival(k, 0).wait_recv()
            send(k, 1).start()
            send(k, 2).start()

        @pl.when((k >= 1) & (k <= 4))
        def _():
            arrival(k - 1, 1).wait_recv()
            send(k - 1, 3).start()
            arrival(k - 1, 2).wait_recv()
            send(k - 1, 4).start()

        @pl.when(k >= 2)
        def _():
            arrival(k - 2, 3).wait_recv()
            arrival(k - 2, 4).wait_recv()
            send(k - 2, 5).start()

        return carry

    def run():
        lax.fori_loop(0, 6, step, 0)

    def done():
        def each(j, carry):
            for kind in range(1, 6):
                send(j, kind).wait_send()
            return carry

        lax.fori_loop(0, 4, each, 0)

    return SimpleNamespace(
        run=run,
        done=done,
        up=lambda j, source: copy(j, 0, source, piece(j, 0), (at.dp, 2)),
        down=lambda j: copy(j, 5, down_place(j), down_place(j), (at.dp, 2)),
    )


def gather_weights(s, at, chunks, between, ready, helper=None, helped=(), before=None):
    def held(k):
        return (s.wa if k < 4 else s.wb), pl.ds((k % 4) * PART, PART)

    def piece(k, block, first=0, count=BLOCK):
        ref, cols = held(k)
        return ref.at[pl.ds(pl.multiple_of(block * BLOCK + first, 16), count), cols]

    def copy(k, kind, ref, target, source=None):
        return pltpu.make_async_remote_copy(
            src_ref=ref if source is None else source,
            dst_ref=ref,
            send_sem=s.gather_send.at[k, kind],
            recv_sem=s.gather_recv.at[k, kind],
            device_id=(target, at.pipe),
            device_id_type=MESH,
        )

    def via_y(k):
        return (0, 80) if k % 2 == 0 else (0, 64)

    def via_x(k):
        return (80, 64) if k % 2 == 0 else (64, 80)

    sib_x, sib_y, sib_d = (
        at.sib + at.step_x,
        at.sib + at.step_y,
        at.sib + at.step_x + at.step_y,
    )

    def sends(k):
        shard = s.in_shard if k < 4 else s.out_shard
        source = shard.at[:, pl.ds((k % 4) * PART, PART)]
        return {
            0: lambda: copy(k, 0, piece(k, at.dp), at.x, source),
            1: lambda: copy(k, 1, piece(k, at.dp), at.y, source),
            2: lambda: copy(k, 2, piece(k, at.dp), at.sib, source),
            3: lambda: copy(k, 3, piece(k, at.x), at.sib),
            4: lambda: copy(k, 4, piece(k, at.x, *via_y(k)), at.y),
            5: lambda: copy(k, 5, piece(k, at.y), at.sib),
            6: lambda: copy(k, 6, piece(k, at.y, *via_x(k)), at.x),
            7: lambda: copy(k, 7, piece(k, at.d), at.sib),
        }

    def arrivals(k):
        return {
            0: lambda: copy(k, 0, piece(k, at.x), at.x),
            1: lambda: copy(k, 1, piece(k, at.y), at.y),
            2: lambda: copy(k, 2, piece(k, at.sib), at.sib),
            3: lambda: copy(k, 3, piece(k, sib_x), at.sib),
            4: lambda: copy(k, 4, piece(k, at.d, *via_y(k)), at.y),
            5: lambda: copy(k, 5, piece(k, sib_y), at.sib),
            6: lambda: copy(k, 6, piece(k, at.d, *via_x(k)), at.x),
            7: lambda: copy(k, 7, piece(k, sib_d), at.sib),
        }

    def start(k, *kinds):
        for kind in kinds:
            sends(k)[kind]().start()

    def arrive(k, *kinds):
        for kind in kinds:
            arrivals(k)[kind]().wait_recv()

    def up(k):
        return helper.up(k - 4, s.out_shard.at[:, pl.ds((k - 4) * PART, PART)])

    for k in range(2):
        start(k, 0, 1, 2)
    for k in helped:
        up(k).start()
    if before is not None:
        before()
    for k in range(chunks + 2):
        if k < chunks:
            arrive(k, 0)
            start(k, 3)
            if k not in helped:
                start(k, 4)
            arrive(k, 1)
            start(k, 5)
            if k not in helped:
                start(k, 6)
            if k + 2 < chunks:
                start(k + 2, 0, 1, 2)
            between(k)
        if 1 <= k <= chunks:
            if k - 1 in helped:
                helper.down(k - 5).wait_recv()
            else:
                arrive(k - 1, 4, 6)
            start(k - 1, 7)
        if k >= 2:
            arrive(k - 2, 2, 3, 5, 7)
            ready(k - 2)
    for k in range(chunks):
        for kind in range(8):
            if k not in helped or kind not in (4, 6):
                sends(k)[kind]().wait_send()
    for k in helped:
        up(k).wait_send()


def scatter_grads(s, at, is_feed, swap, outputs, inputs):
    total = jnp.where(is_feed, 32, 16)
    helper = relay(s, at, 1)

    def up(j):
        return helper.up(j, s.wa.at[block_rows(4 + j), pl.ds(3 * PART, PART)])

    chip = at.dp // 2
    chip_x, chip_y = chip + 1 - 2 * at.x_bit, chip + 2 - 4 * at.y_bit
    chip_d = chip_x + 2 - 4 * at.y_bit

    def unit(u):
        stage = u // 4
        second = is_feed & ((stage == 0) | (stage == 4) | (stage >= 6))
        matrix = jnp.where(second, 1, 0)
        late = jnp.where(stage == 4, 1, jnp.where(stage == 5, 3, stage - 4))
        early = jnp.where(stage == 0, 0, stage - 1)
        group = jnp.where(is_feed, jnp.where(stage >= 4, late, early), stage)
        v, turn, n = u % 4, u % 2, (u % 4) // 2
        near = chip_x + turn * (chip_y - chip_x)
        block = jnp.where(group == 0, chip_d, jnp.where(group == 3, chip, near))
        part = jnp.where(
            group == 3, v, jnp.where(group == 2, 2 * (1 - turn) + n, 2 * turn + n)
        )
        return matrix, group, turn, n, block, part

    def sib_place(u):
        return s.wb.at[block_rows(u % 8), spread(u // 8, PART)]

    def near_place(matrix, turn, slot):
        index = turn * 12 + matrix * 6 + slot
        return s.wa.at[block_rows(index % 8), spread(index // 8, PART)]

    def sib_copy(u):
        return pltpu.make_async_remote_copy(
            src_ref=s.stage.at[u % 4, block_rows(1 - at.core), :],
            dst_ref=sib_place(u),
            send_sem=s.sib_send.at[u],
            recv_sem=s.sib_recv.at[u],
            device_id=(at.sib, at.pipe),
            device_id_type=MESH,
        )

    def near_copy(matrix, turn, slot):
        return pltpu.make_async_remote_copy(
            src_ref=s.near_stage.at[turn, slot],
            dst_ref=near_place(matrix, turn, slot),
            send_sem=s.near_send.at[turn, matrix * 6 + slot],
            recv_sem=s.near_recv.at[turn, matrix * 6 + slot],
            device_id=(at.x + turn * (at.y - at.x), at.pipe),
            device_id_type=MESH,
        )

    def compute(u):
        matrix, group, turn, n, block, part = unit(u)
        first = is_feed & (matrix == 0)
        lhs = jnp.where(first | (jnp.logical_not(is_feed) & (part == 3)), 1, 0)
        rhs = jnp.where(first, 0, 1)

        @pl.when(u >= 4)
        def _():
            sib_copy(u - 4).wait_send()

        rows = pl.ds(pl.multiple_of(block * 288, 16), 288)
        s.stage[u % 4] = product(s.left[lhs, rows, :], s.wide[rhs, :, spread(part, PART)]).astype(
            low
        )
        sib_copy(u).start()

    def settle(u):
        matrix, group, turn, n, block, part = unit(u)
        sib_copy(u).wait_recv()
        own = s.stage[u % 4, block_rows(at.core), :].astype(jnp.float32)
        place = (block_rows(u % 8), spread(u // 8, PART))
        value = own + s.wb[place].astype(jnp.float32)
        slot = group * 2 + n
        first = is_feed & (matrix == 0)
        helped = (at.pipe == 1) & (matrix == 1)

        def taken(from_turn, from_slot):
            near_copy(matrix, from_turn, from_slot).wait_recv()
            index = from_turn * 12 + matrix * 6 + from_slot
            return s.wa[block_rows(index % 8), spread(index // 8, PART)].astype(jnp.float32)

        @pl.when(group < 3)
        def _():
            goes_up = (group == 0) & helped
            again = is_feed & ((matrix == 1) == (slot >= 2)) & ((slot >= 2) | (at.pipe != 1))

            @pl.when(again)
            def _():
                near_copy(1 - matrix, turn, slot).wait_send()

            @pl.when(goes_up)
            def _():
                s.wa[block_rows(4 + part), 3 * PART :] = value.astype(low)

            @pl.when(goes_up)
            def _():
                up(part).start()

            @pl.when(jnp.logical_not(goes_up) & ((group < 2) | helped))
            def _():
                s.near_stage[turn, slot] = value.astype(low)

            @pl.when((group == 2) & jnp.logical_not(helped))
            def _():
                s.near_stage[turn, slot] = (value + taken(1 - turn, n)).astype(low)

            @pl.when(jnp.logical_not(goes_up))
            def _():
                near_copy(matrix, turn, slot).start()

        @pl.when(group == 3)
        def _():
            @pl.when((matrix > 0) | (part >= 2))
            def _():
                grad_copy(s.in_grad, part).wait()

            whole = value + taken(0, 2 + part) + taken(1, (part + 2) % 4 + 2)
            s.wacc[0:BLOCK, spread(1 + part % 2, PART)] = whole

            @pl.when(helped)
            def _():
                helper.down(part).wait_recv()
                rest = s.wa[block_rows(part), 3 * PART :].astype(jnp.float32)
                s.wacc[0:BLOCK, spread(1 + part % 2, PART)] += rest

            @pl.when(first)
            def _():
                grad_copy(s.out_grad, part).start()

            @pl.when(jnp.logical_not(first))
            def _():
                grad_copy(s.in_grad, part).start()

    def grad_copy(held, part):
        return pltpu.make_async_copy(
            s.wacc.at[pl.ds(0, BLOCK), spread(1 + part % 2, PART)],
            held.at[0, :, spread(part, PART)],
            s.out_sem.at[part % 2],
        )

    def step(u, carry):
        @pl.when(u < total)
        def _():
            compute(u)

        @pl.when(u >= 2)
        def _():
            settle(u - 2)

        return carry

    def leg(n, carry):
        third, fourth = total - 5, jnp.where(is_feed, 31, 14)
        marks = (0, 3, 9, third, fourth, total + 2)

        def mark(k):
            value = marks[0]
            for place in range(1, 6):
                value = jnp.where(k == place, marks[place], value)
            return value

        lax.fori_loop(mark(n), mark(n + 1), step, 0)

        @pl.when(n == 0)
        def _():
            condition_back(s, at, swap, is_feed)

        @pl.when(n == 1)
        def _():
            condition_token(s, at, swap, is_feed)

        @pl.when((n == 2) & jnp.logical_not(is_feed))
        def _():
            for copy in time_outs(s):
                copy.wait()

        @pl.when((n == 2) & (at.pipe < 2))
        def _():
            condition_sum(s, at, swap, is_feed)

        @pl.when((n == 2) & (at.pipe == 3))
        def _():
            outputs()

        @pl.when(n == 3)
        def _():
            @pl.when(at.pipe == 2)
            def _():
                helper.run()

            @pl.when(at.pipe < 2)
            def _():
                condition_table(s, at, swap, is_feed)

            @pl.when(at.pipe == 0)
            def _():
                inputs()

        return carry

    for copy in shard_copies(s, is_feed):
        copy.start()
    lax.fori_loop(0, 5, leg, 0)
    matrices = jnp.where(is_feed, 2, 1)

    def rest(k, carry):
        sib_copy(total - 4 + k).wait_send()
        return carry

    lax.fori_loop(0, 4, rest, 0)
    for turn in range(2):
        for slot in range(6):
            near_copy(0 if slot < 2 else matrices - 1, turn, slot).wait_send()

    @pl.when(at.pipe == 1)
    def _():
        for j in range(4):
            up(j).wait_send()

    @pl.when(at.pipe == 2)
    def _():
        helper.done()

    for part in (2, 3):
        grad_copy(s.in_grad, part).wait()

    @pl.when(at.pipe >= 2)
    def _():
        condition_sum(s, at, swap, is_feed)
        condition_table(s, at, swap, is_feed)


def exchange(s, at, number, piece, landing):
    def copy(target, source):
        return pltpu.make_async_remote_copy(
            src_ref=piece(target),
            dst_ref=landing(source),
            send_sem=s.swap_send.at[number, target],
            recv_sem=s.swap_recv.at[number, source],
            device_id=(target, at.pipe),
            device_id_type=MESH,
        )

    others = [(at.dp + k) % 8 for k in range(1, 8)]

    def start():
        for other in others:
            copy(other, at.dp).start()

    def arrive():
        for other in others:
            copy(other, other).wait_recv()

    def done():
        for other in others:
            copy(other, at.dp).wait_send()

    return SimpleNamespace(start=start, arrive=arrive, done=done)


def exchanges(s, at):
    def pair(j):
        return pl.ds(2 * j, 2)

    return SimpleNamespace(
        rows=exchange(s, at, 0, lambda j: s.cond_in, lambda j: s.rows.at[pair(j)]),
        mods=exchange(s, at, 1, lambda j: s.mod_parts.at[pair(j)], lambda j: s.mod_all.at[j]),
        tokens=exchange(s, at, 2, lambda j: s.token, lambda j: s.token_all.at[pair(j)]),
        times=exchange(s, at, 3, lambda j: s.time_parts.at[pair(j)], lambda j: s.time_all.at[j]),
        grads=exchange(s, at, 4, lambda j: s.grad_rows, lambda j: s.grad_all.at[pair(j)]),
        backs=exchange(s, at, 5, lambda j: s.back, lambda j: s.back_all.at[j]),
        ends=exchange(s, at, 6, lambda j: s.end, lambda j: s.end_all.at[j]),
    )


def shard_copies(s, is_feed):
    copies = []
    for part in range(3):
        cols = pl.ds(part * PART, PART)
        rows = pl.ds(part * BLOCK, BLOCK)
        copies.append((s.mod_shard.at[:, cols], s.norm.at[rows, :]))
        copies.append((s.out_shard.at[:, cols], s.branch.at[rows, :]))
    copies.append((s.out_shard.at[:, pl.ds(3 * PART, PART)], s.gb.at[pl.ds(0, BLOCK), :]))
    return [
        pltpu.make_async_copy(source, target, s.shard_sem.at[k])
        for k, (source, target) in enumerate(copies)
    ]


def shard_part(ref, part):
    return ref[pl.ds(part * BLOCK, BLOCK), :]


def stack_rows(source, target, width):
    for k in range(16):
        target[k : k + 1, 0:width] = source[k, :, 0:width]


def chosen(at):
    places = lax.broadcasted_iota(jnp.int32, (PART, BLOCK), 0)
    lanes = lax.broadcasted_iota(jnp.int32, (PART, BLOCK), 1)
    return jnp.where(places == lanes + at.dp * BLOCK, 1.0, 0.0).astype(low)


def condition_front(s, at, swap, is_feed):
    for copy in shard_copies(s, is_feed):
        copy.start()
    s.rows[pl.ds(2 * at.dp, 2)] = s.cond_in[...]
    s.grad_rows[...] = jnp.zeros(s.grad_rows.shape, jnp.float32)
    swap.rows.arrive()
    stack_rows(s.rows, s.flat, PART)
    condition = s.flat[:, 0:PART]
    conditioner = (condition * (1.0 / (1.0 + jnp.exp(-condition)))).astype(low)
    pick = chosen(at)
    own = product(conditioner, pick).astype(low)
    s.own_cond[...] = own
    for copy in shard_copies(s, is_feed):
        copy.wait()
    for part in range(3):
        s.flat[:, part * PART : (part + 1) * PART] = product(own, shard_part(s.norm, part))
    s.flat[:, 3 * PART : 4 * PART] = product(own, s.gb[0:BLOCK, :])
    for k in range(16):
        s.mod_parts[k] = s.flat[k : k + 1, 0 : 4 * PART]
    swap.mods.start()
    s.mod_all[at.dp] = s.mod_parts[pl.ds(2 * at.dp, 2)]


def condition_mods(s, at, swap, is_feed):
    swap.mods.arrive()
    for i in range(2):
        total = jnp.sum(s.mod_all[:, i], axis=0)
        s.mod[i] = total[:, 0 : 3 * PART]
        s.token[i] = total[:, 3 * PART :]

    @pl.when(jnp.logical_not(is_feed))
    def _():
        swap.tokens.start()
        s.token_all[pl.ds(2 * at.dp, 2)] = s.token[...]


def condition_tokens(s, at, swap, is_feed):
    @pl.when(jnp.logical_not(is_feed))
    def _():
        swap.tokens.arrive()
        stack_rows(s.token_all, s.flat, PART)
        own_token = product(s.flat[:, 0:PART].astype(low), chosen(at)).astype(low)
        s.own_token[...] = own_token
        for part in range(3):
            s.flat[:, part * PART : (part + 1) * PART] = product(
                own_token, shard_part(s.branch, part)
            )
        for k in range(16):
            s.time_parts[k] = s.flat[k : k + 1, 0 : 3 * PART]
        swap.times.start()
        s.time_all[at.dp] = s.time_parts[pl.ds(2 * at.dp, 2)]


def condition_times(s, at, swap, is_feed):
    @pl.when(jnp.logical_not(is_feed))
    def _():
        swap.times.arrive()
        for i in range(2):
            s.time[i] = jnp.sum(s.time_all[:, i], axis=0)


def end_copy(s, at, plane):
    return pltpu.make_async_remote_copy(
        src_ref=s.end_parts.at[at.pipe],
        dst_ref=s.end_parts.at[at.pipe],
        send_sem=s.end_send.at[plane],
        recv_sem=s.end_recv.at[at.pipe],
        device_id=(at.dp, plane),
        device_id_type=MESH,
    )


def end_arrival(s, at, plane):
    return pltpu.make_async_remote_copy(
        src_ref=s.end_parts.at[plane],
        dst_ref=s.end_parts.at[plane],
        send_sem=s.end_send.at[plane],
        recv_sem=s.end_recv.at[plane],
        device_id=(at.dp, plane),
        device_id_type=MESH,
    )


def mod_out(s):
    return pltpu.make_async_copy(
        s.wacc.at[pl.ds(0, BLOCK), :], s.mod_grad.at[0], s.shard_sem.at[0]
    )


def time_outs(s):
    held = s.out_grad.at[0]
    return (
        pltpu.make_async_copy(
            s.wacc.at[pl.ds(0, BLOCK), :], held.at[:, pl.ds(0, 3 * PART)], s.shard_sem.at[0]
        ),
        pltpu.make_async_copy(
            s.acc.at[pl.ds(0, BLOCK), :], held.at[:, pl.ds(3 * PART, PART)], s.shard_sem.at[1]
        ),
    )


def condition_back(s, at, swap, is_feed):
    s.grad_all[pl.ds(2 * at.dp, 2)] = s.grad_rows[...]
    swap.grads.arrive()
    stack_rows(s.grad_all, s.flat, 6 * PART)
    for copy in shard_copies(s, is_feed):
        copy.wait()

    @pl.when(jnp.logical_not(is_feed))
    def _():
        token = jnp.zeros((16, BLOCK), jnp.float32)
        for part in range(3):
            grads = s.flat[:, (3 + part) * PART : (4 + part) * PART].astype(low)
            token += product_nt(grads, shard_part(s.branch, part))
        s.back[...] = product_nt(token.astype(low), chosen(at)).astype(low)
        swap.backs.start()
        s.back_all[at.dp] = s.back[...]

    own = s.own_cond[...]
    s.end[...] = jnp.zeros(s.end.shape, jnp.float32)
    for part in range(3):
        cols = slice(part * PART, (part + 1) * PART)
        grads = s.flat[:, cols].astype(low)
        s.wacc[0:BLOCK, cols] = contract_rows(own, grads)
        s.end[...] += product_nt(grads, shard_part(s.norm, part))
    mod_out(s).start()


def condition_token(s, at, swap, is_feed):
    mod_out(s).wait()

    @pl.when(jnp.logical_not(is_feed))
    def _():
        for part in range(3):
            grads = s.flat[:, (3 + part) * PART : (4 + part) * PART].astype(low)
            s.wacc[0:BLOCK, part * PART : (part + 1) * PART] = contract_rows(
                s.own_token[...], grads
            )
        swap.backs.arrive()
        whole = jnp.zeros((16, PART), jnp.float32)
        for k in range(8):
            whole += s.back_all[k].astype(jnp.float32)
        whole = whole.astype(low)
        s.acc[0:BLOCK, :] = contract_rows(s.own_cond[...], whole)
        s.end[...] += product_nt(whole, s.gb[0:BLOCK, :])
        for copy in time_outs(s):
            copy.start()

    s.end_parts[at.pipe] = s.end[...]
    for k in range(1, 4):
        end_copy(s, at, (at.pipe + k) % 4).start()


def condition_sum(s, at, swap, is_feed):
    for k in range(1, 4):
        end_arrival(s, at, (at.pipe + k) % 4).wait_recv()
    s.end[...] = s.end_parts[0] + s.end_parts[1] + s.end_parts[2] + s.end_parts[3]
    swap.ends.start()
    s.end_all[at.dp] = s.end[...]


def condition_table(s, at, swap, is_feed):
    swap.ends.arrive()
    for k in range(8):
        s.flat[:, BLOCK * k : BLOCK * (k + 1)] = s.end_all[k]
    whole = s.flat[:, 0:PART]
    stack_rows(s.rows, s.flat, PART)
    condition = s.flat[:, 0:PART]
    gate = 1.0 / (1.0 + jnp.exp(-condition))
    grads = whole * (gate * (1.0 + condition * (1.0 - gate)))
    for k in range(3):
        term = grads.astype(low)
        s.terms[16 * k : 16 * (k + 1), :] = term
        grads = grads - term.astype(jnp.float32)
    lanes = lax.broadcasted_iota(jnp.int32, (1, 1024), 1).astype(jnp.float32)
    for k in range(16):
        label = s.rows[k, :, PART : PART + 1]
        s.flat[k : k + 1, 0:1024] = jnp.where(lanes == label, 1.0, 0.0)
    hot = s.flat[:, 0:1024].astype(low)
    for k in range(3):
        s.hot[16 * k : 16 * (k + 1), :] = hot


def condition_done(s, at, swap, is_feed):
    for each in (swap.rows, swap.mods, swap.grads, swap.ends):
        each.done()
    for k in range(1, 4):
        end_copy(s, at, (at.pipe + k) % 4).wait_send()

    @pl.when(jnp.logical_not(is_feed))
    def _():
        for each in (swap.tokens, swap.times, swap.backs):
            each.done()


def mega_body(*refs):
    s = SimpleNamespace(**dict(zip(REFS, refs)))
    at = places()
    is_feed = at.pipe % 2 == 1
    pipe = at.pipe
    barrier = pltpu.get_barrier_semaphore()
    swap = exchanges(s, at)
    targets = [((at.dp + k) % 8, pipe) for k in range(1, 8)]
    targets += [(at.dp, (pipe + k) % 4) for k in range(1, 4)]
    for target in targets:
        pl.semaphore_signal(barrier, inc=1, device_id=target, device_id_type=MESH)
    pl.semaphore_wait(barrier, len(targets))
    swap.rows.start()

    def remote(source, target, send, recv, plane):
        return pltpu.make_async_remote_copy(
            src_ref=source,
            dst_ref=target,
            send_sem=send,
            recv_sem=recv,
            device_id=(at.dp, plane),
            device_id_type=MESH,
        )

    def share(i, plane):
        return pl.ds(pl.multiple_of(i * ROWS + plane * 64, 64), 64)

    def token_copy(i, plane):
        return remote(
            s.tokens.at[i],
            s.xin.at[share(i, plane), :],
            s.share_send.at[0, i],
            s.xin_recv.at[i, plane],
            0,
        )

    def cotangent_copy(i, plane):
        return remote(
            s.cotangent.at[i],
            s.gin.at[share(i, plane), :],
            s.share_send.at[1, i],
            s.gin_recv.at[i, plane],
            3,
        )

    def next_copy(i):
        whole = image_rows(i)
        return remote(
            s.xout.at[whole, :],
            s.xin.at[whole, :],
            s.hop_send.at[0, i],
            s.xin_recv.at[i, 0],
            jnp.minimum(pipe + 1, 3),
        )

    def back_copy(i):
        whole = image_rows(i)
        return remote(
            s.gout.at[whole, :],
            s.gin.at[whole, :],
            s.hop_send.at[1, i],
            s.gin_recv.at[i, 3],
            jnp.maximum(pipe - 1, 0),
        )

    def output_copy(i, plane):
        return remote(
            s.xout.at[share(i, plane), :],
            s.out_tokens.at[i],
            s.final_send.at[0, i, plane],
            s.final_recv.at[0, i],
            plane,
        )

    def input_copy(i, plane):
        return remote(
            s.gout.at[share(i, plane), :],
            s.input_share.at[i],
            s.final_send.at[1, i, plane],
            s.final_recv.at[1, i],
            plane,
        )

    def local(source, target, index):
        return pltpu.make_async_copy(source, target, s.local_sem.at[index])

    own_in = local(s.in_shard, s.wa.at[block_rows(at.dp), :], 0)
    own_out = local(s.out_shard, s.wb.at[block_rows(at.dp), :], 1)
    own_in.start()

    @pl.when(is_feed)
    def _():
        own_out.start()

    for i in range(2):
        own_tokens = local(s.tokens.at[i], s.xin.at[pl.ds(i * ROWS, 64), :], 2 + i)
        own_cotangent = local(s.cotangent.at[i], s.gin.at[pl.ds(i * ROWS + 192, 64), :], 4 + i)

        @pl.when(pipe == 0)
        def _():
            own_tokens.start()

        @pl.when(pipe == 3)
        def _():
            own_cotangent.start()

        @pl.when(pipe != 0)
        def _():
            token_copy(i, pipe).start()

    rounds = (condition_front, condition_mods, condition_tokens, condition_times)

    def between(k):
        if k < 4:
            rounds[k](s, at, swap, is_feed)
        if k == 1:
            for i in range(2):

                @pl.when(pipe != 3)
                def _():
                    cotangent_copy(i, pipe).start()

    def ready(k):
        if k == 0:

            def begin(i, carry):
                local(s.tokens.at[i], s.xin.at[share(i, 0), :], 2 + i).wait()
                for plane in range(1, 4):
                    token_copy(i, plane).wait_recv()
                front(i, s)
                return carry

            lax.fori_loop(0, 2, begin, 0)

        def one(n, carry):
            project(n % 2, s, n // 2)
            return carry

        if k == 1:
            lax.fori_loop(0, 4, one, 0)
        if k == 2:
            project(0, s, 2)
            attend_heads(0, s)

    own_in.wait()

    @pl.when(pipe == 0)
    def _():
        gather_weights(s, at, 4, between, ready)

    @pl.when(pipe == 2)
    def _():
        helper = relay(s, at, 0)

        gather_weights(s, at, 4, between, lambda k: None, before=helper.run)
        helper.done()

    def ahead(i, carry):
        next_copy(i).wait_recv()
        front(i, s)
        feed_up(i, s)
        return carry

    def early(k):
        if k == 6:
            lax.fori_loop(0, 2, ahead, 0)

    @pl.when(is_feed)
    def _():
        own_out.wait()

    @pl.when(pipe == 1)
    def _():
        gather_weights(s, at, 8, between, early, relay(s, at, 0), (4, 5, 6, 7))

    @pl.when(pipe == 3)
    def _():
        gather_weights(s, at, 8, between, lambda k: None)

    for i in range(2):

        @pl.when(pipe != 0)
        def _():
            token_copy(i, pipe).wait_send()

    def inputs(i):
        for plane in range(1, 4):
            input_copy(i, plane).start()
        local(s.gout.at[share(i, 0), :], s.input_share.at[i], 4 + i).start()

    def step(n, carry):
        at_end = pipe == 3
        goes_forward = jnp.where(at_end, n % 2 == 0, n < 2)
        i = jnp.where(at_end, n // 2, n % 2)

        @pl.when(goes_forward)
        def _():
            @pl.when(pipe >= 2)
            def _():
                next_copy(i).wait_recv()

            @pl.when(is_feed)
            def _():
                @pl.when(pipe == 3)
                def _():
                    front(i, s)
                    feed_up(i, s)

                feed_down(i, s)
                finish(i, s)

            @pl.when(jnp.logical_not(is_feed))
            def _():
                @pl.when(pipe != 0)
                def _():
                    front(i, s)

                    def one(part, carry):
                        project(i, s, part)
                        return carry

                    lax.fori_loop(0, 3, one, 0)

                @pl.when((pipe == 0) & (i == 1))
                def _():
                    project(1, s, 2)

                @pl.when((pipe != 0) | (i == 1))
                def _():
                    attend_heads(i, s)

                attend_out(i, s)
                finish(i, s)

            @pl.when((pipe < 2) & (i == 0) & (at.core == 0))
            def _():
                next_copy(0).start()

            @pl.when((pipe < 2) & (i == 1))
            def _():
                @pl.when(at.core == 1)
                def _():
                    pl.semaphore_wait(s.turn, 1)
                    next_copy(0).start()

                next_copy(0).wait_send()
                pl.semaphore_signal(
                    s.turn, inc=1, device_id=(at.sib, pipe), device_id_type=MESH
                )
                pl.semaphore_wait(s.turn, 1)
                next_copy(1).start()
                next_copy(1).wait_send()

                @pl.when(at.core == 0)
                def _():
                    pl.semaphore_signal(
                        s.turn, inc=1, device_id=(at.sib, pipe), device_id_type=MESH
                    )

            @pl.when(pipe == 2)
            def _():
                next_copy(i).start()


        @pl.when(jnp.logical_not(goes_forward))
        def _():
            @pl.when(pipe == 3)
            def _():
                local(s.cotangent.at[i], s.gin.at[share(i, 3), :], 4 + i).wait()
                for plane in range(3):
                    cotangent_copy(i, plane).wait_recv()

            @pl.when(pipe != 3)
            def _():
                back_copy(i).wait_recv()

            @pl.when(is_feed)
            def _():
                kernel_feed_backward(i, s)

            @pl.when(jnp.logical_not(is_feed))
            def _():
                kernel_attention_backward(i, s)

            @pl.when(pipe != 0)
            def _():
                back_copy(i).start()

            @pl.when((pipe == 0) & (i == 0))
            def _():
                inputs(0)

        return carry

    lax.fori_loop(0, 4, step, 0)
    swap.grads.start()

    for target, sem in ((at.sib, 0), (at.x, 1), (at.y, 2)):
        pl.semaphore_signal(
            s.free.at[sem], inc=1, device_id=(target, pipe), device_id_type=MESH
        )
    for sem in range(3):
        pl.semaphore_wait(s.free.at[sem], 1)

    def last_inputs(*unused):
        @pl.when(pipe == 0)
        def _():
            inputs(1)

    def outputs(*unused):
        @pl.when(pipe == 3)
        def _():
            for i in range(2):
                for plane in range(3):
                    output_copy(i, plane).start()
                local(s.xout.at[share(i, 3), :], s.out_tokens.at[i], 2 + i).start()

    scatter_grads(s, at, is_feed, swap, outputs, last_inputs)
    condition_done(s, at, swap, is_feed)

    for i in range(2):

        @pl.when(pipe != 3)
        def _():
            cotangent_copy(i, pipe).wait_send()
            output_copy(i, pipe).wait_recv()

        @pl.when(pipe == 2)
        def _():
            next_copy(i).wait_send()

        @pl.when(pipe == 3)
        def _():
            for plane in range(3):
                output_copy(i, plane).wait_send()
            local(s.xout.at[share(i, 3), :], s.out_tokens.at[i], 2 + i).wait()

        @pl.when(pipe != 0)
        def _():
            back_copy(i).wait_send()
            input_copy(i, pipe).wait_recv()

        @pl.when(pipe == 0)
        def _():
            for plane in range(1, 4):
                input_copy(i, plane).wait_send()
            local(s.gout.at[share(i, 0), :], s.input_share.at[i], 4 + i).wait()

    s.input_grad[...] = s.input_share[...].astype(jnp.float32)


SCRATCH = dict(
    xin=pltpu.VMEM((512, 1152), low),
    gin=pltpu.VMEM((512, 1152), low),
    xout=pltpu.VMEM((512, 1152), low),
    gout=pltpu.VMEM((512, 1152), low),
    wa=pltpu.VMEM((1152, 4608), low),
    wb=pltpu.VMEM((1152, 4608), low),
    norm=pltpu.VMEM((512, 1152), low),
    left=pltpu.VMEM((2, 1152, 512), low),
    wide=pltpu.VMEM((2, 512, 4608), low),
    branch=pltpu.VMEM((512, 1152), low),
    acc=pltpu.VMEM((256, 1152), jnp.float32),
    gb=pltpu.VMEM((256, 1152), low),
    wacc=pltpu.VMEM((256, 3456), jnp.float32),
    stage=pltpu.VMEM((4, 288, 1152), low),
    near_stage=pltpu.VMEM((2, 6, 144, 1152), low),
    gather_send=pltpu.SemaphoreType.DMA((8, 8)),
    gather_recv=pltpu.SemaphoreType.DMA((8, 8)),
    sib_send=pltpu.SemaphoreType.DMA((32,)),
    sib_recv=pltpu.SemaphoreType.DMA((32,)),
    near_send=pltpu.SemaphoreType.DMA((2, 12)),
    near_recv=pltpu.SemaphoreType.DMA((2, 12)),
    out_sem=pltpu.SemaphoreType.DMA((2,)),
    share_send=pltpu.SemaphoreType.DMA((2, 2)),
    xin_recv=pltpu.SemaphoreType.DMA((2, 4)),
    gin_recv=pltpu.SemaphoreType.DMA((2, 4)),
    hop_send=pltpu.SemaphoreType.DMA((2, 2)),
    final_send=pltpu.SemaphoreType.DMA((2, 2, 4)),
    final_recv=pltpu.SemaphoreType.DMA((2, 2)),
    local_sem=pltpu.SemaphoreType.DMA((6,)),
    free=pltpu.SemaphoreType.REGULAR((3,)),
    turn=pltpu.SemaphoreType.REGULAR,
    shard_sem=pltpu.SemaphoreType.DMA((7,)),
    swap_send=pltpu.SemaphoreType.DMA((7, 8)),
    swap_recv=pltpu.SemaphoreType.DMA((7, 8)),
    relay_send=pltpu.SemaphoreType.DMA((2, 4, 6)),
    relay_recv=pltpu.SemaphoreType.DMA((2, 4, 6)),
    end_send=pltpu.SemaphoreType.DMA((4,)),
    end_recv=pltpu.SemaphoreType.DMA((4,)),
    mod=pltpu.VMEM((2, 1, 3456), jnp.float32),
    time=pltpu.VMEM((2, 1, 3456), jnp.float32),
    token=pltpu.VMEM((2, 1, 1152), jnp.float32),
    grad_rows=pltpu.VMEM((2, 1, 6912), jnp.float32),
    rows=pltpu.VMEM((16, 1, 1280), jnp.float32),
    flat=pltpu.VMEM((16, 6912), jnp.float32),
    own_cond=pltpu.VMEM((16, 144), low),
    own_token=pltpu.VMEM((16, 144), low),
    mod_parts=pltpu.VMEM((16, 1, 4608), jnp.float32),
    mod_all=pltpu.VMEM((8, 2, 1, 4608), jnp.float32),
    token_all=pltpu.VMEM((16, 1, 1152), jnp.float32),
    time_parts=pltpu.VMEM((16, 1, 3456), jnp.float32),
    time_all=pltpu.VMEM((8, 2, 1, 3456), jnp.float32),
    grad_all=pltpu.VMEM((16, 1, 6912), jnp.float32),
    back=pltpu.VMEM((16, 1152), low),
    back_all=pltpu.VMEM((8, 16, 1152), low),
    end=pltpu.VMEM((16, 144), jnp.float32),
    input_share=pltpu.VMEM((2, 64, 1152), low),
    end_parts=pltpu.VMEM((4, 16, 144), jnp.float32),
    end_all=pltpu.VMEM((8, 16, 144), jnp.float32),
)
REFS = (
    ["tokens", "cotangent", "in_shard", "out_shard", "mod_shard", "cond_in"]
    + ["out_tokens", "input_grad", "terms", "hot", "in_grad", "out_grad", "mod_grad"]
    + list(SCRATCH)
)


def mega(tokens, cotangent, in_shard, out_shard, mod_shard, cond_rows):
    anywhere = pl.BlockSpec(memory_space=pl.ANY)
    near = pl.BlockSpec(memory_space=pltpu.VMEM)

    def wide(array):
        return jax.ShapeDtypeStruct((1,) + array.shape, jnp.float32)

    return pl.pallas_call(
        mega_body,
        out_shape=(
            jax.ShapeDtypeStruct(tokens.shape, low),
            jax.ShapeDtypeStruct(tokens.shape, jnp.float32),
            jax.ShapeDtypeStruct((48, tokens.shape[2]), low),
            jax.ShapeDtypeStruct((48, 1024), low),
            wide(in_shard),
            wide(out_shard),
            wide(mod_shard),
        ),
        in_specs=[anywhere] * 5 + [near],
        out_specs=[anywhere] + [near] * 3 + [anywhere] * 3,
        scratch_shapes=list(SCRATCH.values()),
        compiler_params=pltpu.CompilerParams(
            collective_id=0, has_side_effects=True, vmem_limit_bytes=62 * 2**20
        ),
        cost_estimate=pl.CostEstimate(
            flops=25 * 10**9, bytes_accessed=10**7, transcendentals=10**7
        ),
        name="blocks",
    )(tokens, cotangent, in_shard, out_shard, mod_shard, cond_rows)


def last_body(terms, hot, *refs):
    sources, (table, *targets) = refs[:3], refs[3:7]
    value, *held, sems = refs[7:]
    classes = table.shape[0]
    pieces = [
        (source.at[0, pl.ds(48 * part, 48), :], stage.at[pl.ds(48 * part, 48), :],
         target.at[0, pl.ds(48 * part, 48), :], 3 * k + part)
        for k, (source, stage, target) in enumerate(zip(sources, held, targets))
        for part in range(3)
    ]
    takes = [pltpu.make_async_copy(s, v, sems.at[0, n]) for s, v, t, n in pieces]
    gives = [pltpu.make_async_copy(v, t, sems.at[1, n]) for s, v, t, n in pieces]
    for take in takes:
        take.start()
    for k in range(4):
        count = min(256, classes - 256 * k)
        value[k] = contract_rows(hot[:, 256 * k : 256 * (k + 1)], terms[...])
        part = pltpu.make_async_copy(
            value.at[k, pl.ds(0, count), :],
            table.at[pl.ds(256 * k, count), :],
            sems.at[1, 9 + k],
        )
        part.start()
        gives.append(part)
    for take, give in zip(takes, gives):
        take.wait()
        give.start()
    for give in gives:
        give.wait()


def last_copies(terms, hot, grads, classes):
    anywhere = pl.BlockSpec(memory_space=pl.ANY)
    near = pl.BlockSpec(memory_space=pltpu.VMEM)
    width = terms.shape[1]
    return pl.pallas_call(
        last_body,
        out_shape=[jax.ShapeDtypeStruct((classes, width), jnp.float32)]
        + [jax.ShapeDtypeStruct(grad.shape, jnp.float32) for grad in grads],
        in_specs=[near, near] + [anywhere] * 3,
        out_specs=[anywhere] * 4,
        scratch_shapes=[
            pltpu.VMEM((4, 256, width), jnp.float32),
            *[pltpu.VMEM(grad.shape[1:], jnp.float32) for grad in grads],
            pltpu.SemaphoreType.DMA((2, 13)),
        ],
        compiler_params=pltpu.CompilerParams(vmem_limit_bytes=62 * 2**20),
        name="table",
    )(terms, hot, *grads)


def fast_shards(
    tokens,
    cotangent,
    timesteps,
    labels,
    class_table,
    section_in_weights,
    section_out_weights,
    modulation_weights,
):
    model_width = tokens.shape[2]
    in_shard, out_shard, mod_shard = (
        section_in_weights[0],
        section_out_weights[0],
        modulation_weights[0],
    )
    images = tokens.shape[0]
    classes = class_table.shape[0]
    matches = labels[:, None] == lax.broadcasted_iota(jnp.int32, (images, classes), 1)
    condition = sinusoid(timesteps, model_width) + product(
        matches.astype(jnp.bfloat16), class_table
    )
    named = jnp.broadcast_to(labels.astype(jnp.float32)[:, None], (images, 128))
    cond_rows = jnp.concatenate([condition, named], axis=1)[:, None, :]
    out_tokens, input_grad, terms, hot, *grads = mega(
        tokens, cotangent, in_shard, out_shard, mod_shard, cond_rows
    )
    return (out_tokens, input_grad, *last_copies(terms, hot, grads, classes))


def solution(mesh):
    return jax.shard_map(
        fast_shards if mesh.shape["dp"] == 8 else shards,
        mesh=mesh,
        in_specs=(
            P("dp", "pipe", None),
            P("dp", "pipe", None),
            P("dp"),
            P("dp"),
            P(),
            P("pipe", "dp", None),
            P("pipe", "dp", None),
            P("pipe", "dp", None),
        ),
        out_specs=(
            P("dp", "pipe", None),
            P("dp", "pipe", None),
            P(),
            P("pipe", "dp", None),
            P("pipe", "dp", None),
            P("pipe", "dp", None),
        ),
        check_vma=False,
    )
```

```python
from functools import partial
import math
from types import SimpleNamespace

import jax
import jax.numpy as jnp
from jax import lax
from jax.experimental import pallas as pl
from jax.experimental.pallas import tpu as pltpu
from jax.sharding import PartitionSpec as P

HEADS = 16
HEAD = 72


epsilon = 1e-06
highest = lax.Precision.HIGHEST


def shifted(block, axis, distance):
    devices = range(lax.axis_size(axis))
    route = [(i - distance, i) for i in devices if i - distance in devices]
    return lax.ppermute(block, axis, route)


def sinusoid(step_values, model_width):
    half_width = model_width // 2
    frequencies = jnp.exp(
        -math.log(10000.0) * jnp.arange(half_width, dtype=jnp.float32) / half_width
    )
    angles = step_values.astype(jnp.float32)[:, None] * frequencies[None, :]
    return jnp.concatenate([jnp.cos(angles), jnp.sin(angles)], axis=1)


def product(former, latter):
    return jnp.dot(former, latter, preferred_element_type=jnp.float32)


def contract_rows(former, latter):
    return lax.dot_general(
        former, latter, (((0,), (0,)), ((), ())), preferred_element_type=jnp.float32
    )


def contract_cols(former, latter):
    return lax.dot_general(
        former, latter, (((1,), (1,)), ((), ())), preferred_element_type=jnp.float32
    )


def normalize_rows(row_values):
    centered = row_values - jnp.mean(row_values, axis=-1, keepdims=True)
    inverse = lax.rsqrt(jnp.mean(centered * centered, axis=-1, keepdims=True) + epsilon)
    return (centered * inverse, inverse)


def modulation_front(section_input, mod_row):
    model_width = section_input.shape[1]
    shift_vec = mod_row[:model_width]
    scale_vec = mod_row[model_width : 2 * model_width]
    gate_vec = mod_row[2 * model_width :]
    centred, inverse = normalize_rows(section_input.astype(jnp.float32))
    normed = (centred * (1.0 + scale_vec) + shift_vec).astype(jnp.bfloat16)
    return (normed, centred, inverse, scale_vec, gate_vec)


def modulation_back(grad_normed, centred, inverse, scale_vec, grad_rows, grad_gate):
    grad_shift = jnp.sum(grad_normed, axis=0)
    grad_scale = jnp.sum(grad_normed * centred, axis=0)
    grad_centred = grad_normed * (1.0 + scale_vec)
    grad_input = inverse * (
        grad_centred
        - jnp.mean(grad_centred, axis=-1, keepdims=True)
        - centred * jnp.mean(grad_centred * centred, axis=-1, keepdims=True)
    )
    grad_mod = jnp.concatenate([grad_shift, grad_scale, grad_gate]).astype(jnp.bfloat16)
    return (grad_rows + grad_input, grad_mod)


def attention_parts(section_input, mod_row, time_row, weights):
    in_weight = weights[0]
    model_width = section_input.shape[1]
    tok_len = section_input.shape[0]
    normed, centred, inverse, scale_vec, gate_vec = modulation_front(section_input, mod_row)
    qkv = (product(normed, in_weight[:, : 3 * model_width]) + time_row).astype(jnp.bfloat16)
    split_qkv = qkv.reshape(tok_len, 3, HEADS, HEAD)
    queries = split_qkv[:, 0]
    keyed = split_qkv[:, 1]
    valued = split_qkv[:, 2]
    scores = jnp.einsum(
        "qhd,khd->hqk", queries, keyed, preferred_element_type=jnp.float32
    ) * HEAD ** (-0.5)
    probs_full = jax.nn.softmax(scores, axis=-1)
    probs_low = probs_full.astype(jnp.bfloat16)
    mixed = jnp.einsum("hqk,khd->qhd", probs_low, valued, preferred_element_type=jnp.float32)
    head_rows = mixed.reshape(tok_len, model_width).astype(jnp.bfloat16)
    branch = product(head_rows, in_weight[:, 3 * model_width :])
    section_output = section_input.astype(jnp.float32) + gate_vec * branch
    saved_parts = (
        normed,
        centred,
        inverse,
        scale_vec,
        gate_vec,
        queries,
        keyed,
        valued,
        probs_full,
        probs_low,
        head_rows,
        branch,
    )
    return (section_output, saved_parts)


def attention_forward(section_input, mod_row, time_row, weights):
    return attention_parts(section_input, mod_row, time_row, weights)[0]


def attention_backward(section_input, grad_in, mod_row, time_row, weights):
    in_weight = weights[0]
    model_width = section_input.shape[1]
    tok_len = section_input.shape[0]
    unused, saved_parts = attention_parts(section_input, mod_row, time_row, weights)
    (
        normed,
        centred,
        inverse,
        scale_vec,
        gate_vec,
        queries,
        keyed,
        valued,
        probs_full,
        probs_low,
        head_rows,
        branch,
    ) = saved_parts
    grad_rows = grad_in.astype(jnp.float32)
    grad_branch = (gate_vec * grad_rows).astype(jnp.bfloat16)
    grad_gate = jnp.sum(grad_rows * branch, axis=0)
    grad_heads = contract_cols(grad_branch, in_weight[:, 3 * model_width :]).astype(jnp.bfloat16)
    heads_split = grad_heads.reshape(tok_len, HEADS, HEAD)
    grad_probs = jnp.einsum("qhd,khd->hqk", heads_split, valued, preferred_element_type=jnp.float32)
    grad_value = jnp.einsum(
        "hqk,qhd->khd", probs_low, heads_split, preferred_element_type=jnp.float32
    )
    grad_scores = (
        probs_full * (grad_probs - jnp.sum(probs_full * grad_probs, axis=-1, keepdims=True))
    ).astype(jnp.bfloat16)
    grad_query = jnp.einsum(
        "hqk,khd->qhd", grad_scores, keyed, preferred_element_type=jnp.float32
    ) * HEAD ** (-0.5)
    grad_key = jnp.einsum(
        "hqk,qhd->khd", grad_scores, queries, preferred_element_type=jnp.float32
    ) * HEAD ** (-0.5)
    grad_qkv = (
        jnp.stack([grad_query, grad_key, grad_value], axis=1)
        .reshape(tok_len, 3 * model_width)
        .astype(jnp.bfloat16)
    )
    grad_normed = contract_cols(grad_qkv, in_weight[:, : 3 * model_width])
    grad_time = jnp.sum(grad_qkv, axis=0, dtype=jnp.float32).astype(jnp.bfloat16)
    grad_input, grad_mod = modulation_back(
        grad_normed, centred, inverse, scale_vec, grad_rows, grad_gate
    )
    narrow_zero = jnp.zeros((tok_len, model_width), jnp.bfloat16)
    return (
        grad_input,
        normed,
        jnp.concatenate([grad_qkv, narrow_zero], axis=1),
        grad_branch,
        jnp.concatenate([head_rows, narrow_zero, narrow_zero, narrow_zero], axis=1),
        grad_mod,
        grad_time,
    )


def feed_parts(section_input, mod_row, weights):
    in_weight, out_weight = weights
    normed, centred, inverse, scale_vec, gate_vec = modulation_front(section_input, mod_row)
    pre_act = product(normed, in_weight)
    hidden = jax.nn.gelu(pre_act, approximate=True).astype(jnp.bfloat16)
    branch = contract_cols(hidden, out_weight)
    section_output = section_input.astype(jnp.float32) + gate_vec * branch
    return (
        section_output,
        (normed, centred, inverse, scale_vec, gate_vec, pre_act, hidden, branch),
    )


def feed_forward(section_input, mod_row, time_row, weights):
    return feed_parts(section_input, mod_row, weights)[0]


def feed_backward(section_input, grad_in, mod_row, time_row, weights):
    in_weight, out_weight = weights
    unused, saved_parts = feed_parts(section_input, mod_row, weights)
    normed, centred, inverse, scale_vec, gate_vec, pre_act, hidden, branch = saved_parts
    grad_rows = grad_in.astype(jnp.float32)
    grad_branch = (gate_vec * grad_rows).astype(jnp.bfloat16)
    grad_gate = jnp.sum(grad_rows * branch, axis=0)
    grad_hidden = product(grad_branch, out_weight)
    gelu_pull = jax.vjp(partial(jax.nn.gelu, approximate=True), pre_act)[1]
    grad_pre = gelu_pull(grad_hidden)[0].astype(jnp.bfloat16)
    grad_normed = contract_cols(grad_pre, in_weight)
    grad_input, grad_mod = modulation_back(
        grad_normed, centred, inverse, scale_vec, grad_rows, grad_gate
    )
    return (
        grad_input,
        normed,
        grad_pre,
        grad_branch,
        hidden,
        grad_mod,
        jnp.zeros(grad_mod.shape, jnp.bfloat16),
    )


def spare_forward(section_input, mod_row, time_row, weights):
    return jnp.zeros(section_input.shape, jnp.float32)


def spare_backward(section_input, grad_in, mod_row, time_row, weights):
    tok_len, model_width = section_input.shape
    hidden_width = weights[0].shape[1]
    narrow_zero = jnp.zeros((tok_len, model_width), jnp.bfloat16)
    wide_zero = jnp.zeros((tok_len, hidden_width), jnp.bfloat16)
    row_zero = jnp.zeros((3 * model_width,), jnp.bfloat16)
    return (
        jnp.zeros(section_input.shape, jnp.float32),
        narrow_zero,
        wide_zero,
        narrow_zero,
        wide_zero,
        row_zero,
        row_zero,
    )


def attention_weight_grads(left_one, right_one, left_two, right_two):
    width = left_two.shape[1]
    low = jnp.bfloat16
    qkv_term = contract_rows(left_one, right_one[:, : 3 * width]).astype(low)
    out_term = contract_rows(right_two[:, :width], left_two).astype(low)
    zero_term = jnp.zeros((width, right_two.shape[1]), low)
    return (jnp.concatenate([qkv_term, out_term], axis=1), zero_term)


def feed_weight_grads(left_one, right_one, left_two, right_two):
    low = jnp.bfloat16
    return (
        contract_rows(left_one, right_one).astype(low),
        contract_rows(left_two, right_two).astype(low),
    )


def replace_slot(buffer, slot_index, new_rows, active):
    old_rows = lax.dynamic_index_in_dim(buffer, slot_index, 0, keepdims=False)
    return lax.dynamic_update_index_in_dim(
        buffer, jnp.where(active, new_rows, old_rows), slot_index, 0
    )


def shards(
    tokens,
    cotangent,
    timesteps,
    labels,
    class_table,
    section_in_weights,
    section_out_weights,
    modulation_weights,
):
    micro_count = tokens.shape[0]
    model_width = tokens.shape[2]
    hidden_width = section_in_weights.shape[2]
    section_count = lax.axis_size("pipe")
    section_index = lax.axis_index("pipe")
    last_section = section_count - 1
    section_kind = 1 + section_index % 2
    in_shard, out_shard, mod_shard = (
        section_in_weights[0],
        section_out_weights[0],
        modulation_weights[0],
    )
    whole_tokens, whole_cotangent = (
        lax.all_gather(tokens, "pipe", axis=1, tiled=True),
        lax.all_gather(cotangent, "pipe", axis=1, tiled=True),
    )
    tok_len = whole_tokens.shape[1]
    weights = (
        lax.all_gather(in_shard, "dp", axis=0, tiled=True),
        lax.all_gather(out_shard, "dp", axis=0, tiled=True),
    )
    condition, own_conditioner, own_time, matches, mod_rows, time_rows = conditioning(
        timesteps, labels, class_table, out_shard, mod_shard
    )

    def forward_tick(carry, tick_index):
        incoming, kept_inputs, finals = carry
        micro_index = tick_index - section_index
        active = (micro_index >= 0) & (micro_index < micro_count)
        slot_index = jnp.clip(micro_index, 0, micro_count - 1)
        first_rows = lax.dynamic_index_in_dim(whole_tokens, slot_index, 0, keepdims=False)
        section_input = jnp.where(section_index == 0, first_rows, incoming)
        section_output = lax.switch(
            jnp.where(active, section_kind, 0),
            (spare_forward, attention_forward, feed_forward),
            section_input,
            lax.dynamic_index_in_dim(mod_rows, slot_index, 0, keepdims=False),
            lax.dynamic_index_in_dim(time_rows, slot_index, 0, keepdims=False),
            weights,
        )
        output_low = section_output.astype(jnp.bfloat16)
        kept_inputs = replace_slot(kept_inputs, slot_index, section_input, active)
        finals = replace_slot(
            finals, slot_index, output_low, active & (section_index == last_section)
        )
        incoming = shifted(output_low, "pipe", 1)
        return ((incoming, kept_inputs, finals), None)

    empty_rows = jnp.zeros((tok_len, model_width), jnp.bfloat16)
    empty_store = jnp.zeros((micro_count, tok_len, model_width), jnp.bfloat16)
    forward_out, ignored = lax.scan(
        forward_tick,
        (empty_rows, empty_store, empty_store),
        jnp.arange(micro_count + section_count - 1),
    )
    kept_inputs = forward_out[1]
    finals = forward_out[2]
    wide_store = jnp.zeros((micro_count, tok_len, hidden_width), jnp.bfloat16)
    row_store = jnp.zeros((micro_count, 3 * model_width), jnp.bfloat16)
    start_factors = (empty_store, wide_store, empty_store, wide_store, row_store, row_store)

    def backward_tick(carry, tick_index):
        incoming, factors, input_grads = carry
        micro_index = tick_index - (last_section - section_index)
        active = (micro_index >= 0) & (micro_index < micro_count)
        slot_index = jnp.clip(micro_index, 0, micro_count - 1)
        top_grad = lax.dynamic_index_in_dim(whole_cotangent, slot_index, 0, keepdims=False)
        grad_in = jnp.where(section_index == last_section, top_grad, incoming)
        section_input = lax.dynamic_index_in_dim(kept_inputs, slot_index, 0, keepdims=False)
        results = lax.switch(
            jnp.where(active, section_kind, 0),
            (spare_backward, attention_backward, feed_backward),
            section_input,
            grad_in,
            lax.dynamic_index_in_dim(mod_rows, slot_index, 0, keepdims=False),
            lax.dynamic_index_in_dim(time_rows, slot_index, 0, keepdims=False),
            weights,
        )
        grad_low = results[0].astype(jnp.bfloat16)
        factors = tuple(
            (
                replace_slot(buffer, slot_index, fresh, active)
                for buffer, fresh in zip(factors, results[1:])
            )
        )
        input_grads = replace_slot(
            input_grads, slot_index, grad_low, active & (section_index == 0)
        )
        incoming = shifted(grad_low, "pipe", -1)
        return ((incoming, factors, input_grads), None)

    backward_out, ignored = lax.scan(
        backward_tick,
        (empty_rows, start_factors, empty_store),
        jnp.arange(micro_count + section_count - 1),
    )
    factors = backward_out[1]
    input_grads = backward_out[2]
    flat_rows = micro_count * tok_len
    left_one, right_one, left_two, right_two = (
        stored.reshape(flat_rows, stored.shape[2]) for stored in factors[:4]
    )
    in_term, out_term = lax.cond(
        section_index % 2 == 0,
        attention_weight_grads,
        feed_weight_grads,
        left_one,
        right_one,
        left_two,
        right_two,
    )
    in_grad = lax.psum_scatter(in_term, "dp", scatter_dimension=0, tiled=True)
    out_grad = lax.psum_scatter(out_term, "dp", scatter_dimension=0, tiled=True)
    own_out, own_in = (finals, input_grads)
    keep_out = jnp.where(section_index == last_section, own_out, 0)
    keep_in = jnp.where(section_index == 0, own_in, 0)
    output_share = lax.psum_scatter(keep_out, "pipe", scatter_dimension=1, tiled=True)
    input_share = lax.psum_scatter(keep_in, "pipe", scatter_dimension=1, tiled=True)
    small_outs = conditioning_grads(
        factors[4],
        factors[5],
        condition,
        own_conditioner,
        own_time,
        matches,
        out_shard,
        mod_shard,
        out_grad,
    )
    return (
        output_share,
        input_share.astype(jnp.float32),
        small_outs[0],
        in_grad.astype(jnp.float32)[None],
        small_outs[1][None],
        small_outs[2][None],
    )


def conditioning_grads(
    mod_grads,
    time_grads,
    condition,
    own_conditioner,
    own_time,
    matches,
    out_shard,
    mod_shard,
    out_grad,
):
    model_width = condition.shape[1]
    is_attention = lax.axis_index("pipe") % 2 == 0
    all_mod = lax.all_gather(mod_grads, "dp", axis=0, tiled=True)
    all_time = lax.all_gather(time_grads, "dp", axis=0, tiled=True)
    grad_mod_shard = contract_rows(own_conditioner, all_mod)
    cond_grads = contract_cols(all_mod, mod_shard)
    own_token = contract_cols(all_time, out_shard[:, : 3 * model_width]).astype(jnp.bfloat16)
    all_token = lax.all_gather(own_token, "dp", axis=1, tiled=True)
    token_grads = contract_cols(all_token, out_shard[:, 3 * model_width :])
    cond_grads = cond_grads + jnp.where(is_attention, token_grads, 0.0)
    time_out = jnp.concatenate(
        [contract_rows(own_time, all_time), contract_rows(own_conditioner, all_token)], axis=1
    )
    grad_out_shard = jnp.where(is_attention, time_out, out_grad.astype(jnp.float32))
    every_part = lax.all_gather(cond_grads, "pipe", axis=0)
    whole_grads = lax.all_gather(jnp.sum(every_part, axis=0), "dp", axis=1, tiled=True)
    grad_condition = jax.vjp(jax.nn.silu, condition)[1](whole_grads)[0]
    grad_table = lax.dot_general(
        matches.astype(jnp.float32),
        grad_condition,
        (((0,), (0,)), ((), ())),
        precision=highest,
        preferred_element_type=jnp.float32,
    )
    return (grad_table, grad_out_shard, grad_mod_shard)


def conditioning(timesteps, labels, class_table, out_shard, mod_shard):
    model_width = class_table.shape[1]
    own_rows = out_shard.shape[0]
    own_start = lax.axis_index("dp") * own_rows
    all_steps = lax.all_gather(timesteps, "dp", axis=0, tiled=True)
    all_labels = lax.all_gather(labels, "dp", axis=0, tiled=True)
    image_count = all_steps.shape[0]
    classes = class_table.shape[0]
    matches = all_labels[:, None] == lax.broadcasted_iota(jnp.int32, (image_count, classes), 1)
    condition = sinusoid(all_steps, model_width) + product(
        matches.astype(jnp.bfloat16), class_table
    )
    conditioner = jax.nn.silu(condition).astype(jnp.bfloat16)
    own_conditioner = lax.dynamic_slice_in_dim(conditioner, own_start, own_rows, 1)
    mod_rows = lax.psum_scatter(
        product(own_conditioner, mod_shard), "dp", scatter_dimension=0, tiled=True
    )
    own_time = lax.psum_scatter(
        product(own_conditioner, out_shard[:, 3 * model_width :]),
        "dp",
        scatter_dimension=1,
        tiled=True,
    ).astype(jnp.bfloat16)
    time_rows = lax.psum_scatter(
        product(own_time, out_shard[:, : 3 * model_width]), "dp", scatter_dimension=0, tiled=True
    )
    return (condition, own_conditioner, own_time, matches, mod_rows, time_rows)


ROWS = 256
SPAN = 2304
THIRD = 1152
PART = 1152
BLOCK = 144
GROUP = 4
MESH = pl.DeviceIdType.MESH
low = jnp.bfloat16
GELU_A = math.sqrt(2.0 / math.pi)
GELU_B = 0.044715


def product_nt(former, latter):
    return contract_cols(former, latter)


def spread(index, width):
    return pl.ds(pl.multiple_of(index * width, 128), width)


def image_rows(i):
    return pl.ds(pl.multiple_of(i * ROWS, ROWS), ROWS)


def block_rows(b):
    return pl.ds(pl.multiple_of(b * BLOCK, 16), BLOCK)


def front(i, s):
    rows = image_rows(i)
    xhat, inverse = normalize_rows(s.xin[rows, :].astype(jnp.float32))
    normed = (xhat * (1.0 + s.mod[i, :, PART : 2 * PART]) + s.mod[i, :, 0:PART]).astype(low)
    s.norm[rows, :] = normed
    s.left[0, :, rows] = normed.T


def finish(i, s):
    rows = image_rows(i)
    branch = s.acc[...]
    s.branch[rows, :] = branch.astype(low)
    gate = s.mod[i, :, 2 * PART : 3 * PART]
    s.xout[rows, :] = (s.xin[rows, :].astype(jnp.float32) + gate * branch).astype(low)


def bent(value):
    square = value * value
    wave = jnp.tanh(value * (GELU_A + (GELU_A * GELU_B) * square))
    half = 0.5 + 0.5 * wave
    slope = half + value * (0.5 - 0.5 * (wave * wave)) * (
        GELU_A + (3.0 * GELU_A * GELU_B) * square
    )
    return (value * half).astype(low), slope.astype(low)


def feed_up(i, s):
    rows = image_rows(i)

    def tile(j, carry):
        cols = spread(j, SPAN)
        hidden, slope = bent(product(s.norm[rows, :], s.wa[:, cols]))
        s.wide[0, rows, cols] = hidden
        s.wide[1, rows, cols] = slope
        return carry

    lax.fori_loop(0, s.wa.shape[1] // SPAN, tile, 0)


def feed_down(i, s):
    rows = image_rows(i)

    def tile(j, carry):
        some = pl.ds(pl.multiple_of(j * 384, 384), 384)
        s.acc[:, spread(j, 384)] = product_nt(s.wide[0, rows, :], s.wb[some, :])
        return carry

    lax.fori_loop(0, PART // 384, tile, 0)


def feed_down_up(i, s):
    rows = image_rows(i)
    s.acc[...] = jnp.zeros(s.acc.shape, jnp.float32)

    def tile(j, carry):
        cols = spread(j, SPAN)
        grad_hidden = product(s.gb[...], s.wb[:, cols])
        grad_pre = (grad_hidden * s.wide[1, rows, cols].astype(jnp.float32)).astype(low)
        s.wide[1, rows, cols] = grad_pre
        s.acc[...] += product_nt(grad_pre, s.wa[:, cols])
        return carry

    lax.fori_loop(0, s.wa.shape[1] // SPAN, tile, 0)


def back_start(i, s):
    rows = image_rows(i)
    grad = s.gin[rows, :].astype(jnp.float32)
    gb = (s.mod[i, :, 2 * PART : 3 * PART] * grad).astype(low)
    s.gb[...] = gb
    s.grad_rows[i, :, 2 * PART : 3 * PART] = jnp.sum(
        grad * s.branch[rows, :].astype(jnp.float32), axis=0, keepdims=True
    )
    return gb


def back_finish(i, s):
    rows = image_rows(i)
    xhat, inverse = normalize_rows(s.xin[rows, :].astype(jnp.float32))
    gn = s.acc[...]
    s.grad_rows[i, :, 0:PART] = jnp.sum(gn, axis=0, keepdims=True)
    s.grad_rows[i, :, PART : 2 * PART] = jnp.sum(gn * xhat, axis=0, keepdims=True)
    gx = gn * (1.0 + s.mod[i, :, PART : 2 * PART])
    first = jnp.mean(gx, axis=-1, keepdims=True)
    second = jnp.mean(gx * xhat, axis=-1, keepdims=True)
    grad = s.gin[rows, :].astype(jnp.float32)
    s.gout[rows, :] = (grad + inverse * (gx - first - xhat * second)).astype(low)


def kernel_feed_backward(i, s):
    gb = back_start(i, s)
    s.left[1, :, image_rows(i)] = gb.T
    feed_down_up(i, s)
    back_finish(i, s)


def project(i, s, part):
    rows = image_rows(i)

    def tile(j, carry):
        cols = pl.ds(pl.multiple_of(part * PART + j * THIRD, 128), THIRD)
        value = product(s.norm[rows, :], s.wa[:, cols]) + s.time[i, :, cols]
        s.wide[0, rows, cols] = value.astype(low)
        return carry

    lax.fori_loop(0, PART // THIRD, tile, 0)


def head_window(h):
    start = jnp.minimum((h * HEAD) // 128, PART // 128 - 2)
    offset = h * HEAD - start * 128
    lanes = lax.broadcasted_iota(jnp.int32, (ROWS, 256), 1)
    inside = (lanes >= offset) & (lanes < offset + HEAD)
    return start, inside


def window(start, part):
    return pl.ds(pl.multiple_of(part * PART + start * 128, 128), 256)


def prob_place(i, h):
    return (
        pl.ds(pl.multiple_of((h % 4) * ROWS, ROWS), ROWS),
        pl.ds(pl.multiple_of((4 * i + h // 4) * ROWS, ROWS), ROWS),
    )


def attend_heads(i, s):
    rows = image_rows(i)
    s.acc[...] = jnp.zeros(s.acc.shape, jnp.float32)
    zero = jnp.zeros((), low)

    def score(h, slot):
        start, inside = head_window(h)
        query = jnp.where(inside, s.wide[0, rows, window(start, 0)], zero)
        s.wacc[:, spread(slot, ROWS)] = product_nt(query, s.wide[0, rows, window(start, 1)])

    def soften(h, slot):
        scores = s.wacc[:, spread(slot, ROWS)]
        top = jnp.max(scores, axis=-1, keepdims=True)
        powers = jnp.exp2((scores - top) * (HEAD ** (-0.5) * math.log2(math.e)))
        place = prob_place(i, h)
        s.wb[place[0], place[1]] = (
            powers * (1.0 / jnp.sum(powers, axis=-1, keepdims=True))
        ).astype(low)

    def mix(h):
        start, inside = head_window(h)
        place = prob_place(i, h)
        value = jnp.where(inside, s.wide[0, rows, window(start, 2)], zero)
        s.acc[:, window(start, 0)] += product(s.wb[place[0], place[1]], value)

    for k in range(GROUP):
        score(k, k)

    def group(g, carry):
        for k in range(GROUP):
            soften(GROUP * g + k, k)
        for k in range(GROUP):
            score(jnp.minimum(GROUP * (g + 1) + k, HEADS - 1), k)
        for k in range(GROUP):
            mix(GROUP * g + k)
        return carry

    lax.fori_loop(0, HEADS // GROUP, group, 0)
    mixed = s.acc[...].astype(low)
    s.left[1, :, rows] = mixed.T
    s.wide[0, rows, 3 * PART :] = mixed


def attend_out(i, s):
    rows = image_rows(i)
    s.acc[...] = product(s.wide[0, rows, 3 * PART :], s.wa[:, 3 * PART :])


def kernel_attention_backward(i, s):
    rows = image_rows(i)
    gb = back_start(i, s)
    s.wide[1, rows, 3 * PART :] = gb
    s.gb[...] = product_nt(gb, s.wa[:, 3 * PART :]).astype(low)
    s.wacc[...] = jnp.zeros(s.wacc.shape, jnp.float32)

    zero = jnp.zeros((), low)

    def grad_of_probs(h):
        start, inside = head_window(h)
        grad_head = jnp.where(inside, s.gb[:, window(start, 0)], zero)
        return product_nt(grad_head, s.wide[0, rows, window(start, 2)])

    def grad_of_scores(h, grad_probs):
        place = prob_place(i, h)
        probs = s.wb[place[0], place[1]].astype(jnp.float32)
        mixed = jnp.sum(probs * grad_probs, axis=-1, keepdims=True)
        return (probs * (grad_probs - mixed)).astype(low)

    def grads_of_qkv(h, grad_scores):
        start, inside = head_window(h)
        place = prob_place(i, h)
        query = jnp.where(inside, s.wide[0, rows, window(start, 0)], zero)
        key = jnp.where(inside, s.wide[0, rows, window(start, 1)], zero)
        grad_head = jnp.where(inside, s.gb[:, window(start, 0)], zero)
        s.wacc[:, window(start, 2)] += contract_rows(s.wb[place[0], place[1]], grad_head)
        s.wacc[:, window(start, 0)] += product(grad_scores, key)
        s.wacc[:, window(start, 1)] += contract_rows(grad_scores, query)

    def group(g, carry):
        heads = [GROUP * g + k for k in range(GROUP)]
        first = [grad_of_probs(h) for h in heads]
        second = [grad_of_scores(h, value) for h, value in zip(heads, first)]
        for h, value in zip(heads, second):
            grads_of_qkv(h, value)
        return carry

    lax.fori_loop(0, HEADS // GROUP, group, 0)
    scale = HEAD ** (-0.5)
    for part, factor in ((0, scale), (1, scale), (2, 1.0)):
        cols = pl.ds(part * PART, PART)
        grads = (s.wacc[:, cols] * factor).astype(low)
        s.wide[1, rows, cols] = grads
        s.grad_rows[i, :, pl.ds((3 + part) * PART, PART)] = jnp.sum(
            grads.astype(jnp.float32), axis=0, keepdims=True
        )
    s.acc[...] = jnp.zeros(s.acc.shape, jnp.float32)

    def tile(j, carry):
        cols = spread(j, THIRD)
        s.acc[...] += product_nt(s.wide[1, rows, cols], s.wa[:, cols])
        return carry

    lax.fori_loop(0, 3 * PART // THIRD, tile, 0)
    back_finish(i, s)


def places():
    dp, pipe = lax.axis_index("dp"), lax.axis_index("pipe")
    core, x_bit, y_bit = dp % 2, (dp // 2) % 2, dp // 4
    sib = dp + 1 - 2 * core
    step_x, step_y = 2 - 4 * x_bit, 4 - 8 * y_bit
    return SimpleNamespace(
        dp=dp,
        pipe=pipe,
        core=core,
        sib=sib,
        x=dp + step_x,
        y=dp + step_y,
        d=dp + step_x + step_y,
        step_x=step_x,
        step_y=step_y,
        x_bit=x_bit,
        y_bit=y_bit,
    )


def relay(s, at, phase):
    def piece(j, role, first=0, count=BLOCK):
        index = 4 * j + role
        row = pl.multiple_of(BLOCK * (index % 8) + first, 16)
        return s.wb.at[pl.ds(row, count), spread(2 + index // 8, PART)]

    def copy(j, kind, source, target, device):
        return pltpu.make_async_remote_copy(
            src_ref=source,
            dst_ref=target,
            send_sem=s.relay_send.at[phase, j, kind],
            recv_sem=s.relay_recv.at[phase, j, kind],
            device_id=device,
            device_id_type=MESH,
        )

    def down_place(j):
        if phase == 0:
            return s.wb.at[block_rows(at.d), spread(j, PART)]
        return s.wa.at[block_rows(j), pl.ds(3 * PART, PART)]

    def hop(j, role, first, kind, device):
        part = (0, 80) if first else (80, 64)
        return copy(j, kind, piece(j, role[0], *part), piece(j, role[1], *part), device)

    x, y = (at.x, at.pipe), (at.y, at.pipe)

    def send(j, kind):
        if kind == 1:
            return hop(j, (0, 1), True, 1, x)
        if kind == 2:
            return hop(j, (0, 2), False, 2, y)
        if kind == 3:
            return hop(j, (1, 3), True, 3, y)
        if kind == 4:
            return hop(j, (2, 3), False, 4, x)
        return copy(j, 5, piece(j, 3), down_place(j), (at.dp, 1))

    def arrival(j, kind):
        if kind == 0:
            return copy(j, 0, piece(j, 0), piece(j, 0), (at.dp, 1))
        if kind == 1:
            return hop(j, (1, 1), True, 1, x)
        if kind == 2:
            return hop(j, (2, 2), False, 2, y)
        if kind == 3:
            return hop(j, (3, 3), True, 3, y)
        return hop(j, (3, 3), False, 4, x)

    def step(k, carry):
        @pl.when(k < 4)
        def _():
            arrival(k, 0).wait_recv()
            send(k, 1).start()
            send(k, 2).start()

        @pl.when((k >= 1) & (k <= 4))
        def _():
            arrival(k - 1, 1).wait_recv()
            send(k - 1, 3).start()
            arrival(k - 1, 2).wait_recv()
            send(k - 1, 4).start()

        @pl.when(k >= 2)
        def _():
            arrival(k - 2, 3).wait_recv()
            arrival(k - 2, 4).wait_recv()
            send(k - 2, 5).start()

        return carry

    def run():
        lax.fori_loop(0, 6, step, 0)

    def done():
        def each(j, carry):
            for kind in range(1, 6):
                send(j, kind).wait_send()
            return carry

        lax.fori_loop(0, 4, each, 0)

    return SimpleNamespace(
        run=run,
        done=done,
        up=lambda j, source: copy(j, 0, source, piece(j, 0), (at.dp, 2)),
        down=lambda j: copy(j, 5, down_place(j), down_place(j), (at.dp, 2)),
    )


def gather_weights(s, at, chunks, between, ready, helper=None, helped=(), before=None):
    def held(k):
        return (s.wa if k < 4 else s.wb), pl.ds((k % 4) * PART, PART)

    def piece(k, block, first=0, count=BLOCK):
        ref, cols = held(k)
        return ref.at[pl.ds(pl.multiple_of(block * BLOCK + first, 16), count), cols]

    def copy(k, kind, ref, target, source=None):
        return pltpu.make_async_remote_copy(
            src_ref=ref if source is None else source,
            dst_ref=ref,
            send_sem=s.gather_send.at[k, kind],
            recv_sem=s.gather_recv.at[k, kind],
            device_id=(target, at.pipe),
            device_id_type=MESH,
        )

    def via_y(k):
        return (0, 80) if k % 2 == 0 else (0, 64)

    def via_x(k):
        return (80, 64) if k % 2 == 0 else (64, 80)

    sib_x, sib_y, sib_d = (
        at.sib + at.step_x,
        at.sib + at.step_y,
        at.sib + at.step_x + at.step_y,
    )

    def sends(k):
        shard = s.in_shard if k < 4 else s.out_shard
        source = shard.at[:, pl.ds((k % 4) * PART, PART)]
        return {
            0: lambda: copy(k, 0, piece(k, at.dp), at.x, source),
            1: lambda: copy(k, 1, piece(k, at.dp), at.y, source),
            2: lambda: copy(k, 2, piece(k, at.dp), at.sib, source),
            3: lambda: copy(k, 3, piece(k, at.x), at.sib),
            4: lambda: copy(k, 4, piece(k, at.x, *via_y(k)), at.y),
            5: lambda: copy(k, 5, piece(k, at.y), at.sib),
            6: lambda: copy(k, 6, piece(k, at.y, *via_x(k)), at.x),
            7: lambda: copy(k, 7, piece(k, at.d), at.sib),
        }

    def arrivals(k):
        return {
            0: lambda: copy(k, 0, piece(k, at.x), at.x),
            1: lambda: copy(k, 1, piece(k, at.y), at.y),
            2: lambda: copy(k, 2, piece(k, at.sib), at.sib),
            3: lambda: copy(k, 3, piece(k, sib_x), at.sib),
            4: lambda: copy(k, 4, piece(k, at.d, *via_y(k)), at.y),
            5: lambda: copy(k, 5, piece(k, sib_y), at.sib),
            6: lambda: copy(k, 6, piece(k, at.d, *via_x(k)), at.x),
            7: lambda: copy(k, 7, piece(k, sib_d), at.sib),
        }

    def start(k, *kinds):
        for kind in kinds:
            sends(k)[kind]().start()

    def arrive(k, *kinds):
        for kind in kinds:
            arrivals(k)[kind]().wait_recv()

    def up(k):
        return helper.up(k - 4, s.out_shard.at[:, pl.ds((k - 4) * PART, PART)])

    for k in range(2):
        start(k, 0, 1, 2)
    for k in helped:
        up(k).start()
    if before is not None:
        before()
    for k in range(chunks + 2):
        if k < chunks:
            arrive(k, 0)
            start(k, 3)
            if k not in helped:
                start(k, 4)
            arrive(k, 1)
            start(k, 5)
            if k not in helped:
                start(k, 6)
            if k + 2 < chunks:
                start(k + 2, 0, 1, 2)
            between(k)
        if 1 <= k <= chunks:
            if k - 1 in helped:
                helper.down(k - 5).wait_recv()
            else:
                arrive(k - 1, 4, 6)
            start(k - 1, 7)
        if k >= 2:
            arrive(k - 2, 2, 3, 5, 7)
            ready(k - 2)
    for k in range(chunks):
        for kind in range(8):
            if k not in helped or kind not in (4, 6):
                sends(k)[kind]().wait_send()
    for k in helped:
        up(k).wait_send()


def scatter_grads(s, at, is_feed, swap, outputs, inputs):
    total = jnp.where(is_feed, 32, 16)
    helper = relay(s, at, 1)

    def up(j):
        return helper.up(j, s.wa.at[block_rows(4 + j), pl.ds(3 * PART, PART)])

    chip = at.dp // 2
    chip_x, chip_y = chip + 1 - 2 * at.x_bit, chip + 2 - 4 * at.y_bit
    chip_d = chip_x + 2 - 4 * at.y_bit

    def unit(u):
        stage = u // 4
        second = is_feed & ((stage == 1) | (stage == 4) | (stage >= 6))
        matrix = jnp.where(second, 1, 0)
        group = jnp.where(stage < 2, 0, jnp.where(second, stage - 4, stage - 1))
        group = jnp.where(stage == 4, 1, jnp.where(stage == 5, 3, group))
        group = jnp.where(is_feed, group, stage)
        v, turn, n = u % 4, u % 2, (u % 4) // 2
        near = chip_x + turn * (chip_y - chip_x)
        block = jnp.where(group == 0, chip_d, jnp.where(group == 3, chip, near))
        part = jnp.where(
            group == 3, v, jnp.where(group == 2, 2 * (1 - turn) + n, 2 * turn + n)
        )
        return matrix, group, turn, n, block, part

    def sib_place(u):
        return s.wb.at[block_rows(u % 8), spread(u // 8, PART)]

    def near_place(matrix, turn, slot):
        index = turn * 12 + matrix * 6 + slot
        return s.wa.at[block_rows(index % 8), spread(index // 8, PART)]

    def sib_copy(u):
        return pltpu.make_async_remote_copy(
            src_ref=s.stage.at[u % 4, block_rows(1 - at.core), :],
            dst_ref=sib_place(u),
            send_sem=s.sib_send.at[u],
            recv_sem=s.sib_recv.at[u],
            device_id=(at.sib, at.pipe),
            device_id_type=MESH,
        )

    def near_copy(matrix, turn, slot):
        return pltpu.make_async_remote_copy(
            src_ref=s.near_stage.at[turn, slot],
            dst_ref=near_place(matrix, turn, slot),
            send_sem=s.near_send.at[turn, matrix * 6 + slot],
            recv_sem=s.near_recv.at[turn, matrix * 6 + slot],
            device_id=(at.x + turn * (at.y - at.x), at.pipe),
            device_id_type=MESH,
        )

    def compute(u):
        matrix, group, turn, n, block, part = unit(u)
        first = is_feed & (matrix == 0)
        lhs = jnp.where(first | (jnp.logical_not(is_feed) & (part == 3)), 1, 0)
        rhs = jnp.where(first, 0, 1)

        @pl.when(u >= 4)
        def _():
            sib_copy(u - 4).wait_send()

        rows = pl.ds(pl.multiple_of(block * 288, 16), 288)
        s.stage[u % 4] = product(s.left[lhs, rows, :], s.wide[rhs, :, spread(part, PART)]).astype(
            low
        )
        sib_copy(u).start()

    def settle(u):
        matrix, group, turn, n, block, part = unit(u)
        sib_copy(u).wait_recv()
        own = s.stage[u % 4, block_rows(at.core), :].astype(jnp.float32)
        place = (block_rows(u % 8), spread(u // 8, PART))
        value = own + s.wb[place].astype(jnp.float32)
        slot = group * 2 + n
        first = is_feed & (matrix == 0)
        helped = (at.pipe == 1) & (matrix == 1)

        def taken(from_turn, from_slot):
            near_copy(matrix, from_turn, from_slot).wait_recv()
            index = from_turn * 12 + matrix * 6 + from_slot
            return s.wa[block_rows(index % 8), spread(index // 8, PART)].astype(jnp.float32)

        @pl.when(group < 3)
        def _():
            goes_up = (group == 0) & helped

            @pl.when((matrix == 1) & jnp.logical_not(goes_up))
            def _():
                near_copy(0, turn, slot).wait_send()

            @pl.when(goes_up)
            def _():
                s.wa[block_rows(4 + part), 3 * PART :] = value.astype(low)

            @pl.when(goes_up)
            def _():
                up(part).start()

            @pl.when(jnp.logical_not(goes_up) & ((group < 2) | helped))
            def _():
                s.near_stage[turn, slot] = value.astype(low)

            @pl.when((group == 2) & jnp.logical_not(helped))
            def _():
                s.near_stage[turn, slot] = (value + taken(1 - turn, n)).astype(low)

            @pl.when(jnp.logical_not(goes_up))
            def _():
                near_copy(matrix, turn, slot).start()

        @pl.when(group == 3)
        def _():
            @pl.when((matrix > 0) | (part >= 2))
            def _():
                grad_copy(s.in_grad, part).wait()

            whole = value + taken(0, 2 + part) + taken(1, (part + 2) % 4 + 2)
            s.wacc[0:BLOCK, spread(1 + part % 2, PART)] = whole

            @pl.when(helped)
            def _():
                helper.down(part).wait_recv()
                rest = s.wa[block_rows(part), 3 * PART :].astype(jnp.float32)
                s.wacc[0:BLOCK, spread(1 + part % 2, PART)] += rest

            @pl.when(first)
            def _():
                grad_copy(s.out_grad, part).start()

            @pl.when(jnp.logical_not(first))
            def _():
                grad_copy(s.in_grad, part).start()

    def grad_copy(held, part):
        return pltpu.make_async_copy(
            s.wacc.at[pl.ds(0, BLOCK), spread(1 + part % 2, PART)],
            held.at[0, :, spread(part, PART)],
            s.out_sem.at[part % 2],
        )

    def step(u, carry):
        @pl.when(u < total)
        def _():
            compute(u)

        @pl.when(u >= 2)
        def _():
            settle(u - 2)

        return carry

    def leg(n, carry):
        third = jnp.where(is_feed, 20, total - 5)
        fourth = jnp.where(at.pipe == 1, 27, jnp.where(is_feed, 31, 14))
        marks = (0, 6, 10, third, fourth, total + 2)

        def mark(k):
            value = marks[0]
            for place in range(1, 6):
                value = jnp.where(k == place, marks[place], value)
            return value

        lax.fori_loop(mark(n), mark(n + 1), step, 0)

        @pl.when(n == 0)
        def _():
            condition_back(s, at, swap, is_feed)

        @pl.when(n == 1)
        def _():
            condition_token(s, at, swap, is_feed)

        @pl.when((n == 2) & jnp.logical_not(is_feed))
        def _():
            for copy in time_outs(s):
                copy.wait()

        @pl.when((n == 2) & (at.pipe < 2))
        def _():
            condition_sum(s, at, swap, is_feed)

        @pl.when((n == 2) & (at.pipe == 3))
        def _():
            outputs()

        @pl.when(n == 3)
        def _():
            @pl.when(at.pipe == 2)
            def _():
                helper.run()
                condition_sum(s, at, swap, is_feed)

            @pl.when(at.pipe < 2)
            def _():
                condition_table(s, at, swap, is_feed)

            @pl.when(at.pipe == 0)
            def _():
                inputs()

        return carry

    for copy in shard_copies(s, is_feed):
        copy.start()
    lax.fori_loop(0, 5, leg, 0)
    matrices = jnp.where(is_feed, 2, 1)

    def rest(k, carry):
        sib_copy(total - 4 + k).wait_send()
        return carry

    lax.fori_loop(0, 4, rest, 0)
    for turn in range(2):
        for slot in range(6):
            last = matrices - 1 if slot >= 2 else jnp.where(at.pipe == 1, 0, matrices - 1)
            near_copy(last, turn, slot).wait_send()

    @pl.when(at.pipe == 1)
    def _():
        for j in range(4):
            up(j).wait_send()

    @pl.when(at.pipe == 2)
    def _():
        helper.done()

    for part in (2, 3):
        grad_copy(s.in_grad, part).wait()

    @pl.when(at.pipe == 3)
    def _():
        condition_sum(s, at, swap, is_feed)

    @pl.when(at.pipe >= 2)
    def _():
        condition_table(s, at, swap, is_feed)


def exchange(s, at, number, piece, landing):
    def copy(target, source):
        return pltpu.make_async_remote_copy(
            src_ref=piece(target),
            dst_ref=landing(source),
            send_sem=s.swap_send.at[number, target],
            recv_sem=s.swap_recv.at[number, source],
            device_id=(target, at.pipe),
            device_id_type=MESH,
        )

    others = [(at.dp + k) % 8 for k in range(1, 8)]

    def start():
        for other in others:
            copy(other, at.dp).start()

    def arrive():
        for other in others:
            copy(other, other).wait_recv()

    def done():
        for other in others:
            copy(other, at.dp).wait_send()

    return SimpleNamespace(start=start, arrive=arrive, done=done)


def exchanges(s, at):
    def pair(j):
        return pl.ds(2 * j, 2)

    return SimpleNamespace(
        rows=exchange(s, at, 0, lambda j: s.cond_in, lambda j: s.rows.at[pair(j)]),
        mods=exchange(s, at, 1, lambda j: s.mod_parts.at[pair(j)], lambda j: s.mod_all.at[j]),
        tokens=exchange(s, at, 2, lambda j: s.token, lambda j: s.token_all.at[pair(j)]),
        times=exchange(s, at, 3, lambda j: s.time_parts.at[pair(j)], lambda j: s.time_all.at[j]),
        grads=exchange(s, at, 4, lambda j: s.grad_rows, lambda j: s.grad_all.at[pair(j)]),
        backs=exchange(s, at, 5, lambda j: s.back, lambda j: s.back_all.at[j]),
        ends=exchange(s, at, 6, lambda j: s.end, lambda j: s.end_all.at[j]),
    )


def shard_copies(s, is_feed):
    copies = []
    for part in range(3):
        cols = pl.ds(part * PART, PART)
        rows = pl.ds(part * BLOCK, BLOCK)
        copies.append((s.mod_shard.at[:, cols], s.norm.at[rows, :]))
        copies.append((s.out_shard.at[:, cols], s.branch.at[rows, :]))
    copies.append((s.out_shard.at[:, pl.ds(3 * PART, PART)], s.gb.at[pl.ds(0, BLOCK), :]))
    return [
        pltpu.make_async_copy(source, target, s.shard_sem.at[k])
        for k, (source, target) in enumerate(copies)
    ]


def shard_part(ref, part):
    return ref[pl.ds(part * BLOCK, BLOCK), :]


def stack_rows(source, target, width):
    for k in range(16):
        target[k : k + 1, 0:width] = source[k, :, 0:width]


def chosen(at):
    places = lax.broadcasted_iota(jnp.int32, (PART, BLOCK), 0)
    lanes = lax.broadcasted_iota(jnp.int32, (PART, BLOCK), 1)
    return jnp.where(places == lanes + at.dp * BLOCK, 1.0, 0.0).astype(low)


def condition_front(s, at, swap, is_feed):
    for copy in shard_copies(s, is_feed):
        copy.start()
    s.rows[pl.ds(2 * at.dp, 2)] = s.cond_in[...]
    s.grad_rows[...] = jnp.zeros(s.grad_rows.shape, jnp.float32)
    swap.rows.arrive()
    stack_rows(s.rows, s.flat, PART)
    condition = s.flat[:, 0:PART]
    conditioner = (condition * (1.0 / (1.0 + jnp.exp(-condition)))).astype(low)
    pick = chosen(at)
    own = product(conditioner, pick).astype(low)
    s.own_cond[...] = own
    for copy in shard_copies(s, is_feed):
        copy.wait()
    for part in range(3):
        s.flat[:, part * PART : (part + 1) * PART] = product(own, shard_part(s.norm, part))
    s.flat[:, 3 * PART : 4 * PART] = product(own, s.gb[0:BLOCK, :])
    for k in range(16):
        s.mod_parts[k] = s.flat[k : k + 1, 0 : 4 * PART]
    swap.mods.start()
    s.mod_all[at.dp] = s.mod_parts[pl.ds(2 * at.dp, 2)]


def condition_mods(s, at, swap, is_feed):
    swap.mods.arrive()
    for i in range(2):
        total = jnp.sum(s.mod_all[:, i], axis=0)
        s.mod[i] = total[:, 0 : 3 * PART]
        s.token[i] = total[:, 3 * PART :]

    @pl.when(jnp.logical_not(is_feed))
    def _():
        swap.tokens.start()
        s.token_all[pl.ds(2 * at.dp, 2)] = s.token[...]


def condition_tokens(s, at, swap, is_feed):
    @pl.when(jnp.logical_not(is_feed))
    def _():
        swap.tokens.arrive()
        stack_rows(s.token_all, s.flat, PART)
        own_token = product(s.flat[:, 0:PART].astype(low), chosen(at)).astype(low)
        s.own_token[...] = own_token
        for part in range(3):
            s.flat[:, part * PART : (part + 1) * PART] = product(
                own_token, shard_part(s.branch, part)
            )
        for k in range(16):
            s.time_parts[k] = s.flat[k : k + 1, 0 : 3 * PART]
        swap.times.start()
        s.time_all[at.dp] = s.time_parts[pl.ds(2 * at.dp, 2)]


def condition_times(s, at, swap, is_feed):
    @pl.when(jnp.logical_not(is_feed))
    def _():
        swap.times.arrive()
        for i in range(2):
            s.time[i] = jnp.sum(s.time_all[:, i], axis=0)


def end_copy(s, at, plane):
    return pltpu.make_async_remote_copy(
        src_ref=s.end_parts.at[at.pipe],
        dst_ref=s.end_parts.at[at.pipe],
        send_sem=s.end_send.at[plane],
        recv_sem=s.end_recv.at[at.pipe],
        device_id=(at.dp, plane),
        device_id_type=MESH,
    )


def end_arrival(s, at, plane):
    return pltpu.make_async_remote_copy(
        src_ref=s.end_parts.at[plane],
        dst_ref=s.end_parts.at[plane],
        send_sem=s.end_send.at[plane],
        recv_sem=s.end_recv.at[plane],
        device_id=(at.dp, plane),
        device_id_type=MESH,
    )


def mod_out(s):
    return pltpu.make_async_copy(
        s.wacc.at[pl.ds(0, BLOCK), :], s.mod_grad.at[0], s.shard_sem.at[0]
    )


def time_outs(s):
    held = s.out_grad.at[0]
    return (
        pltpu.make_async_copy(
            s.wacc.at[pl.ds(0, BLOCK), :], held.at[:, pl.ds(0, 3 * PART)], s.shard_sem.at[0]
        ),
        pltpu.make_async_copy(
            s.acc.at[pl.ds(0, BLOCK), :], held.at[:, pl.ds(3 * PART, PART)], s.shard_sem.at[1]
        ),
    )


def condition_back(s, at, swap, is_feed):
    s.grad_all[pl.ds(2 * at.dp, 2)] = s.grad_rows[...]
    swap.grads.arrive()
    stack_rows(s.grad_all, s.flat, 6 * PART)
    for copy in shard_copies(s, is_feed):
        copy.wait()

    @pl.when(jnp.logical_not(is_feed))
    def _():
        token = jnp.zeros((16, BLOCK), jnp.float32)
        for part in range(3):
            grads = s.flat[:, (3 + part) * PART : (4 + part) * PART].astype(low)
            token += product_nt(grads, shard_part(s.branch, part))
        s.back[...] = product_nt(token.astype(low), chosen(at)).astype(low)
        swap.backs.start()
        s.back_all[at.dp] = s.back[...]

    own = s.own_cond[...]
    s.end[...] = jnp.zeros(s.end.shape, jnp.float32)
    for part in range(3):
        cols = slice(part * PART, (part + 1) * PART)
        grads = s.flat[:, cols].astype(low)
        s.wacc[0:BLOCK, cols] = contract_rows(own, grads)
        s.end[...] += product_nt(grads, shard_part(s.norm, part))
    mod_out(s).start()


def condition_token(s, at, swap, is_feed):
    mod_out(s).wait()

    @pl.when(jnp.logical_not(is_feed))
    def _():
        for part in range(3):
            grads = s.flat[:, (3 + part) * PART : (4 + part) * PART].astype(low)
            s.wacc[0:BLOCK, part * PART : (part + 1) * PART] = contract_rows(
                s.own_token[...], grads
            )
        swap.backs.arrive()
        whole = jnp.zeros((16, PART), jnp.float32)
        for k in range(8):
            whole += s.back_all[k].astype(jnp.float32)
        whole = whole.astype(low)
        s.acc[0:BLOCK, :] = contract_rows(s.own_cond[...], whole)
        s.end[...] += product_nt(whole, s.gb[0:BLOCK, :])
        for copy in time_outs(s):
            copy.start()

    s.end_parts[at.pipe] = s.end[...]
    for k in range(1, 4):
        end_copy(s, at, (at.pipe + k) % 4).start()


def condition_sum(s, at, swap, is_feed):
    for k in range(1, 4):
        end_arrival(s, at, (at.pipe + k) % 4).wait_recv()
    s.end[...] = s.end_parts[0] + s.end_parts[1] + s.end_parts[2] + s.end_parts[3]
    swap.ends.start()
    s.end_all[at.dp] = s.end[...]


def condition_table(s, at, swap, is_feed):
    swap.ends.arrive()
    for k in range(8):
        s.flat[:, BLOCK * k : BLOCK * (k + 1)] = s.end_all[k]
    whole = s.flat[:, 0:PART]
    stack_rows(s.rows, s.flat, PART)
    condition = s.flat[:, 0:PART]
    gate = 1.0 / (1.0 + jnp.exp(-condition))
    grads = whole * (gate * (1.0 + condition * (1.0 - gate)))
    for k in range(3):
        term = grads.astype(low)
        s.terms[16 * k : 16 * (k + 1), :] = term
        grads = grads - term.astype(jnp.float32)
    lanes = lax.broadcasted_iota(jnp.int32, (1, 1024), 1).astype(jnp.float32)
    for k in range(16):
        label = s.rows[k, :, PART : PART + 1]
        s.flat[k : k + 1, 0:1024] = jnp.where(lanes == label, 1.0, 0.0)
    hot = s.flat[:, 0:1024].astype(low)
    for k in range(3):
        s.hot[16 * k : 16 * (k + 1), :] = hot


def condition_done(s, at, swap, is_feed):
    for each in (swap.rows, swap.mods, swap.grads, swap.ends):
        each.done()
    for k in range(1, 4):
        end_copy(s, at, (at.pipe + k) % 4).wait_send()

    @pl.when(jnp.logical_not(is_feed))
    def _():
        for each in (swap.tokens, swap.times, swap.backs):
            each.done()


def mega_body(*refs):
    s = SimpleNamespace(**dict(zip(REFS, refs)))
    at = places()
    is_feed = at.pipe % 2 == 1
    pipe = at.pipe
    barrier = pltpu.get_barrier_semaphore()
    swap = exchanges(s, at)
    targets = [((at.dp + k) % 8, pipe) for k in range(1, 8)]
    targets += [(at.dp, (pipe + k) % 4) for k in range(1, 4)]
    for target in targets:
        pl.semaphore_signal(barrier, inc=1, device_id=target, device_id_type=MESH)
    pl.semaphore_wait(barrier, len(targets))
    swap.rows.start()

    def remote(source, target, send, recv, plane):
        return pltpu.make_async_remote_copy(
            src_ref=source,
            dst_ref=target,
            send_sem=send,
            recv_sem=recv,
            device_id=(at.dp, plane),
            device_id_type=MESH,
        )

    def share(i, plane):
        return pl.ds(pl.multiple_of(i * ROWS + plane * 64, 64), 64)

    def token_copy(i, plane):
        return remote(
            s.tokens.at[i],
            s.xin.at[share(i, plane), :],
            s.share_send.at[0, i],
            s.xin_recv.at[i, plane],
            0,
        )

    def cotangent_copy(i, plane):
        return remote(
            s.cotangent.at[i],
            s.gin.at[share(i, plane), :],
            s.share_send.at[1, i],
            s.gin_recv.at[i, plane],
            3,
        )

    def next_copy(i):
        whole = image_rows(i)
        return remote(
            s.xout.at[whole, :],
            s.xin.at[whole, :],
            s.hop_send.at[0, i],
            s.xin_recv.at[i, 0],
            jnp.minimum(pipe + 1, 3),
        )

    def back_copy(i):
        whole = image_rows(i)
        return remote(
            s.gout.at[whole, :],
            s.gin.at[whole, :],
            s.hop_send.at[1, i],
            s.gin_recv.at[i, 3],
            jnp.maximum(pipe - 1, 0),
        )

    def output_copy(i, plane):
        return remote(
            s.xout.at[share(i, plane), :],
            s.out_tokens.at[i],
            s.final_send.at[0, i, plane],
            s.final_recv.at[0, i],
            plane,
        )

    def input_copy(i, plane):
        return remote(
            s.gout.at[share(i, plane), :],
            s.input_share.at[i],
            s.final_send.at[1, i, plane],
            s.final_recv.at[1, i],
            plane,
        )

    def local(source, target, index):
        return pltpu.make_async_copy(source, target, s.local_sem.at[index])

    own_in = local(s.in_shard, s.wa.at[block_rows(at.dp), :], 0)
    own_out = local(s.out_shard, s.wb.at[block_rows(at.dp), :], 1)
    own_in.start()

    @pl.when(is_feed)
    def _():
        own_out.start()

    for i in range(2):
        own_tokens = local(s.tokens.at[i], s.xin.at[pl.ds(i * ROWS, 64), :], 2 + i)
        own_cotangent = local(s.cotangent.at[i], s.gin.at[pl.ds(i * ROWS + 192, 64), :], 4 + i)

        @pl.when(pipe == 0)
        def _():
            own_tokens.start()

        @pl.when(pipe == 3)
        def _():
            own_cotangent.start()

        @pl.when(pipe != 0)
        def _():
            token_copy(i, pipe).start()

    rounds = (condition_front, condition_mods, condition_tokens, condition_times)

    def between(k):
        if k < 4:
            rounds[k](s, at, swap, is_feed)
        if k == 1:
            for i in range(2):

                @pl.when(pipe != 3)
                def _():
                    cotangent_copy(i, pipe).start()

    def ready(k):
        if k == 0:

            def begin(i, carry):
                local(s.tokens.at[i], s.xin.at[share(i, 0), :], 2 + i).wait()
                for plane in range(1, 4):
                    token_copy(i, plane).wait_recv()
                front(i, s)
                return carry

            lax.fori_loop(0, 2, begin, 0)

        def one(n, carry):
            project(n % 2, s, n // 2)
            return carry

        if k == 1:
            lax.fori_loop(0, 4, one, 0)
        if k == 2:
            project(0, s, 2)
            attend_heads(0, s)

    own_in.wait()

    @pl.when(pipe == 0)
    def _():
        gather_weights(s, at, 4, between, ready)

    @pl.when(pipe == 2)
    def _():
        helper = relay(s, at, 0)

        gather_weights(s, at, 4, between, lambda k: None, before=helper.run)
        helper.done()

    def ahead(i, carry):
        next_copy(i).wait_recv()
        front(i, s)
        feed_up(i, s)
        return carry

    def early(k):
        if k == 6:
            lax.fori_loop(0, 2, ahead, 0)

    @pl.when(is_feed)
    def _():
        own_out.wait()

    @pl.when(pipe == 1)
    def _():
        gather_weights(s, at, 8, between, early, relay(s, at, 0), (4, 5, 6, 7))

    @pl.when(pipe == 3)
    def _():
        gather_weights(s, at, 8, between, lambda k: None)

    for i in range(2):

        @pl.when(pipe != 0)
        def _():
            token_copy(i, pipe).wait_send()

    def inputs(i):
        for plane in range(1, 4):
            input_copy(i, plane).start()
        local(s.gout.at[share(i, 0), :], s.input_share.at[i], 4 + i).start()

    def step(n, carry):
        at_end = pipe == 3
        goes_forward = jnp.where(at_end, n % 2 == 0, n < 2)
        i = jnp.where(at_end, n // 2, n % 2)

        @pl.when(goes_forward)
        def _():
            @pl.when(pipe >= 2)
            def _():
                next_copy(i).wait_recv()

            @pl.when(is_feed)
            def _():
                @pl.when(pipe == 3)
                def _():
                    front(i, s)
                    feed_up(i, s)

                feed_down(i, s)
                finish(i, s)

            @pl.when(jnp.logical_not(is_feed))
            def _():
                @pl.when(pipe != 0)
                def _():
                    front(i, s)

                    def one(part, carry):
                        project(i, s, part)
                        return carry

                    lax.fori_loop(0, 3, one, 0)

                @pl.when((pipe == 0) & (i == 1))
                def _():
                    project(1, s, 2)

                @pl.when((pipe != 0) | (i == 1))
                def _():
                    attend_heads(i, s)

                attend_out(i, s)
                finish(i, s)

            @pl.when((pipe < 2) & (i == 0) & (at.core == 0))
            def _():
                next_copy(0).start()

            @pl.when((pipe < 2) & (i == 1))
            def _():
                @pl.when(at.core == 1)
                def _():
                    pl.semaphore_wait(s.turn, 1)
                    next_copy(0).start()

                next_copy(0).wait_send()
                pl.semaphore_signal(
                    s.turn, inc=1, device_id=(at.sib, pipe), device_id_type=MESH
                )
                pl.semaphore_wait(s.turn, 1)
                next_copy(1).start()
                next_copy(1).wait_send()

                @pl.when(at.core == 0)
                def _():
                    pl.semaphore_signal(
                        s.turn, inc=1, device_id=(at.sib, pipe), device_id_type=MESH
                    )

            @pl.when(pipe == 2)
            def _():
                next_copy(i).start()


        @pl.when(jnp.logical_not(goes_forward))
        def _():
            @pl.when(pipe == 3)
            def _():
                local(s.cotangent.at[i], s.gin.at[share(i, 3), :], 4 + i).wait()
                for plane in range(3):
                    cotangent_copy(i, plane).wait_recv()

            @pl.when(pipe != 3)
            def _():
                back_copy(i).wait_recv()

            @pl.when(is_feed)
            def _():
                kernel_feed_backward(i, s)

            @pl.when(jnp.logical_not(is_feed))
            def _():
                kernel_attention_backward(i, s)

            @pl.when(pipe != 0)
            def _():
                back_copy(i).start()

            @pl.when((pipe == 0) & (i == 0))
            def _():
                inputs(0)

        return carry

    lax.fori_loop(0, 4, step, 0)
    swap.grads.start()

    for target, sem in ((at.sib, 0), (at.x, 1), (at.y, 2)):
        pl.semaphore_signal(
            s.free.at[sem], inc=1, device_id=(target, pipe), device_id_type=MESH
        )
    for sem in range(3):
        pl.semaphore_wait(s.free.at[sem], 1)

    def last_inputs(*unused):
        @pl.when(pipe == 0)
        def _():
            inputs(1)

    def outputs(*unused):
        @pl.when(pipe == 3)
        def _():
            for i in range(2):
                for plane in range(3):
                    output_copy(i, plane).start()
                local(s.xout.at[share(i, 3), :], s.out_tokens.at[i], 2 + i).start()

    scatter_grads(s, at, is_feed, swap, outputs, last_inputs)
    condition_done(s, at, swap, is_feed)

    for i in range(2):

        @pl.when(pipe != 3)
        def _():
            cotangent_copy(i, pipe).wait_send()
            output_copy(i, pipe).wait_recv()

        @pl.when(pipe == 2)
        def _():
            next_copy(i).wait_send()

        @pl.when(pipe == 3)
        def _():
            for plane in range(3):
                output_copy(i, plane).wait_send()
            local(s.xout.at[share(i, 3), :], s.out_tokens.at[i], 2 + i).wait()

        @pl.when(pipe != 0)
        def _():
            back_copy(i).wait_send()
            input_copy(i, pipe).wait_recv()

        @pl.when(pipe == 0)
        def _():
            for plane in range(1, 4):
                input_copy(i, plane).wait_send()
            local(s.gout.at[share(i, 0), :], s.input_share.at[i], 4 + i).wait()

    s.input_grad[...] = s.input_share[...].astype(jnp.float32)


SCRATCH = dict(
    xin=pltpu.VMEM((512, 1152), low),
    gin=pltpu.VMEM((512, 1152), low),
    xout=pltpu.VMEM((512, 1152), low),
    gout=pltpu.VMEM((512, 1152), low),
    wa=pltpu.VMEM((1152, 4608), low),
    wb=pltpu.VMEM((1152, 4608), low),
    norm=pltpu.VMEM((512, 1152), low),
    left=pltpu.VMEM((2, 1152, 512), low),
    wide=pltpu.VMEM((2, 512, 4608), low),
    branch=pltpu.VMEM((512, 1152), low),
    acc=pltpu.VMEM((256, 1152), jnp.float32),
    gb=pltpu.VMEM((256, 1152), low),
    wacc=pltpu.VMEM((256, 3456), jnp.float32),
    stage=pltpu.VMEM((4, 288, 1152), low),
    near_stage=pltpu.VMEM((2, 6, 144, 1152), low),
    gather_send=pltpu.SemaphoreType.DMA((8, 8)),
    gather_recv=pltpu.SemaphoreType.DMA((8, 8)),
    sib_send=pltpu.SemaphoreType.DMA((32,)),
    sib_recv=pltpu.SemaphoreType.DMA((32,)),
    near_send=pltpu.SemaphoreType.DMA((2, 12)),
    near_recv=pltpu.SemaphoreType.DMA((2, 12)),
    out_sem=pltpu.SemaphoreType.DMA((2,)),
    share_send=pltpu.SemaphoreType.DMA((2, 2)),
    xin_recv=pltpu.SemaphoreType.DMA((2, 4)),
    gin_recv=pltpu.SemaphoreType.DMA((2, 4)),
    hop_send=pltpu.SemaphoreType.DMA((2, 2)),
    final_send=pltpu.SemaphoreType.DMA((2, 2, 4)),
    final_recv=pltpu.SemaphoreType.DMA((2, 2)),
    local_sem=pltpu.SemaphoreType.DMA((6,)),
    free=pltpu.SemaphoreType.REGULAR((3,)),
    turn=pltpu.SemaphoreType.REGULAR,
    shard_sem=pltpu.SemaphoreType.DMA((7,)),
    swap_send=pltpu.SemaphoreType.DMA((7, 8)),
    swap_recv=pltpu.SemaphoreType.DMA((7, 8)),
    relay_send=pltpu.SemaphoreType.DMA((2, 4, 6)),
    relay_recv=pltpu.SemaphoreType.DMA((2, 4, 6)),
    end_send=pltpu.SemaphoreType.DMA((4,)),
    end_recv=pltpu.SemaphoreType.DMA((4,)),
    mod=pltpu.VMEM((2, 1, 3456), jnp.float32),
    time=pltpu.VMEM((2, 1, 3456), jnp.float32),
    token=pltpu.VMEM((2, 1, 1152), jnp.float32),
    grad_rows=pltpu.VMEM((2, 1, 6912), jnp.float32),
    rows=pltpu.VMEM((16, 1, 1280), jnp.float32),
    flat=pltpu.VMEM((16, 6912), jnp.float32),
    own_cond=pltpu.VMEM((16, 144), low),
    own_token=pltpu.VMEM((16, 144), low),
    mod_parts=pltpu.VMEM((16, 1, 4608), jnp.float32),
    mod_all=pltpu.VMEM((8, 2, 1, 4608), jnp.float32),
    token_all=pltpu.VMEM((16, 1, 1152), jnp.float32),
    time_parts=pltpu.VMEM((16, 1, 3456), jnp.float32),
    time_all=pltpu.VMEM((8, 2, 1, 3456), jnp.float32),
    grad_all=pltpu.VMEM((16, 1, 6912), jnp.float32),
    back=pltpu.VMEM((16, 1152), low),
    back_all=pltpu.VMEM((8, 16, 1152), low),
    end=pltpu.VMEM((16, 144), jnp.float32),
    input_share=pltpu.VMEM((2, 64, 1152), low),
    end_parts=pltpu.VMEM((4, 16, 144), jnp.float32),
    end_all=pltpu.VMEM((8, 16, 144), jnp.float32),
)
REFS = (
    ["tokens", "cotangent", "in_shard", "out_shard", "mod_shard", "cond_in"]
    + ["out_tokens", "input_grad", "terms", "hot", "in_grad", "out_grad", "mod_grad"]
    + list(SCRATCH)
)


def mega(tokens, cotangent, in_shard, out_shard, mod_shard, cond_rows):
    anywhere = pl.BlockSpec(memory_space=pl.ANY)
    near = pl.BlockSpec(memory_space=pltpu.VMEM)

    def wide(array):
        return jax.ShapeDtypeStruct((1,) + array.shape, jnp.float32)

    return pl.pallas_call(
        mega_body,
        out_shape=(
            jax.ShapeDtypeStruct(tokens.shape, low),
            jax.ShapeDtypeStruct(tokens.shape, jnp.float32),
            jax.ShapeDtypeStruct((48, tokens.shape[2]), low),
            jax.ShapeDtypeStruct((48, 1024), low),
            wide(in_shard),
            wide(out_shard),
            wide(mod_shard),
        ),
        in_specs=[anywhere] * 5 + [near],
        out_specs=[anywhere] + [near] * 3 + [anywhere] * 3,
        scratch_shapes=list(SCRATCH.values()),
        compiler_params=pltpu.CompilerParams(
            collective_id=0, has_side_effects=True, vmem_limit_bytes=62 * 2**20
        ),
        cost_estimate=pl.CostEstimate(
            flops=25 * 10**9, bytes_accessed=10**7, transcendentals=10**7
        ),
        name="blocks",
    )(tokens, cotangent, in_shard, out_shard, mod_shard, cond_rows)


def last_body(terms, hot, *refs):
    sources, (table, *targets) = refs[:3], refs[3:7]
    value, *held, sems = refs[7:]
    classes = table.shape[0]
    pieces = [
        (source.at[0, pl.ds(48 * part, 48), :], stage.at[pl.ds(48 * part, 48), :],
         target.at[0, pl.ds(48 * part, 48), :], 3 * k + part)
        for k, (source, stage, target) in enumerate(zip(sources, held, targets))
        for part in range(3)
    ]
    takes = [pltpu.make_async_copy(s, v, sems.at[0, n]) for s, v, t, n in pieces]
    gives = [pltpu.make_async_copy(v, t, sems.at[1, n]) for s, v, t, n in pieces]
    for take in takes:
        take.start()
    for k in range(4):
        count = min(256, classes - 256 * k)
        value[k] = contract_rows(hot[:, 256 * k : 256 * (k + 1)], terms[...])
        part = pltpu.make_async_copy(
            value.at[k, pl.ds(0, count), :],
            table.at[pl.ds(256 * k, count), :],
            sems.at[1, 9 + k],
        )
        part.start()
        gives.append(part)
    for take, give in zip(takes, gives):
        take.wait()
        give.start()
    for give in gives:
        give.wait()


def last_copies(terms, hot, grads, classes):
    anywhere = pl.BlockSpec(memory_space=pl.ANY)
    near = pl.BlockSpec(memory_space=pltpu.VMEM)
    width = terms.shape[1]
    return pl.pallas_call(
        last_body,
        out_shape=[jax.ShapeDtypeStruct((classes, width), jnp.float32)]
        + [jax.ShapeDtypeStruct(grad.shape, jnp.float32) for grad in grads],
        in_specs=[near, near] + [anywhere] * 3,
        out_specs=[anywhere] * 4,
        scratch_shapes=[
            pltpu.VMEM((4, 256, width), jnp.float32),
            *[pltpu.VMEM(grad.shape[1:], jnp.float32) for grad in grads],
            pltpu.SemaphoreType.DMA((2, 13)),
        ],
        compiler_params=pltpu.CompilerParams(vmem_limit_bytes=62 * 2**20),
        name="table",
    )(terms, hot, *grads)


def fast_shards(
    tokens,
    cotangent,
    timesteps,
    labels,
    class_table,
    section_in_weights,
    section_out_weights,
    modulation_weights,
):
    model_width = tokens.shape[2]
    in_shard, out_shard, mod_shard = (
        section_in_weights[0],
        section_out_weights[0],
        modulation_weights[0],
    )
    images = tokens.shape[0]
    classes = class_table.shape[0]
    matches = labels[:, None] == lax.broadcasted_iota(jnp.int32, (images, classes), 1)
    condition = sinusoid(timesteps, model_width) + product(
        matches.astype(jnp.bfloat16), class_table
    )
    named = jnp.broadcast_to(labels.astype(jnp.float32)[:, None], (images, 128))
    cond_rows = jnp.concatenate([condition, named], axis=1)[:, None, :]
    out_tokens, input_grad, terms, hot, *grads = mega(
        tokens, cotangent, in_shard, out_shard, mod_shard, cond_rows
    )
    return (out_tokens, input_grad, *last_copies(terms, hot, grads, classes))


def solution(mesh):
    return jax.shard_map(
        fast_shards if mesh.shape["dp"] == 8 else shards,
        mesh=mesh,
        in_specs=(
            P("dp", "pipe", None),
            P("dp", "pipe", None),
            P("dp"),
            P("dp"),
            P(),
            P("pipe", "dp", None),
            P("pipe", "dp", None),
            P("pipe", "dp", None),
        ),
        out_specs=(
            P("dp", "pipe", None),
            P("dp", "pipe", None),
            P(),
            P("pipe", "dp", None),
            P("pipe", "dp", None),
            P("pipe", "dp", None),
        ),
        check_vma=False,
    )
```

```python
from functools import partial
import math
from types import SimpleNamespace

import jax
import jax.numpy as jnp
from jax import lax
from jax.experimental import pallas as pl
from jax.experimental.pallas import tpu as pltpu
from jax.sharding import PartitionSpec as P

HEADS = 16
HEAD = 72


epsilon = 1e-06
highest = lax.Precision.HIGHEST


def shifted(block, axis, distance):
    devices = range(lax.axis_size(axis))
    route = [(i - distance, i) for i in devices if i - distance in devices]
    return lax.ppermute(block, axis, route)


def sinusoid(step_values, model_width):
    half_width = model_width // 2
    frequencies = jnp.exp(
        -math.log(10000.0) * jnp.arange(half_width, dtype=jnp.float32) / half_width
    )
    angles = step_values.astype(jnp.float32)[:, None] * frequencies[None, :]
    return jnp.concatenate([jnp.cos(angles), jnp.sin(angles)], axis=1)


def product(former, latter):
    return jnp.dot(former, latter, preferred_element_type=jnp.float32)


def contract_rows(former, latter):
    return lax.dot_general(
        former, latter, (((0,), (0,)), ((), ())), preferred_element_type=jnp.float32
    )


def contract_cols(former, latter):
    return lax.dot_general(
        former, latter, (((1,), (1,)), ((), ())), preferred_element_type=jnp.float32
    )


def normalize_rows(row_values):
    centered = row_values - jnp.mean(row_values, axis=-1, keepdims=True)
    inverse = lax.rsqrt(jnp.mean(centered * centered, axis=-1, keepdims=True) + epsilon)
    return (centered * inverse, inverse)


def modulation_front(section_input, mod_row):
    model_width = section_input.shape[1]
    shift_vec = mod_row[:model_width]
    scale_vec = mod_row[model_width : 2 * model_width]
    gate_vec = mod_row[2 * model_width :]
    centred, inverse = normalize_rows(section_input.astype(jnp.float32))
    normed = (centred * (1.0 + scale_vec) + shift_vec).astype(jnp.bfloat16)
    return (normed, centred, inverse, scale_vec, gate_vec)


def modulation_back(grad_normed, centred, inverse, scale_vec, grad_rows, grad_gate):
    grad_shift = jnp.sum(grad_normed, axis=0)
    grad_scale = jnp.sum(grad_normed * centred, axis=0)
    grad_centred = grad_normed * (1.0 + scale_vec)
    grad_input = inverse * (
        grad_centred
        - jnp.mean(grad_centred, axis=-1, keepdims=True)
        - centred * jnp.mean(grad_centred * centred, axis=-1, keepdims=True)
    )
    grad_mod = jnp.concatenate([grad_shift, grad_scale, grad_gate]).astype(jnp.bfloat16)
    return (grad_rows + grad_input, grad_mod)


def attention_parts(section_input, mod_row, time_row, weights):
    in_weight = weights[0]
    model_width = section_input.shape[1]
    tok_len = section_input.shape[0]
    normed, centred, inverse, scale_vec, gate_vec = modulation_front(section_input, mod_row)
    qkv = (product(normed, in_weight[:, : 3 * model_width]) + time_row).astype(jnp.bfloat16)
    split_qkv = qkv.reshape(tok_len, 3, HEADS, HEAD)
    queries = split_qkv[:, 0]
    keyed = split_qkv[:, 1]
    valued = split_qkv[:, 2]
    scores = jnp.einsum(
        "qhd,khd->hqk", queries, keyed, preferred_element_type=jnp.float32
    ) * HEAD ** (-0.5)
    probs_full = jax.nn.softmax(scores, axis=-1)
    probs_low = probs_full.astype(jnp.bfloat16)
    mixed = jnp.einsum("hqk,khd->qhd", probs_low, valued, preferred_element_type=jnp.float32)
    head_rows = mixed.reshape(tok_len, model_width).astype(jnp.bfloat16)
    branch = product(head_rows, in_weight[:, 3 * model_width :])
    section_output = section_input.astype(jnp.float32) + gate_vec * branch
    saved_parts = (
        normed,
        centred,
        inverse,
        scale_vec,
        gate_vec,
        queries,
        keyed,
        valued,
        probs_full,
        probs_low,
        head_rows,
        branch,
    )
    return (section_output, saved_parts)


def attention_forward(section_input, mod_row, time_row, weights):
    return attention_parts(section_input, mod_row, time_row, weights)[0]


def attention_backward(section_input, grad_in, mod_row, time_row, weights):
    in_weight = weights[0]
    model_width = section_input.shape[1]
    tok_len = section_input.shape[0]
    unused, saved_parts = attention_parts(section_input, mod_row, time_row, weights)
    (
        normed,
        centred,
        inverse,
        scale_vec,
        gate_vec,
        queries,
        keyed,
        valued,
        probs_full,
        probs_low,
        head_rows,
        branch,
    ) = saved_parts
    grad_rows = grad_in.astype(jnp.float32)
    grad_branch = (gate_vec * grad_rows).astype(jnp.bfloat16)
    grad_gate = jnp.sum(grad_rows * branch, axis=0)
    grad_heads = contract_cols(grad_branch, in_weight[:, 3 * model_width :]).astype(jnp.bfloat16)
    heads_split = grad_heads.reshape(tok_len, HEADS, HEAD)
    grad_probs = jnp.einsum("qhd,khd->hqk", heads_split, valued, preferred_element_type=jnp.float32)
    grad_value = jnp.einsum(
        "hqk,qhd->khd", probs_low, heads_split, preferred_element_type=jnp.float32
    )
    grad_scores = (
        probs_full * (grad_probs - jnp.sum(probs_full * grad_probs, axis=-1, keepdims=True))
    ).astype(jnp.bfloat16)
    grad_query = jnp.einsum(
        "hqk,khd->qhd", grad_scores, keyed, preferred_element_type=jnp.float32
    ) * HEAD ** (-0.5)
    grad_key = jnp.einsum(
        "hqk,qhd->khd", grad_scores, queries, preferred_element_type=jnp.float32
    ) * HEAD ** (-0.5)
    grad_qkv = (
        jnp.stack([grad_query, grad_key, grad_value], axis=1)
        .reshape(tok_len, 3 * model_width)
        .astype(jnp.bfloat16)
    )
    grad_normed = contract_cols(grad_qkv, in_weight[:, : 3 * model_width])
    grad_time = jnp.sum(grad_qkv, axis=0, dtype=jnp.float32).astype(jnp.bfloat16)
    grad_input, grad_mod = modulation_back(
        grad_normed, centred, inverse, scale_vec, grad_rows, grad_gate
    )
    narrow_zero = jnp.zeros((tok_len, model_width), jnp.bfloat16)
    return (
        grad_input,
        normed,
        jnp.concatenate([grad_qkv, narrow_zero], axis=1),
        grad_branch,
        jnp.concatenate([head_rows, narrow_zero, narrow_zero, narrow_zero], axis=1),
        grad_mod,
        grad_time,
    )


def feed_parts(section_input, mod_row, weights):
    in_weight, out_weight = weights
    normed, centred, inverse, scale_vec, gate_vec = modulation_front(section_input, mod_row)
    pre_act = product(normed, in_weight)
    hidden = jax.nn.gelu(pre_act, approximate=True).astype(jnp.bfloat16)
    branch = contract_cols(hidden, out_weight)
    section_output = section_input.astype(jnp.float32) + gate_vec * branch
    return (
        section_output,
        (normed, centred, inverse, scale_vec, gate_vec, pre_act, hidden, branch),
    )


def feed_forward(section_input, mod_row, time_row, weights):
    return feed_parts(section_input, mod_row, weights)[0]


def feed_backward(section_input, grad_in, mod_row, time_row, weights):
    in_weight, out_weight = weights
    unused, saved_parts = feed_parts(section_input, mod_row, weights)
    normed, centred, inverse, scale_vec, gate_vec, pre_act, hidden, branch = saved_parts
    grad_rows = grad_in.astype(jnp.float32)
    grad_branch = (gate_vec * grad_rows).astype(jnp.bfloat16)
    grad_gate = jnp.sum(grad_rows * branch, axis=0)
    grad_hidden = product(grad_branch, out_weight)
    gelu_pull = jax.vjp(partial(jax.nn.gelu, approximate=True), pre_act)[1]
    grad_pre = gelu_pull(grad_hidden)[0].astype(jnp.bfloat16)
    grad_normed = contract_cols(grad_pre, in_weight)
    grad_input, grad_mod = modulation_back(
        grad_normed, centred, inverse, scale_vec, grad_rows, grad_gate
    )
    return (
        grad_input,
        normed,
        grad_pre,
        grad_branch,
        hidden,
        grad_mod,
        jnp.zeros(grad_mod.shape, jnp.bfloat16),
    )


def spare_forward(section_input, mod_row, time_row, weights):
    return jnp.zeros(section_input.shape, jnp.float32)


def spare_backward(section_input, grad_in, mod_row, time_row, weights):
    tok_len, model_width = section_input.shape
    hidden_width = weights[0].shape[1]
    narrow_zero = jnp.zeros((tok_len, model_width), jnp.bfloat16)
    wide_zero = jnp.zeros((tok_len, hidden_width), jnp.bfloat16)
    row_zero = jnp.zeros((3 * model_width,), jnp.bfloat16)
    return (
        jnp.zeros(section_input.shape, jnp.float32),
        narrow_zero,
        wide_zero,
        narrow_zero,
        wide_zero,
        row_zero,
        row_zero,
    )


def attention_weight_grads(left_one, right_one, left_two, right_two):
    width = left_two.shape[1]
    low = jnp.bfloat16
    qkv_term = contract_rows(left_one, right_one[:, : 3 * width]).astype(low)
    out_term = contract_rows(right_two[:, :width], left_two).astype(low)
    zero_term = jnp.zeros((width, right_two.shape[1]), low)
    return (jnp.concatenate([qkv_term, out_term], axis=1), zero_term)


def feed_weight_grads(left_one, right_one, left_two, right_two):
    low = jnp.bfloat16
    return (
        contract_rows(left_one, right_one).astype(low),
        contract_rows(left_two, right_two).astype(low),
    )


def replace_slot(buffer, slot_index, new_rows, active):
    old_rows = lax.dynamic_index_in_dim(buffer, slot_index, 0, keepdims=False)
    return lax.dynamic_update_index_in_dim(
        buffer, jnp.where(active, new_rows, old_rows), slot_index, 0
    )


def shards(
    tokens,
    cotangent,
    timesteps,
    labels,
    class_table,
    section_in_weights,
    section_out_weights,
    modulation_weights,
):
    micro_count = tokens.shape[0]
    model_width = tokens.shape[2]
    hidden_width = section_in_weights.shape[2]
    section_count = lax.axis_size("pipe")
    section_index = lax.axis_index("pipe")
    last_section = section_count - 1
    section_kind = 1 + section_index % 2
    in_shard, out_shard, mod_shard = (
        section_in_weights[0],
        section_out_weights[0],
        modulation_weights[0],
    )
    whole_tokens, whole_cotangent = (
        lax.all_gather(tokens, "pipe", axis=1, tiled=True),
        lax.all_gather(cotangent, "pipe", axis=1, tiled=True),
    )
    tok_len = whole_tokens.shape[1]
    weights = (
        lax.all_gather(in_shard, "dp", axis=0, tiled=True),
        lax.all_gather(out_shard, "dp", axis=0, tiled=True),
    )
    condition, own_conditioner, own_time, matches, mod_rows, time_rows = conditioning(
        timesteps, labels, class_table, out_shard, mod_shard
    )

    def forward_tick(carry, tick_index):
        incoming, kept_inputs, finals = carry
        micro_index = tick_index - section_index
        active = (micro_index >= 0) & (micro_index < micro_count)
        slot_index = jnp.clip(micro_index, 0, micro_count - 1)
        first_rows = lax.dynamic_index_in_dim(whole_tokens, slot_index, 0, keepdims=False)
        section_input = jnp.where(section_index == 0, first_rows, incoming)
        section_output = lax.switch(
            jnp.where(active, section_kind, 0),
            (spare_forward, attention_forward, feed_forward),
            section_input,
            lax.dynamic_index_in_dim(mod_rows, slot_index, 0, keepdims=False),
            lax.dynamic_index_in_dim(time_rows, slot_index, 0, keepdims=False),
            weights,
        )
        output_low = section_output.astype(jnp.bfloat16)
        kept_inputs = replace_slot(kept_inputs, slot_index, section_input, active)
        finals = replace_slot(
            finals, slot_index, output_low, active & (section_index == last_section)
        )
        incoming = shifted(output_low, "pipe", 1)
        return ((incoming, kept_inputs, finals), None)

    empty_rows = jnp.zeros((tok_len, model_width), jnp.bfloat16)
    empty_store = jnp.zeros((micro_count, tok_len, model_width), jnp.bfloat16)
    forward_out, ignored = lax.scan(
        forward_tick,
        (empty_rows, empty_store, empty_store),
        jnp.arange(micro_count + section_count - 1),
    )
    kept_inputs = forward_out[1]
    finals = forward_out[2]
    wide_store = jnp.zeros((micro_count, tok_len, hidden_width), jnp.bfloat16)
    row_store = jnp.zeros((micro_count, 3 * model_width), jnp.bfloat16)
    start_factors = (empty_store, wide_store, empty_store, wide_store, row_store, row_store)

    def backward_tick(carry, tick_index):
        incoming, factors, input_grads = carry
        micro_index = tick_index - (last_section - section_index)
        active = (micro_index >= 0) & (micro_index < micro_count)
        slot_index = jnp.clip(micro_index, 0, micro_count - 1)
        top_grad = lax.dynamic_index_in_dim(whole_cotangent, slot_index, 0, keepdims=False)
        grad_in = jnp.where(section_index == last_section, top_grad, incoming)
        section_input = lax.dynamic_index_in_dim(kept_inputs, slot_index, 0, keepdims=False)
        results = lax.switch(
            jnp.where(active, section_kind, 0),
            (spare_backward, attention_backward, feed_backward),
            section_input,
            grad_in,
            lax.dynamic_index_in_dim(mod_rows, slot_index, 0, keepdims=False),
            lax.dynamic_index_in_dim(time_rows, slot_index, 0, keepdims=False),
            weights,
        )
        grad_low = results[0].astype(jnp.bfloat16)
        factors = tuple(
            (
                replace_slot(buffer, slot_index, fresh, active)
                for buffer, fresh in zip(factors, results[1:])
            )
        )
        input_grads = replace_slot(
            input_grads, slot_index, grad_low, active & (section_index == 0)
        )
        incoming = shifted(grad_low, "pipe", -1)
        return ((incoming, factors, input_grads), None)

    backward_out, ignored = lax.scan(
        backward_tick,
        (empty_rows, start_factors, empty_store),
        jnp.arange(micro_count + section_count - 1),
    )
    factors = backward_out[1]
    input_grads = backward_out[2]
    flat_rows = micro_count * tok_len
    left_one, right_one, left_two, right_two = (
        stored.reshape(flat_rows, stored.shape[2]) for stored in factors[:4]
    )
    in_term, out_term = lax.cond(
        section_index % 2 == 0,
        attention_weight_grads,
        feed_weight_grads,
        left_one,
        right_one,
        left_two,
        right_two,
    )
    in_grad = lax.psum_scatter(in_term, "dp", scatter_dimension=0, tiled=True)
    out_grad = lax.psum_scatter(out_term, "dp", scatter_dimension=0, tiled=True)
    own_out, own_in = (finals, input_grads)
    keep_out = jnp.where(section_index == last_section, own_out, 0)
    keep_in = jnp.where(section_index == 0, own_in, 0)
    output_share = lax.psum_scatter(keep_out, "pipe", scatter_dimension=1, tiled=True)
    input_share = lax.psum_scatter(keep_in, "pipe", scatter_dimension=1, tiled=True)
    small_outs = conditioning_grads(
        factors[4],
        factors[5],
        condition,
        own_conditioner,
        own_time,
        matches,
        out_shard,
        mod_shard,
        out_grad,
    )
    return (
        output_share,
        input_share.astype(jnp.float32),
        small_outs[0],
        in_grad.astype(jnp.float32)[None],
        small_outs[1][None],
        small_outs[2][None],
    )


def conditioning_grads(
    mod_grads,
    time_grads,
    condition,
    own_conditioner,
    own_time,
    matches,
    out_shard,
    mod_shard,
    out_grad,
):
    model_width = condition.shape[1]
    is_attention = lax.axis_index("pipe") % 2 == 0
    all_mod = lax.all_gather(mod_grads, "dp", axis=0, tiled=True)
    all_time = lax.all_gather(time_grads, "dp", axis=0, tiled=True)
    grad_mod_shard = contract_rows(own_conditioner, all_mod)
    cond_grads = contract_cols(all_mod, mod_shard)
    own_token = contract_cols(all_time, out_shard[:, : 3 * model_width]).astype(jnp.bfloat16)
    all_token = lax.all_gather(own_token, "dp", axis=1, tiled=True)
    token_grads = contract_cols(all_token, out_shard[:, 3 * model_width :])
    cond_grads = cond_grads + jnp.where(is_attention, token_grads, 0.0)
    time_out = jnp.concatenate(
        [contract_rows(own_time, all_time), contract_rows(own_conditioner, all_token)], axis=1
    )
    grad_out_shard = jnp.where(is_attention, time_out, out_grad.astype(jnp.float32))
    every_part = lax.all_gather(cond_grads, "pipe", axis=0)
    whole_grads = lax.all_gather(jnp.sum(every_part, axis=0), "dp", axis=1, tiled=True)
    grad_condition = jax.vjp(jax.nn.silu, condition)[1](whole_grads)[0]
    grad_table = lax.dot_general(
        matches.astype(jnp.float32),
        grad_condition,
        (((0,), (0,)), ((), ())),
        precision=highest,
        preferred_element_type=jnp.float32,
    )
    return (grad_table, grad_out_shard, grad_mod_shard)


def conditioning(timesteps, labels, class_table, out_shard, mod_shard):
    model_width = class_table.shape[1]
    own_rows = out_shard.shape[0]
    own_start = lax.axis_index("dp") * own_rows
    all_steps = lax.all_gather(timesteps, "dp", axis=0, tiled=True)
    all_labels = lax.all_gather(labels, "dp", axis=0, tiled=True)
    image_count = all_steps.shape[0]
    classes = class_table.shape[0]
    matches = all_labels[:, None] == lax.broadcasted_iota(jnp.int32, (image_count, classes), 1)
    condition = sinusoid(all_steps, model_width) + product(
        matches.astype(jnp.bfloat16), class_table
    )
    conditioner = jax.nn.silu(condition).astype(jnp.bfloat16)
    own_conditioner = lax.dynamic_slice_in_dim(conditioner, own_start, own_rows, 1)
    mod_rows = lax.psum_scatter(
        product(own_conditioner, mod_shard), "dp", scatter_dimension=0, tiled=True
    )
    own_time = lax.psum_scatter(
        product(own_conditioner, out_shard[:, 3 * model_width :]),
        "dp",
        scatter_dimension=1,
        tiled=True,
    ).astype(jnp.bfloat16)
    time_rows = lax.psum_scatter(
        product(own_time, out_shard[:, : 3 * model_width]), "dp", scatter_dimension=0, tiled=True
    )
    return (condition, own_conditioner, own_time, matches, mod_rows, time_rows)


ROWS = 256
SPAN = 2304
THIRD = 1152
PART = 1152
BLOCK = 144
GROUP = 4
MESH = pl.DeviceIdType.MESH
low = jnp.bfloat16
GELU_A = math.sqrt(2.0 / math.pi)
GELU_B = 0.044715


def product_nt(former, latter):
    return contract_cols(former, latter)


def spread(index, width):
    return pl.ds(pl.multiple_of(index * width, 128), width)


def image_rows(i):
    return pl.ds(pl.multiple_of(i * ROWS, ROWS), ROWS)


def block_rows(b):
    return pl.ds(pl.multiple_of(b * BLOCK, 16), BLOCK)


def front(i, s):
    rows = image_rows(i)
    xhat, inverse = normalize_rows(s.xin[rows, :].astype(jnp.float32))
    normed = (xhat * (1.0 + s.mod[i, :, PART : 2 * PART]) + s.mod[i, :, 0:PART]).astype(low)
    s.norm[rows, :] = normed
    s.left[0, :, rows] = normed.T


def finish(i, s):
    rows = image_rows(i)
    branch = s.acc[...]
    s.branch[rows, :] = branch.astype(low)
    gate = s.mod[i, :, 2 * PART : 3 * PART]
    s.xout[rows, :] = (s.xin[rows, :].astype(jnp.float32) + gate * branch).astype(low)


def bent(value):
    square = value * value
    wave = jnp.tanh(value * (GELU_A + (GELU_A * GELU_B) * square))
    half = 0.5 + 0.5 * wave
    slope = half + value * (0.5 - 0.5 * (wave * wave)) * (
        GELU_A + (3.0 * GELU_A * GELU_B) * square
    )
    return (value * half).astype(low), slope.astype(low)


def feed_up(i, s):
    rows = image_rows(i)

    def tile(j, carry):
        cols = spread(j, SPAN)
        hidden, slope = bent(product(s.norm[rows, :], s.wa[:, cols]))
        s.wide[0, rows, cols] = hidden
        s.wide[1, rows, cols] = slope
        return carry

    lax.fori_loop(0, s.wa.shape[1] // SPAN, tile, 0)


def feed_down(i, s):
    rows = image_rows(i)

    def tile(j, carry):
        some = pl.ds(pl.multiple_of(j * 384, 384), 384)
        s.acc[:, spread(j, 384)] = product_nt(s.wide[0, rows, :], s.wb[some, :])
        return carry

    lax.fori_loop(0, PART // 384, tile, 0)


def feed_down_up(i, s):
    rows = image_rows(i)
    s.acc[...] = jnp.zeros(s.acc.shape, jnp.float32)

    def tile(j, carry):
        cols = spread(j, SPAN)
        grad_hidden = product(s.gb[...], s.wb[:, cols])
        grad_pre = (grad_hidden * s.wide[1, rows, cols].astype(jnp.float32)).astype(low)
        s.wide[1, rows, cols] = grad_pre
        s.acc[...] += product_nt(grad_pre, s.wa[:, cols])
        return carry

    lax.fori_loop(0, s.wa.shape[1] // SPAN, tile, 0)


def back_start(i, s):
    rows = image_rows(i)
    grad = s.gin[rows, :].astype(jnp.float32)
    gb = (s.mod[i, :, 2 * PART : 3 * PART] * grad).astype(low)
    s.gb[...] = gb
    s.grad_rows[i, :, 2 * PART : 3 * PART] = jnp.sum(
        grad * s.branch[rows, :].astype(jnp.float32), axis=0, keepdims=True
    )
    return gb


def back_finish(i, s):
    rows = image_rows(i)
    xhat, inverse = normalize_rows(s.xin[rows, :].astype(jnp.float32))
    gn = s.acc[...]
    s.grad_rows[i, :, 0:PART] = jnp.sum(gn, axis=0, keepdims=True)
    s.grad_rows[i, :, PART : 2 * PART] = jnp.sum(gn * xhat, axis=0, keepdims=True)
    gx = gn * (1.0 + s.mod[i, :, PART : 2 * PART])
    first = jnp.mean(gx, axis=-1, keepdims=True)
    second = jnp.mean(gx * xhat, axis=-1, keepdims=True)
    grad = s.gin[rows, :].astype(jnp.float32)
    s.gout[rows, :] = (grad + inverse * (gx - first - xhat * second)).astype(low)


def kernel_feed_backward(i, s):
    gb = back_start(i, s)
    s.left[1, :, image_rows(i)] = gb.T
    feed_down_up(i, s)
    back_finish(i, s)


def project(i, s, part):
    rows = image_rows(i)

    def tile(j, carry):
        cols = pl.ds(pl.multiple_of(part * PART + j * THIRD, 128), THIRD)
        value = product(s.norm[rows, :], s.wa[:, cols]) + s.time[i, :, cols]
        s.wide[0, rows, cols] = value.astype(low)
        return carry

    lax.fori_loop(0, PART // THIRD, tile, 0)


def head_window(h):
    start = jnp.minimum((h * HEAD) // 128, PART // 128 - 2)
    offset = h * HEAD - start * 128
    lanes = lax.broadcasted_iota(jnp.int32, (ROWS, 256), 1)
    inside = (lanes >= offset) & (lanes < offset + HEAD)
    return start, inside


def window(start, part):
    return pl.ds(pl.multiple_of(part * PART + start * 128, 128), 256)


def prob_place(i, h):
    return (
        pl.ds(pl.multiple_of((h % 4) * ROWS, ROWS), ROWS),
        pl.ds(pl.multiple_of((4 * i + h // 4) * ROWS, ROWS), ROWS),
    )


def attend_heads(i, s):
    rows = image_rows(i)
    s.acc[...] = jnp.zeros(s.acc.shape, jnp.float32)
    zero = jnp.zeros((), low)

    def score(h, slot):
        start, inside = head_window(h)
        query = jnp.where(inside, s.wide[0, rows, window(start, 0)], zero)
        s.wacc[:, spread(slot, ROWS)] = product_nt(query, s.wide[0, rows, window(start, 1)])

    def soften(h, slot):
        scores = s.wacc[:, spread(slot, ROWS)]
        top = jnp.max(scores, axis=-1, keepdims=True)
        powers = jnp.exp2((scores - top) * (HEAD ** (-0.5) * math.log2(math.e)))
        place = prob_place(i, h)
        s.wb[place[0], place[1]] = (
            powers * (1.0 / jnp.sum(powers, axis=-1, keepdims=True))
        ).astype(low)

    def mix(h):
        start, inside = head_window(h)
        place = prob_place(i, h)
        value = jnp.where(inside, s.wide[0, rows, window(start, 2)], zero)
        s.acc[:, window(start, 0)] += product(s.wb[place[0], place[1]], value)

    for k in range(GROUP):
        score(k, k)

    def group(g, carry):
        for k in range(GROUP):
            soften(GROUP * g + k, k)
        for k in range(GROUP):
            score(jnp.minimum(GROUP * (g + 1) + k, HEADS - 1), k)
        for k in range(GROUP):
            mix(GROUP * g + k)
        return carry

    lax.fori_loop(0, HEADS // GROUP, group, 0)
    mixed = s.acc[...].astype(low)
    s.left[1, :, rows] = mixed.T
    s.wide[0, rows, 3 * PART :] = mixed


def attend_out(i, s):
    rows = image_rows(i)
    s.acc[...] = product(s.wide[0, rows, 3 * PART :], s.wa[:, 3 * PART :])


def kernel_attention_backward(i, s):
    rows = image_rows(i)
    gb = back_start(i, s)
    s.wide[1, rows, 3 * PART :] = gb
    s.gb[...] = product_nt(gb, s.wa[:, 3 * PART :]).astype(low)
    s.wacc[...] = jnp.zeros(s.wacc.shape, jnp.float32)

    zero = jnp.zeros((), low)

    def grad_of_probs(h):
        start, inside = head_window(h)
        grad_head = jnp.where(inside, s.gb[:, window(start, 0)], zero)
        return product_nt(grad_head, s.wide[0, rows, window(start, 2)])

    def grad_of_scores(h, grad_probs):
        place = prob_place(i, h)
        probs = s.wb[place[0], place[1]].astype(jnp.float32)
        mixed = jnp.sum(probs * grad_probs, axis=-1, keepdims=True)
        return (probs * (grad_probs - mixed)).astype(low)

    def grads_of_qkv(h, grad_scores):
        start, inside = head_window(h)
        place = prob_place(i, h)
        query = jnp.where(inside, s.wide[0, rows, window(start, 0)], zero)
        key = jnp.where(inside, s.wide[0, rows, window(start, 1)], zero)
        grad_head = jnp.where(inside, s.gb[:, window(start, 0)], zero)
        s.wacc[:, window(start, 2)] += contract_rows(s.wb[place[0], place[1]], grad_head)
        s.wacc[:, window(start, 0)] += product(grad_scores, key)
        s.wacc[:, window(start, 1)] += contract_rows(grad_scores, query)

    def group(g, carry):
        heads = [GROUP * g + k for k in range(GROUP)]
        first = [grad_of_probs(h) for h in heads]
        second = [grad_of_scores(h, value) for h, value in zip(heads, first)]
        for h, value in zip(heads, second):
            grads_of_qkv(h, value)
        return carry

    lax.fori_loop(0, HEADS // GROUP, group, 0)
    scale = HEAD ** (-0.5)
    for part, factor in ((0, scale), (1, scale), (2, 1.0)):
        cols = pl.ds(part * PART, PART)
        grads = (s.wacc[:, cols] * factor).astype(low)
        s.wide[1, rows, cols] = grads
        s.grad_rows[i, :, pl.ds((3 + part) * PART, PART)] = jnp.sum(
            grads.astype(jnp.float32), axis=0, keepdims=True
        )
    s.acc[...] = jnp.zeros(s.acc.shape, jnp.float32)

    def tile(j, carry):
        cols = spread(j, THIRD)
        s.acc[...] += product_nt(s.wide[1, rows, cols], s.wa[:, cols])
        return carry

    lax.fori_loop(0, 3 * PART // THIRD, tile, 0)
    back_finish(i, s)


def places():
    dp, pipe = lax.axis_index("dp"), lax.axis_index("pipe")
    core, x_bit, y_bit = dp % 2, (dp // 2) % 2, dp // 4
    sib = dp + 1 - 2 * core
    step_x, step_y = 2 - 4 * x_bit, 4 - 8 * y_bit
    return SimpleNamespace(
        dp=dp,
        pipe=pipe,
        core=core,
        sib=sib,
        x=dp + step_x,
        y=dp + step_y,
        d=dp + step_x + step_y,
        step_x=step_x,
        step_y=step_y,
        x_bit=x_bit,
        y_bit=y_bit,
    )


def relay(s, at, phase):
    def piece(j, role, first=0, count=BLOCK):
        index = 4 * j + role
        row = pl.multiple_of(BLOCK * (index % 8) + first, 16)
        return s.wb.at[pl.ds(row, count), spread(2 + index // 8, PART)]

    def copy(j, kind, source, target, device):
        return pltpu.make_async_remote_copy(
            src_ref=source,
            dst_ref=target,
            send_sem=s.relay_send.at[phase, j, kind],
            recv_sem=s.relay_recv.at[phase, j, kind],
            device_id=device,
            device_id_type=MESH,
        )

    def down_place(j):
        if phase == 0:
            return s.wb.at[block_rows(at.d), spread(j, PART)]
        return s.wa.at[block_rows(j), pl.ds(3 * PART, PART)]

    def hop(j, role, first, kind, device):
        part = (0, 80) if first else (80, 64)
        return copy(j, kind, piece(j, role[0], *part), piece(j, role[1], *part), device)

    x, y = (at.x, at.pipe), (at.y, at.pipe)

    def send(j, kind):
        if kind == 1:
            return hop(j, (0, 1), True, 1, x)
        if kind == 2:
            return hop(j, (0, 2), False, 2, y)
        if kind == 3:
            return hop(j, (1, 3), True, 3, y)
        if kind == 4:
            return hop(j, (2, 3), False, 4, x)
        return copy(j, 5, piece(j, 3), down_place(j), (at.dp, 1))

    def arrival(j, kind):
        if kind == 0:
            return copy(j, 0, piece(j, 0), piece(j, 0), (at.dp, 1))
        if kind == 1:
            return hop(j, (1, 1), True, 1, x)
        if kind == 2:
            return hop(j, (2, 2), False, 2, y)
        if kind == 3:
            return hop(j, (3, 3), True, 3, y)
        return hop(j, (3, 3), False, 4, x)

    def step(k, carry):
        @pl.when(k < 4)
        def _():
            arrival(k, 0).wait_recv()
            send(k, 1).start()
            send(k, 2).start()

        @pl.when((k >= 1) & (k <= 4))
        def _():
            arrival(k - 1, 1).wait_recv()
            send(k - 1, 3).start()
            arrival(k - 1, 2).wait_recv()
            send(k - 1, 4).start()

        @pl.when(k >= 2)
        def _():
            arrival(k - 2, 3).wait_recv()
            arrival(k - 2, 4).wait_recv()
            send(k - 2, 5).start()

        return carry

    def run():
        lax.fori_loop(0, 6, step, 0)

    def done():
        def each(j, carry):
            for kind in range(1, 6):
                send(j, kind).wait_send()
            return carry

        lax.fori_loop(0, 4, each, 0)

    return SimpleNamespace(
        run=run,
        done=done,
        up=lambda j, source: copy(j, 0, source, piece(j, 0), (at.dp, 2)),
        down=lambda j: copy(j, 5, down_place(j), down_place(j), (at.dp, 2)),
    )


def gather_weights(s, at, chunks, between, ready, helper=None, helped=(), before=None):
    def held(k):
        return (s.wa if k < 4 else s.wb), pl.ds((k % 4) * PART, PART)

    def piece(k, block, first=0, count=BLOCK):
        ref, cols = held(k)
        return ref.at[pl.ds(pl.multiple_of(block * BLOCK + first, 16), count), cols]

    def copy(k, kind, ref, target, source=None):
        return pltpu.make_async_remote_copy(
            src_ref=ref if source is None else source,
            dst_ref=ref,
            send_sem=s.gather_send.at[k, kind],
            recv_sem=s.gather_recv.at[k, kind],
            device_id=(target, at.pipe),
            device_id_type=MESH,
        )

    def via_y(k):
        return (0, 80) if k % 2 == 0 else (0, 64)

    def via_x(k):
        return (80, 64) if k % 2 == 0 else (64, 80)

    sib_x, sib_y, sib_d = (
        at.sib + at.step_x,
        at.sib + at.step_y,
        at.sib + at.step_x + at.step_y,
    )

    def sends(k):
        shard = s.in_shard if k < 4 else s.out_shard
        source = shard.at[:, pl.ds((k % 4) * PART, PART)]
        return {
            0: lambda: copy(k, 0, piece(k, at.dp), at.x, source),
            1: lambda: copy(k, 1, piece(k, at.dp), at.y, source),
            2: lambda: copy(k, 2, piece(k, at.dp), at.sib, source),
            3: lambda: copy(k, 3, piece(k, at.x), at.sib),
            4: lambda: copy(k, 4, piece(k, at.x, *via_y(k)), at.y),
            5: lambda: copy(k, 5, piece(k, at.y), at.sib),
            6: lambda: copy(k, 6, piece(k, at.y, *via_x(k)), at.x),
            7: lambda: copy(k, 7, piece(k, at.d), at.sib),
        }

    def arrivals(k):
        return {
            0: lambda: copy(k, 0, piece(k, at.x), at.x),
            1: lambda: copy(k, 1, piece(k, at.y), at.y),
            2: lambda: copy(k, 2, piece(k, at.sib), at.sib),
            3: lambda: copy(k, 3, piece(k, sib_x), at.sib),
            4: lambda: copy(k, 4, piece(k, at.d, *via_y(k)), at.y),
            5: lambda: copy(k, 5, piece(k, sib_y), at.sib),
            6: lambda: copy(k, 6, piece(k, at.d, *via_x(k)), at.x),
            7: lambda: copy(k, 7, piece(k, sib_d), at.sib),
        }

    def start(k, *kinds):
        for kind in kinds:
            sends(k)[kind]().start()

    def arrive(k, *kinds):
        for kind in kinds:
            arrivals(k)[kind]().wait_recv()

    def up(k):
        return helper.up(k - 4, s.out_shard.at[:, pl.ds((k - 4) * PART, PART)])

    for k in range(2):
        start(k, 0, 1, 2)
    for k in helped:
        up(k).start()
    if before is not None:
        before()
    for k in range(chunks + 2):
        if k < chunks:
            arrive(k, 0)
            start(k, 3)
            if k not in helped:
                start(k, 4)
            arrive(k, 1)
            start(k, 5)
            if k not in helped:
                start(k, 6)
            if k + 2 < chunks:
                start(k + 2, 0, 1, 2)
            between(k)
        if 1 <= k <= chunks:
            if k - 1 in helped:
                helper.down(k - 5).wait_recv()
            else:
                arrive(k - 1, 4, 6)
            start(k - 1, 7)
        if k >= 2:
            arrive(k - 2, 2, 3, 5, 7)
            ready(k - 2)
    for k in range(chunks):
        for kind in range(8):
            if k not in helped or kind not in (4, 6):
                sends(k)[kind]().wait_send()
    for k in helped:
        up(k).wait_send()


def scatter_grads(s, at, is_feed, swap, outputs, inputs):
    total = jnp.where(is_feed, 32, 16)
    helper = relay(s, at, 1)

    def up(j):
        return helper.up(j, s.wa.at[block_rows(4 + j), pl.ds(3 * PART, PART)])

    chip = at.dp // 2
    chip_x, chip_y = chip + 1 - 2 * at.x_bit, chip + 2 - 4 * at.y_bit
    chip_d = chip_x + 2 - 4 * at.y_bit

    def unit(u):
        stage = u // 4
        second = is_feed & ((stage == 1) | (stage == 4) | (stage >= 6))
        matrix = jnp.where(second, 1, 0)
        group = jnp.where(stage < 2, 0, jnp.where(second, stage - 4, stage - 1))
        group = jnp.where(stage == 4, 1, jnp.where(stage == 5, 3, group))
        group = jnp.where(is_feed, group, stage)
        v, turn, n = u % 4, u % 2, (u % 4) // 2
        near = chip_x + turn * (chip_y - chip_x)
        block = jnp.where(group == 0, chip_d, jnp.where(group == 3, chip, near))
        part = jnp.where(
            group == 3, v, jnp.where(group == 2, 2 * (1 - turn) + n, 2 * turn + n)
        )
        return matrix, group, turn, n, block, part

    def sib_place(u):
        return s.wb.at[block_rows(u % 8), spread(u // 8, PART)]

    def near_place(matrix, turn, slot):
        index = turn * 12 + matrix * 6 + slot
        return s.wa.at[block_rows(index % 8), spread(index // 8, PART)]

    def sib_copy(u):
        return pltpu.make_async_remote_copy(
            src_ref=s.stage.at[u % 4, block_rows(1 - at.core), :],
            dst_ref=sib_place(u),
            send_sem=s.sib_send.at[u],
            recv_sem=s.sib_recv.at[u],
            device_id=(at.sib, at.pipe),
            device_id_type=MESH,
        )

    def near_copy(matrix, turn, slot):
        return pltpu.make_async_remote_copy(
            src_ref=s.near_stage.at[turn, slot],
            dst_ref=near_place(matrix, turn, slot),
            send_sem=s.near_send.at[turn, matrix * 6 + slot],
            recv_sem=s.near_recv.at[turn, matrix * 6 + slot],
            device_id=(at.x + turn * (at.y - at.x), at.pipe),
            device_id_type=MESH,
        )

    def compute(u):
        matrix, group, turn, n, block, part = unit(u)
        first = is_feed & (matrix == 0)
        lhs = jnp.where(first | (jnp.logical_not(is_feed) & (part == 3)), 1, 0)
        rhs = jnp.where(first, 0, 1)

        @pl.when(u >= 4)
        def _():
            sib_copy(u - 4).wait_send()

        rows = pl.ds(pl.multiple_of(block * 288, 16), 288)
        s.stage[u % 4] = product(s.left[lhs, rows, :], s.wide[rhs, :, spread(part, PART)]).astype(
            low
        )
        sib_copy(u).start()

    def settle(u):
        matrix, group, turn, n, block, part = unit(u)
        sib_copy(u).wait_recv()
        own = s.stage[u % 4, block_rows(at.core), :].astype(jnp.float32)
        place = (block_rows(u % 8), spread(u // 8, PART))
        value = own + s.wb[place].astype(jnp.float32)
        slot = group * 2 + n
        first = is_feed & (matrix == 0)
        helped = (at.pipe == 1) & (matrix == 1)

        def taken(from_turn, from_slot):
            near_copy(matrix, from_turn, from_slot).wait_recv()
            index = from_turn * 12 + matrix * 6 + from_slot
            return s.wa[block_rows(index % 8), spread(index // 8, PART)].astype(jnp.float32)

        @pl.when(group < 3)
        def _():
            goes_up = (group == 0) & helped

            @pl.when((matrix == 1) & jnp.logical_not(goes_up))
            def _():
                near_copy(0, turn, slot).wait_send()

            @pl.when(goes_up)
            def _():
                s.wa[block_rows(4 + part), 3 * PART :] = value.astype(low)

            @pl.when(goes_up)
            def _():
                up(part).start()

            @pl.when(jnp.logical_not(goes_up) & ((group < 2) | helped))
            def _():
                s.near_stage[turn, slot] = value.astype(low)

            @pl.when((group == 2) & jnp.logical_not(helped))
            def _():
                s.near_stage[turn, slot] = (value + taken(1 - turn, n)).astype(low)

            @pl.when(jnp.logical_not(goes_up))
            def _():
                near_copy(matrix, turn, slot).start()

        @pl.when(group == 3)
        def _():
            @pl.when((matrix > 0) | (part >= 2))
            def _():
                grad_copy(s.in_grad, part).wait()

            whole = value + taken(0, 2 + part) + taken(1, (part + 2) % 4 + 2)
            s.wacc[0:BLOCK, spread(1 + part % 2, PART)] = whole

            @pl.when(helped)
            def _():
                helper.down(part).wait_recv()
                rest = s.wa[block_rows(part), 3 * PART :].astype(jnp.float32)
                s.wacc[0:BLOCK, spread(1 + part % 2, PART)] += rest

            @pl.when(first)
            def _():
                grad_copy(s.out_grad, part).start()

            @pl.when(jnp.logical_not(first))
            def _():
                grad_copy(s.in_grad, part).start()

    def grad_copy(held, part):
        return pltpu.make_async_copy(
            s.wacc.at[pl.ds(0, BLOCK), spread(1 + part % 2, PART)],
            held.at[0, :, spread(part, PART)],
            s.out_sem.at[part % 2],
        )

    def step(u, carry):
        @pl.when(u < total)
        def _():
            compute(u)

        @pl.when(u >= 2)
        def _():
            settle(u - 2)

        return carry

    def leg(n, carry):
        third = jnp.where(is_feed, 20, total - 5)
        fourth = jnp.where(at.pipe == 1, 27, jnp.where(is_feed, 31, 14))
        marks = (0, 6, 10, third, fourth, total + 2)

        def mark(k):
            value = marks[0]
            for place in range(1, 6):
                value = jnp.where(k == place, marks[place], value)
            return value

        lax.fori_loop(mark(n), mark(n + 1), step, 0)

        @pl.when(n == 0)
        def _():
            condition_back(s, at, swap, is_feed)

        @pl.when(n == 1)
        def _():
            condition_token(s, at, swap, is_feed)

        @pl.when((n == 2) & jnp.logical_not(is_feed))
        def _():
            for copy in time_outs(s):
                copy.wait()

        @pl.when((n == 2) & (at.pipe < 2))
        def _():
            condition_sum(s, at, swap, is_feed)

        @pl.when((n == 2) & (at.pipe == 3))
        def _():
            outputs()

        @pl.when(n == 3)
        def _():
            @pl.when(at.pipe == 2)
            def _():
                helper.run()
                condition_sum(s, at, swap, is_feed)

            @pl.when(at.pipe < 2)
            def _():
                condition_table(s, at, swap, is_feed)

            @pl.when(at.pipe == 0)
            def _():
                inputs()

        return carry

    for copy in shard_copies(s, is_feed):
        copy.start()
    lax.fori_loop(0, 5, leg, 0)
    matrices = jnp.where(is_feed, 2, 1)

    def rest(k, carry):
        sib_copy(total - 4 + k).wait_send()
        return carry

    lax.fori_loop(0, 4, rest, 0)
    for turn in range(2):
        for slot in range(6):
            last = matrices - 1 if slot >= 2 else jnp.where(at.pipe == 1, 0, matrices - 1)
            near_copy(last, turn, slot).wait_send()

    @pl.when(at.pipe == 1)
    def _():
        for j in range(4):
            up(j).wait_send()

    @pl.when(at.pipe == 2)
    def _():
        helper.done()

    for part in (2, 3):
        grad_copy(s.in_grad, part).wait()

    @pl.when(at.pipe == 3)
    def _():
        condition_sum(s, at, swap, is_feed)

    @pl.when(at.pipe >= 2)
    def _():
        condition_table(s, at, swap, is_feed)


def exchange(s, at, number, piece, landing):
    def copy(target, source):
        return pltpu.make_async_remote_copy(
            src_ref=piece(target),
            dst_ref=landing(source),
            send_sem=s.swap_send.at[number, target],
            recv_sem=s.swap_recv.at[number, source],
            device_id=(target, at.pipe),
            device_id_type=MESH,
        )

    others = [(at.dp + k) % 8 for k in range(1, 8)]

    def start():
        for other in others:
            copy(other, at.dp).start()

    def arrive():
        for other in others:
            copy(other, other).wait_recv()

    def done():
        for other in others:
            copy(other, at.dp).wait_send()

    return SimpleNamespace(start=start, arrive=arrive, done=done)


def exchanges(s, at):
    def pair(j):
        return pl.ds(2 * j, 2)

    return SimpleNamespace(
        rows=exchange(s, at, 0, lambda j: s.cond_in, lambda j: s.rows.at[pair(j)]),
        mods=exchange(s, at, 1, lambda j: s.mod_parts.at[pair(j)], lambda j: s.mod_all.at[j]),
        tokens=exchange(s, at, 2, lambda j: s.token, lambda j: s.token_all.at[pair(j)]),
        times=exchange(s, at, 3, lambda j: s.time_parts.at[pair(j)], lambda j: s.time_all.at[j]),
        grads=exchange(s, at, 4, lambda j: s.grad_rows, lambda j: s.grad_all.at[pair(j)]),
        backs=exchange(s, at, 5, lambda j: s.back, lambda j: s.back_all.at[j]),
        ends=exchange(s, at, 6, lambda j: s.end, lambda j: s.end_all.at[j]),
    )


def shard_copies(s, is_feed):
    copies = []
    for part in range(3):
        cols = pl.ds(part * PART, PART)
        rows = pl.ds(part * BLOCK, BLOCK)
        copies.append((s.mod_shard.at[:, cols], s.norm.at[rows, :]))
        copies.append((s.out_shard.at[:, cols], s.branch.at[rows, :]))
    copies.append((s.out_shard.at[:, pl.ds(3 * PART, PART)], s.gb.at[pl.ds(0, BLOCK), :]))
    return [
        pltpu.make_async_copy(source, target, s.shard_sem.at[k])
        for k, (source, target) in enumerate(copies)
    ]


def shard_part(ref, part):
    return ref[pl.ds(part * BLOCK, BLOCK), :]


def stack_rows(source, target, width):
    for k in range(16):
        target[k : k + 1, 0:width] = source[k, :, 0:width]


def chosen(at):
    places = lax.broadcasted_iota(jnp.int32, (PART, BLOCK), 0)
    lanes = lax.broadcasted_iota(jnp.int32, (PART, BLOCK), 1)
    return jnp.where(places == lanes + at.dp * BLOCK, 1.0, 0.0).astype(low)


def condition_front(s, at, swap, is_feed):
    for copy in shard_copies(s, is_feed):
        copy.start()
    s.rows[pl.ds(2 * at.dp, 2)] = s.cond_in[...]
    s.grad_rows[...] = jnp.zeros(s.grad_rows.shape, jnp.float32)
    swap.rows.arrive()
    stack_rows(s.rows, s.flat, PART)
    condition = s.flat[:, 0:PART]
    conditioner = (condition * (1.0 / (1.0 + jnp.exp(-condition)))).astype(low)
    pick = chosen(at)
    own = product(conditioner, pick).astype(low)
    s.own_cond[...] = own
    for copy in shard_copies(s, is_feed):
        copy.wait()
    for part in range(3):
        s.flat[:, part * PART : (part + 1) * PART] = product(own, shard_part(s.norm, part))
    s.flat[:, 3 * PART : 4 * PART] = product(own, s.gb[0:BLOCK, :])
    for k in range(16):
        s.mod_parts[k] = s.flat[k : k + 1, 0 : 4 * PART]
    swap.mods.start()
    s.mod_all[at.dp] = s.mod_parts[pl.ds(2 * at.dp, 2)]


def condition_mods(s, at, swap, is_feed):
    swap.mods.arrive()
    for i in range(2):
        total = jnp.sum(s.mod_all[:, i], axis=0)
        s.mod[i] = total[:, 0 : 3 * PART]
        s.token[i] = total[:, 3 * PART :]

    @pl.when(jnp.logical_not(is_feed))
    def _():
        swap.tokens.start()
        s.token_all[pl.ds(2 * at.dp, 2)] = s.token[...]


def condition_tokens(s, at, swap, is_feed):
    @pl.when(jnp.logical_not(is_feed))
    def _():
        swap.tokens.arrive()
        stack_rows(s.token_all, s.flat, PART)
        own_token = product(s.flat[:, 0:PART].astype(low), chosen(at)).astype(low)
        s.own_token[...] = own_token
        for part in range(3):
            s.flat[:, part * PART : (part + 1) * PART] = product(
                own_token, shard_part(s.branch, part)
            )
        for k in range(16):
            s.time_parts[k] = s.flat[k : k + 1, 0 : 3 * PART]
        swap.times.start()
        s.time_all[at.dp] = s.time_parts[pl.ds(2 * at.dp, 2)]


def condition_times(s, at, swap, is_feed):
    @pl.when(jnp.logical_not(is_feed))
    def _():
        swap.times.arrive()
        for i in range(2):
            s.time[i] = jnp.sum(s.time_all[:, i], axis=0)


def end_copy(s, at, plane):
    return pltpu.make_async_remote_copy(
        src_ref=s.end_parts.at[at.pipe],
        dst_ref=s.end_parts.at[at.pipe],
        send_sem=s.end_send.at[plane],
        recv_sem=s.end_recv.at[at.pipe],
        device_id=(at.dp, plane),
        device_id_type=MESH,
    )


def end_arrival(s, at, plane):
    return pltpu.make_async_remote_copy(
        src_ref=s.end_parts.at[plane],
        dst_ref=s.end_parts.at[plane],
        send_sem=s.end_send.at[plane],
        recv_sem=s.end_recv.at[plane],
        device_id=(at.dp, plane),
        device_id_type=MESH,
    )


def mod_out(s):
    return pltpu.make_async_copy(
        s.wacc.at[pl.ds(0, BLOCK), :], s.mod_grad.at[0], s.shard_sem.at[0]
    )


def time_outs(s):
    held = s.out_grad.at[0]
    return (
        pltpu.make_async_copy(
            s.wacc.at[pl.ds(0, BLOCK), :], held.at[:, pl.ds(0, 3 * PART)], s.shard_sem.at[0]
        ),
        pltpu.make_async_copy(
            s.acc.at[pl.ds(0, BLOCK), :], held.at[:, pl.ds(3 * PART, PART)], s.shard_sem.at[1]
        ),
    )


def condition_back(s, at, swap, is_feed):
    s.grad_all[pl.ds(2 * at.dp, 2)] = s.grad_rows[...]
    swap.grads.arrive()
    stack_rows(s.grad_all, s.flat, 6 * PART)
    for copy in shard_copies(s, is_feed):
        copy.wait()

    @pl.when(jnp.logical_not(is_feed))
    def _():
        token = jnp.zeros((16, BLOCK), jnp.float32)
        for part in range(3):
            grads = s.flat[:, (3 + part) * PART : (4 + part) * PART].astype(low)
            token += product_nt(grads, shard_part(s.branch, part))
        s.back[...] = product_nt(token.astype(low), chosen(at)).astype(low)
        swap.backs.start()
        s.back_all[at.dp] = s.back[...]

    own = s.own_cond[...]
    s.end[...] = jnp.zeros(s.end.shape, jnp.float32)
    for part in range(3):
        cols = slice(part * PART, (part + 1) * PART)
        grads = s.flat[:, cols].astype(low)
        s.wacc[0:BLOCK, cols] = contract_rows(own, grads)
        s.end[...] += product_nt(grads, shard_part(s.norm, part))
    mod_out(s).start()


def condition_token(s, at, swap, is_feed):
    mod_out(s).wait()

    @pl.when(jnp.logical_not(is_feed))
    def _():
        for part in range(3):
            grads = s.flat[:, (3 + part) * PART : (4 + part) * PART].astype(low)
            s.wacc[0:BLOCK, part * PART : (part + 1) * PART] = contract_rows(
                s.own_token[...], grads
            )
        swap.backs.arrive()
        whole = jnp.zeros((16, PART), jnp.float32)
        for k in range(8):
            whole += s.back_all[k].astype(jnp.float32)
        whole = whole.astype(low)
        s.acc[0:BLOCK, :] = contract_rows(s.own_cond[...], whole)
        s.end[...] += product_nt(whole, s.gb[0:BLOCK, :])
        for copy in time_outs(s):
            copy.start()

    s.end_parts[at.pipe] = s.end[...]
    for k in range(1, 4):
        end_copy(s, at, (at.pipe + k) % 4).start()


def condition_sum(s, at, swap, is_feed):
    for k in range(1, 4):
        end_arrival(s, at, (at.pipe + k) % 4).wait_recv()
    s.end[...] = s.end_parts[0] + s.end_parts[1] + s.end_parts[2] + s.end_parts[3]
    swap.ends.start()
    s.end_all[at.dp] = s.end[...]


def condition_table(s, at, swap, is_feed):
    swap.ends.arrive()
    for k in range(8):
        s.flat[:, BLOCK * k : BLOCK * (k + 1)] = s.end_all[k]
    whole = s.flat[:, 0:PART]
    stack_rows(s.rows, s.flat, PART)
    condition = s.flat[:, 0:PART]
    gate = 1.0 / (1.0 + jnp.exp(-condition))
    grads = whole * (gate * (1.0 + condition * (1.0 - gate)))
    for k in range(3):
        term = grads.astype(low)
        s.terms[16 * k : 16 * (k + 1), :] = term
        grads = grads - term.astype(jnp.float32)
    lanes = lax.broadcasted_iota(jnp.int32, (1, 1024), 1).astype(jnp.float32)
    for k in range(16):
        label = s.rows[k, :, PART : PART + 1]
        s.flat[k : k + 1, 0:1024] = jnp.where(lanes == label, 1.0, 0.0)
    hot = s.flat[:, 0:1024].astype(low)
    for k in range(3):
        s.hot[16 * k : 16 * (k + 1), :] = hot


def condition_done(s, at, swap, is_feed):
    for each in (swap.rows, swap.mods, swap.grads, swap.ends):
        each.done()
    for k in range(1, 4):
        end_copy(s, at, (at.pipe + k) % 4).wait_send()

    @pl.when(jnp.logical_not(is_feed))
    def _():
        for each in (swap.tokens, swap.times, swap.backs):
            each.done()


def mega_body(*refs):
    s = SimpleNamespace(**dict(zip(REFS, refs)))
    at = places()
    is_feed = at.pipe % 2 == 1
    pipe = at.pipe
    barrier = pltpu.get_barrier_semaphore()
    swap = exchanges(s, at)
    targets = [((at.dp + k) % 8, pipe) for k in range(1, 8)]
    targets += [(at.dp, (pipe + k) % 4) for k in range(1, 4)]
    for target in targets:
        pl.semaphore_signal(barrier, inc=1, device_id=target, device_id_type=MESH)
    pl.semaphore_wait(barrier, len(targets))
    swap.rows.start()

    def remote(source, target, send, recv, plane):
        return pltpu.make_async_remote_copy(
            src_ref=source,
            dst_ref=target,
            send_sem=send,
            recv_sem=recv,
            device_id=(at.dp, plane),
            device_id_type=MESH,
        )

    def share(i, plane):
        return pl.ds(pl.multiple_of(i * ROWS + plane * 64, 64), 64)

    def token_copy(i, plane):
        return remote(
            s.tokens.at[i],
            s.xin.at[share(i, plane), :],
            s.share_send.at[0, i],
            s.xin_recv.at[i, plane],
            0,
        )

    def cotangent_copy(i, plane):
        return remote(
            s.cotangent.at[i],
            s.gin.at[share(i, plane), :],
            s.share_send.at[1, i],
            s.gin_recv.at[i, plane],
            3,
        )

    def next_copy(i):
        whole = image_rows(i)
        return remote(
            s.xout.at[whole, :],
            s.xin.at[whole, :],
            s.hop_send.at[0, i],
            s.xin_recv.at[i, 0],
            jnp.minimum(pipe + 1, 3),
        )

    def back_copy(i):
        whole = image_rows(i)
        return remote(
            s.gout.at[whole, :],
            s.gin.at[whole, :],
            s.hop_send.at[1, i],
            s.gin_recv.at[i, 3],
            jnp.maximum(pipe - 1, 0),
        )

    def output_copy(i, plane):
        return remote(
            s.xout.at[share(i, plane), :],
            s.out_tokens.at[i],
            s.final_send.at[0, i, plane],
            s.final_recv.at[0, i],
            plane,
        )

    def input_copy(i, plane):
        return remote(
            s.gout.at[share(i, plane), :],
            s.input_share.at[i],
            s.final_send.at[1, i, plane],
            s.final_recv.at[1, i],
            plane,
        )

    def local(source, target, index):
        return pltpu.make_async_copy(source, target, s.local_sem.at[index])

    own_in = local(s.in_shard, s.wa.at[block_rows(at.dp), :], 0)
    own_out = local(s.out_shard, s.wb.at[block_rows(at.dp), :], 1)
    own_in.start()

    @pl.when(is_feed)
    def _():
        own_out.start()

    for i in range(2):
        own_tokens = local(s.tokens.at[i], s.xin.at[pl.ds(i * ROWS, 64), :], 2 + i)
        own_cotangent = local(s.cotangent.at[i], s.gin.at[pl.ds(i * ROWS + 192, 64), :], 4 + i)

        @pl.when(pipe == 0)
        def _():
            own_tokens.start()

        @pl.when(pipe == 3)
        def _():
            own_cotangent.start()

        @pl.when(pipe != 0)
        def _():
            token_copy(i, pipe).start()

    rounds = (condition_front, condition_mods, condition_tokens, condition_times)

    def between(k):
        if k < 4:
            rounds[k](s, at, swap, is_feed)
        if k == 1:
            for i in range(2):

                @pl.when(pipe != 3)
                def _():
                    cotangent_copy(i, pipe).start()

    def ready(k):
        if k == 0:

            def begin(i, carry):
                local(s.tokens.at[i], s.xin.at[share(i, 0), :], 2 + i).wait()
                for plane in range(1, 4):
                    token_copy(i, plane).wait_recv()
                front(i, s)
                return carry

            lax.fori_loop(0, 2, begin, 0)

        def one(n, carry):
            project(0, s, n)
            return carry

        if k == 1:
            lax.fori_loop(0, 2, one, 0)
        if k == 2:
            project(0, s, 2)
            attend_heads(0, s)

    own_in.wait()

    @pl.when(pipe == 0)
    def _():
        gather_weights(s, at, 4, between, ready)

    @pl.when(pipe == 2)
    def _():
        helper = relay(s, at, 0)

        gather_weights(s, at, 4, between, lambda k: None, before=helper.run)
        helper.done()

    def early(k):
        if k == 6:
            next_copy(0).wait_recv()
            front(0, s)
            feed_up(0, s)

    @pl.when(is_feed)
    def _():
        own_out.wait()

    @pl.when(pipe == 1)
    def _():
        gather_weights(s, at, 8, between, early, relay(s, at, 0), (4, 5, 6, 7))

    @pl.when(pipe == 3)
    def _():
        gather_weights(s, at, 8, between, lambda k: None)

    for i in range(2):

        @pl.when(pipe != 0)
        def _():
            token_copy(i, pipe).wait_send()

    def inputs(i):
        for plane in range(1, 4):
            input_copy(i, plane).start()
        local(s.gout.at[share(i, 0), :], s.input_share.at[i], 4 + i).start()

    def step(n, carry):
        at_end = pipe == 3
        goes_forward = jnp.where(at_end, n % 2 == 0, n < 2)
        i = jnp.where(at_end, n // 2, n % 2)

        @pl.when(goes_forward)
        def _():
            @pl.when((pipe >= 2) | ((pipe == 1) & (i == 1)))
            def _():
                next_copy(i).wait_recv()

            @pl.when(is_feed)
            def _():
                @pl.when((pipe == 3) | (i == 1))
                def _():
                    front(i, s)
                    feed_up(i, s)

                feed_down(i, s)
                finish(i, s)

            @pl.when(jnp.logical_not(is_feed))
            def _():
                @pl.when(pipe != 0)
                def _():
                    front(i, s)

                @pl.when((pipe != 0) | (i == 1))
                def _():
                    def one(part, carry):
                        project(i, s, part)
                        return carry

                    lax.fori_loop(0, 3, one, 0)
                    attend_heads(i, s)

                attend_out(i, s)
                finish(i, s)

            @pl.when((pipe < 2) & (i == 0) & (at.core == 0))
            def _():
                next_copy(0).start()

            @pl.when((pipe < 2) & (i == 1))
            def _():
                @pl.when(at.core == 1)
                def _():
                    pl.semaphore_wait(s.turn, 1)
                    next_copy(0).start()

                next_copy(0).wait_send()
                pl.semaphore_signal(
                    s.turn, inc=1, device_id=(at.sib, pipe), device_id_type=MESH
                )
                pl.semaphore_wait(s.turn, 1)
                next_copy(1).start()
                next_copy(1).wait_send()

                @pl.when(at.core == 0)
                def _():
                    pl.semaphore_signal(
                        s.turn, inc=1, device_id=(at.sib, pipe), device_id_type=MESH
                    )

            @pl.when(pipe == 2)
            def _():
                next_copy(i).start()


        @pl.when(jnp.logical_not(goes_forward))
        def _():
            @pl.when(pipe == 3)
            def _():
                local(s.cotangent.at[i], s.gin.at[share(i, 3), :], 4 + i).wait()
                for plane in range(3):
                    cotangent_copy(i, plane).wait_recv()

            @pl.when(pipe != 3)
            def _():
                back_copy(i).wait_recv()

            @pl.when(is_feed)
            def _():
                kernel_feed_backward(i, s)

            @pl.when(jnp.logical_not(is_feed))
            def _():
                kernel_attention_backward(i, s)

            @pl.when(pipe != 0)
            def _():
                back_copy(i).start()

            @pl.when((pipe == 0) & (i == 0))
            def _():
                inputs(0)

        return carry

    lax.fori_loop(0, 4, step, 0)
    swap.grads.start()

    for target, sem in ((at.sib, 0), (at.x, 1), (at.y, 2)):
        pl.semaphore_signal(
            s.free.at[sem], inc=1, device_id=(target, pipe), device_id_type=MESH
        )
    for sem in range(3):
        pl.semaphore_wait(s.free.at[sem], 1)

    def last_inputs(*unused):
        @pl.when(pipe == 0)
        def _():
            inputs(1)

    def outputs(*unused):
        @pl.when(pipe == 3)
        def _():
            for i in range(2):
                for plane in range(3):
                    output_copy(i, plane).start()
                local(s.xout.at[share(i, 3), :], s.out_tokens.at[i], 2 + i).start()

    scatter_grads(s, at, is_feed, swap, outputs, last_inputs)
    condition_done(s, at, swap, is_feed)

    for i in range(2):

        @pl.when(pipe != 3)
        def _():
            cotangent_copy(i, pipe).wait_send()
            output_copy(i, pipe).wait_recv()

        @pl.when(pipe == 2)
        def _():
            next_copy(i).wait_send()

        @pl.when(pipe == 3)
        def _():
            for plane in range(3):
                output_copy(i, plane).wait_send()
            local(s.xout.at[share(i, 3), :], s.out_tokens.at[i], 2 + i).wait()

        @pl.when(pipe != 0)
        def _():
            back_copy(i).wait_send()
            input_copy(i, pipe).wait_recv()

        @pl.when(pipe == 0)
        def _():
            for plane in range(1, 4):
                input_copy(i, plane).wait_send()
            local(s.gout.at[share(i, 0), :], s.input_share.at[i], 4 + i).wait()

    s.input_grad[...] = s.input_share[...].astype(jnp.float32)


SCRATCH = dict(
    xin=pltpu.VMEM((512, 1152), low),
    gin=pltpu.VMEM((512, 1152), low),
    xout=pltpu.VMEM((512, 1152), low),
    gout=pltpu.VMEM((512, 1152), low),
    wa=pltpu.VMEM((1152, 4608), low),
    wb=pltpu.VMEM((1152, 4608), low),
    norm=pltpu.VMEM((512, 1152), low),
    left=pltpu.VMEM((2, 1152, 512), low),
    wide=pltpu.VMEM((2, 512, 4608), low),
    branch=pltpu.VMEM((512, 1152), low),
    acc=pltpu.VMEM((256, 1152), jnp.float32),
    gb=pltpu.VMEM((256, 1152), low),
    wacc=pltpu.VMEM((256, 3456), jnp.float32),
    stage=pltpu.VMEM((4, 288, 1152), low),
    near_stage=pltpu.VMEM((2, 6, 144, 1152), low),
    gather_send=pltpu.SemaphoreType.DMA((8, 8)),
    gather_recv=pltpu.SemaphoreType.DMA((8, 8)),
    sib_send=pltpu.SemaphoreType.DMA((32,)),
    sib_recv=pltpu.SemaphoreType.DMA((32,)),
    near_send=pltpu.SemaphoreType.DMA((2, 12)),
    near_recv=pltpu.SemaphoreType.DMA((2, 12)),
    out_sem=pltpu.SemaphoreType.DMA((2,)),
    share_send=pltpu.SemaphoreType.DMA((2, 2)),
    xin_recv=pltpu.SemaphoreType.DMA((2, 4)),
    gin_recv=pltpu.SemaphoreType.DMA((2, 4)),
    hop_send=pltpu.SemaphoreType.DMA((2, 2)),
    final_send=pltpu.SemaphoreType.DMA((2, 2, 4)),
    final_recv=pltpu.SemaphoreType.DMA((2, 2)),
    local_sem=pltpu.SemaphoreType.DMA((6,)),
    free=pltpu.SemaphoreType.REGULAR((3,)),
    turn=pltpu.SemaphoreType.REGULAR,
    shard_sem=pltpu.SemaphoreType.DMA((7,)),
    swap_send=pltpu.SemaphoreType.DMA((7, 8)),
    swap_recv=pltpu.SemaphoreType.DMA((7, 8)),
    relay_send=pltpu.SemaphoreType.DMA((2, 4, 6)),
    relay_recv=pltpu.SemaphoreType.DMA((2, 4, 6)),
    end_send=pltpu.SemaphoreType.DMA((4,)),
    end_recv=pltpu.SemaphoreType.DMA((4,)),
    mod=pltpu.VMEM((2, 1, 3456), jnp.float32),
    time=pltpu.VMEM((2, 1, 3456), jnp.float32),
    token=pltpu.VMEM((2, 1, 1152), jnp.float32),
    grad_rows=pltpu.VMEM((2, 1, 6912), jnp.float32),
    rows=pltpu.VMEM((16, 1, 1280), jnp.float32),
    flat=pltpu.VMEM((16, 6912), jnp.float32),
    own_cond=pltpu.VMEM((16, 144), low),
    own_token=pltpu.VMEM((16, 144), low),
    mod_parts=pltpu.VMEM((16, 1, 4608), jnp.float32),
    mod_all=pltpu.VMEM((8, 2, 1, 4608), jnp.float32),
    token_all=pltpu.VMEM((16, 1, 1152), jnp.float32),
    time_parts=pltpu.VMEM((16, 1, 3456), jnp.float32),
    time_all=pltpu.VMEM((8, 2, 1, 3456), jnp.float32),
    grad_all=pltpu.VMEM((16, 1, 6912), jnp.float32),
    back=pltpu.VMEM((16, 1152), low),
    back_all=pltpu.VMEM((8, 16, 1152), low),
    end=pltpu.VMEM((16, 144), jnp.float32),
    input_share=pltpu.VMEM((2, 64, 1152), low),
    end_parts=pltpu.VMEM((4, 16, 144), jnp.float32),
    end_all=pltpu.VMEM((8, 16, 144), jnp.float32),
)
REFS = (
    ["tokens", "cotangent", "in_shard", "out_shard", "mod_shard", "cond_in"]
    + ["out_tokens", "input_grad", "terms", "hot", "in_grad", "out_grad", "mod_grad"]
    + list(SCRATCH)
)


def mega(tokens, cotangent, in_shard, out_shard, mod_shard, cond_rows):
    anywhere = pl.BlockSpec(memory_space=pl.ANY)
    near = pl.BlockSpec(memory_space=pltpu.VMEM)

    def wide(array):
        return jax.ShapeDtypeStruct((1,) + array.shape, jnp.float32)

    return pl.pallas_call(
        mega_body,
        out_shape=(
            jax.ShapeDtypeStruct(tokens.shape, low),
            jax.ShapeDtypeStruct(tokens.shape, jnp.float32),
            jax.ShapeDtypeStruct((48, tokens.shape[2]), low),
            jax.ShapeDtypeStruct((48, 1024), low),
            wide(in_shard),
            wide(out_shard),
            wide(mod_shard),
        ),
        in_specs=[anywhere] * 5 + [near],
        out_specs=[anywhere] + [near] * 3 + [anywhere] * 3,
        scratch_shapes=list(SCRATCH.values()),
        compiler_params=pltpu.CompilerParams(
            collective_id=0, has_side_effects=True, vmem_limit_bytes=62 * 2**20
        ),
        cost_estimate=pl.CostEstimate(
            flops=25 * 10**9, bytes_accessed=10**7, transcendentals=10**7
        ),
        name="blocks",
    )(tokens, cotangent, in_shard, out_shard, mod_shard, cond_rows)


def last_body(terms, hot, *refs):
    sources, (table, *targets) = refs[:3], refs[3:7]
    value, *held, sems = refs[7:]
    classes = table.shape[0]
    pieces = [
        (source.at[0, pl.ds(48 * part, 48), :], stage.at[pl.ds(48 * part, 48), :],
         target.at[0, pl.ds(48 * part, 48), :], 3 * k + part)
        for k, (source, stage, target) in enumerate(zip(sources, held, targets))
        for part in range(3)
    ]
    takes = [pltpu.make_async_copy(s, v, sems.at[0, n]) for s, v, t, n in pieces]
    gives = [pltpu.make_async_copy(v, t, sems.at[1, n]) for s, v, t, n in pieces]
    for take in takes:
        take.start()
    for k in range(4):
        count = min(256, classes - 256 * k)
        value[k] = contract_rows(hot[:, 256 * k : 256 * (k + 1)], terms[...])
        part = pltpu.make_async_copy(
            value.at[k, pl.ds(0, count), :],
            table.at[pl.ds(256 * k, count), :],
            sems.at[1, 9 + k],
        )
        part.start()
        gives.append(part)
    for take, give in zip(takes, gives):
        take.wait()
        give.start()
    for give in gives:
        give.wait()


def last_copies(terms, hot, grads, classes):
    anywhere = pl.BlockSpec(memory_space=pl.ANY)
    near = pl.BlockSpec(memory_space=pltpu.VMEM)
    width = terms.shape[1]
    return pl.pallas_call(
        last_body,
        out_shape=[jax.ShapeDtypeStruct((classes, width), jnp.float32)]
        + [jax.ShapeDtypeStruct(grad.shape, jnp.float32) for grad in grads],
        in_specs=[near, near] + [anywhere] * 3,
        out_specs=[anywhere] * 4,
        scratch_shapes=[
            pltpu.VMEM((4, 256, width), jnp.float32),
            *[pltpu.VMEM(grad.shape[1:], jnp.float32) for grad in grads],
            pltpu.SemaphoreType.DMA((2, 13)),
        ],
        compiler_params=pltpu.CompilerParams(vmem_limit_bytes=62 * 2**20),
        name="table",
    )(terms, hot, *grads)


def fast_shards(
    tokens,
    cotangent,
    timesteps,
    labels,
    class_table,
    section_in_weights,
    section_out_weights,
    modulation_weights,
):
    model_width = tokens.shape[2]
    in_shard, out_shard, mod_shard = (
        section_in_weights[0],
        section_out_weights[0],
        modulation_weights[0],
    )
    images = tokens.shape[0]
    classes = class_table.shape[0]
    matches = labels[:, None] == lax.broadcasted_iota(jnp.int32, (images, classes), 1)
    condition = sinusoid(timesteps, model_width) + product(
        matches.astype(jnp.bfloat16), class_table
    )
    named = jnp.broadcast_to(labels.astype(jnp.float32)[:, None], (images, 128))
    cond_rows = jnp.concatenate([condition, named], axis=1)[:, None, :]
    out_tokens, input_grad, terms, hot, *grads = mega(
        tokens, cotangent, in_shard, out_shard, mod_shard, cond_rows
    )
    return (out_tokens, input_grad, *last_copies(terms, hot, grads, classes))


def solution(mesh):
    return jax.shard_map(
        fast_shards if mesh.shape["dp"] == 8 else shards,
        mesh=mesh,
        in_specs=(
            P("dp", "pipe", None),
            P("dp", "pipe", None),
            P("dp"),
            P("dp"),
            P(),
            P("pipe", "dp", None),
            P("pipe", "dp", None),
            P("pipe", "dp", None),
        ),
        out_specs=(
            P("dp", "pipe", None),
            P("dp", "pipe", None),
            P(),
            P("pipe", "dp", None),
            P("pipe", "dp", None),
            P("pipe", "dp", None),
        ),
        check_vma=False,
    )
```

```python
from functools import partial
import math
from types import SimpleNamespace

import jax
import jax.numpy as jnp
from jax import lax
from jax.experimental import pallas as pl
from jax.experimental.pallas import tpu as pltpu
from jax.sharding import PartitionSpec as P

HEADS = 16
HEAD = 72


epsilon = 1e-06
highest = lax.Precision.HIGHEST


def shifted(block, axis, distance):
    devices = range(lax.axis_size(axis))
    route = [(i - distance, i) for i in devices if i - distance in devices]
    return lax.ppermute(block, axis, route)


def sinusoid(step_values, model_width):
    half_width = model_width // 2
    frequencies = jnp.exp(
        -math.log(10000.0) * jnp.arange(half_width, dtype=jnp.float32) / half_width
    )
    angles = step_values.astype(jnp.float32)[:, None] * frequencies[None, :]
    return jnp.concatenate([jnp.cos(angles), jnp.sin(angles)], axis=1)


def product(former, latter):
    return jnp.dot(former, latter, preferred_element_type=jnp.float32)


def contract_rows(former, latter):
    return lax.dot_general(
        former, latter, (((0,), (0,)), ((), ())), preferred_element_type=jnp.float32
    )


def contract_cols(former, latter):
    return lax.dot_general(
        former, latter, (((1,), (1,)), ((), ())), preferred_element_type=jnp.float32
    )


def normalize_rows(row_values):
    centered = row_values - jnp.mean(row_values, axis=-1, keepdims=True)
    inverse = lax.rsqrt(jnp.mean(centered * centered, axis=-1, keepdims=True) + epsilon)
    return (centered * inverse, inverse)


def modulation_front(section_input, mod_row):
    model_width = section_input.shape[1]
    shift_vec = mod_row[:model_width]
    scale_vec = mod_row[model_width : 2 * model_width]
    gate_vec = mod_row[2 * model_width :]
    centred, inverse = normalize_rows(section_input.astype(jnp.float32))
    normed = (centred * (1.0 + scale_vec) + shift_vec).astype(jnp.bfloat16)
    return (normed, centred, inverse, scale_vec, gate_vec)


def modulation_back(grad_normed, centred, inverse, scale_vec, grad_rows, grad_gate):
    grad_shift = jnp.sum(grad_normed, axis=0)
    grad_scale = jnp.sum(grad_normed * centred, axis=0)
    grad_centred = grad_normed * (1.0 + scale_vec)
    grad_input = inverse * (
        grad_centred
        - jnp.mean(grad_centred, axis=-1, keepdims=True)
        - centred * jnp.mean(grad_centred * centred, axis=-1, keepdims=True)
    )
    grad_mod = jnp.concatenate([grad_shift, grad_scale, grad_gate]).astype(jnp.bfloat16)
    return (grad_rows + grad_input, grad_mod)


def attention_parts(section_input, mod_row, time_row, weights):
    in_weight = weights[0]
    model_width = section_input.shape[1]
    tok_len = section_input.shape[0]
    normed, centred, inverse, scale_vec, gate_vec = modulation_front(section_input, mod_row)
    qkv = (product(normed, in_weight[:, : 3 * model_width]) + time_row).astype(jnp.bfloat16)
    split_qkv = qkv.reshape(tok_len, 3, HEADS, HEAD)
    queries = split_qkv[:, 0]
    keyed = split_qkv[:, 1]
    valued = split_qkv[:, 2]
    scores = jnp.einsum(
        "qhd,khd->hqk", queries, keyed, preferred_element_type=jnp.float32
    ) * HEAD ** (-0.5)
    probs_full = jax.nn.softmax(scores, axis=-1)
    probs_low = probs_full.astype(jnp.bfloat16)
    mixed = jnp.einsum("hqk,khd->qhd", probs_low, valued, preferred_element_type=jnp.float32)
    head_rows = mixed.reshape(tok_len, model_width).astype(jnp.bfloat16)
    branch = product(head_rows, in_weight[:, 3 * model_width :])
    section_output = section_input.astype(jnp.float32) + gate_vec * branch
    saved_parts = (
        normed,
        centred,
        inverse,
        scale_vec,
        gate_vec,
        queries,
        keyed,
        valued,
        probs_full,
        probs_low,
        head_rows,
        branch,
    )
    return (section_output, saved_parts)


def attention_forward(section_input, mod_row, time_row, weights):
    return attention_parts(section_input, mod_row, time_row, weights)[0]


def attention_backward(section_input, grad_in, mod_row, time_row, weights):
    in_weight = weights[0]
    model_width = section_input.shape[1]
    tok_len = section_input.shape[0]
    unused, saved_parts = attention_parts(section_input, mod_row, time_row, weights)
    (
        normed,
        centred,
        inverse,
        scale_vec,
        gate_vec,
        queries,
        keyed,
        valued,
        probs_full,
        probs_low,
        head_rows,
        branch,
    ) = saved_parts
    grad_rows = grad_in.astype(jnp.float32)
    grad_branch = (gate_vec * grad_rows).astype(jnp.bfloat16)
    grad_gate = jnp.sum(grad_rows * branch, axis=0)
    grad_heads = contract_cols(grad_branch, in_weight[:, 3 * model_width :]).astype(jnp.bfloat16)
    heads_split = grad_heads.reshape(tok_len, HEADS, HEAD)
    grad_probs = jnp.einsum("qhd,khd->hqk", heads_split, valued, preferred_element_type=jnp.float32)
    grad_value = jnp.einsum(
        "hqk,qhd->khd", probs_low, heads_split, preferred_element_type=jnp.float32
    )
    grad_scores = (
        probs_full * (grad_probs - jnp.sum(probs_full * grad_probs, axis=-1, keepdims=True))
    ).astype(jnp.bfloat16)
    grad_query = jnp.einsum(
        "hqk,khd->qhd", grad_scores, keyed, preferred_element_type=jnp.float32
    ) * HEAD ** (-0.5)
    grad_key = jnp.einsum(
        "hqk,qhd->khd", grad_scores, queries, preferred_element_type=jnp.float32
    ) * HEAD ** (-0.5)
    grad_qkv = (
        jnp.stack([grad_query, grad_key, grad_value], axis=1)
        .reshape(tok_len, 3 * model_width)
        .astype(jnp.bfloat16)
    )
    grad_normed = contract_cols(grad_qkv, in_weight[:, : 3 * model_width])
    grad_time = jnp.sum(grad_qkv, axis=0, dtype=jnp.float32).astype(jnp.bfloat16)
    grad_input, grad_mod = modulation_back(
        grad_normed, centred, inverse, scale_vec, grad_rows, grad_gate
    )
    narrow_zero = jnp.zeros((tok_len, model_width), jnp.bfloat16)
    return (
        grad_input,
        normed,
        jnp.concatenate([grad_qkv, narrow_zero], axis=1),
        grad_branch,
        jnp.concatenate([head_rows, narrow_zero, narrow_zero, narrow_zero], axis=1),
        grad_mod,
        grad_time,
    )


def feed_parts(section_input, mod_row, weights):
    in_weight, out_weight = weights
    normed, centred, inverse, scale_vec, gate_vec = modulation_front(section_input, mod_row)
    pre_act = product(normed, in_weight)
    hidden = jax.nn.gelu(pre_act, approximate=True).astype(jnp.bfloat16)
    branch = contract_cols(hidden, out_weight)
    section_output = section_input.astype(jnp.float32) + gate_vec * branch
    return (
        section_output,
        (normed, centred, inverse, scale_vec, gate_vec, pre_act, hidden, branch),
    )


def feed_forward(section_input, mod_row, time_row, weights):
    return feed_parts(section_input, mod_row, weights)[0]


def feed_backward(section_input, grad_in, mod_row, time_row, weights):
    in_weight, out_weight = weights
    unused, saved_parts = feed_parts(section_input, mod_row, weights)
    normed, centred, inverse, scale_vec, gate_vec, pre_act, hidden, branch = saved_parts
    grad_rows = grad_in.astype(jnp.float32)
    grad_branch = (gate_vec * grad_rows).astype(jnp.bfloat16)
    grad_gate = jnp.sum(grad_rows * branch, axis=0)
    grad_hidden = product(grad_branch, out_weight)
    gelu_pull = jax.vjp(partial(jax.nn.gelu, approximate=True), pre_act)[1]
    grad_pre = gelu_pull(grad_hidden)[0].astype(jnp.bfloat16)
    grad_normed = contract_cols(grad_pre, in_weight)
    grad_input, grad_mod = modulation_back(
        grad_normed, centred, inverse, scale_vec, grad_rows, grad_gate
    )
    return (
        grad_input,
        normed,
        grad_pre,
        grad_branch,
        hidden,
        grad_mod,
        jnp.zeros(grad_mod.shape, jnp.bfloat16),
    )


def spare_forward(section_input, mod_row, time_row, weights):
    return jnp.zeros(section_input.shape, jnp.float32)


def spare_backward(section_input, grad_in, mod_row, time_row, weights):
    tok_len, model_width = section_input.shape
    hidden_width = weights[0].shape[1]
    narrow_zero = jnp.zeros((tok_len, model_width), jnp.bfloat16)
    wide_zero = jnp.zeros((tok_len, hidden_width), jnp.bfloat16)
    row_zero = jnp.zeros((3 * model_width,), jnp.bfloat16)
    return (
        jnp.zeros(section_input.shape, jnp.float32),
        narrow_zero,
        wide_zero,
        narrow_zero,
        wide_zero,
        row_zero,
        row_zero,
    )


def attention_weight_grads(left_one, right_one, left_two, right_two):
    width = left_two.shape[1]
    low = jnp.bfloat16
    qkv_term = contract_rows(left_one, right_one[:, : 3 * width]).astype(low)
    out_term = contract_rows(right_two[:, :width], left_two).astype(low)
    zero_term = jnp.zeros((width, right_two.shape[1]), low)
    return (jnp.concatenate([qkv_term, out_term], axis=1), zero_term)


def feed_weight_grads(left_one, right_one, left_two, right_two):
    low = jnp.bfloat16
    return (
        contract_rows(left_one, right_one).astype(low),
        contract_rows(left_two, right_two).astype(low),
    )


def replace_slot(buffer, slot_index, new_rows, active):
    old_rows = lax.dynamic_index_in_dim(buffer, slot_index, 0, keepdims=False)
    return lax.dynamic_update_index_in_dim(
        buffer, jnp.where(active, new_rows, old_rows), slot_index, 0
    )


def shards(
    tokens,
    cotangent,
    timesteps,
    labels,
    class_table,
    section_in_weights,
    section_out_weights,
    modulation_weights,
):
    micro_count = tokens.shape[0]
    model_width = tokens.shape[2]
    hidden_width = section_in_weights.shape[2]
    section_count = lax.axis_size("pipe")
    section_index = lax.axis_index("pipe")
    last_section = section_count - 1
    section_kind = 1 + section_index % 2
    in_shard, out_shard, mod_shard = (
        section_in_weights[0],
        section_out_weights[0],
        modulation_weights[0],
    )
    whole_tokens, whole_cotangent = (
        lax.all_gather(tokens, "pipe", axis=1, tiled=True),
        lax.all_gather(cotangent, "pipe", axis=1, tiled=True),
    )
    tok_len = whole_tokens.shape[1]
    weights = (
        lax.all_gather(in_shard, "dp", axis=0, tiled=True),
        lax.all_gather(out_shard, "dp", axis=0, tiled=True),
    )
    condition, own_conditioner, own_time, matches, mod_rows, time_rows = conditioning(
        timesteps, labels, class_table, out_shard, mod_shard
    )

    def forward_tick(carry, tick_index):
        incoming, kept_inputs, finals = carry
        micro_index = tick_index - section_index
        active = (micro_index >= 0) & (micro_index < micro_count)
        slot_index = jnp.clip(micro_index, 0, micro_count - 1)
        first_rows = lax.dynamic_index_in_dim(whole_tokens, slot_index, 0, keepdims=False)
        section_input = jnp.where(section_index == 0, first_rows, incoming)
        section_output = lax.switch(
            jnp.where(active, section_kind, 0),
            (spare_forward, attention_forward, feed_forward),
            section_input,
            lax.dynamic_index_in_dim(mod_rows, slot_index, 0, keepdims=False),
            lax.dynamic_index_in_dim(time_rows, slot_index, 0, keepdims=False),
            weights,
        )
        output_low = section_output.astype(jnp.bfloat16)
        kept_inputs = replace_slot(kept_inputs, slot_index, section_input, active)
        finals = replace_slot(
            finals, slot_index, output_low, active & (section_index == last_section)
        )
        incoming = shifted(output_low, "pipe", 1)
        return ((incoming, kept_inputs, finals), None)

    empty_rows = jnp.zeros((tok_len, model_width), jnp.bfloat16)
    empty_store = jnp.zeros((micro_count, tok_len, model_width), jnp.bfloat16)
    forward_out, ignored = lax.scan(
        forward_tick,
        (empty_rows, empty_store, empty_store),
        jnp.arange(micro_count + section_count - 1),
    )
    kept_inputs = forward_out[1]
    finals = forward_out[2]
    wide_store = jnp.zeros((micro_count, tok_len, hidden_width), jnp.bfloat16)
    row_store = jnp.zeros((micro_count, 3 * model_width), jnp.bfloat16)
    start_factors = (empty_store, wide_store, empty_store, wide_store, row_store, row_store)

    def backward_tick(carry, tick_index):
        incoming, factors, input_grads = carry
        micro_index = tick_index - (last_section - section_index)
        active = (micro_index >= 0) & (micro_index < micro_count)
        slot_index = jnp.clip(micro_index, 0, micro_count - 1)
        top_grad = lax.dynamic_index_in_dim(whole_cotangent, slot_index, 0, keepdims=False)
        grad_in = jnp.where(section_index == last_section, top_grad, incoming)
        section_input = lax.dynamic_index_in_dim(kept_inputs, slot_index, 0, keepdims=False)
        results = lax.switch(
            jnp.where(active, section_kind, 0),
            (spare_backward, attention_backward, feed_backward),
            section_input,
            grad_in,
            lax.dynamic_index_in_dim(mod_rows, slot_index, 0, keepdims=False),
            lax.dynamic_index_in_dim(time_rows, slot_index, 0, keepdims=False),
            weights,
        )
        grad_low = results[0].astype(jnp.bfloat16)
        factors = tuple(
            (
                replace_slot(buffer, slot_index, fresh, active)
                for buffer, fresh in zip(factors, results[1:])
            )
        )
        input_grads = replace_slot(
            input_grads, slot_index, grad_low, active & (section_index == 0)
        )
        incoming = shifted(grad_low, "pipe", -1)
        return ((incoming, factors, input_grads), None)

    backward_out, ignored = lax.scan(
        backward_tick,
        (empty_rows, start_factors, empty_store),
        jnp.arange(micro_count + section_count - 1),
    )
    factors = backward_out[1]
    input_grads = backward_out[2]
    flat_rows = micro_count * tok_len
    left_one, right_one, left_two, right_two = (
        stored.reshape(flat_rows, stored.shape[2]) for stored in factors[:4]
    )
    in_term, out_term = lax.cond(
        section_index % 2 == 0,
        attention_weight_grads,
        feed_weight_grads,
        left_one,
        right_one,
        left_two,
        right_two,
    )
    in_grad = lax.psum_scatter(in_term, "dp", scatter_dimension=0, tiled=True)
    out_grad = lax.psum_scatter(out_term, "dp", scatter_dimension=0, tiled=True)
    own_out, own_in = (finals, input_grads)
    keep_out = jnp.where(section_index == last_section, own_out, 0)
    keep_in = jnp.where(section_index == 0, own_in, 0)
    output_share = lax.psum_scatter(keep_out, "pipe", scatter_dimension=1, tiled=True)
    input_share = lax.psum_scatter(keep_in, "pipe", scatter_dimension=1, tiled=True)
    small_outs = conditioning_grads(
        factors[4],
        factors[5],
        condition,
        own_conditioner,
        own_time,
        matches,
        out_shard,
        mod_shard,
        out_grad,
    )
    return (
        output_share,
        input_share.astype(jnp.float32),
        small_outs[0],
        in_grad.astype(jnp.float32)[None],
        small_outs[1][None],
        small_outs[2][None],
    )


def conditioning_grads(
    mod_grads,
    time_grads,
    condition,
    own_conditioner,
    own_time,
    matches,
    out_shard,
    mod_shard,
    out_grad,
):
    model_width = condition.shape[1]
    is_attention = lax.axis_index("pipe") % 2 == 0
    all_mod = lax.all_gather(mod_grads, "dp", axis=0, tiled=True)
    all_time = lax.all_gather(time_grads, "dp", axis=0, tiled=True)
    grad_mod_shard = contract_rows(own_conditioner, all_mod)
    cond_grads = contract_cols(all_mod, mod_shard)
    own_token = contract_cols(all_time, out_shard[:, : 3 * model_width]).astype(jnp.bfloat16)
    all_token = lax.all_gather(own_token, "dp", axis=1, tiled=True)
    token_grads = contract_cols(all_token, out_shard[:, 3 * model_width :])
    cond_grads = cond_grads + jnp.where(is_attention, token_grads, 0.0)
    time_out = jnp.concatenate(
        [contract_rows(own_time, all_time), contract_rows(own_conditioner, all_token)], axis=1
    )
    grad_out_shard = jnp.where(is_attention, time_out, out_grad.astype(jnp.float32))
    every_part = lax.all_gather(cond_grads, "pipe", axis=0)
    whole_grads = lax.all_gather(jnp.sum(every_part, axis=0), "dp", axis=1, tiled=True)
    grad_condition = jax.vjp(jax.nn.silu, condition)[1](whole_grads)[0]
    grad_table = lax.dot_general(
        matches.astype(jnp.float32),
        grad_condition,
        (((0,), (0,)), ((), ())),
        precision=highest,
        preferred_element_type=jnp.float32,
    )
    return (grad_table, grad_out_shard, grad_mod_shard)


def conditioning(timesteps, labels, class_table, out_shard, mod_shard):
    model_width = class_table.shape[1]
    own_rows = out_shard.shape[0]
    own_start = lax.axis_index("dp") * own_rows
    all_steps = lax.all_gather(timesteps, "dp", axis=0, tiled=True)
    all_labels = lax.all_gather(labels, "dp", axis=0, tiled=True)
    image_count = all_steps.shape[0]
    classes = class_table.shape[0]
    matches = all_labels[:, None] == lax.broadcasted_iota(jnp.int32, (image_count, classes), 1)
    condition = sinusoid(all_steps, model_width) + product(
        matches.astype(jnp.bfloat16), class_table
    )
    conditioner = jax.nn.silu(condition).astype(jnp.bfloat16)
    own_conditioner = lax.dynamic_slice_in_dim(conditioner, own_start, own_rows, 1)
    mod_rows = lax.psum_scatter(
        product(own_conditioner, mod_shard), "dp", scatter_dimension=0, tiled=True
    )
    own_time = lax.psum_scatter(
        product(own_conditioner, out_shard[:, 3 * model_width :]),
        "dp",
        scatter_dimension=1,
        tiled=True,
    ).astype(jnp.bfloat16)
    time_rows = lax.psum_scatter(
        product(own_time, out_shard[:, : 3 * model_width]), "dp", scatter_dimension=0, tiled=True
    )
    return (condition, own_conditioner, own_time, matches, mod_rows, time_rows)


ROWS = 256
SPAN = 2304
THIRD = 1152
PART = 1152
BLOCK = 144
GROUP = 4
MESH = pl.DeviceIdType.MESH
low = jnp.bfloat16
GELU_A = math.sqrt(2.0 / math.pi)
GELU_B = 0.044715


def product_nt(former, latter):
    return contract_cols(former, latter)


def spread(index, width):
    return pl.ds(pl.multiple_of(index * width, 128), width)


def image_rows(i):
    return pl.ds(pl.multiple_of(i * ROWS, ROWS), ROWS)


def block_rows(b):
    return pl.ds(pl.multiple_of(b * BLOCK, 16), BLOCK)


def front(i, s):
    rows = image_rows(i)
    xhat, inverse = normalize_rows(s.xin[rows, :].astype(jnp.float32))
    normed = (xhat * (1.0 + s.mod[i, :, PART : 2 * PART]) + s.mod[i, :, 0:PART]).astype(low)
    s.norm[rows, :] = normed
    s.left[0, :, rows] = normed.T


def finish(i, s):
    rows = image_rows(i)
    branch = s.acc[...]
    s.branch[rows, :] = branch.astype(low)
    gate = s.mod[i, :, 2 * PART : 3 * PART]
    s.xout[rows, :] = (s.xin[rows, :].astype(jnp.float32) + gate * branch).astype(low)


def bent(value):
    square = value * value
    wave = jnp.tanh(value * (GELU_A + (GELU_A * GELU_B) * square))
    half = 0.5 + 0.5 * wave
    slope = half + value * (0.5 - 0.5 * (wave * wave)) * (
        GELU_A + (3.0 * GELU_A * GELU_B) * square
    )
    return (value * half).astype(low), slope.astype(low)


def feed_up(i, s):
    rows = image_rows(i)

    def tile(j, carry):
        cols = spread(j, SPAN)
        hidden, slope = bent(product(s.norm[rows, :], s.wa[:, cols]))
        s.wide[0, rows, cols] = hidden
        s.wide[1, rows, cols] = slope
        return carry

    lax.fori_loop(0, s.wa.shape[1] // SPAN, tile, 0)


def feed_down(i, s):
    rows = image_rows(i)

    def tile(j, carry):
        some = pl.ds(pl.multiple_of(j * 384, 384), 384)
        s.acc[:, spread(j, 384)] = product_nt(s.wide[0, rows, :], s.wb[some, :])
        return carry

    lax.fori_loop(0, PART // 384, tile, 0)


def feed_down_up(i, s):
    rows = image_rows(i)
    s.acc[...] = jnp.zeros(s.acc.shape, jnp.float32)

    def tile(j, carry):
        cols = spread(j, SPAN)
        grad_hidden = product(s.gb[...], s.wb[:, cols])
        grad_pre = (grad_hidden * s.wide[1, rows, cols].astype(jnp.float32)).astype(low)
        s.wide[1, rows, cols] = grad_pre
        s.acc[...] += product_nt(grad_pre, s.wa[:, cols])
        return carry

    lax.fori_loop(0, s.wa.shape[1] // SPAN, tile, 0)


def back_start(i, s):
    rows = image_rows(i)
    grad = s.gin[rows, :].astype(jnp.float32)
    gb = (s.mod[i, :, 2 * PART : 3 * PART] * grad).astype(low)
    s.gb[...] = gb
    s.grad_rows[i, :, 2 * PART : 3 * PART] = jnp.sum(
        grad * s.branch[rows, :].astype(jnp.float32), axis=0, keepdims=True
    )
    return gb


def back_finish(i, s):
    rows = image_rows(i)
    xhat, inverse = normalize_rows(s.xin[rows, :].astype(jnp.float32))
    gn = s.acc[...]
    s.grad_rows[i, :, 0:PART] = jnp.sum(gn, axis=0, keepdims=True)
    s.grad_rows[i, :, PART : 2 * PART] = jnp.sum(gn * xhat, axis=0, keepdims=True)
    gx = gn * (1.0 + s.mod[i, :, PART : 2 * PART])
    first = jnp.mean(gx, axis=-1, keepdims=True)
    second = jnp.mean(gx * xhat, axis=-1, keepdims=True)
    grad = s.gin[rows, :].astype(jnp.float32)
    s.gout[rows, :] = (grad + inverse * (gx - first - xhat * second)).astype(low)


def kernel_feed_backward(i, s):
    gb = back_start(i, s)
    s.left[1, :, image_rows(i)] = gb.T
    feed_down_up(i, s)
    back_finish(i, s)


def project(i, s, part):
    rows = image_rows(i)

    def tile(j, carry):
        cols = pl.ds(pl.multiple_of(part * PART + j * THIRD, 128), THIRD)
        value = product(s.norm[rows, :], s.wa[:, cols]) + s.time[i, :, cols]
        s.wide[0, rows, cols] = value.astype(low)
        return carry

    lax.fori_loop(0, PART // THIRD, tile, 0)


def head_window(h):
    start = jnp.minimum((h * HEAD) // 128, PART // 128 - 2)
    offset = h * HEAD - start * 128
    lanes = lax.broadcasted_iota(jnp.int32, (ROWS, 256), 1)
    inside = (lanes >= offset) & (lanes < offset + HEAD)
    return start, inside


def window(start, part):
    return pl.ds(pl.multiple_of(part * PART + start * 128, 128), 256)


def prob_place(i, h):
    return (
        pl.ds(pl.multiple_of((h % 4) * ROWS, ROWS), ROWS),
        pl.ds(pl.multiple_of((4 * i + h // 4) * ROWS, ROWS), ROWS),
    )


def attend_heads(i, s):
    rows = image_rows(i)
    s.acc[...] = jnp.zeros(s.acc.shape, jnp.float32)
    zero = jnp.zeros((), low)

    def score(h, slot):
        start, inside = head_window(h)
        query = jnp.where(inside, s.wide[0, rows, window(start, 0)], zero)
        s.wacc[:, spread(slot, ROWS)] = product_nt(query, s.wide[0, rows, window(start, 1)])

    def soften(h, slot):
        scores = s.wacc[:, spread(slot, ROWS)]
        top = jnp.max(scores, axis=-1, keepdims=True)
        powers = jnp.exp2((scores - top) * (HEAD ** (-0.5) * math.log2(math.e)))
        place = prob_place(i, h)
        s.wb[place[0], place[1]] = (
            powers * (1.0 / jnp.sum(powers, axis=-1, keepdims=True))
        ).astype(low)

    def mix(h):
        start, inside = head_window(h)
        place = prob_place(i, h)
        value = jnp.where(inside, s.wide[0, rows, window(start, 2)], zero)
        s.acc[:, window(start, 0)] += product(s.wb[place[0], place[1]], value)

    for k in range(GROUP):
        score(k, k)

    def group(g, carry):
        for k in range(GROUP):
            soften(GROUP * g + k, k)
        for k in range(GROUP):
            score(jnp.minimum(GROUP * (g + 1) + k, HEADS - 1), k)
        for k in range(GROUP):
            mix(GROUP * g + k)
        return carry

    lax.fori_loop(0, HEADS // GROUP, group, 0)
    mixed = s.acc[...].astype(low)
    s.left[1, :, rows] = mixed.T
    s.wide[0, rows, 3 * PART :] = mixed


def attend_out(i, s):
    rows = image_rows(i)
    s.acc[...] = product(s.wide[0, rows, 3 * PART :], s.wa[:, 3 * PART :])


def kernel_attention_backward(i, s):
    rows = image_rows(i)
    gb = back_start(i, s)
    s.wide[1, rows, 3 * PART :] = gb
    s.gb[...] = product_nt(gb, s.wa[:, 3 * PART :]).astype(low)
    s.wacc[...] = jnp.zeros(s.wacc.shape, jnp.float32)

    zero = jnp.zeros((), low)

    def grad_of_probs(h):
        start, inside = head_window(h)
        grad_head = jnp.where(inside, s.gb[:, window(start, 0)], zero)
        return product_nt(grad_head, s.wide[0, rows, window(start, 2)])

    def grad_of_scores(h, grad_probs):
        place = prob_place(i, h)
        probs = s.wb[place[0], place[1]].astype(jnp.float32)
        mixed = jnp.sum(probs * grad_probs, axis=-1, keepdims=True)
        return (probs * (grad_probs - mixed)).astype(low)

    def grads_of_qkv(h, grad_scores):
        start, inside = head_window(h)
        place = prob_place(i, h)
        query = jnp.where(inside, s.wide[0, rows, window(start, 0)], zero)
        key = jnp.where(inside, s.wide[0, rows, window(start, 1)], zero)
        grad_head = jnp.where(inside, s.gb[:, window(start, 0)], zero)
        s.wacc[:, window(start, 2)] += contract_rows(s.wb[place[0], place[1]], grad_head)
        s.wacc[:, window(start, 0)] += product(grad_scores, key)
        s.wacc[:, window(start, 1)] += contract_rows(grad_scores, query)

    def group(g, carry):
        heads = [GROUP * g + k for k in range(GROUP)]
        first = [grad_of_probs(h) for h in heads]
        second = [grad_of_scores(h, value) for h, value in zip(heads, first)]
        for h, value in zip(heads, second):
            grads_of_qkv(h, value)
        return carry

    lax.fori_loop(0, HEADS // GROUP, group, 0)
    scale = HEAD ** (-0.5)
    for part, factor in ((0, scale), (1, scale), (2, 1.0)):
        cols = pl.ds(part * PART, PART)
        grads = (s.wacc[:, cols] * factor).astype(low)
        s.wide[1, rows, cols] = grads
        s.grad_rows[i, :, pl.ds((3 + part) * PART, PART)] = jnp.sum(
            grads.astype(jnp.float32), axis=0, keepdims=True
        )
    s.acc[...] = jnp.zeros(s.acc.shape, jnp.float32)

    def tile(j, carry):
        cols = spread(j, THIRD)
        s.acc[...] += product_nt(s.wide[1, rows, cols], s.wa[:, cols])
        return carry

    lax.fori_loop(0, 3 * PART // THIRD, tile, 0)
    back_finish(i, s)


def places():
    dp, pipe = lax.axis_index("dp"), lax.axis_index("pipe")
    core, x_bit, y_bit = dp % 2, (dp // 2) % 2, dp // 4
    sib = dp + 1 - 2 * core
    step_x, step_y = 2 - 4 * x_bit, 4 - 8 * y_bit
    return SimpleNamespace(
        dp=dp,
        pipe=pipe,
        core=core,
        sib=sib,
        x=dp + step_x,
        y=dp + step_y,
        d=dp + step_x + step_y,
        step_x=step_x,
        step_y=step_y,
        x_bit=x_bit,
        y_bit=y_bit,
    )


def relay(s, at, phase):
    def piece(j, role, first=0, count=BLOCK):
        index = 4 * j + role
        row = pl.multiple_of(BLOCK * (index % 8) + first, 16)
        return s.wb.at[pl.ds(row, count), spread(2 + index // 8, PART)]

    def copy(j, kind, source, target, device):
        return pltpu.make_async_remote_copy(
            src_ref=source,
            dst_ref=target,
            send_sem=s.relay_send.at[phase, j, kind],
            recv_sem=s.relay_recv.at[phase, j, kind],
            device_id=device,
            device_id_type=MESH,
        )

    def down_place(j):
        if phase == 0:
            return s.wb.at[block_rows(at.d), spread(j, PART)]
        return s.wa.at[block_rows(j), pl.ds(3 * PART, PART)]

    def hop(j, role, first, kind, device):
        part = (0, 80) if first else (80, 64)
        return copy(j, kind, piece(j, role[0], *part), piece(j, role[1], *part), device)

    x, y = (at.x, at.pipe), (at.y, at.pipe)

    def send(j, kind):
        if kind == 1:
            return hop(j, (0, 1), True, 1, x)
        if kind == 2:
            return hop(j, (0, 2), False, 2, y)
        if kind == 3:
            return hop(j, (1, 3), True, 3, y)
        if kind == 4:
            return hop(j, (2, 3), False, 4, x)
        return copy(j, 5, piece(j, 3), down_place(j), (at.dp, 1))

    def arrival(j, kind):
        if kind == 0:
            return copy(j, 0, piece(j, 0), piece(j, 0), (at.dp, 1))
        if kind == 1:
            return hop(j, (1, 1), True, 1, x)
        if kind == 2:
            return hop(j, (2, 2), False, 2, y)
        if kind == 3:
            return hop(j, (3, 3), True, 3, y)
        return hop(j, (3, 3), False, 4, x)

    def step(k, carry):
        @pl.when(k < 4)
        def _():
            arrival(k, 0).wait_recv()
            send(k, 1).start()
            send(k, 2).start()

        @pl.when((k >= 1) & (k <= 4))
        def _():
            arrival(k - 1, 1).wait_recv()
            send(k - 1, 3).start()
            arrival(k - 1, 2).wait_recv()
            send(k - 1, 4).start()

        @pl.when(k >= 2)
        def _():
            arrival(k - 2, 3).wait_recv()
            arrival(k - 2, 4).wait_recv()
            send(k - 2, 5).start()

        return carry

    def run():
        lax.fori_loop(0, 6, step, 0)

    def done():
        def each(j, carry):
            for kind in range(1, 6):
                send(j, kind).wait_send()
            return carry

        lax.fori_loop(0, 4, each, 0)

    return SimpleNamespace(
        run=run,
        done=done,
        up=lambda j, source: copy(j, 0, source, piece(j, 0), (at.dp, 2)),
        down=lambda j: copy(j, 5, down_place(j), down_place(j), (at.dp, 2)),
    )


def gather_weights(s, at, chunks, between, ready, helper=None, helped=(), before=None):
    def held(k):
        return (s.wa if k < 4 else s.wb), pl.ds((k % 4) * PART, PART)

    def piece(k, block, first=0, count=BLOCK):
        ref, cols = held(k)
        return ref.at[pl.ds(pl.multiple_of(block * BLOCK + first, 16), count), cols]

    def copy(k, kind, ref, target, source=None):
        return pltpu.make_async_remote_copy(
            src_ref=ref if source is None else source,
            dst_ref=ref,
            send_sem=s.gather_send.at[k, kind],
            recv_sem=s.gather_recv.at[k, kind],
            device_id=(target, at.pipe),
            device_id_type=MESH,
        )

    def via_y(k):
        return (0, 80) if k % 2 == 0 else (0, 64)

    def via_x(k):
        return (80, 64) if k % 2 == 0 else (64, 80)

    sib_x, sib_y, sib_d = (
        at.sib + at.step_x,
        at.sib + at.step_y,
        at.sib + at.step_x + at.step_y,
    )

    def sends(k):
        shard = s.in_shard if k < 4 else s.out_shard
        source = shard.at[:, pl.ds((k % 4) * PART, PART)]
        return {
            0: lambda: copy(k, 0, piece(k, at.dp), at.x, source),
            1: lambda: copy(k, 1, piece(k, at.dp), at.y, source),
            2: lambda: copy(k, 2, piece(k, at.dp), at.sib, source),
            3: lambda: copy(k, 3, piece(k, at.x), at.sib),
            4: lambda: copy(k, 4, piece(k, at.x, *via_y(k)), at.y),
            5: lambda: copy(k, 5, piece(k, at.y), at.sib),
            6: lambda: copy(k, 6, piece(k, at.y, *via_x(k)), at.x),
            7: lambda: copy(k, 7, piece(k, at.d), at.sib),
        }

    def arrivals(k):
        return {
            0: lambda: copy(k, 0, piece(k, at.x), at.x),
            1: lambda: copy(k, 1, piece(k, at.y), at.y),
            2: lambda: copy(k, 2, piece(k, at.sib), at.sib),
            3: lambda: copy(k, 3, piece(k, sib_x), at.sib),
            4: lambda: copy(k, 4, piece(k, at.d, *via_y(k)), at.y),
            5: lambda: copy(k, 5, piece(k, sib_y), at.sib),
            6: lambda: copy(k, 6, piece(k, at.d, *via_x(k)), at.x),
            7: lambda: copy(k, 7, piece(k, sib_d), at.sib),
        }

    def start(k, *kinds):
        for kind in kinds:
            sends(k)[kind]().start()

    def arrive(k, *kinds):
        for kind in kinds:
            arrivals(k)[kind]().wait_recv()

    def up(k):
        return helper.up(k - 4, s.out_shard.at[:, pl.ds((k - 4) * PART, PART)])

    for k in range(2):
        start(k, 0, 1, 2)
    for k in helped:
        up(k).start()
    if before is not None:
        before()
    for k in range(chunks + 2):
        if k < chunks:
            arrive(k, 0)
            start(k, 3)
            if k not in helped:
                start(k, 4)
            arrive(k, 1)
            start(k, 5)
            if k not in helped:
                start(k, 6)
            if k + 2 < chunks:
                start(k + 2, 0, 1, 2)
            between(k)
        if 1 <= k <= chunks:
            if k - 1 in helped:
                helper.down(k - 5).wait_recv()
            else:
                arrive(k - 1, 4, 6)
            start(k - 1, 7)
        if k >= 2:
            arrive(k - 2, 2, 3, 5, 7)
            ready(k - 2)
    for k in range(chunks):
        for kind in range(8):
            if k not in helped or kind not in (4, 6):
                sends(k)[kind]().wait_send()
    for k in helped:
        up(k).wait_send()


def scatter_grads(s, at, is_feed, swap, outputs, inputs):
    total = jnp.where(is_feed, 32, 16)
    helper = relay(s, at, 1)

    def up(j):
        return helper.up(j, s.wa.at[block_rows(4 + j), pl.ds(3 * PART, PART)])

    chip = at.dp // 2
    chip_x, chip_y = chip + 1 - 2 * at.x_bit, chip + 2 - 4 * at.y_bit
    chip_d = chip_x + 2 - 4 * at.y_bit

    def unit(u):
        stage = u // 4
        second = is_feed & ((stage == 1) | (stage == 4) | (stage >= 6))
        matrix = jnp.where(second, 1, 0)
        group = jnp.where(stage < 2, 0, jnp.where(second, stage - 4, stage - 1))
        group = jnp.where(stage == 4, 1, jnp.where(stage == 5, 3, group))
        group = jnp.where(is_feed, group, stage)
        v, turn, n = u % 4, u % 2, (u % 4) // 2
        near = chip_x + turn * (chip_y - chip_x)
        block = jnp.where(group == 0, chip_d, jnp.where(group == 3, chip, near))
        part = jnp.where(
            group == 3, v, jnp.where(group == 2, 2 * (1 - turn) + n, 2 * turn + n)
        )
        return matrix, group, turn, n, block, part

    def sib_place(u):
        return s.wb.at[block_rows(u % 8), spread(u // 8, PART)]

    def near_place(matrix, turn, slot):
        index = turn * 12 + matrix * 6 + slot
        return s.wa.at[block_rows(index % 8), spread(index // 8, PART)]

    def sib_copy(u):
        return pltpu.make_async_remote_copy(
            src_ref=s.stage.at[u % 4, block_rows(1 - at.core), :],
            dst_ref=sib_place(u),
            send_sem=s.sib_send.at[u],
            recv_sem=s.sib_recv.at[u],
            device_id=(at.sib, at.pipe),
            device_id_type=MESH,
        )

    def near_copy(matrix, turn, slot):
        return pltpu.make_async_remote_copy(
            src_ref=s.near_stage.at[turn, slot],
            dst_ref=near_place(matrix, turn, slot),
            send_sem=s.near_send.at[turn, matrix * 6 + slot],
            recv_sem=s.near_recv.at[turn, matrix * 6 + slot],
            device_id=(at.x + turn * (at.y - at.x), at.pipe),
            device_id_type=MESH,
        )

    def compute(u):
        matrix, group, turn, n, block, part = unit(u)
        first = is_feed & (matrix == 0)
        lhs = jnp.where(first | (jnp.logical_not(is_feed) & (part == 3)), 1, 0)
        rhs = jnp.where(first, 0, 1)

        @pl.when(u >= 4)
        def _():
            sib_copy(u - 4).wait_send()

        rows = pl.ds(pl.multiple_of(block * 288, 16), 288)
        s.stage[u % 4] = product(s.left[lhs, rows, :], s.wide[rhs, :, spread(part, PART)]).astype(
            low
        )
        sib_copy(u).start()

    def settle(u):
        matrix, group, turn, n, block, part = unit(u)
        sib_copy(u).wait_recv()
        own = s.stage[u % 4, block_rows(at.core), :].astype(jnp.float32)
        place = (block_rows(u % 8), spread(u // 8, PART))
        value = own + s.wb[place].astype(jnp.float32)
        slot = group * 2 + n
        first = is_feed & (matrix == 0)
        helped = (at.pipe == 1) & (matrix == 1)

        def taken(from_turn, from_slot):
            near_copy(matrix, from_turn, from_slot).wait_recv()
            index = from_turn * 12 + matrix * 6 + from_slot
            return s.wa[block_rows(index % 8), spread(index // 8, PART)].astype(jnp.float32)

        @pl.when(group < 3)
        def _():
            goes_up = (group == 0) & helped

            @pl.when((matrix == 1) & jnp.logical_not(goes_up))
            def _():
                near_copy(0, turn, slot).wait_send()

            @pl.when(goes_up)
            def _():
                s.wa[block_rows(4 + part), 3 * PART :] = value.astype(low)

            @pl.when(goes_up)
            def _():
                up(part).start()

            @pl.when(jnp.logical_not(goes_up) & ((group < 2) | helped))
            def _():
                s.near_stage[turn, slot] = value.astype(low)

            @pl.when((group == 2) & jnp.logical_not(helped))
            def _():
                s.near_stage[turn, slot] = (value + taken(1 - turn, n)).astype(low)

            @pl.when(jnp.logical_not(goes_up))
            def _():
                near_copy(matrix, turn, slot).start()

        @pl.when(group == 3)
        def _():
            @pl.when((matrix > 0) | (part >= 2))
            def _():
                grad_copy(s.in_grad, part).wait()

            whole = value + taken(0, 2 + part) + taken(1, (part + 2) % 4 + 2)
            s.wacc[0:BLOCK, spread(1 + part % 2, PART)] = whole

            @pl.when(helped)
            def _():
                helper.down(part).wait_recv()
                rest = s.wa[block_rows(part), 3 * PART :].astype(jnp.float32)
                s.wacc[0:BLOCK, spread(1 + part % 2, PART)] += rest

            @pl.when(first)
            def _():
                grad_copy(s.out_grad, part).start()

            @pl.when(jnp.logical_not(first))
            def _():
                grad_copy(s.in_grad, part).start()

    def grad_copy(held, part):
        return pltpu.make_async_copy(
            s.wacc.at[pl.ds(0, BLOCK), spread(1 + part % 2, PART)],
            held.at[0, :, spread(part, PART)],
            s.out_sem.at[part % 2],
        )

    def step(u, carry):
        @pl.when(u < total)
        def _():
            compute(u)

        @pl.when(u >= 2)
        def _():
            settle(u - 2)

        return carry

    def leg(n, carry):
        third = jnp.where(is_feed, 20, total - 5)
        fourth = jnp.where(at.pipe == 1, 27, jnp.where(is_feed, 31, 14))
        marks = (0, 6, 10, third, fourth, total + 2)

        def mark(k):
            value = marks[0]
            for place in range(1, 6):
                value = jnp.where(k == place, marks[place], value)
            return value

        lax.fori_loop(mark(n), mark(n + 1), step, 0)

        @pl.when(n == 0)
        def _():
            condition_back(s, at, swap, is_feed)

        @pl.when(n == 1)
        def _():
            condition_token(s, at, swap, is_feed)

        @pl.when((n == 2) & jnp.logical_not(is_feed))
        def _():
            for copy in time_outs(s):
                copy.wait()

        @pl.when((n == 2) & (at.pipe < 2))
        def _():
            condition_sum(s, at, swap, is_feed)

        @pl.when((n == 2) & (at.pipe == 3))
        def _():
            outputs()

        @pl.when(n == 3)
        def _():
            @pl.when(at.pipe == 2)
            def _():
                helper.run()
                condition_sum(s, at, swap, is_feed)

            @pl.when(at.pipe < 2)
            def _():
                condition_table(s, at, swap, is_feed)

            @pl.when(at.pipe == 0)
            def _():
                inputs()

        return carry

    for copy in shard_copies(s, is_feed):
        copy.start()
    lax.fori_loop(0, 5, leg, 0)
    matrices = jnp.where(is_feed, 2, 1)

    def rest(k, carry):
        sib_copy(total - 4 + k).wait_send()
        return carry

    lax.fori_loop(0, 4, rest, 0)
    for turn in range(2):
        for slot in range(6):
            last = matrices - 1 if slot >= 2 else jnp.where(at.pipe == 1, 0, matrices - 1)
            near_copy(last, turn, slot).wait_send()

    @pl.when(at.pipe == 1)
    def _():
        for j in range(4):
            up(j).wait_send()

    @pl.when(at.pipe == 2)
    def _():
        helper.done()

    for part in (2, 3):
        grad_copy(s.in_grad, part).wait()

    @pl.when(at.pipe == 3)
    def _():
        condition_sum(s, at, swap, is_feed)

    @pl.when(at.pipe >= 2)
    def _():
        condition_table(s, at, swap, is_feed)


def exchange(s, at, number, piece, landing):
    def copy(target, source):
        return pltpu.make_async_remote_copy(
            src_ref=piece(target),
            dst_ref=landing(source),
            send_sem=s.swap_send.at[number, target],
            recv_sem=s.swap_recv.at[number, source],
            device_id=(target, at.pipe),
            device_id_type=MESH,
        )

    others = [(at.dp + k) % 8 for k in range(1, 8)]

    def start():
        for other in others:
            copy(other, at.dp).start()

    def arrive():
        for other in others:
            copy(other, other).wait_recv()

    def done():
        for other in others:
            copy(other, at.dp).wait_send()

    return SimpleNamespace(start=start, arrive=arrive, done=done)


def exchanges(s, at):
    def pair(j):
        return pl.ds(2 * j, 2)

    return SimpleNamespace(
        rows=exchange(s, at, 0, lambda j: s.cond_in, lambda j: s.rows.at[pair(j)]),
        mods=exchange(s, at, 1, lambda j: s.mod_parts.at[pair(j)], lambda j: s.mod_all.at[j]),
        tokens=exchange(s, at, 2, lambda j: s.token, lambda j: s.token_all.at[pair(j)]),
        times=exchange(s, at, 3, lambda j: s.time_parts.at[pair(j)], lambda j: s.time_all.at[j]),
        grads=exchange(s, at, 4, lambda j: s.grad_rows, lambda j: s.grad_all.at[pair(j)]),
        backs=exchange(s, at, 5, lambda j: s.back, lambda j: s.back_all.at[j]),
        ends=exchange(s, at, 6, lambda j: s.end, lambda j: s.end_all.at[j]),
    )


def shard_copies(s, is_feed):
    copies = []
    for part in range(3):
        cols = pl.ds(part * PART, PART)
        rows = pl.ds(part * BLOCK, BLOCK)
        copies.append((s.mod_shard.at[:, cols], s.norm.at[rows, :]))
        copies.append((s.out_shard.at[:, cols], s.branch.at[rows, :]))
    copies.append((s.out_shard.at[:, pl.ds(3 * PART, PART)], s.gb.at[pl.ds(0, BLOCK), :]))
    return [
        pltpu.make_async_copy(source, target, s.shard_sem.at[k])
        for k, (source, target) in enumerate(copies)
    ]


def shard_part(ref, part):
    return ref[pl.ds(part * BLOCK, BLOCK), :]


def stack_rows(source, target, width):
    for k in range(16):
        target[k : k + 1, 0:width] = source[k, :, 0:width]


def chosen(at):
    places = lax.broadcasted_iota(jnp.int32, (PART, BLOCK), 0)
    lanes = lax.broadcasted_iota(jnp.int32, (PART, BLOCK), 1)
    return jnp.where(places == lanes + at.dp * BLOCK, 1.0, 0.0).astype(low)


def condition_front(s, at, swap, is_feed):
    for copy in shard_copies(s, is_feed):
        copy.start()
    s.rows[pl.ds(2 * at.dp, 2)] = s.cond_in[...]
    s.grad_rows[...] = jnp.zeros(s.grad_rows.shape, jnp.float32)
    swap.rows.arrive()
    stack_rows(s.rows, s.flat, PART)
    condition = s.flat[:, 0:PART]
    conditioner = (condition * (1.0 / (1.0 + jnp.exp(-condition)))).astype(low)
    pick = chosen(at)
    own = product(conditioner, pick).astype(low)
    s.own_cond[...] = own
    for copy in shard_copies(s, is_feed):
        copy.wait()
    for part in range(3):
        s.flat[:, part * PART : (part + 1) * PART] = product(own, shard_part(s.norm, part))
    s.flat[:, 3 * PART : 4 * PART] = product(own, s.gb[0:BLOCK, :])
    for k in range(16):
        s.mod_parts[k] = s.flat[k : k + 1, 0 : 4 * PART]
    swap.mods.start()
    s.mod_all[at.dp] = s.mod_parts[pl.ds(2 * at.dp, 2)]


def condition_mods(s, at, swap, is_feed):
    swap.mods.arrive()
    for i in range(2):
        total = jnp.sum(s.mod_all[:, i], axis=0)
        s.mod[i] = total[:, 0 : 3 * PART]
        s.token[i] = total[:, 3 * PART :]

    @pl.when(jnp.logical_not(is_feed))
    def _():
        swap.tokens.start()
        s.token_all[pl.ds(2 * at.dp, 2)] = s.token[...]


def condition_tokens(s, at, swap, is_feed):
    @pl.when(jnp.logical_not(is_feed))
    def _():
        swap.tokens.arrive()
        stack_rows(s.token_all, s.flat, PART)
        own_token = product(s.flat[:, 0:PART].astype(low), chosen(at)).astype(low)
        s.own_token[...] = own_token
        for part in range(3):
            s.flat[:, part * PART : (part + 1) * PART] = product(
                own_token, shard_part(s.branch, part)
            )
        for k in range(16):
            s.time_parts[k] = s.flat[k : k + 1, 0 : 3 * PART]
        swap.times.start()
        s.time_all[at.dp] = s.time_parts[pl.ds(2 * at.dp, 2)]


def condition_times(s, at, swap, is_feed):
    @pl.when(jnp.logical_not(is_feed))
    def _():
        swap.times.arrive()
        for i in range(2):
            s.time[i] = jnp.sum(s.time_all[:, i], axis=0)


def end_copy(s, at, plane):
    return pltpu.make_async_remote_copy(
        src_ref=s.end_parts.at[at.pipe],
        dst_ref=s.end_parts.at[at.pipe],
        send_sem=s.end_send.at[plane],
        recv_sem=s.end_recv.at[at.pipe],
        device_id=(at.dp, plane),
        device_id_type=MESH,
    )


def end_arrival(s, at, plane):
    return pltpu.make_async_remote_copy(
        src_ref=s.end_parts.at[plane],
        dst_ref=s.end_parts.at[plane],
        send_sem=s.end_send.at[plane],
        recv_sem=s.end_recv.at[plane],
        device_id=(at.dp, plane),
        device_id_type=MESH,
    )


def mod_out(s):
    return pltpu.make_async_copy(
        s.wacc.at[pl.ds(0, BLOCK), :], s.mod_grad.at[0], s.shard_sem.at[0]
    )


def time_outs(s):
    held = s.out_grad.at[0]
    return (
        pltpu.make_async_copy(
            s.wacc.at[pl.ds(0, BLOCK), :], held.at[:, pl.ds(0, 3 * PART)], s.shard_sem.at[0]
        ),
        pltpu.make_async_copy(
            s.acc.at[pl.ds(0, BLOCK), :], held.at[:, pl.ds(3 * PART, PART)], s.shard_sem.at[1]
        ),
    )


def condition_back(s, at, swap, is_feed):
    s.grad_all[pl.ds(2 * at.dp, 2)] = s.grad_rows[...]
    swap.grads.arrive()
    stack_rows(s.grad_all, s.flat, 6 * PART)
    for copy in shard_copies(s, is_feed):
        copy.wait()

    @pl.when(jnp.logical_not(is_feed))
    def _():
        token = jnp.zeros((16, BLOCK), jnp.float32)
        for part in range(3):
            grads = s.flat[:, (3 + part) * PART : (4 + part) * PART].astype(low)
            token += product_nt(grads, shard_part(s.branch, part))
        s.back[...] = product_nt(token.astype(low), chosen(at)).astype(low)
        swap.backs.start()
        s.back_all[at.dp] = s.back[...]

    own = s.own_cond[...]
    s.end[...] = jnp.zeros(s.end.shape, jnp.float32)
    for part in range(3):
        cols = slice(part * PART, (part + 1) * PART)
        grads = s.flat[:, cols].astype(low)
        s.wacc[0:BLOCK, cols] = contract_rows(own, grads)
        s.end[...] += product_nt(grads, shard_part(s.norm, part))
    mod_out(s).start()


def condition_token(s, at, swap, is_feed):
    mod_out(s).wait()

    @pl.when(jnp.logical_not(is_feed))
    def _():
        for part in range(3):
            grads = s.flat[:, (3 + part) * PART : (4 + part) * PART].astype(low)
            s.wacc[0:BLOCK, part * PART : (part + 1) * PART] = contract_rows(
                s.own_token[...], grads
            )
        swap.backs.arrive()
        whole = jnp.zeros((16, PART), jnp.float32)
        for k in range(8):
            whole += s.back_all[k].astype(jnp.float32)
        whole = whole.astype(low)
        s.acc[0:BLOCK, :] = contract_rows(s.own_cond[...], whole)
        s.end[...] += product_nt(whole, s.gb[0:BLOCK, :])
        for copy in time_outs(s):
            copy.start()

    s.end_parts[at.pipe] = s.end[...]
    for k in range(1, 4):
        end_copy(s, at, (at.pipe + k) % 4).start()


def condition_sum(s, at, swap, is_feed):
    for k in range(1, 4):
        end_arrival(s, at, (at.pipe + k) % 4).wait_recv()
    s.end[...] = s.end_parts[0] + s.end_parts[1] + s.end_parts[2] + s.end_parts[3]
    swap.ends.start()
    s.end_all[at.dp] = s.end[...]


def condition_table(s, at, swap, is_feed):
    swap.ends.arrive()
    for k in range(8):
        s.flat[:, BLOCK * k : BLOCK * (k + 1)] = s.end_all[k]
    whole = s.flat[:, 0:PART]
    stack_rows(s.rows, s.flat, PART)
    condition = s.flat[:, 0:PART]
    gate = 1.0 / (1.0 + jnp.exp(-condition))
    grads = whole * (gate * (1.0 + condition * (1.0 - gate)))
    for k in range(3):
        term = grads.astype(low)
        s.terms[16 * k : 16 * (k + 1), :] = term
        grads = grads - term.astype(jnp.float32)
    lanes = lax.broadcasted_iota(jnp.int32, (1, 1024), 1).astype(jnp.float32)
    for k in range(16):
        label = s.rows[k, :, PART : PART + 1]
        s.flat[k : k + 1, 0:1024] = jnp.where(lanes == label, 1.0, 0.0)
    hot = s.flat[:, 0:1024].astype(low)
    for k in range(3):
        s.hot[16 * k : 16 * (k + 1), :] = hot


def condition_done(s, at, swap, is_feed):
    for each in (swap.rows, swap.mods, swap.grads, swap.ends):
        each.done()
    for k in range(1, 4):
        end_copy(s, at, (at.pipe + k) % 4).wait_send()

    @pl.when(jnp.logical_not(is_feed))
    def _():
        for each in (swap.tokens, swap.times, swap.backs):
            each.done()


def mega_body(*refs):
    s = SimpleNamespace(**dict(zip(REFS, refs)))
    at = places()
    is_feed = at.pipe % 2 == 1
    pipe = at.pipe
    barrier = pltpu.get_barrier_semaphore()
    swap = exchanges(s, at)
    targets = [((at.dp + k) % 8, pipe) for k in range(1, 8)]
    targets += [(at.dp, (pipe + k) % 4) for k in range(1, 4)]
    for target in targets:
        pl.semaphore_signal(barrier, inc=1, device_id=target, device_id_type=MESH)
    pl.semaphore_wait(barrier, len(targets))
    swap.rows.start()

    def remote(source, target, send, recv, plane):
        return pltpu.make_async_remote_copy(
            src_ref=source,
            dst_ref=target,
            send_sem=send,
            recv_sem=recv,
            device_id=(at.dp, plane),
            device_id_type=MESH,
        )

    def share(i, plane):
        return pl.ds(pl.multiple_of(i * ROWS + plane * 64, 64), 64)

    def token_copy(i, plane):
        return remote(
            s.tokens.at[i],
            s.xin.at[share(i, plane), :],
            s.share_send.at[0, i],
            s.xin_recv.at[i, plane],
            0,
        )

    def cotangent_copy(i, plane):
        return remote(
            s.cotangent.at[i],
            s.gin.at[share(i, plane), :],
            s.share_send.at[1, i],
            s.gin_recv.at[i, plane],
            3,
        )

    def next_copy(i):
        whole = image_rows(i)
        return remote(
            s.xout.at[whole, :],
            s.xin.at[whole, :],
            s.hop_send.at[0, i],
            s.xin_recv.at[i, 0],
            jnp.minimum(pipe + 1, 3),
        )

    def back_copy(i):
        whole = image_rows(i)
        return remote(
            s.gout.at[whole, :],
            s.gin.at[whole, :],
            s.hop_send.at[1, i],
            s.gin_recv.at[i, 3],
            jnp.maximum(pipe - 1, 0),
        )

    def output_copy(i, plane):
        return remote(
            s.xout.at[share(i, plane), :],
            s.out_tokens.at[i],
            s.final_send.at[0, i, plane],
            s.final_recv.at[0, i],
            plane,
        )

    def input_copy(i, plane):
        return remote(
            s.gout.at[share(i, plane), :],
            s.input_share.at[i],
            s.final_send.at[1, i, plane],
            s.final_recv.at[1, i],
            plane,
        )

    def local(source, target, index):
        return pltpu.make_async_copy(source, target, s.local_sem.at[index])

    own_in = local(s.in_shard, s.wa.at[block_rows(at.dp), :], 0)
    own_out = local(s.out_shard, s.wb.at[block_rows(at.dp), :], 1)
    own_in.start()

    @pl.when(is_feed)
    def _():
        own_out.start()

    for i in range(2):
        own_tokens = local(s.tokens.at[i], s.xin.at[pl.ds(i * ROWS, 64), :], 2 + i)
        own_cotangent = local(s.cotangent.at[i], s.gin.at[pl.ds(i * ROWS + 192, 64), :], 4 + i)

        @pl.when(pipe == 0)
        def _():
            own_tokens.start()

        @pl.when(pipe == 3)
        def _():
            own_cotangent.start()

        @pl.when(pipe != 0)
        def _():
            token_copy(i, pipe).start()

    rounds = (condition_front, condition_mods, condition_tokens, condition_times)

    def between(k):
        if k < 4:
            rounds[k](s, at, swap, is_feed)
        if k == 1:
            for i in range(2):

                @pl.when(pipe != 3)
                def _():
                    cotangent_copy(i, pipe).start()

    def ready(k):
        if k == 0:

            def begin(i, carry):
                local(s.tokens.at[i], s.xin.at[share(i, 0), :], 2 + i).wait()
                for plane in range(1, 4):
                    token_copy(i, plane).wait_recv()
                front(i, s)
                return carry

            lax.fori_loop(0, 2, begin, 0)

        def one(n, carry):
            project(0, s, n)
            return carry

        if k == 1:
            lax.fori_loop(0, 2, one, 0)
        if k == 2:
            project(0, s, 2)
            attend_heads(0, s)

    own_in.wait()

    @pl.when(pipe == 0)
    def _():
        gather_weights(s, at, 4, between, ready)

    @pl.when(pipe == 2)
    def _():
        helper = relay(s, at, 0)

        gather_weights(s, at, 4, between, lambda k: None, before=helper.run)
        helper.done()

    def early(k):
        if k == 6:
            next_copy(0).wait_recv()
            front(0, s)
            feed_up(0, s)

    @pl.when(is_feed)
    def _():
        own_out.wait()

    @pl.when(pipe == 1)
    def _():
        gather_weights(s, at, 8, between, early, relay(s, at, 0), (4, 5, 6, 7))

    @pl.when(pipe == 3)
    def _():
        gather_weights(s, at, 8, between, lambda k: None)

    for i in range(2):

        @pl.when(pipe != 0)
        def _():
            token_copy(i, pipe).wait_send()

    def inputs(i):
        for plane in range(1, 4):
            input_copy(i, plane).start()
        local(s.gout.at[share(i, 0), :], s.input_share.at[i], 4 + i).start()

    def give_turn():
        next_copy(0).wait_send()
        pl.semaphore_signal(s.turn, inc=1, device_id=(at.sib, pipe), device_id_type=MESH)

    def step(n, carry):
        at_end = pipe == 3
        goes_forward = jnp.where(at_end, n % 2 == 0, n < 2)
        i = jnp.where(at_end, n // 2, n % 2)

        @pl.when(goes_forward)
        def _():
            @pl.when((pipe >= 2) | ((pipe == 1) & (i == 1)))
            def _():
                next_copy(i).wait_recv()

            @pl.when(is_feed)
            def _():
                @pl.when((pipe == 3) | (i == 1))
                def _():
                    front(i, s)
                    feed_up(i, s)

                feed_down(i, s)
                finish(i, s)

            @pl.when(jnp.logical_not(is_feed))
            def _():
                @pl.when(pipe != 0)
                def _():
                    front(i, s)

                @pl.when((pipe != 0) | (i == 1))
                def _():
                    def one(part, carry):
                        project(i, s, part)
                        return carry

                    lax.fori_loop(0, 3, one, 0)

                    @pl.when(pipe == 0)
                    def _():
                        give_turn()

                    attend_heads(i, s)

                attend_out(i, s)
                finish(i, s)

            @pl.when((pipe < 2) & (i == 0) & ((at.core == 0) | (pipe == 0)))
            def _():
                @pl.when(at.core == 1)
                def _():
                    pl.semaphore_wait(s.turn, 1)

                next_copy(0).start()

            @pl.when((pipe < 2) & (i == 1))
            def _():
                @pl.when((at.core == 1) & (pipe == 1))
                def _():
                    pl.semaphore_wait(s.turn, 1)
                    next_copy(0).start()

                @pl.when(pipe == 1)
                def _():
                    give_turn()

                pl.semaphore_wait(s.turn, 1)
                next_copy(1).start()
                next_copy(1).wait_send()

                @pl.when(at.core == 0)
                def _():
                    pl.semaphore_signal(
                        s.turn, inc=1, device_id=(at.sib, pipe), device_id_type=MESH
                    )

            @pl.when(pipe == 2)
            def _():
                next_copy(i).start()


        @pl.when(jnp.logical_not(goes_forward))
        def _():
            @pl.when(pipe == 3)
            def _():
                local(s.cotangent.at[i], s.gin.at[share(i, 3), :], 4 + i).wait()
                for plane in range(3):
                    cotangent_copy(i, plane).wait_recv()

            @pl.when(pipe != 3)
            def _():
                back_copy(i).wait_recv()

            @pl.when(is_feed)
            def _():
                kernel_feed_backward(i, s)

            @pl.when(jnp.logical_not(is_feed))
            def _():
                kernel_attention_backward(i, s)

            @pl.when(pipe != 0)
            def _():
                back_copy(i).start()

            @pl.when((pipe == 0) & (i == 0))
            def _():
                inputs(0)

        return carry

    lax.fori_loop(0, 4, step, 0)
    swap.grads.start()

    for target, sem in ((at.sib, 0), (at.x, 1), (at.y, 2)):
        pl.semaphore_signal(
            s.free.at[sem], inc=1, device_id=(target, pipe), device_id_type=MESH
        )
    for sem in range(3):
        pl.semaphore_wait(s.free.at[sem], 1)

    def last_inputs(*unused):
        @pl.when(pipe == 0)
        def _():
            inputs(1)

    def outputs(*unused):
        @pl.when(pipe == 3)
        def _():
            for i in range(2):
                for plane in range(3):
                    output_copy(i, plane).start()
                local(s.xout.at[share(i, 3), :], s.out_tokens.at[i], 2 + i).start()

    scatter_grads(s, at, is_feed, swap, outputs, last_inputs)
    condition_done(s, at, swap, is_feed)

    for i in range(2):

        @pl.when(pipe != 3)
        def _():
            cotangent_copy(i, pipe).wait_send()
            output_copy(i, pipe).wait_recv()

        @pl.when(pipe == 2)
        def _():
            next_copy(i).wait_send()

        @pl.when(pipe == 3)
        def _():
            for plane in range(3):
                output_copy(i, plane).wait_send()
            local(s.xout.at[share(i, 3), :], s.out_tokens.at[i], 2 + i).wait()

        @pl.when(pipe != 0)
        def _():
            back_copy(i).wait_send()
            input_copy(i, pipe).wait_recv()

        @pl.when(pipe == 0)
        def _():
            for plane in range(1, 4):
                input_copy(i, plane).wait_send()
            local(s.gout.at[share(i, 0), :], s.input_share.at[i], 4 + i).wait()

    s.input_grad[...] = s.input_share[...].astype(jnp.float32)


SCRATCH = dict(
    xin=pltpu.VMEM((512, 1152), low),
    gin=pltpu.VMEM((512, 1152), low),
    xout=pltpu.VMEM((512, 1152), low),
    gout=pltpu.VMEM((512, 1152), low),
    wa=pltpu.VMEM((1152, 4608), low),
    wb=pltpu.VMEM((1152, 4608), low),
    norm=pltpu.VMEM((512, 1152), low),
    left=pltpu.VMEM((2, 1152, 512), low),
    wide=pltpu.VMEM((2, 512, 4608), low),
    branch=pltpu.VMEM((512, 1152), low),
    acc=pltpu.VMEM((256, 1152), jnp.float32),
    gb=pltpu.VMEM((256, 1152), low),
    wacc=pltpu.VMEM((256, 3456), jnp.float32),
    stage=pltpu.VMEM((4, 288, 1152), low),
    near_stage=pltpu.VMEM((2, 6, 144, 1152), low),
    gather_send=pltpu.SemaphoreType.DMA((8, 8)),
    gather_recv=pltpu.SemaphoreType.DMA((8, 8)),
    sib_send=pltpu.SemaphoreType.DMA((32,)),
    sib_recv=pltpu.SemaphoreType.DMA((32,)),
    near_send=pltpu.SemaphoreType.DMA((2, 12)),
    near_recv=pltpu.SemaphoreType.DMA((2, 12)),
    out_sem=pltpu.SemaphoreType.DMA((2,)),
    share_send=pltpu.SemaphoreType.DMA((2, 2)),
    xin_recv=pltpu.SemaphoreType.DMA((2, 4)),
    gin_recv=pltpu.SemaphoreType.DMA((2, 4)),
    hop_send=pltpu.SemaphoreType.DMA((2, 2)),
    final_send=pltpu.SemaphoreType.DMA((2, 2, 4)),
    final_recv=pltpu.SemaphoreType.DMA((2, 2)),
    local_sem=pltpu.SemaphoreType.DMA((6,)),
    free=pltpu.SemaphoreType.REGULAR((3,)),
    turn=pltpu.SemaphoreType.REGULAR,
    shard_sem=pltpu.SemaphoreType.DMA((7,)),
    swap_send=pltpu.SemaphoreType.DMA((7, 8)),
    swap_recv=pltpu.SemaphoreType.DMA((7, 8)),
    relay_send=pltpu.SemaphoreType.DMA((2, 4, 6)),
    relay_recv=pltpu.SemaphoreType.DMA((2, 4, 6)),
    end_send=pltpu.SemaphoreType.DMA((4,)),
    end_recv=pltpu.SemaphoreType.DMA((4,)),
    mod=pltpu.VMEM((2, 1, 3456), jnp.float32),
    time=pltpu.VMEM((2, 1, 3456), jnp.float32),
    token=pltpu.VMEM((2, 1, 1152), jnp.float32),
    grad_rows=pltpu.VMEM((2, 1, 6912), jnp.float32),
    rows=pltpu.VMEM((16, 1, 1280), jnp.float32),
    flat=pltpu.VMEM((16, 6912), jnp.float32),
    own_cond=pltpu.VMEM((16, 144), low),
    own_token=pltpu.VMEM((16, 144), low),
    mod_parts=pltpu.VMEM((16, 1, 4608), jnp.float32),
    mod_all=pltpu.VMEM((8, 2, 1, 4608), jnp.float32),
    token_all=pltpu.VMEM((16, 1, 1152), jnp.float32),
    time_parts=pltpu.VMEM((16, 1, 3456), jnp.float32),
    time_all=pltpu.VMEM((8, 2, 1, 3456), jnp.float32),
    grad_all=pltpu.VMEM((16, 1, 6912), jnp.float32),
    back=pltpu.VMEM((16, 1152), low),
    back_all=pltpu.VMEM((8, 16, 1152), low),
    end=pltpu.VMEM((16, 144), jnp.float32),
    input_share=pltpu.VMEM((2, 64, 1152), low),
    end_parts=pltpu.VMEM((4, 16, 144), jnp.float32),
    end_all=pltpu.VMEM((8, 16, 144), jnp.float32),
)
REFS = (
    ["tokens", "cotangent", "in_shard", "out_shard", "mod_shard", "cond_in"]
    + ["out_tokens", "input_grad", "terms", "hot", "in_grad", "out_grad", "mod_grad"]
    + list(SCRATCH)
)


def mega(tokens, cotangent, in_shard, out_shard, mod_shard, cond_rows):
    anywhere = pl.BlockSpec(memory_space=pl.ANY)
    near = pl.BlockSpec(memory_space=pltpu.VMEM)

    def wide(array):
        return jax.ShapeDtypeStruct((1,) + array.shape, jnp.float32)

    return pl.pallas_call(
        mega_body,
        out_shape=(
            jax.ShapeDtypeStruct(tokens.shape, low),
            jax.ShapeDtypeStruct(tokens.shape, jnp.float32),
            jax.ShapeDtypeStruct((48, tokens.shape[2]), low),
            jax.ShapeDtypeStruct((48, 1024), low),
            wide(in_shard),
            wide(out_shard),
            wide(mod_shard),
        ),
        in_specs=[anywhere] * 5 + [near],
        out_specs=[anywhere] + [near] * 3 + [anywhere] * 3,
        scratch_shapes=list(SCRATCH.values()),
        compiler_params=pltpu.CompilerParams(
            collective_id=0, has_side_effects=True, vmem_limit_bytes=62 * 2**20
        ),
        cost_estimate=pl.CostEstimate(
            flops=25 * 10**9, bytes_accessed=10**7, transcendentals=10**7
        ),
        name="blocks",
    )(tokens, cotangent, in_shard, out_shard, mod_shard, cond_rows)


def last_body(terms, hot, *refs):
    sources, (table, *targets) = refs[:3], refs[3:7]
    value, *held, sems = refs[7:]
    classes = table.shape[0]
    pieces = [
        (source.at[0, pl.ds(48 * part, 48), :], stage.at[pl.ds(48 * part, 48), :],
         target.at[0, pl.ds(48 * part, 48), :], 3 * k + part)
        for k, (source, stage, target) in enumerate(zip(sources, held, targets))
        for part in range(3)
    ]
    takes = [pltpu.make_async_copy(s, v, sems.at[0, n]) for s, v, t, n in pieces]
    gives = [pltpu.make_async_copy(v, t, sems.at[1, n]) for s, v, t, n in pieces]
    for take in takes:
        take.start()
    for k in range(4):
        count = min(256, classes - 256 * k)
        value[k] = contract_rows(hot[:, 256 * k : 256 * (k + 1)], terms[...])
        part = pltpu.make_async_copy(
            value.at[k, pl.ds(0, count), :],
            table.at[pl.ds(256 * k, count), :],
            sems.at[1, 9 + k],
        )
        part.start()
        gives.append(part)
    for take, give in zip(takes, gives):
        take.wait()
        give.start()
    for give in gives:
        give.wait()


def last_copies(terms, hot, grads, classes):
    anywhere = pl.BlockSpec(memory_space=pl.ANY)
    near = pl.BlockSpec(memory_space=pltpu.VMEM)
    width = terms.shape[1]
    return pl.pallas_call(
        last_body,
        out_shape=[jax.ShapeDtypeStruct((classes, width), jnp.float32)]
        + [jax.ShapeDtypeStruct(grad.shape, jnp.float32) for grad in grads],
        in_specs=[near, near] + [anywhere] * 3,
        out_specs=[anywhere] * 4,
        scratch_shapes=[
            pltpu.VMEM((4, 256, width), jnp.float32),
            *[pltpu.VMEM(grad.shape[1:], jnp.float32) for grad in grads],
            pltpu.SemaphoreType.DMA((2, 13)),
        ],
        compiler_params=pltpu.CompilerParams(vmem_limit_bytes=62 * 2**20),
        name="table",
    )(terms, hot, *grads)


def fast_shards(
    tokens,
    cotangent,
    timesteps,
    labels,
    class_table,
    section_in_weights,
    section_out_weights,
    modulation_weights,
):
    model_width = tokens.shape[2]
    in_shard, out_shard, mod_shard = (
        section_in_weights[0],
        section_out_weights[0],
        modulation_weights[0],
    )
    images = tokens.shape[0]
    classes = class_table.shape[0]
    matches = labels[:, None] == lax.broadcasted_iota(jnp.int32, (images, classes), 1)
    condition = sinusoid(timesteps, model_width) + product(
        matches.astype(jnp.bfloat16), class_table
    )
    named = jnp.broadcast_to(labels.astype(jnp.float32)[:, None], (images, 128))
    cond_rows = jnp.concatenate([condition, named], axis=1)[:, None, :]
    out_tokens, input_grad, terms, hot, *grads = mega(
        tokens, cotangent, in_shard, out_shard, mod_shard, cond_rows
    )
    return (out_tokens, input_grad, *last_copies(terms, hot, grads, classes))


def solution(mesh):
    return jax.shard_map(
        fast_shards if mesh.shape["dp"] == 8 else shards,
        mesh=mesh,
        in_specs=(
            P("dp", "pipe", None),
            P("dp", "pipe", None),
            P("dp"),
            P("dp"),
            P(),
            P("pipe", "dp", None),
            P("pipe", "dp", None),
            P("pipe", "dp", None),
        ),
        out_specs=(
            P("dp", "pipe", None),
            P("dp", "pipe", None),
            P(),
            P("pipe", "dp", None),
            P("pipe", "dp", None),
            P("pipe", "dp", None),
        ),
        check_vma=False,
    )
```
